32 devices in a mesh: dp: 16 (over z, x, core), blk: 2 (over y).
Axes of the slice: x: 2, y: 2, z: 4, core: 2. Of those that a mesh axis runs over, the one named last changes fastest.
Arguments:
- tokens: bfloat16 [32, 512, 768], P('dp', 'blk'), may hold values from -6 to 6
- boxes: int32 [2, 32, 512], P(None, 'dp', 'blk'), may hold values from 0 to 1000
- lengths: int32 [32], P('dp'), may hold values from 40 to 512, as said below
- wqkv: bfloat16 [768, 2304], P('dp', 'blk'), may hold values from -0.21875 to 0.21875
- wbox: bfloat16 [768, 768], P('dp', 'blk'), may hold values from -0.375 to 0.375
- wout: bfloat16 [768, 768], P('dp', 'blk'), may hold values from -1.75 to 1.75
- wup: bfloat16 [768, 3072], P('dp', 'blk'), may hold values from -0.21875 to 0.21875
- wdown: bfloat16 [3072, 768], P('dp', 'blk'), may hold values from -0.109375 to 0.109375
- vectors: bfloat16 [9216], P(('dp', 'blk')), may hold values from -1.5 to 1.6
- cotangent: bfloat16 [32, 512, 768], P('dp', 'blk'), may hold values from -6 to 6
Outputs:
- output: bfloat16 [32, 512, 768], P('dp', 'blk')
- tokens_grad: float32 [32, 512, 768], P('dp', 'blk')
- wqkv_grad: float32 [768, 2304], P('dp', 'blk')
- wbox_grad: float32 [768, 768], P('dp', 'blk')
- wout_grad: float32 [768, 768], P('dp', 'blk')
- wup_grad: float32 [768, 3072], P('dp', 'blk')
- wdown_grad: float32 [3072, 768], P('dp', 'blk')
- vectors_grad: float32 [9216], P(('dp', 'blk'))
The draws below stay inside these ranges and needn't reach their ends.
Inputs may be any that keep to these rules, and one draw needn't show every extreme that they name: `lengths`: in each run of 2 pages that one index of dp holds, one page, drawn from the seed, has more than 256 real tokens; one page of all, drawn from the seed, has all 512.
All inputs are finite; a program needn't handle non-finite values.
Results may differ from the reference program's by a relative error of at most 0.023.
Values may be sent and summed in bfloat16 or wider, within the bound.
A program may use at most 256 MiB of HBM per device.

```python
import math
import jax
import jax.numpy as jnp
from jax import lax

D = 768
HEADS = 12
HEAD = 64
FF = 3072
FREQ = 192
PAGE_LEN = 512
BOX_DIM = 768
BLOCK = 256
PAGES_GRP = 2
PAGES = 32
MIN_LEN = 40


def draw_lengths(key, part):
    key = jax.random.fold_in(key, 11)
    first_key, second_key, third_key, fourth_key = jax.random.split(key, 4)
    drawn_lengths = jax.random.randint(first_key, (PAGES,), MIN_LEN, PAGE_LEN + 1)
    chosen_page = jax.random.randint(second_key, (PAGES // PAGES_GRP,), 0, PAGES_GRP)
    long_lengths = jax.random.randint(third_key, (PAGES,), PAGE_LEN - BLOCK + 1, PAGE_LEN + 1)
    full_page = jax.random.randint(fourth_key, (), 0, PAGES // PAGES_GRP)
    position_index = jnp.arange(PAGES, dtype=jnp.int32)
    owner_page = jnp.repeat(chosen_page, PAGES_GRP)
    is_long = position_index % PAGES_GRP == owner_page
    is_full = is_long & (position_index // PAGES_GRP == full_page)
    result = jnp.where(is_long, long_lengths, drawn_lengths)
    return jnp.where(is_full, PAGE_LEN, result).astype(jnp.int32)


def draw_vectors(key, part):
    key = jax.random.fold_in(key, 23)
    position_index = jnp.arange(8 * D + FF, dtype=jnp.int32)
    first_gain = (position_index >= 3 * D) & (position_index < 4 * D)
    second_gain = (position_index >= 6 * D + FF) & (position_index < 7 * D + FF)
    is_gain = first_gain | second_gain
    base_draw = jax.random.normal(key, position_index.shape, jnp.float32)
    result = jnp.where(is_gain, jnp.clip(1.0 + 0.2 * base_draw, 0.4, 1.6), jnp.clip(0.3 * base_draw, -1.5, 1.5))
    return result.astype(jnp.bfloat16)


def plant(entries, own_key, least, high):
    index_at = [jax.random.randint(jax.random.fold_in(own_key, axis), (), 0, length) for axis, length in enumerate(entries.shape)]
    longest = entries.shape.index(max(entries.shape))
    beside = index_at[:longest] + [(index_at[longest] + 1) % entries.shape[longest]] + index_at[longest + 1:]
    return entries.at[tuple(index_at)].set(least).at[tuple(beside)].set(high)


def block_scale(stream_key, dims, cuts, smallest, top_value):
    def one(position, parts):
        draws = jax.random.uniform(jax.random.fold_in(jax.random.fold_in(stream_key, 6), position), (parts,), jnp.float32, smallest / len(cuts), top_value / len(cuts))
        return jnp.repeat(jnp.exp(draws), dims[position] // parts).reshape((-1,) + (1,) * (len(dims) - position - 1))

    factor_of = one(*cuts[0])
    for cut in cuts[1:]:
        factor_of = factor_of * one(*cut)
    return factor_of


def gaussian(key, shape, deviation, reach, cuts=(), held_as=jnp.bfloat16):
    values = deviation * jax.random.normal(key, shape, jnp.float32)
    if cuts:
        values = values * block_scale(key, shape, cuts, -0.22, 0.18)
    return jnp.clip(values, -reach, reach).astype(held_as)


def setup_inputs(seed: int = 0) -> dict:
    streams_of = jax.random.split(jax.random.key(seed), 11)
    tokens = gaussian(streams_of[0], (PAGES, PAGE_LEN, D), 1.0, 6.0, ((0, 16), (1, 2)))
    boxes = plant(jax.random.randint(streams_of[1], (2, PAGES, PAGE_LEN), 0, 1001), jax.random.fold_in(streams_of[1], 1), 0, 1000).astype(jnp.int32)
    lengths = draw_lengths(jax.random.fold_in(streams_of[10], 71), 0)
    wqkv = gaussian(streams_of[3], (D, 3 * D), D ** -0.5, 0.21875, ((0, 16), (1, 2)))
    wbox = gaussian(streams_of[4], (D, BOX_DIM), (4 * HEAD) ** -0.5, 0.375, ((0, 16), (1, 2)))
    wout = gaussian(streams_of[5], (D, D), (max(D // 64, 1)) ** -0.5, 1.75, ((0, 16), (1, 2)))
    wup = gaussian(streams_of[6], (D, FF), D ** -0.5, 0.21875, ((0, 16), (1, 2)))
    wdown = gaussian(streams_of[7], (FF, D), FF ** -0.5, 0.109375, ((0, 16), (1, 2)))
    vectors = draw_vectors(jax.random.fold_in(streams_of[10], 71), 0)
    cotangent = gaussian(streams_of[9], (PAGES, PAGE_LEN, D), 1.0, 6.0, ((0, 16), (1, 2)))
    return {"tokens": tokens, "boxes": boxes, "lengths": lengths, "wqkv": wqkv, "wbox": wbox, "wout": wout, "wup": wup, "wdown": wdown, "vectors": vectors, "cotangent": cotangent}


@jax.custom_vjp
def low(v):
    return lax.optimization_barrier(v.astype(jnp.bfloat16)).astype(jnp.float32)

@jax.custom_vjp
def low_back(v):
    return v

def low_keep(v):
    return (low(v), None)

def low_pass(kept, grad):
    return (grad,)

def back_keep(v):
    return (v, None)

def back_low(kept, grad):
    return (low(grad),)
low.defvjp(low_keep, low_pass)
low_back.defvjp(back_keep, back_low)
EPSILON = 1e-12
MASKED = -1e+30
HIGHEST = lax.Precision.HIGHEST

def box_table(boxes):
    frequency = jnp.exp(jnp.arange(FREQ, dtype=jnp.float32) * (-math.log(10000.0) / FREQ))
    across = boxes[0].astype(jnp.float32)[..., None] * frequency
    upward = boxes[1].astype(jnp.float32)[..., None] * frequency
    return jnp.concatenate([jnp.cos(across), jnp.sin(across), jnp.cos(upward), jnp.sin(upward)], axis=-1)

def rotate(coeffs, own_table):
    cos_across, sin_across, cos_upward, sin_upward = jnp.split(own_table[..., None, :], 4, axis=-1)
    on_sine_across, on_cosine_across, on_sine_upward, on_cosine_upward = jnp.split(coeffs, 4, axis=-1)
    return jnp.concatenate([on_sine_across * sin_across + on_cosine_across * cos_across, on_cosine_across * sin_across - on_sine_across * cos_across, on_sine_upward * sin_upward + on_cosine_upward * cos_upward, on_cosine_upward * sin_upward - on_sine_upward * cos_upward], axis=-1)

def layer_norm(hidden, norm_gain, norm_shift):
    row_mean = lax.optimization_barrier(jnp.mean(hidden, axis=-1, keepdims=True))
    centered = hidden - row_mean
    variance = lax.optimization_barrier(jnp.mean(centered * centered, axis=-1, keepdims=True))
    return centered * lax.rsqrt(variance + EPSILON) * norm_gain + norm_shift

def unpack(vector_all, model_width, hidden_units):
    cuts = [model_width] * 5 + [hidden_units] + [model_width] * 3
    pieces = []
    offset = 0
    for length_here in cuts:
        pieces.append(vector_all[offset:offset + length_here])
        offset = offset + length_here
    return pieces

def encoder_layer(token_group, box_group, length_group, wqkv, wbox, wout, wup, wdown, vector_all):
    bias_query, bias_value, bias_out, gain_one, shift_one, bias_up, bias_down, gain_two, shift_two = unpack(vector_all, D, FF)
    page_count = token_group.shape[0]
    flat_tokens = token_group.reshape(-1, D)
    projected = jnp.dot(flat_tokens, wqkv, precision=HIGHEST, preferred_element_type=jnp.float32)
    query_low = low(low_back(projected[:, :D] + bias_query))
    key_low = low(low_back(projected[:, D:2 * D]))
    value_low = low(low_back(projected[:, 2 * D:] + bias_value))
    head_shape = (page_count, PAGE_LEN, HEADS, HEAD)
    heads_q = query_low.reshape(head_shape)
    heads_k = key_low.reshape(head_shape)
    heads_v = value_low.reshape(head_shape)
    own_table = box_table(box_group)
    coeffs = low_back(jnp.einsum('pqhd,hdc->pqhc', heads_q, wbox.reshape(HEADS, HEAD, BOX_DIM), precision=HIGHEST))
    box_query = low(rotate(coeffs, own_table))
    box_keys = low(own_table)
    text_part = jnp.einsum('pqhd,pkhd->phqk', heads_q, heads_k, precision=HIGHEST)
    box_part = jnp.einsum('pqhc,pkc->phqk', box_query, box_keys, precision=HIGHEST)
    raw_scores = low_back((text_part + box_part) * HEAD ** (-0.5))
    is_valid = jnp.arange(PAGE_LEN, dtype=jnp.int32)[None, :] < length_group[:, None]
    masked = jnp.where(is_valid[:, None, None, :], raw_scores, MASKED)
    probs_low = low(jax.nn.softmax(masked, axis=-1))
    mixed_heads = jnp.einsum('phqk,pkhd->pqhd', probs_low, heads_v, precision=HIGHEST)
    mixed_low = low(low_back(mixed_heads.reshape(-1, D)))
    attended = low_back(jnp.dot(mixed_low, wout, precision=HIGHEST, preferred_element_type=jnp.float32) + bias_out)
    first_norm = layer_norm(flat_tokens + attended, gain_one, shift_one)
    first_low = low(first_norm)
    pre_act = low_back(jnp.dot(first_low, wup, precision=HIGHEST, preferred_element_type=jnp.float32) + bias_up)
    hidden_low = low(jax.nn.gelu(pre_act, approximate=False))
    branch = low_back(jnp.dot(hidden_low, wdown, precision=HIGHEST, preferred_element_type=jnp.float32) + bias_down)
    return layer_norm(first_norm + branch, gain_two, shift_two).reshape(token_group.shape)

def reference(tokens, boxes, lengths, wqkv, wbox, wout, wup, wdown, vectors, cotangent):
    group_size = math.gcd(PAGES, 8)
    group_count = PAGES // group_size
    box_groups = jnp.transpose(boxes.reshape(2, group_count, group_size, PAGE_LEN), (1, 0, 2, 3))
    length_groups = lengths.reshape(group_count, group_size)

    def forward(token_all, wqkv_all, wbox_all, wout_all, wup_all, wdown_all, vector_all):

        def one_group(group_data):
            return encoder_layer(group_data[0], group_data[1], group_data[2], wqkv_all, wbox_all, wout_all, wup_all, wdown_all, vector_all)
        token_groups = token_all.reshape(group_count, group_size, PAGE_LEN, D)
        result = lax.map(jax.checkpoint(one_group), (token_groups, box_groups, length_groups))
        return result.reshape(PAGES, PAGE_LEN, D)
    output, pullback = jax.vjp(forward, tokens.astype(jnp.float32), wqkv.astype(jnp.float32), wbox.astype(jnp.float32), wout.astype(jnp.float32), wup.astype(jnp.float32), wdown.astype(jnp.float32), vectors.astype(jnp.float32))
    gradients = pullback(cotangent.astype(jnp.float32))
    return (output.astype(jnp.bfloat16), gradients[0], gradients[1], gradients[2], gradients[3], gradients[4], gradients[5], gradients[6])
```

```python
from functools import partial
import math

import jax
import jax.numpy as jnp
from jax import lax
from jax.sharding import PartitionSpec as P

HEADS = 12
HEAD = 64
FREQ = 192
BOX_DIM = 768

EPSILON = 1e-12
MASKED = -1e30


def box_table(boxes):
    frequency = jnp.exp(jnp.arange(FREQ, dtype=jnp.float32) * (-math.log(10000.0) / FREQ))
    across = boxes[0].astype(jnp.float32)[..., None] * frequency
    upward = boxes[1].astype(jnp.float32)[..., None] * frequency
    return jnp.concatenate(
        [jnp.cos(across), jnp.sin(across), jnp.cos(upward), jnp.sin(upward)], axis=-1
    )


def rotate(coeffs, own_table):
    cos_across, sin_across, cos_upward, sin_upward = jnp.split(own_table[..., None, :], 4, axis=-1)
    sa, ca, sb, cb = jnp.split(coeffs, 4, axis=-1)
    return jnp.concatenate(
        [
            sa * sin_across + ca * cos_across,
            ca * sin_across - sa * cos_across,
            sb * sin_upward + cb * cos_upward,
            cb * sin_upward - sb * cos_upward,
        ],
        axis=-1,
    )


def unrotate(grad_rows, own_table):
    cos_across, sin_across, cos_upward, sin_upward = jnp.split(own_table[..., None, :], 4, axis=-1)
    d1a, d2a, d1b, d2b = jnp.split(grad_rows, 4, axis=-1)
    return jnp.concatenate(
        [
            d1a * sin_across - d2a * cos_across,
            d1a * cos_across + d2a * sin_across,
            d1b * sin_upward - d2b * cos_upward,
            d1b * cos_upward + d2b * sin_upward,
        ],
        axis=-1,
    )


def normalize(hidden):
    row_mean = jnp.mean(hidden, axis=-1, keepdims=True)
    centered = hidden - row_mean
    inverse = lax.rsqrt(jnp.mean(centered * centered, axis=-1, keepdims=True) + EPSILON)
    return centered * inverse, inverse


def normalize_back(grad, unit, inverse, gain):
    scaled = grad * gain
    mean_grad = jnp.mean(scaled, axis=-1, keepdims=True)
    mean_unit = jnp.mean(scaled * unit, axis=-1, keepdims=True)
    d_hidden = inverse * (scaled - mean_grad - unit * mean_unit)
    return d_hidden, jnp.sum(grad * unit, axis=0), jnp.sum(grad, axis=0)


def unpack(vector_all, model_width, hidden_units):
    cuts = [model_width] * 5 + [hidden_units] + [model_width] * 3
    pieces = []
    offset = 0
    for length_here in cuts:
        pieces.append(vector_all[offset : offset + length_here])
        offset = offset + length_here
    return pieces


def dot32(a, b):
    return jnp.dot(a, b, preferred_element_type=jnp.float32)


def gather_weight(shard):
    part = lax.all_gather(shard, "blk", axis=1, tiled=True)
    return lax.all_gather(part, "dp", axis=0, tiled=True)


def scatter_weight(grad):
    part = lax.psum_scatter(grad.astype(jnp.bfloat16), "dp", scatter_dimension=0, tiled=True)
    return lax.psum_scatter(part, "blk", scatter_dimension=1, tiled=True).astype(jnp.float32)


def general_layer(tokens, boxes, lengths, wqkv, wbox, wout, wup, wdown, vectors, cotangent):
    blocks = lax.axis_size("blk")
    pages_here = tokens.shape[0] // blocks
    model_width = tokens.shape[2]
    to_pages = partial(
        lax.all_to_all, axis_name="blk", split_axis=0, concat_axis=1, tiled=True
    )
    from_pages = partial(
        lax.all_to_all, axis_name="blk", split_axis=1, concat_axis=0, tiled=True
    )
    page_tokens = to_pages(tokens)
    page_boxes = lax.all_to_all(boxes, "blk", split_axis=1, concat_axis=2, tiled=True)
    page_lengths = lax.dynamic_slice(lengths, (lax.axis_index("blk") * pages_here,), (pages_here,))
    full_qkv = gather_weight(wqkv)
    full_box = gather_weight(wbox)
    full_out = gather_weight(wout)
    full_up = gather_weight(wup)
    full_down = gather_weight(wdown)
    full_vec = lax.all_gather(vectors, ("dp", "blk"), axis=0, tiled=True).astype(jnp.float32)
    page_cotangent = to_pages(cotangent)
    hidden_units = full_up.shape[1]
    bq, bv, bo, g1, e1, b1, b2, g2, e2 = unpack(full_vec, model_width, hidden_units)
    page_len = page_tokens.shape[1]
    score_scale = HEAD ** (-0.5)

    x = page_tokens.reshape(-1, model_width)
    projected = dot32(x, full_qkv)
    head_shape = (pages_here, page_len, HEADS, HEAD)
    q = (projected[:, :model_width] + bq).astype(jnp.bfloat16).reshape(head_shape)
    k = projected[:, model_width : 2 * model_width].astype(jnp.bfloat16).reshape(head_shape)
    v = (projected[:, 2 * model_width :] + bv).astype(jnp.bfloat16).reshape(head_shape)
    table = box_table(page_boxes)
    box_heads = full_box.reshape(HEADS, HEAD, BOX_DIM)
    coeffs = jnp.einsum("pqhd,hdc->pqhc", q, box_heads, preferred_element_type=jnp.float32)
    box_query = rotate(coeffs, table).astype(jnp.bfloat16)
    box_keys = table.astype(jnp.bfloat16)
    scores = (
        jnp.einsum("pqhd,pkhd->phqk", q, k, preferred_element_type=jnp.float32)
        + jnp.einsum("pqhc,pkc->phqk", box_query, box_keys, preferred_element_type=jnp.float32)
    ) * score_scale
    is_valid = (jnp.arange(page_len)[None, :] < page_lengths[:, None])[:, None, None, :]
    masked = jnp.where(is_valid, scores, MASKED)
    probs = jax.nn.softmax(masked, axis=-1)
    probs_low = probs.astype(jnp.bfloat16)
    mixed = jnp.einsum("phqk,pkhd->pqhd", probs_low, v, preferred_element_type=jnp.float32)
    mixed_low = mixed.astype(jnp.bfloat16).reshape(-1, model_width)
    unit1, inv1 = normalize(x.astype(jnp.float32) + dot32(mixed_low, full_out) + bo)
    y1 = unit1 * g1 + e1
    y1_low = y1.astype(jnp.bfloat16)
    pre = dot32(y1_low, full_up) + b1
    hidden = jax.nn.gelu(pre, approximate=False).astype(jnp.bfloat16)
    unit2, inv2 = normalize(y1 + dot32(hidden, full_down) + b2)
    output = (unit2 * g2 + e2).astype(jnp.bfloat16)

    seed = page_cotangent.reshape(-1, model_width).astype(jnp.float32)
    d_h2, d_g2, d_e2 = normalize_back(seed, unit2, inv2, g2)
    d_f = d_h2.astype(jnp.bfloat16)
    d_hidden = dot32(d_f, full_down.T)
    d_pre = jax.vjp(partial(jax.nn.gelu, approximate=False), pre)[1](d_hidden)[0]
    d_pre = d_pre.astype(jnp.bfloat16)
    d_wdown = dot32(hidden.T, d_f)
    d_wup = dot32(y1_low.T, d_pre)
    d_y1 = dot32(d_pre, full_up.T) + d_h2
    d_h1, d_g1, d_e1 = normalize_back(d_y1, unit1, inv1, g1)
    d_a = d_h1.astype(jnp.bfloat16)
    d_wout = dot32(mixed_low.T, d_a)
    d_mixed = dot32(d_a, full_out.T).astype(jnp.bfloat16).reshape(head_shape)
    row_delta = jnp.einsum("pqhd,pqhd->phq", d_mixed.astype(jnp.float32), mixed)
    d_probs = jnp.einsum("pqhd,pkhd->phqk", d_mixed, v, preferred_element_type=jnp.float32)
    d_raw = (probs * (d_probs - row_delta[..., None])).astype(jnp.bfloat16)
    d_q = jnp.einsum("phqk,pkhd->pqhd", d_raw, k, preferred_element_type=jnp.float32)
    d_box_q = jnp.einsum("phqk,pkc->pqhc", d_raw, box_keys, preferred_element_type=jnp.float32)
    d_k = jnp.einsum("phqk,pqhd->pkhd", d_raw, q, preferred_element_type=jnp.float32)
    d_v = jnp.einsum("phqk,pqhd->pkhd", probs_low, d_mixed, preferred_element_type=jnp.float32)
    d_coeffs = unrotate(d_box_q * score_scale, table).astype(jnp.bfloat16)
    d_q = d_q * score_scale + jnp.einsum(
        "pqhc,hdc->pqhd", d_coeffs, box_heads, preferred_element_type=jnp.float32
    )
    d_wbox = jnp.einsum("pqhd,pqhc->hdc", q, d_coeffs, preferred_element_type=jnp.float32)
    flat = (-1, model_width)
    d_q = d_q.astype(jnp.bfloat16).reshape(flat)
    d_k = (d_k * score_scale).astype(jnp.bfloat16).reshape(flat)
    d_v = d_v.astype(jnp.bfloat16).reshape(flat)
    d_c = jnp.concatenate([d_q, d_k, d_v], axis=1)
    d_wqkv = dot32(x.T, d_c)
    d_x = dot32(d_c, full_qkv.T) + d_h1
    total = partial(jnp.sum, axis=0, dtype=jnp.float32)
    vector_grad = jnp.concatenate(
        [total(d_q), total(d_v), total(d_a), d_g1, d_e1, total(d_pre), total(d_f), d_g2, d_e2]
    )
    return (
        from_pages(output.reshape(page_tokens.shape)),
        from_pages(d_x.reshape(page_tokens.shape)),
        scatter_weight(d_wqkv),
        scatter_weight(d_wbox.reshape(model_width, BOX_DIM)),
        scatter_weight(d_wout),
        scatter_weight(d_wup),
        scatter_weight(d_wdown),
        lax.psum_scatter(vector_grad, ("dp", "blk"), scatter_dimension=0, tiled=True),
    )


def solution(mesh):
    in_specs = (
        P("dp", "blk", None),
        P(None, "dp", "blk"),
        P("dp"),
        P("dp", "blk"),
        P("dp", "blk"),
        P("dp", "blk"),
        P("dp", "blk"),
        P("dp", "blk"),
        P(("dp", "blk")),
        P("dp", "blk", None),
    )
    out_specs = (
        P("dp", "blk", None),
        P("dp", "blk", None),
        P("dp", "blk"),
        P("dp", "blk"),
        P("dp", "blk"),
        P("dp", "blk"),
        P("dp", "blk"),
        P(("dp", "blk")),
    )
    return jax.shard_map(
        general_layer, mesh=mesh, in_specs=in_specs, out_specs=out_specs, check_vma=False
    )
```

```python
from functools import partial
import math

import jax
import jax.numpy as jnp
import numpy as np
from jax import lax
from jax.experimental import pallas as pl
from jax.experimental.pallas import tpu as pltpu
from jax.sharding import PartitionSpec as P

HEADS = 12
HEAD = 64
FREQ = 192
BOX_DIM = 768

EPSILON = 1e-12
MASKED = -1e30


def box_table(boxes):
    frequency = jnp.exp(jnp.arange(FREQ, dtype=jnp.float32) * (-math.log(10000.0) / FREQ))
    across = boxes[0].astype(jnp.float32)[..., None] * frequency
    upward = boxes[1].astype(jnp.float32)[..., None] * frequency
    return jnp.concatenate(
        [jnp.cos(across), jnp.sin(across), jnp.cos(upward), jnp.sin(upward)], axis=-1
    )


def rotate(coeffs, own_table):
    cos_across, sin_across, cos_upward, sin_upward = jnp.split(own_table[..., None, :], 4, axis=-1)
    sa, ca, sb, cb = jnp.split(coeffs, 4, axis=-1)
    return jnp.concatenate(
        [
            sa * sin_across + ca * cos_across,
            ca * sin_across - sa * cos_across,
            sb * sin_upward + cb * cos_upward,
            cb * sin_upward - sb * cos_upward,
        ],
        axis=-1,
    )


def unrotate(grad_rows, own_table):
    cos_across, sin_across, cos_upward, sin_upward = jnp.split(own_table[..., None, :], 4, axis=-1)
    d1a, d2a, d1b, d2b = jnp.split(grad_rows, 4, axis=-1)
    return jnp.concatenate(
        [
            d1a * sin_across - d2a * cos_across,
            d1a * cos_across + d2a * sin_across,
            d1b * sin_upward - d2b * cos_upward,
            d1b * cos_upward + d2b * sin_upward,
        ],
        axis=-1,
    )


def normalize(hidden):
    row_mean = jnp.mean(hidden, axis=-1, keepdims=True)
    centered = hidden - row_mean
    inverse = lax.rsqrt(jnp.mean(centered * centered, axis=-1, keepdims=True) + EPSILON)
    return centered * inverse, inverse


def normalize_back(grad, unit, inverse, gain):
    scaled = grad * gain
    mean_grad = jnp.mean(scaled, axis=-1, keepdims=True)
    mean_unit = jnp.mean(scaled * unit, axis=-1, keepdims=True)
    d_hidden = inverse * (scaled - mean_grad - unit * mean_unit)
    return d_hidden, jnp.sum(grad * unit, axis=0), jnp.sum(grad, axis=0)


def unpack(vector_all, model_width, hidden_units):
    cuts = [model_width] * 5 + [hidden_units] + [model_width] * 3
    pieces = []
    offset = 0
    for length_here in cuts:
        pieces.append(vector_all[offset : offset + length_here])
        offset = offset + length_here
    return pieces


def dot32(a, b):
    return jnp.dot(a, b, preferred_element_type=jnp.float32)


def gather_weight(shard):
    part = lax.all_gather(shard, "blk", axis=1, tiled=True)
    return lax.all_gather(part, "dp", axis=0, tiled=True)


def scatter_weight(grad):
    part = lax.psum_scatter(grad.astype(jnp.bfloat16), "dp", scatter_dimension=0, tiled=True)
    return lax.psum_scatter(part, "blk", scatter_dimension=1, tiled=True).astype(jnp.float32)


def general_layer(tokens, boxes, lengths, wqkv, wbox, wout, wup, wdown, vectors, cotangent):
    blocks = lax.axis_size("blk")
    pages_here = tokens.shape[0] // blocks
    model_width = tokens.shape[2]
    to_pages = partial(
        lax.all_to_all, axis_name="blk", split_axis=0, concat_axis=1, tiled=True
    )
    from_pages = partial(
        lax.all_to_all, axis_name="blk", split_axis=1, concat_axis=0, tiled=True
    )
    page_tokens = to_pages(tokens)
    page_boxes = lax.all_to_all(boxes, "blk", split_axis=1, concat_axis=2, tiled=True)
    page_lengths = lax.dynamic_slice(lengths, (lax.axis_index("blk") * pages_here,), (pages_here,))
    full_qkv = gather_weight(wqkv)
    full_box = gather_weight(wbox)
    full_out = gather_weight(wout)
    full_up = gather_weight(wup)
    full_down = gather_weight(wdown)
    full_vec = lax.all_gather(vectors, ("dp", "blk"), axis=0, tiled=True).astype(jnp.float32)
    page_cotangent = to_pages(cotangent)
    hidden_units = full_up.shape[1]
    bq, bv, bo, g1, e1, b1, b2, g2, e2 = unpack(full_vec, model_width, hidden_units)
    page_len = page_tokens.shape[1]
    score_scale = HEAD ** (-0.5)

    x = page_tokens.reshape(-1, model_width)
    projected = dot32(x, full_qkv)
    head_shape = (pages_here, page_len, HEADS, HEAD)
    q = (projected[:, :model_width] + bq).astype(jnp.bfloat16).reshape(head_shape)
    k = projected[:, model_width : 2 * model_width].astype(jnp.bfloat16).reshape(head_shape)
    v = (projected[:, 2 * model_width :] + bv).astype(jnp.bfloat16).reshape(head_shape)
    table = box_table(page_boxes)
    box_heads = full_box.reshape(HEADS, HEAD, BOX_DIM)
    coeffs = jnp.einsum("pqhd,hdc->pqhc", q, box_heads, preferred_element_type=jnp.float32)
    box_query = rotate(coeffs, table).astype(jnp.bfloat16)
    box_keys = table.astype(jnp.bfloat16)
    scores = (
        jnp.einsum("pqhd,pkhd->phqk", q, k, preferred_element_type=jnp.float32)
        + jnp.einsum("pqhc,pkc->phqk", box_query, box_keys, preferred_element_type=jnp.float32)
    ) * score_scale
    is_valid = (jnp.arange(page_len)[None, :] < page_lengths[:, None])[:, None, None, :]
    masked = jnp.where(is_valid, scores, MASKED)
    probs = jax.nn.softmax(masked, axis=-1)
    probs_low = probs.astype(jnp.bfloat16)
    mixed = jnp.einsum("phqk,pkhd->pqhd", probs_low, v, preferred_element_type=jnp.float32)
    mixed_low = mixed.astype(jnp.bfloat16).reshape(-1, model_width)
    unit1, inv1 = normalize(x.astype(jnp.float32) + dot32(mixed_low, full_out) + bo)
    y1 = unit1 * g1 + e1
    y1_low = y1.astype(jnp.bfloat16)
    pre = dot32(y1_low, full_up) + b1
    hidden = jax.nn.gelu(pre, approximate=False).astype(jnp.bfloat16)
    unit2, inv2 = normalize(y1 + dot32(hidden, full_down) + b2)
    output = (unit2 * g2 + e2).astype(jnp.bfloat16)

    seed = page_cotangent.reshape(-1, model_width).astype(jnp.float32)
    d_h2, d_g2, d_e2 = normalize_back(seed, unit2, inv2, g2)
    d_f = d_h2.astype(jnp.bfloat16)
    d_hidden = dot32(d_f, full_down.T)
    d_pre = jax.vjp(partial(jax.nn.gelu, approximate=False), pre)[1](d_hidden)[0]
    d_pre = d_pre.astype(jnp.bfloat16)
    d_wdown = dot32(hidden.T, d_f)
    d_wup = dot32(y1_low.T, d_pre)
    d_y1 = dot32(d_pre, full_up.T) + d_h2
    d_h1, d_g1, d_e1 = normalize_back(d_y1, unit1, inv1, g1)
    d_a = d_h1.astype(jnp.bfloat16)
    d_wout = dot32(mixed_low.T, d_a)
    d_mixed = dot32(d_a, full_out.T).astype(jnp.bfloat16).reshape(head_shape)
    row_delta = jnp.einsum("pqhd,pqhd->phq", d_mixed.astype(jnp.float32), mixed)
    d_probs = jnp.einsum("pqhd,pkhd->phqk", d_mixed, v, preferred_element_type=jnp.float32)
    d_raw = (probs * (d_probs - row_delta[..., None])).astype(jnp.bfloat16)
    d_q = jnp.einsum("phqk,pkhd->pqhd", d_raw, k, preferred_element_type=jnp.float32)
    d_box_q = jnp.einsum("phqk,pkc->pqhc", d_raw, box_keys, preferred_element_type=jnp.float32)
    d_k = jnp.einsum("phqk,pqhd->pkhd", d_raw, q, preferred_element_type=jnp.float32)
    d_v = jnp.einsum("phqk,pqhd->pkhd", probs_low, d_mixed, preferred_element_type=jnp.float32)
    d_coeffs = unrotate(d_box_q * score_scale, table).astype(jnp.bfloat16)
    d_q = d_q * score_scale + jnp.einsum(
        "pqhc,hdc->pqhd", d_coeffs, box_heads, preferred_element_type=jnp.float32
    )
    d_wbox = jnp.einsum("pqhd,pqhc->hdc", q, d_coeffs, preferred_element_type=jnp.float32)
    flat = (-1, model_width)
    d_q = d_q.astype(jnp.bfloat16).reshape(flat)
    d_k = (d_k * score_scale).astype(jnp.bfloat16).reshape(flat)
    d_v = d_v.astype(jnp.bfloat16).reshape(flat)
    d_c = jnp.concatenate([d_q, d_k, d_v], axis=1)
    d_wqkv = dot32(x.T, d_c)
    d_x = dot32(d_c, full_qkv.T) + d_h1
    total = partial(jnp.sum, axis=0, dtype=jnp.float32)
    vector_grad = jnp.concatenate(
        [total(d_q), total(d_v), total(d_a), d_g1, d_e1, total(d_pre), total(d_f), d_g2, d_e2]
    )
    return (
        from_pages(output.reshape(page_tokens.shape)),
        from_pages(d_x.reshape(page_tokens.shape)),
        scatter_weight(d_wqkv),
        scatter_weight(d_wbox.reshape(model_width, BOX_DIM)),
        scatter_weight(d_wout),
        scatter_weight(d_wup),
        scatter_weight(d_wdown),
        lax.psum_scatter(vector_grad, ("dp", "blk"), scatter_dimension=0, tiled=True),
    )


MESH = pl.DeviceIdType.MESH
WEIGHTS = ("qkv", "box", "out", "up", "down")
ROT = 4
ALL = slice(None)


def by_columns(name, height, first, left, right):
    return (
        name,
        (0, height, first, left),
        (0, height, first + left, right),
        (0, height, first, left + right),
    )


def by_rows(name, height, first, count):
    half = height // 2
    return (
        name,
        (0, half, first, count),
        (half, half, first, count),
        (0, height, first, count),
    )


def window(piece):
    return (pl.ds(piece[0], piece[1]), pl.ds(piece[2], piece[3]))


class Place:
    def __init__(self, depth):
        self.depth = depth
        dp = lax.axis_index("dp")
        self.y = lax.axis_index("blk")
        self.z = lax.div(dp, 4)
        self.x = lax.rem(lax.div(dp, 2), 2)
        self.c = lax.rem(dp, 2)
        x, y, z, c = self.x, self.y, self.z, self.c
        self.z_peers = [(lax.rem(z + k, depth) * 4 + x * 2 + c, y) for k in range(1, depth)]
        self.z_from = [lax.rem(z + depth - k, depth) for k in range(1, depth)]
        self.x_peer = (dp + 2 - 4 * x, y)
        self.y_peer = (dp, 1 - y)
        self.c_peer = (dp + 1 - 2 * c, y)

    def greet(self):
        barrier = pltpu.get_barrier_semaphore()
        peers = self.z_peers + [self.x_peer, self.y_peer, self.c_peer]
        for peer in peers:
            pl.semaphore_signal(barrier, inc=1, device_id=peer, device_id_type=MESH)
        pl.semaphore_wait(barrier, len(peers))


def remote(src, dst, sems, at, peer):
    return pltpu.make_async_remote_copy(
        src, dst, sems[0].at[at], sems[1].at[at], device_id=peer, device_id_type=MESH
    )


class Gather:
    def __init__(self, place, groups, shards, full, z_sems, xy_sems, c_sems, own_sem):
        self.place, self.groups, self.shards, self.full = place, groups, shards, full
        self.z_sems, self.xy_sems, self.c_sems, self.own_sem = z_sems, xy_sems, c_sems, own_sem
        self.count = len(groups)

    def z_copy(self, g, k, arriving=False):
        p = self.place
        name, _, _, both = self.groups[g]
        cut = window(both)
        z = p.z_from[k] if arriving else p.z
        return remote(
            self.shards[name].at[cut],
            self.full[name].at[(p.y, z, p.x, p.c) + cut],
            self.z_sems,
            (g, k),
            p.z_peers[k],
        )

    def own_copy(self, g):
        p = self.place
        name, _, _, both = self.groups[g]
        cut = window(both)
        return pltpu.make_async_copy(
            self.shards[name].at[cut],
            self.full[name].at[(p.y, p.z, p.x, p.c) + cut],
            self.own_sem.at[g],
        )

    def xy_copy(self, g, i, arriving=False):
        p = self.place
        name, left, right, _ = self.groups[g]
        a, b = window(left), window(right)
        y = 1 - p.y if arriving else p.y
        x = 1 - p.x if arriving else p.x
        index, peer = (
            ((y, ALL, p.x, p.c) + b, p.y_peer),
            ((p.y, ALL, x, p.c) + a, p.x_peer),
            ((y, ALL, ALL, p.c) + a, p.y_peer),
            ((ALL, ALL, x, p.c) + b, p.x_peer),
        )[i]
        ref = self.full[name].at[index]
        return remote(ref, ref, self.xy_sems, (g, i), peer)

    def c_copy(self, g, arriving=False):
        p = self.place
        name, _, _, both = self.groups[g]
        c = 1 - p.c if arriving else p.c
        ref = self.full[name].at[(ALL, ALL, ALL, c) + window(both)]
        return remote(ref, ref, self.c_sems, (g,), p.c_peer)

    def start(self, g):
        for k in range(self.place.depth - 1):
            self.z_copy(g, k).start()
        self.own_copy(g).start()

    def first(self, g):
        self.own_copy(g).wait()
        for k in range(self.place.depth - 1):
            self.z_copy(g, k, True).wait_recv()
        self.xy_copy(g, 0).start()
        self.xy_copy(g, 1).start()

    def second(self, g):
        self.xy_copy(g, 1, True).wait_recv()
        self.xy_copy(g, 2).start()
        self.xy_copy(g, 0, True).wait_recv()
        self.xy_copy(g, 3).start()

    def third(self, g):
        self.xy_copy(g, 2, True).wait_recv()
        self.xy_copy(g, 3, True).wait_recv()
        self.c_copy(g).start()

    def ready(self, g):
        self.c_copy(g, True).wait_recv()

    def ticks(self, ahead):
        out = [[partial(self.start, g) for g in range(min(ahead, self.count))]]
        for t in range(self.count + 3):
            tick = []
            if t < self.count:
                if t + ahead < self.count:
                    tick.append(partial(self.start, t + ahead))
                tick.append(partial(self.first, t))
            if 0 <= t - 1 < self.count:
                tick.append(partial(self.second, t - 1))
            if 0 <= t - 2 < self.count:
                tick.append(partial(self.third, t - 2))
            if 0 <= t - 3 < self.count:
                tick.append(partial(self.ready, t - 3))
            out.append(tick)
        return out

    def drain(self):
        for g in range(self.count):
            for k in range(self.place.depth - 1):
                self.z_copy(g, k).wait_send()
            for i in range(4):
                self.xy_copy(g, i).wait_send()
            self.c_copy(g).wait_send()


def sine_cosine(angle):
    turns = jnp.floor(angle * (2.0 / math.pi) + 0.5)
    rest = angle - turns * 1.5703125
    rest = rest - turns * 4.837512969970703125e-4
    rest = rest - turns * 7.54978995489188216e-8
    square = rest * rest
    sine = rest + rest * square * (
        -1.6666654611e-1 + square * (8.3321608736e-3 + square * -1.9515295891e-4)
    )
    cosine = (
        1.0
        - 0.5 * square
        + square
        * square
        * (
            4.166664568298827e-2
            + square * (-1.388731625493765e-3 + square * 2.443315711809948e-5)
        )
    )
    quarter = turns.astype(jnp.int32)
    odd = (quarter & 1) == 1
    sine_sign = jnp.where((quarter & 2) == 2, -1.0, 1.0)
    cosine_sign = jnp.where(((quarter + 1) & 2) == 2, -1.0, 1.0)
    return (
        sine_sign * jnp.where(odd, cosine, sine),
        cosine_sign * jnp.where(odd, sine, cosine),
    )


def dot_t(a, b):
    return lax.dot_general(a, b, (((1,), (1,)), ((), ())), preferred_element_type=jnp.float32)


def dot_n(a, b):
    return lax.dot_general(a, b, (((0,), (0,)), ((), ())), preferred_element_type=jnp.float32)


def lanes(start, size):
    return pl.ds(pl.multiple_of(start, 128), size)


BQ, BV, BO, G1, E1, B1, B2, G2, E2 = 0, 768, 1536, 2304, 3072, 3840, 6912, 7680, 8448
VECTORS = 9216


def forward_kernel(plan, *refs):
    depth, groups, page_len, width = plan
    block = page_len // 2
    refs = iter(refs)
    take = lambda n: [next(refs) for _ in range(n)]
    tokens, cotangent, boxes, lengths, piece, frequency = take(6)
    shards = dict(zip(WEIGHTS, take(5)))
    full_out = dict(zip(WEIGHTS, take(5)))
    (x_out, ct_out, qkv_out, table_out, p_out, o_out, unit1_out, inv1_out) = take(8)
    (g_out, d_out, unit2_out, inv2_out, vec_out) = take(5)
    full = dict(zip(WEIGHTS, take(5)))
    (x_own, boxes_peer, pieces, vec, qkv, table, keys, box_w, p_slots, o_own, o_low) = take(11)
    (unit1, inv1, y1_low, hidden, slope, unit2, inv2) = take(7)
    z_sems, xy_sems, c_sems = take(2), take(2), take(2)
    (own_sem,) = take(1)
    vz_sems, vxy_sems, vc_sems = take(2), take(2), take(2)
    ex_sems = take(2)
    (local_sem, p_sem, out_sem) = take(3)

    place = Place(depth)
    y, z, x, c = place.y, place.z, place.x, place.c
    gather = Gather(place, groups, shards, full, z_sems, xy_sems, c_sems, own_sem)

    def swap(i, source, target, arriving=False):
        at = (1 - y) if arriving else y
        return remote(
            source.at[1 - y], target.at[pl.ds(pl.multiple_of(at * block, block), block)],
            ex_sems, (i,), place.y_peer,
        )

    def keep(i, source, target):
        return pltpu.make_async_copy(
            source.at[y], target.at[pl.ds(pl.multiple_of(y * block, block), block)],
            local_sem.at[i],
        )

    box_swap = remote(boxes, boxes_peer, ex_sems, (2,), place.y_peer)

    def vector_z(k, arriving=False):
        at = place.z_from[k] if arriving else z
        return remote(piece, pieces.at[y, at, x, c], vz_sems, (k,), place.z_peers[k])

    def vector_xy(i, arriving=False):
        at_x = 1 - x if arriving else x
        at_y = 1 - y if arriving else y
        index = ((y, ALL, at_x, c), (at_y, ALL, ALL, c))[i]
        ref = pieces.at[index]
        return remote(ref, ref, vxy_sems, (i,), (place.x_peer, place.y_peer)[i])

    def vector_c(arriving=False):
        ref = pieces.at[:, :, :, 1 - c if arriving else c]
        return remote(ref, ref, vc_sems, (0,), place.c_peer)

    vector_own = pltpu.make_async_copy(piece, pieces.at[y, z, x, c], local_sem.at[2])

    ready = [False] * gather.count
    ticks = gather.ticks(AHEAD)
    position = [0]

    def tick(n=1):
        for _ in range(n):
            if position[0] < len(ticks):
                for event in ticks[position[0]]:
                    event()
                position[0] += 1

    def need(g):
        while position[0] < g + 5:
            tick()

    outgoing = []

    def send_out(ref, out):
        copy = pltpu.make_async_copy(ref, out, out_sem.at[len(outgoing)])
        copy.start()
        outgoing.append(copy)

    place.greet()
    box_swap.start()
    swap(0, tokens, x_own).start()
    for k in range(depth - 1):
        vector_z(k).start()
    vector_own.start()
    tick()
    keep(0, tokens, x_own).start()
    keep(1, cotangent, ct_out).start()

    vector_own.wait()
    for k in range(depth - 1):
        vector_z(k, True).wait_recv()
    vector_xy(0).start()
    tick()
    vector_xy(0, True).wait_recv()
    vector_xy(1).start()

    box_swap.wait_recv()
    mine, other = boxes[...], boxes_peer[...]
    first_block = y == 0
    mine = jnp.where(first_block, mine[:, 0, :], mine[:, 1, :])
    other = jnp.where(first_block, other[:, 0, :], other[:, 1, :])
    both = jnp.concatenate(
        [jnp.where(first_block, mine, other), jnp.where(first_block, other, mine)], axis=1
    ).astype(jnp.float32)
    both = jnp.concatenate([both, jnp.zeros((6, page_len), jnp.float32)], axis=0)
    across_up = both.T
    lane = lax.broadcasted_iota(jnp.int32, (1, 2 * FREQ), 1)
    angle = jnp.where(lane < FREQ, across_up[:, 0:1], across_up[:, 1:2]) * frequency[...]
    sine, cosine = sine_cosine(angle)
    table[0], table[1] = cosine, sine
    keys[0], keys[1] = cosine.astype(jnp.bfloat16), sine.astype(jnp.bfloat16)
    send_out(table, table_out)
    tick()
    vector_xy(1, True).wait_recv()
    vector_c().start()

    keep(0, tokens, x_own).wait()
    swap(0, tokens, x_own, True).wait_recv()
    send_out(x_own, x_out)
    tick()
    vector_c(True).wait_recv()
    vec[...] = jnp.zeros_like(vec)
    for dz in range(depth):
        for dx in range(2):
            for dc in range(2):
                for dy in range(2):
                    device = ((dz * 2 + dx) * 2 + dc) * 2 + dy
                    start = device * (VECTORS // (8 * depth)) // 128 * 128
                    vec[:, start : start + 384] += pieces[dy, dz, dx, dc]
    send_out(vec, vec_out)

    def vector(start, size=width):
        return vec[:, start : start + size]

    def project(first, count):
        def body(h, carry):
            w = full["qkv"].at[h][:, :, :, :, first : first + count].reshape(width, count)
            out = jnp.dot(x_own[...], w, preferred_element_type=jnp.float32)
            start = pl.multiple_of(h * 1152 + first, 128)
            column = start + lax.broadcasted_iota(jnp.int32, (1, count), 1)
            bias = bias_qkv[:, lanes(start, count)]
            qkv[:, lanes(start, count)] = (out + bias).astype(jnp.bfloat16)
            return carry

        lax.fori_loop(0, 2, body, 0)

    bias_qkv = next(refs)
    bias_qkv[:, 0:width] = vector(BQ)
    bias_qkv[:, width : 2 * width] = jnp.zeros((1, width), jnp.float32)
    bias_qkv[:, 2 * width : 3 * width] = vector(BV)
    for g, (name, left, right, cut) in enumerate(groups):
        if name == "qkv":
            need(g)
            project(cut[2], cut[3])
    send_out(qkv, qkv_out)

    box_group = [g for g, group in enumerate(groups) if group[0] == "box"][-1]
    need(box_group)
    low = full["box"].at[0][...].reshape(width, 2 * FREQ)
    high = full["box"].at[1][...].reshape(width, 2 * FREQ)
    box_w[...] = jnp.concatenate(
        [low[:, :FREQ], high[:, :FREQ], low[:, FREQ:], high[:, FREQ:]], axis=1
    )
    page_length = jnp.where(first_block, lengths[0], lengths[1])
    valid = lax.broadcasted_iota(jnp.int32, (1, page_len), 1) < page_length
    head_lane = lax.broadcasted_iota(jnp.int32, (1, 128), 1)

    def p_copy(p, slot):
        return pltpu.make_async_copy(p_slots.at[slot], p_out.at[p], p_sem.at[slot])

    first_tick = position[0]
    per_pair = PAIR_TICKS

    def pair(p, carry):
        for i, event_list in enumerate(ticks[first_tick : first_tick + len(per_pair)]):
            @pl.when(p == per_pair[i])
            def _():
                for event in event_list:
                    event()

        slot = lax.rem(p, 2)

        @pl.when(p >= 2)
        def _():
            p_copy(p - 2, slot).wait()

        q = qkv[:, lanes(p * 128, 128)]
        k = qkv[:, lanes(width + p * 128, 128)]
        v = qkv[:, lanes(2 * width + p * 128, 128)]
        w = box_w[pl.ds(pl.multiple_of(p * 128, 128), 128), :]
        outs = []
        for i in range(2):
            of_head = (head_lane < HEAD) == (i == 0)
            q_head = jnp.where(of_head, q, jnp.zeros_like(q))
            u = jnp.dot(q_head, w, preferred_element_type=jnp.float32)
            on_sine, on_cosine = u[:, : 2 * FREQ], u[:, 2 * FREQ :]
            cosine, sine = table[0], table[1]
            b_cosine = (on_sine * sine + on_cosine * cosine).astype(jnp.bfloat16)
            b_sine = (on_cosine * sine - on_sine * cosine).astype(jnp.bfloat16)
            s = dot_t(q_head, k) + dot_t(b_cosine, keys[0]) + dot_t(b_sine, keys[1])
            s = jnp.where(valid, s, MASKED)
            top = jnp.max(s, axis=1, keepdims=True)
            e = jnp.exp((s - top) * (HEAD**-0.5))
            probs = (e * (1.0 / jnp.sum(e, axis=1, keepdims=True))).astype(jnp.bfloat16)
            p_slots[slot, i] = probs
            outs.append(jnp.dot(probs, v, preferred_element_type=jnp.float32))
        mixed = jnp.where(head_lane < HEAD, outs[0], outs[1])
        o_own[:, lanes(p * 128, 128)] = mixed
        o_low[:, lanes(p * 128, 128)] = mixed.astype(jnp.bfloat16)
        p_copy(p, slot).start()
        return carry

    lax.fori_loop(0, HEADS // 2, pair, 0)
    position[0] += len(per_pair)
    p_copy(4, 0).wait()
    p_copy(5, 1).wait()
    send_out(o_own, o_out)

    def last_of(name):
        return [g for g, group in enumerate(groups) if group[0] == name][-1]

    def weight_out(name):
        send_out(full[name], full_out[name])

    weight_out("qkv")
    weight_out("box")
    need(last_of("out"))
    weight_out("out")
    for h in range(2):
        w = full["out"].at[h][...].reshape(width, 384)
        cut = slice(h * 384, (h + 1) * 384)
        o_own_part = jnp.dot(o_low[...], w, preferred_element_type=jnp.float32)
        unit2[:, cut] = x_own[:, cut].astype(jnp.float32) + o_own_part + vec[:, BO + h * 384 : BO + (h + 1) * 384]

    def norm(hidden_sum):
        mean = jnp.mean(hidden_sum, axis=1, keepdims=True)
        centered = hidden_sum - mean
        inverse = lax.rsqrt(jnp.mean(centered * centered, axis=1, keepdims=True) + EPSILON)
        return centered * inverse, inverse

    unit, inverse = norm(unit2[...])
    unit1[...] = unit
    inv1[...] = jnp.broadcast_to(inverse, (page_len, 128))
    y1 = unit * vector(G1) + vector(E1)
    y1_low[...] = y1.astype(jnp.bfloat16)
    unit2[...] = y1 + vector(B2)
    send_out(unit1, unit1_out)
    send_out(inv1, inv1_out)

    def up_tile(first, h, t):
        start = pl.multiple_of(first + t * 256, 128)
        w = full["up"].at[h][:, :, :, :, pl.ds(start, 256)].reshape(width, 256)
        at = lanes(h * 1536 + start, 256)
        pre = jnp.dot(y1_low[...], w, preferred_element_type=jnp.float32)
        pre = pre + vec[:, lanes(B1 + h * 1536 + start, 256)]
        half = 0.5 + 0.5 * lax.erf(pre * (2.0**-0.5))
        hidden[:, at] = (pre * half).astype(jnp.bfloat16)
        bell = jnp.exp(pre * pre * -0.5) * ((2.0 * math.pi) ** -0.5)
        slope[:, at] = (half + pre * bell).astype(jnp.bfloat16)

    for g, (name, left, right, cut) in enumerate(groups):
        if name == "up":
            need(g)
            tiles = cut[3] // 256

            def body(i, carry, first=cut[2], tiles=tiles):
                up_tile(first, lax.div(i, tiles), lax.rem(i, tiles))
                return carry

            lax.fori_loop(0, 2 * tiles, body, 0)
    send_out(hidden, g_out)
    send_out(slope, d_out)
    weight_out("up")

    for g, (name, left, right, cut) in enumerate(groups):
        if name == "down":
            need(g)
            first, count = cut[2], cut[3]

            def body(h, carry, first=first, count=count):
                w = full["down"].at[h][:, :, :, :, first : first + count].reshape(4 * width, count)
                at = lanes(h * 384 + first, count)
                unit2[:, at] += jnp.dot(hidden[...], w, preferred_element_type=jnp.float32)
                return carry

            lax.fori_loop(0, 2, body, 0)
        if name == "up" and g == last_of("up"):
            swap(1, cotangent, ct_out).start()
    weight_out("down")
    unit, inverse = norm(unit2[...])
    unit2[...] = unit
    inv2[...] = jnp.broadcast_to(inverse, (page_len, 128))
    send_out(unit2, unit2_out)
    send_out(inv2, inv2_out)

    gather.drain()
    for k in range(depth - 1):
        vector_z(k).wait_send()
    vector_xy(0).wait_send()
    vector_xy(1).wait_send()
    vector_c().wait_send()
    box_swap.wait_send()
    swap(0, tokens, x_own).wait_send()
    swap(1, cotangent, ct_out).wait_send()
    swap(1, cotangent, ct_out, True).wait_recv()
    keep(1, cotangent, ct_out).wait()
    for copy in outgoing:
        copy.wait()


AHEAD = 2
PAIR_TICKS = (1, 4)


def forward_call(depth, tokens, cotangent, boxes, lengths, piece, shards):
    page_len = tokens.shape[1] * 2
    width = tokens.shape[2]
    heights = {n: s.shape[0] for n, s in zip(WEIGHTS, shards)}
    groups = [
        by_columns("qkv", heights["qkv"], 0, 256, 384),
        by_columns("qkv", heights["qkv"], 640, 256, 256),
        by_columns("box", heights["box"], 0, 128, 256),
        by_columns("out", heights["out"], 0, 256, 128),
        by_columns("up", heights["up"], 0, 384, 384),
        by_columns("up", heights["up"], 768, 384, 384),
        by_rows("down", heights["down"], 0, 256),
        by_rows("down", heights["down"], 256, 128),
    ]
    count = len(groups)
    frequency = np.exp(np.arange(FREQ) * (-math.log(10000.0) / FREQ)).astype(np.float32)
    frequency = jnp.asarray(np.tile(frequency, 2)[None, :])
    full = [jax.ShapeDtypeStruct((2, depth, 2, 2) + s.shape, jnp.bfloat16) for s in shards]
    low, single = jnp.bfloat16, jnp.float32
    kinds = dict(
        x=((page_len, width), low),
        ct=((page_len, width), low),
        qkv=((page_len, 3 * width), low),
        table=((2, page_len, 2 * FREQ), single),
        p=((HEADS // 2, 2, page_len, page_len), low),
        o=((page_len, width), single),
        unit1=((page_len, width), single),
        inv1=((page_len, 128), single),
        g=((page_len, 4 * width), low),
        d=((page_len, 4 * width), low),
        unit2=((page_len, width), single),
        inv2=((page_len, 128), single),
        vec=((1, VECTORS + 128), single),
    )
    outs = full + [jax.ShapeDtypeStruct(*kinds[k]) for k in kinds]
    anywhere = pl.BlockSpec(memory_space=pl.ANY)
    vmem = pl.BlockSpec(memory_space=pltpu.VMEM)
    smem = pl.BlockSpec(memory_space=pltpu.SMEM)
    dma = pltpu.SemaphoreType.DMA
    scratch = [pltpu.VMEM(f.shape, f.dtype) for f in full]
    scratch += [
        pltpu.VMEM((page_len, width), low),
        pltpu.VMEM(boxes.shape, jnp.int32),
        pltpu.VMEM((2, depth, 2, 2, 1, 384), single),
        pltpu.VMEM((1, VECTORS + 128), single),
        pltpu.VMEM((page_len, 3 * width), low),
        pltpu.VMEM((2, page_len, 2 * FREQ), single),
        pltpu.VMEM((2, page_len, 2 * FREQ), low),
        pltpu.VMEM((width, BOX_DIM), low),
        pltpu.VMEM((2, 2, page_len, page_len), low),
        pltpu.VMEM((page_len, width), single),
        pltpu.VMEM((page_len, width), low),
        pltpu.VMEM((page_len, width), single),
        pltpu.VMEM((page_len, 128), single),
        pltpu.VMEM((page_len, width), low),
        pltpu.VMEM((page_len, 4 * width), low),
        pltpu.VMEM((page_len, 4 * width), low),
        pltpu.VMEM((page_len, width), single),
        pltpu.VMEM((page_len, 128), single),
    ]
    scratch += [dma((count, depth - 1))] * 2 + [dma((count, 4))] * 2 + [dma((count,))] * 2
    scratch += [dma((count,))]
    scratch += [dma((depth - 1,))] * 2 + [dma((2,))] * 2 + [dma((1,))] * 2
    scratch += [dma((3,))] * 2 + [dma((3,)), dma((2,)), dma((18,))]
    scratch += [pltpu.VMEM((1, 3 * width), single)]
    plan = (depth, groups, page_len, width)
    results = pl.pallas_call(
        partial(forward_kernel, plan),
        out_shape=outs,
        in_specs=[anywhere, anywhere, vmem, smem, vmem, vmem] + [anywhere] * 5,
        out_specs=[anywhere] * len(outs),
        scratch_shapes=scratch,
        compiler_params=pltpu.CompilerParams(
            collective_id=0, has_side_effects=True, vmem_limit_bytes=VMEM_LIMIT
        ),
    )(tokens, cotangent, boxes, lengths, piece, frequency, *shards)
    return dict(zip(WEIGHTS, results[:5])), dict(zip(kinds, results[5:]))


VMEM_LIMIT = 60 * 2**20


def fast_layer(tokens, boxes, lengths, wqkv, wbox, wout, wup, wdown, vectors, cotangent):
    depth = lax.axis_size("dp") // 4
    width = tokens.shape[2]
    device = lax.axis_index("dp") * 2 + lax.axis_index("blk")
    own = vectors.shape[0]
    offset = lax.rem(device * own, 128)
    piece = lax.dynamic_update_slice(
        jnp.zeros((384,), jnp.float32), vectors.astype(jnp.float32), (offset,)
    )[None, :]
    shards = (wqkv, wbox, wout, wup, wdown)
    full, kept = forward_call(depth, tokens, cotangent, boxes, lengths, piece, shards)

    def whole(name):
        w = full[name]
        w = w.reshape(2, -1, w.shape[-1])
        return jnp.concatenate([w[0], w[1]], axis=1)

    vec = kept["vec"][0, :VECTORS]
    bq, bv, bo, g1, e1, b1, b2, g2, e2 = unpack(vec, width, 4 * width)
    x = kept["x"]
    page_len = x.shape[0]
    head_shape = (page_len, HEADS, HEAD)
    q, k, v = (kept["qkv"][:, i * width : (i + 1) * width].reshape(head_shape) for i in range(3))
    cosine, sine = kept["table"][0], kept["table"][1]
    table = jnp.concatenate(
        [cosine[:, :FREQ], sine[:, :FREQ], cosine[:, FREQ:], sine[:, FREQ:]], axis=1
    )
    keys = table.astype(jnp.bfloat16)
    probs = kept["p"].reshape(HEADS, page_len, page_len)
    mixed_low = kept["o"].astype(jnp.bfloat16)
    unit1, inv1, unit2, inv2 = kept["unit1"], kept["inv1"][:, :1], kept["unit2"], kept["inv2"][:, :1]
    hidden = kept["g"]
    y1_low = (unit1 * g1 + e1).astype(jnp.bfloat16)
    output = (unit2 * g2 + e2).astype(jnp.bfloat16)
    seed = kept["ct"].astype(jnp.float32)
    d_h2, d_g2, d_e2 = normalize_back(seed, unit2, inv2, g2)
    d_f = d_h2.astype(jnp.bfloat16)
    d_hidden = dot32(d_f, whole("down").T)
    d_pre = (d_hidden * kept["d"].astype(jnp.float32)).astype(jnp.bfloat16)
    d_wdown = dot32(hidden.T, d_f)
    d_wup = dot32(y1_low.T, d_pre)
    d_y1 = dot32(d_pre, whole("up").T) + d_h2
    d_h1, d_g1, d_e1 = normalize_back(d_y1, unit1, inv1, g1)
    d_a = d_h1.astype(jnp.bfloat16)
    d_wout = dot32(mixed_low.T, d_a)
    d_mixed = dot32(d_a, whole("out").T).astype(jnp.bfloat16).reshape(head_shape)
    row_delta = jnp.einsum("qhd,qhd->hq", d_mixed.astype(jnp.float32), kept["o"].reshape(head_shape))
    d_probs = jnp.einsum("qhd,khd->hqk", d_mixed, v, preferred_element_type=jnp.float32)
    d_raw = (probs * (d_probs - row_delta[..., None])).astype(jnp.bfloat16)
    scale = HEAD**-0.5
    d_q = jnp.einsum("hqk,khd->qhd", d_raw, k, preferred_element_type=jnp.float32)
    d_box_q = jnp.einsum("hqk,kc->qhc", d_raw, keys, preferred_element_type=jnp.float32)
    d_k = jnp.einsum("hqk,qhd->khd", d_raw, q, preferred_element_type=jnp.float32)
    d_v = jnp.einsum("hqk,qhd->khd", probs, d_mixed, preferred_element_type=jnp.float32)
    d_coeffs = unrotate(d_box_q * scale, table).astype(jnp.bfloat16)
    box_heads = whole("box").reshape(HEADS, HEAD, BOX_DIM)
    d_q = d_q * scale + jnp.einsum(
        "qhc,hdc->qhd", d_coeffs, box_heads, preferred_element_type=jnp.float32
    )
    d_wbox = jnp.einsum("qhd,qhc->hdc", q, d_coeffs, preferred_element_type=jnp.float32)
    flat = (-1, width)
    d_q = d_q.astype(jnp.bfloat16).reshape(flat)
    d_k = (d_k * scale).astype(jnp.bfloat16).reshape(flat)
    d_v = d_v.astype(jnp.bfloat16).reshape(flat)
    d_c = jnp.concatenate([d_q, d_k, d_v], axis=1)
    d_wqkv = dot32(x.T, d_c)
    d_x = dot32(d_c, whole("qkv").T) + d_h1
    total = partial(jnp.sum, axis=0, dtype=jnp.float32)
    vector_grad = jnp.concatenate(
        [total(d_q), total(d_v), total(d_a), d_g1, d_e1, total(d_pre), total(d_f), d_g2, d_e2]
    )
    from_pages = partial(
        lax.all_to_all, axis_name="blk", split_axis=1, concat_axis=0, tiled=True
    )
    return (
        from_pages(output[None]),
        from_pages(d_x[None]),
        scatter_weight(d_wqkv),
        scatter_weight(d_wbox.reshape(width, BOX_DIM)),
        scatter_weight(d_wout),
        scatter_weight(d_wup),
        scatter_weight(d_wdown),
        lax.psum_scatter(vector_grad, ("dp", "blk"), scatter_dimension=0, tiled=True),
    )


def on_device(*args):
    tokens, wqkv, wbox, wdown = args[0], args[3], args[4], args[7]
    blocks, groups = lax.axis_size("blk"), lax.axis_size("dp")
    fits = (
        blocks == 2
        and groups % 4 == 0
        and tokens.shape[0] == 2
        and wqkv.shape[0] % 16 == 0
        and wdown.shape[0] % 32 == 0
        and wbox.shape[1] == 2 * FREQ
    )
    return fast_layer(*args) if fits else general_layer(*args)


def solution(mesh):
    in_specs = (
        P("dp", "blk", None),
        P(None, "dp", "blk"),
        P("dp"),
        P("dp", "blk"),
        P("dp", "blk"),
        P("dp", "blk"),
        P("dp", "blk"),
        P("dp", "blk"),
        P(("dp", "blk")),
        P("dp", "blk", None),
    )
    out_specs = (
        P("dp", "blk", None),
        P("dp", "blk", None),
        P("dp", "blk"),
        P("dp", "blk"),
        P("dp", "blk"),
        P("dp", "blk"),
        P("dp", "blk"),
        P(("dp", "blk")),
    )
    return jax.shard_map(
        on_device, mesh=mesh, in_specs=in_specs, out_specs=out_specs, check_vma=False
    )
```

```python
from functools import partial
import math

import jax
import jax.numpy as jnp
import numpy as np
from jax import lax
from jax.experimental import pallas as pl
from jax.experimental.pallas import tpu as pltpu
from jax.sharding import PartitionSpec as P

HEADS = 12
HEAD = 64
FREQ = 192
BOX_DIM = 768

EPSILON = 1e-12
MASKED = -1e30


def box_table(boxes):
    frequency = jnp.exp(jnp.arange(FREQ, dtype=jnp.float32) * (-math.log(10000.0) / FREQ))
    across = boxes[0].astype(jnp.float32)[..., None] * frequency
    upward = boxes[1].astype(jnp.float32)[..., None] * frequency
    return jnp.concatenate(
        [jnp.cos(across), jnp.sin(across), jnp.cos(upward), jnp.sin(upward)], axis=-1
    )


def rotate(coeffs, own_table):
    cos_across, sin_across, cos_upward, sin_upward = jnp.split(own_table[..., None, :], 4, axis=-1)
    sa, ca, sb, cb = jnp.split(coeffs, 4, axis=-1)
    return jnp.concatenate(
        [
            sa * sin_across + ca * cos_across,
            ca * sin_across - sa * cos_across,
            sb * sin_upward + cb * cos_upward,
            cb * sin_upward - sb * cos_upward,
        ],
        axis=-1,
    )


def unrotate(grad_rows, own_table):
    cos_across, sin_across, cos_upward, sin_upward = jnp.split(own_table[..., None, :], 4, axis=-1)
    d1a, d2a, d1b, d2b = jnp.split(grad_rows, 4, axis=-1)
    return jnp.concatenate(
        [
            d1a * sin_across - d2a * cos_across,
            d1a * cos_across + d2a * sin_across,
            d1b * sin_upward - d2b * cos_upward,
            d1b * cos_upward + d2b * sin_upward,
        ],
        axis=-1,
    )


def normalize(hidden):
    row_mean = jnp.mean(hidden, axis=-1, keepdims=True)
    centered = hidden - row_mean
    inverse = lax.rsqrt(jnp.mean(centered * centered, axis=-1, keepdims=True) + EPSILON)
    return centered * inverse, inverse


def normalize_back(grad, unit, inverse, gain):
    scaled = grad * gain
    mean_grad = jnp.mean(scaled, axis=-1, keepdims=True)
    mean_unit = jnp.mean(scaled * unit, axis=-1, keepdims=True)
    d_hidden = inverse * (scaled - mean_grad - unit * mean_unit)
    return d_hidden, jnp.sum(grad * unit, axis=0), jnp.sum(grad, axis=0)


def unpack(vector_all, model_width, hidden_units):
    cuts = [model_width] * 5 + [hidden_units] + [model_width] * 3
    pieces = []
    offset = 0
    for length_here in cuts:
        pieces.append(vector_all[offset : offset + length_here])
        offset = offset + length_here
    return pieces


def dot32(a, b):
    return jnp.dot(a, b, preferred_element_type=jnp.float32)


def gather_weight(shard):
    part = lax.all_gather(shard, "blk", axis=1, tiled=True)
    return lax.all_gather(part, "dp", axis=0, tiled=True)


def scatter_weight(grad):
    part = lax.psum_scatter(grad.astype(jnp.bfloat16), "dp", scatter_dimension=0, tiled=True)
    return lax.psum_scatter(part, "blk", scatter_dimension=1, tiled=True).astype(jnp.float32)


def general_layer(tokens, boxes, lengths, wqkv, wbox, wout, wup, wdown, vectors, cotangent):
    blocks = lax.axis_size("blk")
    pages_here = tokens.shape[0] // blocks
    model_width = tokens.shape[2]
    to_pages = partial(
        lax.all_to_all, axis_name="blk", split_axis=0, concat_axis=1, tiled=True
    )
    from_pages = partial(
        lax.all_to_all, axis_name="blk", split_axis=1, concat_axis=0, tiled=True
    )
    page_tokens = to_pages(tokens)
    page_boxes = lax.all_to_all(boxes, "blk", split_axis=1, concat_axis=2, tiled=True)
    page_lengths = lax.dynamic_slice(lengths, (lax.axis_index("blk") * pages_here,), (pages_here,))
    full_qkv = gather_weight(wqkv)
    full_box = gather_weight(wbox)
    full_out = gather_weight(wout)
    full_up = gather_weight(wup)
    full_down = gather_weight(wdown)
    full_vec = lax.all_gather(vectors, ("dp", "blk"), axis=0, tiled=True).astype(jnp.float32)
    page_cotangent = to_pages(cotangent)
    hidden_units = full_up.shape[1]
    bq, bv, bo, g1, e1, b1, b2, g2, e2 = unpack(full_vec, model_width, hidden_units)
    page_len = page_tokens.shape[1]
    score_scale = HEAD ** (-0.5)

    x = page_tokens.reshape(-1, model_width)
    projected = dot32(x, full_qkv)
    head_shape = (pages_here, page_len, HEADS, HEAD)
    q = (projected[:, :model_width] + bq).astype(jnp.bfloat16).reshape(head_shape)
    k = projected[:, model_width : 2 * model_width].astype(jnp.bfloat16).reshape(head_shape)
    v = (projected[:, 2 * model_width :] + bv).astype(jnp.bfloat16).reshape(head_shape)
    table = box_table(page_boxes)
    box_heads = full_box.reshape(HEADS, HEAD, BOX_DIM)
    coeffs = jnp.einsum("pqhd,hdc->pqhc", q, box_heads, preferred_element_type=jnp.float32)
    box_query = rotate(coeffs, table).astype(jnp.bfloat16)
    box_keys = table.astype(jnp.bfloat16)
    scores = (
        jnp.einsum("pqhd,pkhd->phqk", q, k, preferred_element_type=jnp.float32)
        + jnp.einsum("pqhc,pkc->phqk", box_query, box_keys, preferred_element_type=jnp.float32)
    ) * score_scale
    is_valid = (jnp.arange(page_len)[None, :] < page_lengths[:, None])[:, None, None, :]
    masked = jnp.where(is_valid, scores, MASKED)
    probs = jax.nn.softmax(masked, axis=-1)
    probs_low = probs.astype(jnp.bfloat16)
    mixed = jnp.einsum("phqk,pkhd->pqhd", probs_low, v, preferred_element_type=jnp.float32)
    mixed_low = mixed.astype(jnp.bfloat16).reshape(-1, model_width)
    unit1, inv1 = normalize(x.astype(jnp.float32) + dot32(mixed_low, full_out) + bo)
    y1 = unit1 * g1 + e1
    y1_low = y1.astype(jnp.bfloat16)
    pre = dot32(y1_low, full_up) + b1
    hidden = jax.nn.gelu(pre, approximate=False).astype(jnp.bfloat16)
    unit2, inv2 = normalize(y1 + dot32(hidden, full_down) + b2)
    output = (unit2 * g2 + e2).astype(jnp.bfloat16)

    seed = page_cotangent.reshape(-1, model_width).astype(jnp.float32)
    d_h2, d_g2, d_e2 = normalize_back(seed, unit2, inv2, g2)
    d_f = d_h2.astype(jnp.bfloat16)
    d_hidden = dot32(d_f, full_down.T)
    d_pre = jax.vjp(partial(jax.nn.gelu, approximate=False), pre)[1](d_hidden)[0]
    d_pre = d_pre.astype(jnp.bfloat16)
    d_wdown = dot32(hidden.T, d_f)
    d_wup = dot32(y1_low.T, d_pre)
    d_y1 = dot32(d_pre, full_up.T) + d_h2
    d_h1, d_g1, d_e1 = normalize_back(d_y1, unit1, inv1, g1)
    d_a = d_h1.astype(jnp.bfloat16)
    d_wout = dot32(mixed_low.T, d_a)
    d_mixed = dot32(d_a, full_out.T).astype(jnp.bfloat16).reshape(head_shape)
    row_delta = jnp.einsum("pqhd,pqhd->phq", d_mixed.astype(jnp.float32), mixed)
    d_probs = jnp.einsum("pqhd,pkhd->phqk", d_mixed, v, preferred_element_type=jnp.float32)
    d_raw = (probs * (d_probs - row_delta[..., None])).astype(jnp.bfloat16)
    d_q = jnp.einsum("phqk,pkhd->pqhd", d_raw, k, preferred_element_type=jnp.float32)
    d_box_q = jnp.einsum("phqk,pkc->pqhc", d_raw, box_keys, preferred_element_type=jnp.float32)
    d_k = jnp.einsum("phqk,pqhd->pkhd", d_raw, q, preferred_element_type=jnp.float32)
    d_v = jnp.einsum("phqk,pqhd->pkhd", probs_low, d_mixed, preferred_element_type=jnp.float32)
    d_coeffs = unrotate(d_box_q * score_scale, table).astype(jnp.bfloat16)
    d_q = d_q * score_scale + jnp.einsum(
        "pqhc,hdc->pqhd", d_coeffs, box_heads, preferred_element_type=jnp.float32
    )
    d_wbox = jnp.einsum("pqhd,pqhc->hdc", q, d_coeffs, preferred_element_type=jnp.float32)
    flat = (-1, model_width)
    d_q = d_q.astype(jnp.bfloat16).reshape(flat)
    d_k = (d_k * score_scale).astype(jnp.bfloat16).reshape(flat)
    d_v = d_v.astype(jnp.bfloat16).reshape(flat)
    d_c = jnp.concatenate([d_q, d_k, d_v], axis=1)
    d_wqkv = dot32(x.T, d_c)
    d_x = dot32(d_c, full_qkv.T) + d_h1
    total = partial(jnp.sum, axis=0, dtype=jnp.float32)
    vector_grad = jnp.concatenate(
        [total(d_q), total(d_v), total(d_a), d_g1, d_e1, total(d_pre), total(d_f), d_g2, d_e2]
    )
    return (
        from_pages(output.reshape(page_tokens.shape)),
        from_pages(d_x.reshape(page_tokens.shape)),
        scatter_weight(d_wqkv),
        scatter_weight(d_wbox.reshape(model_width, BOX_DIM)),
        scatter_weight(d_wout),
        scatter_weight(d_wup),
        scatter_weight(d_wdown),
        lax.psum_scatter(vector_grad, ("dp", "blk"), scatter_dimension=0, tiled=True),
    )


MESH = pl.DeviceIdType.MESH
WEIGHTS = ("qkv", "box", "out", "up", "down")
ROT = 4
ALL = slice(None)


def by_columns(name, height, first, left, right):
    return (
        name,
        (0, height, first, left),
        (0, height, first + left, right),
        (0, height, first, left + right),
    )


def by_rows(name, height, first, count):
    half = height // 2
    return (
        name,
        (0, half, first, count),
        (half, half, first, count),
        (0, height, first, count),
    )


def window(piece):
    return (pl.ds(piece[0], piece[1]), pl.ds(piece[2], piece[3]))


class Place:
    def __init__(self, depth):
        self.depth = depth
        dp = lax.axis_index("dp")
        self.y = lax.axis_index("blk")
        self.z = lax.div(dp, 4)
        self.x = lax.rem(lax.div(dp, 2), 2)
        self.c = lax.rem(dp, 2)
        x, y, z, c = self.x, self.y, self.z, self.c
        self.z_peers = [(lax.rem(z + k, depth) * 4 + x * 2 + c, y) for k in range(1, depth)]
        self.z_from = [lax.rem(z + depth - k, depth) for k in range(1, depth)]
        self.x_peer = (dp + 2 - 4 * x, y)
        self.y_peer = (dp, 1 - y)
        self.c_peer = (dp + 1 - 2 * c, y)

    def greet(self):
        barrier = pltpu.get_barrier_semaphore()
        peers = self.z_peers + [self.x_peer, self.y_peer, self.c_peer]
        for peer in peers:
            pl.semaphore_signal(barrier, inc=1, device_id=peer, device_id_type=MESH)
        pl.semaphore_wait(barrier, len(peers))


def remote(src, dst, sems, at, peer):
    return pltpu.make_async_remote_copy(
        src, dst, sems[0].at[at], sems[1].at[at], device_id=peer, device_id_type=MESH
    )


class Gather:
    def __init__(self, place, groups, shards, full, z_sems, xy_sems, c_sems, own_sem):
        self.place, self.groups, self.shards, self.full = place, groups, shards, full
        self.z_sems, self.xy_sems, self.c_sems, self.own_sem = z_sems, xy_sems, c_sems, own_sem
        self.count = len(groups)

    def z_copy(self, g, k, arriving=False):
        p = self.place
        name, _, _, both = self.groups[g]
        cut = window(both)
        z = p.z_from[k] if arriving else p.z
        return remote(
            self.shards[name].at[cut],
            self.full[name].at[(p.y, z, p.x, p.c) + cut],
            self.z_sems,
            (g, k),
            p.z_peers[k],
        )

    def own_copy(self, g):
        p = self.place
        name, _, _, both = self.groups[g]
        cut = window(both)
        return pltpu.make_async_copy(
            self.shards[name].at[cut],
            self.full[name].at[(p.y, p.z, p.x, p.c) + cut],
            self.own_sem.at[g],
        )

    def xy_copy(self, g, i, arriving=False):
        p = self.place
        name, left, right, _ = self.groups[g]
        a, b = window(left), window(right)
        y = 1 - p.y if arriving else p.y
        x = 1 - p.x if arriving else p.x
        index, peer = (
            ((y, ALL, p.x, p.c) + b, p.y_peer),
            ((p.y, ALL, x, p.c) + a, p.x_peer),
            ((y, ALL, ALL, p.c) + a, p.y_peer),
            ((ALL, ALL, x, p.c) + b, p.x_peer),
        )[i]
        ref = self.full[name].at[index]
        return remote(ref, ref, self.xy_sems, (g, i), peer)

    def c_copy(self, g, arriving=False):
        p = self.place
        name, _, _, both = self.groups[g]
        c = 1 - p.c if arriving else p.c
        ref = self.full[name].at[(ALL, ALL, ALL, c) + window(both)]
        return remote(ref, ref, self.c_sems, (g,), p.c_peer)

    def start(self, g):
        for k in range(self.place.depth - 1):
            self.z_copy(g, k).start()
        self.own_copy(g).start()

    def first(self, g):
        self.own_copy(g).wait()
        for k in range(self.place.depth - 1):
            self.z_copy(g, k, True).wait_recv()
        self.xy_copy(g, 0).start()
        self.xy_copy(g, 1).start()

    def second(self, g):
        self.xy_copy(g, 1, True).wait_recv()
        self.xy_copy(g, 2).start()
        self.xy_copy(g, 0, True).wait_recv()
        self.xy_copy(g, 3).start()

    def third(self, g):
        self.xy_copy(g, 2, True).wait_recv()
        self.xy_copy(g, 3, True).wait_recv()
        self.c_copy(g).start()

    def ready(self, g):
        self.c_copy(g, True).wait_recv()

    def ticks(self, ahead):
        out = [[partial(self.start, g) for g in range(min(ahead, self.count))]]
        for t in range(self.count + 3):
            tick = []
            if t < self.count:
                if t + ahead < self.count:
                    tick.append(partial(self.start, t + ahead))
                tick.append(partial(self.first, t))
            if 0 <= t - 1 < self.count:
                tick.append(partial(self.second, t - 1))
            if 0 <= t - 2 < self.count:
                tick.append(partial(self.third, t - 2))
            if 0 <= t - 3 < self.count:
                tick.append(partial(self.ready, t - 3))
            out.append(tick)
        return out

    def drain(self):
        for g in range(self.count):
            for k in range(self.place.depth - 1):
                self.z_copy(g, k).wait_send()
            for i in range(4):
                self.xy_copy(g, i).wait_send()
            self.c_copy(g).wait_send()


def sine_cosine(angle):
    turns = jnp.floor(angle * (2.0 / math.pi) + 0.5)
    rest = angle - turns * 1.5703125
    rest = rest - turns * 4.837512969970703125e-4
    rest = rest - turns * 7.54978995489188216e-8
    square = rest * rest
    sine = rest + rest * square * (
        -1.6666654611e-1 + square * (8.3321608736e-3 + square * -1.9515295891e-4)
    )
    cosine = (
        1.0
        - 0.5 * square
        + square
        * square
        * (
            4.166664568298827e-2
            + square * (-1.388731625493765e-3 + square * 2.443315711809948e-5)
        )
    )
    quarter = turns.astype(jnp.int32)
    odd = (quarter & 1) == 1
    sine_sign = jnp.where((quarter & 2) == 2, -1.0, 1.0)
    cosine_sign = jnp.where(((quarter + 1) & 2) == 2, -1.0, 1.0)
    return (
        sine_sign * jnp.where(odd, cosine, sine),
        cosine_sign * jnp.where(odd, sine, cosine),
    )


def dot_t(a, b):
    return lax.dot_general(a, b, (((1,), (1,)), ((), ())), preferred_element_type=jnp.float32)


def dot_n(a, b):
    return lax.dot_general(a, b, (((0,), (0,)), ((), ())), preferred_element_type=jnp.float32)


def lanes(start, size):
    return pl.ds(pl.multiple_of(start, 128), size)


BQ, BV, BO, G1, E1, B1, B2, G2, E2 = 0, 768, 1536, 2304, 3072, 3840, 6912, 7680, 8448
VECTORS = 9216


def forward_kernel(plan, *refs):
    depth, groups, page_len, width = plan
    block = page_len // 2
    refs = iter(refs)
    take = lambda n: [next(refs) for _ in range(n)]
    tokens, cotangent, boxes, lengths, piece, frequency = take(6)
    shards = dict(zip(WEIGHTS, take(5)))
    full_out = dict(zip(WEIGHTS, take(5)))
    (x_out, ct_out, qkv_out, table_out, p_out, o_out, unit1_out, inv1_out) = take(8)
    (g_out, d_out, unit2_out, inv2_out, vec_out) = take(5)
    full = dict(zip(WEIGHTS, take(5)))
    (x_own, boxes_peer, pieces, vec, qkv, table, keys, box_w, p_slots, o_own, o_low) = take(11)
    (unit1, inv1, y1_low, hidden, slope, unit2, inv2) = take(7)
    z_sems, xy_sems, c_sems = take(2), take(2), take(2)
    (own_sem,) = take(1)
    vz_sems, vxy_sems, vc_sems = take(2), take(2), take(2)
    ex_sems = take(2)
    (local_sem, p_sem, out_sem) = take(3)

    place = Place(depth)
    y, z, x, c = place.y, place.z, place.x, place.c
    gather = Gather(place, groups, shards, full, z_sems, xy_sems, c_sems, own_sem)

    def swap(i, source, target, arriving=False):
        at = (1 - y) if arriving else y
        return remote(
            source.at[1 - y], target.at[pl.ds(pl.multiple_of(at * block, block), block)],
            ex_sems, (i,), place.y_peer,
        )

    def keep(i, source, target):
        return pltpu.make_async_copy(
            source.at[y], target.at[pl.ds(pl.multiple_of(y * block, block), block)],
            local_sem.at[i],
        )

    box_swap = remote(boxes, boxes_peer, ex_sems, (2,), place.y_peer)

    def vector_z(k, arriving=False):
        at = place.z_from[k] if arriving else z
        return remote(piece, pieces.at[y, at, x, c], vz_sems, (k,), place.z_peers[k])

    def vector_xy(i, arriving=False):
        at_x = 1 - x if arriving else x
        at_y = 1 - y if arriving else y
        index = ((y, ALL, at_x, c), (at_y, ALL, ALL, c))[i]
        ref = pieces.at[index]
        return remote(ref, ref, vxy_sems, (i,), (place.x_peer, place.y_peer)[i])

    def vector_c(arriving=False):
        ref = pieces.at[:, :, :, 1 - c if arriving else c]
        return remote(ref, ref, vc_sems, (0,), place.c_peer)

    vector_own = pltpu.make_async_copy(piece, pieces.at[y, z, x, c], local_sem.at[2])

    ready = [False] * gather.count
    ticks = gather.ticks(AHEAD)
    position = [0]

    def tick(n=1):
        for _ in range(n):
            if position[0] < len(ticks):
                for event in ticks[position[0]]:
                    event()
                position[0] += 1

    def need(g):
        while position[0] < g + 5:
            tick()

    outgoing = []

    def send_out(ref, out):
        copy = pltpu.make_async_copy(ref, out, out_sem.at[len(outgoing)])
        copy.start()
        outgoing.append(copy)

    place.greet()
    box_swap.start()
    swap(0, tokens, x_own).start()
    for k in range(depth - 1):
        vector_z(k).start()
    vector_own.start()
    tick()
    keep(0, tokens, x_own).start()
    keep(1, cotangent, ct_out).start()

    vector_own.wait()
    for k in range(depth - 1):
        vector_z(k, True).wait_recv()
    vector_xy(0).start()
    tick()
    vector_xy(0, True).wait_recv()
    vector_xy(1).start()

    box_swap.wait_recv()
    mine, other = boxes[...], boxes_peer[...]
    first_block = y == 0
    mine = jnp.where(first_block, mine[:, 0, :], mine[:, 1, :])
    other = jnp.where(first_block, other[:, 0, :], other[:, 1, :])
    both = jnp.concatenate(
        [jnp.where(first_block, mine, other), jnp.where(first_block, other, mine)], axis=1
    ).astype(jnp.float32)
    both = jnp.concatenate([both, jnp.zeros((6, page_len), jnp.float32)], axis=0)
    across_up = both.T
    lane = lax.broadcasted_iota(jnp.int32, (1, 2 * FREQ), 1)
    angle = jnp.where(lane < FREQ, across_up[:, 0:1], across_up[:, 1:2]) * frequency[...]
    sine, cosine = sine_cosine(angle)
    table[0], table[1] = cosine, sine
    keys[0], keys[1] = cosine.astype(jnp.bfloat16), sine.astype(jnp.bfloat16)
    send_out(table, table_out)
    tick()
    vector_xy(1, True).wait_recv()
    vector_c().start()

    keep(0, tokens, x_own).wait()
    swap(0, tokens, x_own, True).wait_recv()
    send_out(x_own, x_out)
    tick()
    vector_c(True).wait_recv()
    vec[...] = jnp.zeros_like(vec)
    for dz in range(depth):
        for dx in range(2):
            for dc in range(2):
                for dy in range(2):
                    device = ((dz * 2 + dx) * 2 + dc) * 2 + dy
                    start = device * (VECTORS // (8 * depth)) // 128 * 128
                    vec[:, start : start + 384] += pieces[dy, dz, dx, dc]
    send_out(vec, vec_out)

    def vector(start, size=width):
        return vec[:, start : start + size]

    def project(first, count):
        def body(h, carry):
            w = full["qkv"].at[h][:, :, :, :, first : first + count].reshape(width, count)
            out = jnp.dot(x_own[...], w, preferred_element_type=jnp.float32)
            start = pl.multiple_of(h * 1152 + first, 128)
            column = start + lax.broadcasted_iota(jnp.int32, (1, count), 1)
            bias = bias_qkv[:, lanes(start, count)]
            qkv[:, lanes(start, count)] = (out + bias).astype(jnp.bfloat16)
            return carry

        lax.fori_loop(0, 2, body, 0)

    bias_qkv = next(refs)
    bias_qkv[:, 0:width] = vector(BQ)
    bias_qkv[:, width : 2 * width] = jnp.zeros((1, width), jnp.float32)
    bias_qkv[:, 2 * width : 3 * width] = vector(BV)
    for g, (name, left, right, cut) in enumerate(groups):
        if name == "qkv":
            need(g)
            project(cut[2], cut[3])
    send_out(qkv, qkv_out)

    box_group = [g for g, group in enumerate(groups) if group[0] == "box"][-1]
    need(box_group)
    low = full["box"].at[0][...].reshape(width, 2 * FREQ)
    high = full["box"].at[1][...].reshape(width, 2 * FREQ)
    box_w[...] = jnp.concatenate(
        [low[:, :FREQ], high[:, :FREQ], low[:, FREQ:], high[:, FREQ:]], axis=1
    )
    page_length = jnp.where(first_block, lengths[0], lengths[1])
    valid = lax.broadcasted_iota(jnp.int32, (1, page_len), 1) < page_length
    head_lane = lax.broadcasted_iota(jnp.int32, (1, 128), 1)

    def p_copy(p, slot):
        return pltpu.make_async_copy(p_slots.at[slot], p_out.at[p], p_sem.at[slot])

    first_tick = position[0]
    per_pair = PAIR_TICKS

    def pair(p, carry):
        for i, event_list in enumerate(ticks[first_tick : first_tick + len(per_pair)]):
            @pl.when(p == per_pair[i])
            def _():
                for event in event_list:
                    event()

        slot = lax.rem(p, 2)

        @pl.when(p >= 2)
        def _():
            p_copy(p - 2, slot).wait()

        q = qkv[:, lanes(p * 128, 128)]
        k = qkv[:, lanes(width + p * 128, 128)]
        v = qkv[:, lanes(2 * width + p * 128, 128)]
        w = box_w[pl.ds(pl.multiple_of(p * 128, 128), 128), :]
        outs = []
        for i in range(2):
            of_head = (head_lane < HEAD) == (i == 0)
            q_head = jnp.where(of_head, q, jnp.zeros_like(q))
            u = jnp.dot(q_head, w, preferred_element_type=jnp.float32)
            on_sine, on_cosine = u[:, : 2 * FREQ], u[:, 2 * FREQ :]
            cosine, sine = table[0], table[1]
            b_cosine = (on_sine * sine + on_cosine * cosine).astype(jnp.bfloat16)
            b_sine = (on_cosine * sine - on_sine * cosine).astype(jnp.bfloat16)
            s = dot_t(q_head, k) + dot_t(b_cosine, keys[0]) + dot_t(b_sine, keys[1])
            s = jnp.where(valid, s, MASKED)
            top = jnp.max(s, axis=1, keepdims=True)
            e = jnp.exp((s - top) * (HEAD**-0.5))
            probs = (e * (1.0 / jnp.sum(e, axis=1, keepdims=True))).astype(jnp.bfloat16)
            p_slots[slot, i] = probs
            outs.append(jnp.dot(probs, v, preferred_element_type=jnp.float32))
        mixed = jnp.where(head_lane < HEAD, outs[0], outs[1])
        o_own[:, lanes(p * 128, 128)] = mixed
        o_low[:, lanes(p * 128, 128)] = mixed.astype(jnp.bfloat16)
        p_copy(p, slot).start()
        return carry

    lax.fori_loop(0, HEADS // 2, pair, 0)
    position[0] += len(per_pair)
    p_copy(4, 0).wait()
    p_copy(5, 1).wait()
    send_out(o_own, o_out)

    def last_of(name):
        return [g for g, group in enumerate(groups) if group[0] == name][-1]

    def weight_out(name):
        send_out(full[name], full_out[name])

    weight_out("qkv")
    weight_out("box")
    need(last_of("out"))
    weight_out("out")
    for h in range(2):
        w = full["out"].at[h][...].reshape(width, 384)
        cut = slice(h * 384, (h + 1) * 384)
        o_own_part = jnp.dot(o_low[...], w, preferred_element_type=jnp.float32)
        unit2[:, cut] = x_own[:, cut].astype(jnp.float32) + o_own_part + vec[:, BO + h * 384 : BO + (h + 1) * 384]

    def norm(hidden_sum):
        mean = jnp.mean(hidden_sum, axis=1, keepdims=True)
        centered = hidden_sum - mean
        inverse = lax.rsqrt(jnp.mean(centered * centered, axis=1, keepdims=True) + EPSILON)
        return centered * inverse, inverse

    unit, inverse = norm(unit2[...])
    unit1[...] = unit
    inv1[...] = jnp.broadcast_to(inverse, (page_len, 128))
    y1 = unit * vector(G1) + vector(E1)
    y1_low[...] = y1.astype(jnp.bfloat16)
    unit2[...] = y1 + vector(B2)
    send_out(unit1, unit1_out)
    send_out(inv1, inv1_out)

    def up_tile(first, h, t):
        start = pl.multiple_of(first + t * 256, 128)
        w = full["up"].at[h][:, :, :, :, pl.ds(start, 256)].reshape(width, 256)
        at = lanes(h * 1536 + start, 256)
        pre = jnp.dot(y1_low[...], w, preferred_element_type=jnp.float32)
        pre = pre + vec[:, lanes(B1 + h * 1536 + start, 256)]
        half = 0.5 + 0.5 * lax.erf(pre * (2.0**-0.5))
        hidden[:, at] = (pre * half).astype(jnp.bfloat16)
        bell = jnp.exp(pre * pre * -0.5) * ((2.0 * math.pi) ** -0.5)
        slope[:, at] = (half + pre * bell).astype(jnp.bfloat16)

    for g, (name, left, right, cut) in enumerate(groups):
        if name == "up":
            need(g)
            tiles = cut[3] // 256

            def body(i, carry, first=cut[2], tiles=tiles):
                up_tile(first, lax.div(i, tiles), lax.rem(i, tiles))
                return carry

            lax.fori_loop(0, 2 * tiles, body, 0)
    send_out(hidden, g_out)
    send_out(slope, d_out)
    weight_out("up")

    for g, (name, left, right, cut) in enumerate(groups):
        if name == "down":
            need(g)
            first, count = cut[2], cut[3]

            def body(h, carry, first=first, count=count):
                w = full["down"].at[h][:, :, :, :, first : first + count].reshape(4 * width, count)
                at = lanes(h * 384 + first, count)
                unit2[:, at] += jnp.dot(hidden[...], w, preferred_element_type=jnp.float32)
                return carry

            lax.fori_loop(0, 2, body, 0)
        if name == "up" and g == last_of("up"):
            swap(1, cotangent, ct_out).start()
    weight_out("down")
    unit, inverse = norm(unit2[...])
    unit2[...] = unit
    inv2[...] = jnp.broadcast_to(inverse, (page_len, 128))
    send_out(unit2, unit2_out)
    send_out(inv2, inv2_out)

    gather.drain()
    for k in range(depth - 1):
        vector_z(k).wait_send()
    vector_xy(0).wait_send()
    vector_xy(1).wait_send()
    vector_c().wait_send()
    box_swap.wait_send()
    swap(0, tokens, x_own).wait_send()
    swap(1, cotangent, ct_out).wait_send()
    swap(1, cotangent, ct_out, True).wait_recv()
    keep(1, cotangent, ct_out).wait()
    for copy in outgoing:
        copy.wait()


AHEAD = 2
PAIR_TICKS = (1, 4)


def forward_call(depth, tokens, cotangent, boxes, lengths, piece, shards):
    page_len = tokens.shape[1] * 2
    width = tokens.shape[2]
    heights = {n: s.shape[0] for n, s in zip(WEIGHTS, shards)}
    groups = [
        by_columns("qkv", heights["qkv"], 0, 256, 384),
        by_columns("qkv", heights["qkv"], 640, 256, 256),
        by_columns("box", heights["box"], 0, 128, 256),
        by_columns("out", heights["out"], 0, 256, 128),
        by_columns("up", heights["up"], 0, 384, 384),
        by_columns("up", heights["up"], 768, 384, 384),
        by_rows("down", heights["down"], 0, 256),
        by_rows("down", heights["down"], 256, 128),
    ]
    count = len(groups)
    frequency = np.exp(np.arange(FREQ) * (-math.log(10000.0) / FREQ)).astype(np.float32)
    frequency = jnp.asarray(np.tile(frequency, 2)[None, :])
    full = [jax.ShapeDtypeStruct((2, depth, 2, 2) + s.shape, jnp.bfloat16) for s in shards]
    low, single = jnp.bfloat16, jnp.float32
    kinds = dict(
        x=((page_len, width), low),
        ct=((page_len, width), low),
        qkv=((page_len, 3 * width), low),
        table=((2, page_len, 2 * FREQ), single),
        p=((HEADS // 2, 2, page_len, page_len), low),
        o=((page_len, width), single),
        unit1=((page_len, width), single),
        inv1=((page_len, 128), single),
        g=((page_len, 4 * width), low),
        d=((page_len, 4 * width), low),
        unit2=((page_len, width), single),
        inv2=((page_len, 128), single),
        vec=((1, VECTORS + 128), single),
    )
    outs = full + [jax.ShapeDtypeStruct(*kinds[k]) for k in kinds]
    anywhere = pl.BlockSpec(memory_space=pl.ANY)
    vmem = pl.BlockSpec(memory_space=pltpu.VMEM)
    smem = pl.BlockSpec(memory_space=pltpu.SMEM)
    dma = pltpu.SemaphoreType.DMA
    scratch = [pltpu.VMEM(f.shape, f.dtype) for f in full]
    scratch += [
        pltpu.VMEM((page_len, width), low),
        pltpu.VMEM(boxes.shape, jnp.int32),
        pltpu.VMEM((2, depth, 2, 2, 1, 384), single),
        pltpu.VMEM((1, VECTORS + 128), single),
        pltpu.VMEM((page_len, 3 * width), low),
        pltpu.VMEM((2, page_len, 2 * FREQ), single),
        pltpu.VMEM((2, page_len, 2 * FREQ), low),
        pltpu.VMEM((width, BOX_DIM), low),
        pltpu.VMEM((2, 2, page_len, page_len), low),
        pltpu.VMEM((page_len, width), single),
        pltpu.VMEM((page_len, width), low),
        pltpu.VMEM((page_len, width), single),
        pltpu.VMEM((page_len, 128), single),
        pltpu.VMEM((page_len, width), low),
        pltpu.VMEM((page_len, 4 * width), low),
        pltpu.VMEM((page_len, 4 * width), low),
        pltpu.VMEM((page_len, width), single),
        pltpu.VMEM((page_len, 128), single),
    ]
    scratch += [dma((count, depth - 1))] * 2 + [dma((count, 4))] * 2 + [dma((count,))] * 2
    scratch += [dma((count,))]
    scratch += [dma((depth - 1,))] * 2 + [dma((2,))] * 2 + [dma((1,))] * 2
    scratch += [dma((3,))] * 2 + [dma((3,)), dma((2,)), dma((18,))]
    scratch += [pltpu.VMEM((1, 3 * width), single)]
    plan = (depth, groups, page_len, width)
    results = pl.pallas_call(
        partial(forward_kernel, plan),
        out_shape=outs,
        in_specs=[anywhere, anywhere, vmem, smem, vmem, vmem] + [anywhere] * 5,
        out_specs=[anywhere] * len(outs),
        scratch_shapes=scratch,
        compiler_params=pltpu.CompilerParams(
            collective_id=0, has_side_effects=True, vmem_limit_bytes=VMEM_LIMIT
        ),
    )(tokens, cotangent, boxes, lengths, piece, frequency, *shards)
    return dict(zip(WEIGHTS, results[:5])), dict(zip(kinds, results[5:]))


VMEM_LIMIT = 60 * 2**20


class Scatter:
    def __init__(self, place, groups, stored, landing, summed, sems):
        self.place, self.groups, self.stored, self.summed = place, groups, stored, summed
        self.c_land, self.a1, self.b1, self.a2, self.b2, self.z_land = landing
        self.c_sems, self.xy_sems, self.z_sems = sems
        self.sent = set()

    def c_copy(self, g):
        p = self.place
        _, store, _, _, both, _ = self.groups[g]
        ref = self.stored[store].at[(ALL, ALL, ALL, 1 - p.c) + window(both)]
        return remote(ref, self.c_land[g], self.c_sems, (g,), p.c_peer)

    def xy_copy(self, g, i):
        p = self.place
        _, store, left, right, _, _ = self.groups[g]
        a, b = window(left), window(right)
        index, land, peer = (
            ((1 - p.y, ALL, ALL, p.c) + a, self.a1[g], p.y_peer),
            ((ALL, ALL, 1 - p.x, p.c) + b, self.b1[g], p.x_peer),
            ((p.y, ALL, 1 - p.x, p.c) + a, self.a2[g], p.x_peer),
            ((1 - p.y, ALL, p.x, p.c) + b, self.b2[g], p.y_peer),
        )[i]
        return remote(self.stored[store].at[index], land, self.xy_sems, (g, i), peer)

    def z_copy(self, g, k):
        p = self.place
        _, store, _, _, both, _ = self.groups[g]
        there = lax.rem(p.z + k + 1, p.depth)
        ref = self.stored[store].at[(p.y, there, p.x, p.c) + window(both)]
        return remote(ref, self.z_land[g].at[k], self.z_sems, (g, k), p.z_peers[k])

    def add(self, g, piece, outer, arrived):
        store = self.stored[self.groups[g][1]]
        cut = window(piece)

        def body(i, carry):
            here, there = outer(i)
            store[here + cut] = (
                store[here + cut].astype(jnp.float32) + arrived[there].astype(jnp.float32)
            ).astype(jnp.bfloat16)
            return carry

        return body

    def run(self, count, body):
        lax.fori_loop(0, count, body, 0)

    def start(self, g):
        self.c_copy(g).start()

    def first(self, g):
        p, d = self.place, self.place.depth
        _, _, left, right, both, _ = self.groups[g]
        self.c_copy(g).wait_recv()

        def outer(i):
            dy, dz, dx = lax.div(i, 2 * d), lax.rem(lax.div(i, 2), d), lax.rem(i, 2)
            return (dy, dz, dx, p.c), (dy, dz, dx)

        self.run(4 * d, self.add(g, both, outer, self.c_land[g]))
        self.xy_copy(g, 0).start()
        self.xy_copy(g, 1).start()

    def second(self, g):
        p, d = self.place, self.place.depth
        _, _, left, right, _, _ = self.groups[g]
        self.xy_copy(g, 0).wait_recv()

        def outer_a(i):
            dz, dx = lax.div(i, 2), lax.rem(i, 2)
            return (p.y, dz, dx, p.c), (dz, dx)

        self.run(2 * d, self.add(g, left, outer_a, self.a1[g]))
        self.xy_copy(g, 2).start()
        self.xy_copy(g, 1).wait_recv()

        def outer_b(i):
            dy, dz = lax.div(i, d), lax.rem(i, d)
            return (dy, dz, p.x, p.c), (dy, dz)

        self.run(2 * d, self.add(g, right, outer_b, self.b1[g]))
        self.xy_copy(g, 3).start()

    def third(self, g):
        p, d = self.place, self.place.depth
        _, _, left, right, _, _ = self.groups[g]

        def outer(i):
            return (p.y, i, p.x, p.c), (i,)

        self.xy_copy(g, 2).wait_recv()
        self.run(d, self.add(g, left, outer, self.a2[g]))
        self.xy_copy(g, 3).wait_recv()
        self.run(d, self.add(g, right, outer, self.b2[g]))
        for k in range(d - 1):
            self.z_copy(g, k).start()

    def fourth(self, g):
        p, d = self.place, self.place.depth
        name, store, _, _, both, result = self.groups[g]
        for k in range(d - 1):
            self.z_copy(g, k).wait_recv()
        total = self.stored[store][(p.y, p.z, p.x, p.c) + window(both)].astype(jnp.float32)
        for k in range(d - 1):
            total = total + self.z_land[g][k].astype(jnp.float32)
        self.summed[name][window(result)] = total

    def left(self, g):
        if g in self.sent:
            return
        self.sent.add(g)
        self.c_copy(g).wait_send()
        for i in range(4):
            self.xy_copy(g, i).wait_send()
        for k in range(self.place.depth - 1):
            self.z_copy(g, k).wait_send()


def backward_kernel(plan, *refs):
    depth, groups, page_len, width = plan
    block = page_len // 2
    refs = iter(refs)
    take = lambda n: [next(refs) for _ in range(n)]
    w_in = dict(zip(WEIGHTS, take(5)))
    (x_in, ct_in, qkv_in, table_in, p_in, o_in, unit1_in, inv1_in) = take(8)
    (g_in, d_in, unit2_in, inv2_in, vec_in) = take(5)
    out_out, dx_out = take(2)
    grad_out = dict(zip(WEIGHTS, take(5)))
    (piece_out,) = take(1)
    stored = dict(zip(("box", "out", "up", "down"), take(4)))
    count = len(groups)
    landing = [take(count) for _ in range(6)]
    summed = dict(zip(WEIGHTS, take(5)))
    w_box, w_out, box_w, box_g = take(4)
    (x_own, ct, qkv, table, keys, o_own, unit1, inv1, hidden, slope, unit2, inv2, vec) = take(13)
    (y1_low, d_a, d_mixed, out_low, dx_low, vec_g) = take(6)
    pieces, pc_land, py_land, px_land, pz_land, piece_sum = take(6)
    c_sems, xy_sems, z_sems = take(2), take(2), take(2)
    v_sems, vz_sems, ex_sems = take(2), take(2), take(2)
    in_sem, p_sem, out_sem = take(3)

    place = Place(depth)
    y, z, x, c = place.y, place.z, place.x, place.c
    scatter = Scatter(place, groups, stored, landing, summed, (c_sems, xy_sems, z_sems))

    sources = dict(
        unit2=(unit2_in, unit2),
        ct=(ct_in, ct),
        inv2=(inv2_in, inv2),
        vec=(vec_in, vec),
        g=(g_in, hidden),
        d=(d_in, slope),
        unit1=(unit1_in, unit1),
        inv1=(inv1_in, inv1),
        w_out=(w_in["out"], w_out),
        w_box=(w_in["box"], w_box),
        o=(o_in, o_own),
        qkv=(qkv_in, qkv),
        table=(table_in, table),
        x=(x_in, x_own),
    )
    order = list(sources)

    def fetch(name):
        source, target = sources[name]
        return pltpu.make_async_copy(source, target, in_sem.at[order.index(name)])

    def fetch_weight(name, target):
        at = len(order) + ("down", "up", "qkv").index(name)
        return pltpu.make_async_copy(w_in[name], target, in_sem.at[at])

    def vector(start, size=width):
        return vec[:, start : start + size]

    def total(value):
        return jnp.sum(value.astype(jnp.float32), axis=0, keepdims=True)

    def norm_back(grad, unit, inverse, gain):
        scaled = grad * gain
        mean_grad = jnp.mean(scaled, axis=1, keepdims=True)
        mean_unit = jnp.mean(scaled * unit, axis=1, keepdims=True)
        return inverse * (scaled - mean_grad - unit * mean_unit)

    names = [group[0] for group in groups]
    pending = []

    def stages(g):
        tick = []
        if 0 <= g < count:
            tick.append(partial(scatter.first, g))
        if 0 <= g - 1 < count:
            tick.append(partial(scatter.second, g - 1))
        if 0 <= g - 2 < count:
            tick.append(partial(scatter.third, g - 2))
        if 0 <= g - 3 < count:
            tick.append(partial(scatter.fourth, g - 3))
        return tick

    timeline = [stages(t) for t in range(count + 3)]
    position = [0]

    def tick(n=1):
        for _ in range(n):
            for event in timeline[position[0]]:
                event()
            position[0] += 1

    for name in order:
        fetch(name).start()

    fetch("unit2").wait()
    fetch("ct").wait()
    fetch("inv2").wait()
    fetch("vec").wait()
    unit = unit2[...]
    out_low[...] = (unit * vector(G2) + vector(E2)).astype(jnp.bfloat16)
    seed = ct[...].astype(jnp.float32)
    vec_g[:, G2 : G2 + width] = total(seed * unit)
    vec_g[:, E2 : E2 + width] = total(seed)
    d_h2 = norm_back(seed, unit, inv2[:, 0:1], vector(G2))
    unit2[...] = d_h2
    ct[...] = d_h2.astype(jnp.bfloat16)
    d_f = ct
    vec_g[:, B2 : B2 + width] = total(d_f[...])

    def rows(at):
        return pl.ds(pl.multiple_of(at * block, block), block)

    out_swap = remote(out_low.at[rows(1 - y)], out_out.at[y], ex_sems, (0,), place.y_peer)
    out_keep = pltpu.make_async_copy(out_low.at[rows(y)], out_out.at[y], out_sem.at[0])
    dx_swap = remote(dx_low.at[0], dx_low.at[1], ex_sems, (1,), place.y_peer)

    def with_down(w_down):
        fetch_weight("down", w_down).start()
        fetch("g").wait()

        def grad_tile(t, carry):
            rows_g = hidden[:, lanes(t * width, width)]
            part = dot_n(rows_g, d_f[...]).astype(jnp.bfloat16)
            stored["down"][0, t] = part[:, :384].reshape(2, 2, -1, 384)
            stored["down"][1, t] = part[:, 384:].reshape(2, 2, -1, 384)
            return carry

        lax.fori_loop(0, depth, grad_tile, 0)
        place.greet()
        for g in range(count):
            if names[g] == "down":
                scatter.start(g)
        out_swap.start()
        out_keep.start()
        fetch_weight("down", w_down).wait()
        fetch("d").wait()

        def slope_tile(t, carry):
            w0 = w_down.at[0, t][...].reshape(width, 384)
            w1 = w_down.at[1, t][...].reshape(width, 384)
            d_hidden = dot_t(d_f[:, :384], w0) + dot_t(d_f[:, 384:], w1)
            at = lanes(t * width, width)
            d_pre = (d_hidden * slope[:, at].astype(jnp.float32)).astype(jnp.bfloat16)
            slope[:, at] = d_pre
            vec_g[:, lanes(B1 + t * width, width)] = total(d_pre)
            return carry

        lax.fori_loop(0, depth, slope_tile, 0)

    pl.run_scoped(with_down, pltpu.VMEM(w_in["down"].shape, jnp.bfloat16))
    tick()

    fetch("unit1").wait()
    fetch("inv1").wait()
    y1_low[...] = (unit1[...] * vector(G1) + vector(E1)).astype(jnp.bfloat16)

    def with_up(w_up):
        fetch_weight("up", w_up).start()

        def up_tile(i, carry):
            h, part = lax.rem(i, 2), lax.div(i, 2)
            tile = dot_n(y1_low[...], slope[:, lanes(h * 1536 + part * width, width)])
            stored["up"][h, :, :, :, :, lanes(part * width, width)] = tile.astype(
                jnp.bfloat16
            ).reshape(depth, 2, 2, -1, width)
            return carry

        lax.fori_loop(0, 4, up_tile, 0)
        for g in range(count):
            if names[g] == "up":
                scatter.start(g)
        tick()
        fetch_weight("up", w_up).wait()

        def back_tile(h, carry):
            w = w_up.at[h][...].reshape(width, 1536)
            unit2[...] += dot_t(slope[:, lanes(h * 1536, 1536)], w)
            return carry

        lax.fori_loop(0, 2, back_tile, 0)

    pl.run_scoped(with_up, pltpu.VMEM(w_in["up"].shape, jnp.bfloat16))

    unit = unit1[...]
    d_y1 = unit2[...]
    vec_g[:, G1 : G1 + width] = total(d_y1 * unit)
    vec_g[:, E1 : E1 + width] = total(d_y1)
    d_h1 = norm_back(d_y1, unit, inv1[:, 0:1], vector(G1))
    unit1[...] = d_h1
    d_a[...] = d_h1.astype(jnp.bfloat16)
    vec_g[:, BO : BO + width] = total(d_a[...])
    fetch("w_out").wait()
    fetch("o").wait()
    d_mixed[...] = (
        dot_t(d_a[:, :384], w_out.at[0][...].reshape(width, 384))
        + dot_t(d_a[:, 384:], w_out.at[1][...].reshape(width, 384))
    ).astype(jnp.bfloat16)
    part = dot_n(o_own[...].astype(jnp.bfloat16), d_a[...]).astype(jnp.bfloat16)
    for h in range(2):
        stored["out"][h] = part[:, h * 384 : (h + 1) * 384].reshape(depth, 2, 2, -1, 384)
    scatter.start(names.index("out"))

    for name in ("w_box", "qkv", "table", "x"):
        fetch(name).wait()
    low = w_box.at[0][...].reshape(width, 2 * FREQ)
    high = w_box.at[1][...].reshape(width, 2 * FREQ)
    box_w[...] = jnp.concatenate(
        [low[:, :FREQ], high[:, :FREQ], low[:, FREQ:], high[:, FREQ:]], axis=1
    )
    keys[...] = table[...].astype(jnp.bfloat16)
    table[...] = table[...] * (HEAD**-0.5)
    head_lane = lax.broadcasted_iota(jnp.int32, (1, 128), 1)

    def p_copy(p, slot, i):
        at = lanes((slot * 2 + i) * page_len, page_len)
        return pltpu.make_async_copy(p_in.at[p, i], hidden.at[:, at], p_sem.at[slot, i])

    p_copy(0, 0, 0).start()
    p_copy(0, 0, 1).start()

    def with_qkv(w_qkv):
        fetch_weight("qkv", w_qkv).start()
        first_tick = position[0]

        def pair(p, carry):
            for i, at in enumerate(BACK_TICKS):
                @pl.when(p == at)
                def _():
                    for event in timeline[first_tick + i]:
                        event()

            slot = lax.rem(p, 2)

            @pl.when(p < HEADS // 2 - 1)
            def _():
                p_copy(p + 1, 1 - slot, 0).start()
                p_copy(p + 1, 1 - slot, 1).start()

            p_copy(p, slot, 0).wait()
            p_copy(p, slot, 1).wait()
            q = qkv[:, lanes(p * 128, 128)]
            k = qkv[:, lanes(width + p * 128, 128)]
            v = qkv[:, lanes(2 * width + p * 128, 128)]
            w = box_w[pl.ds(pl.multiple_of(p * 128, 128), 128), :]
            d_o = d_mixed[:, lanes(p * 128, 128)]
            weighted = d_o.astype(jnp.float32) * o_own[:, lanes(p * 128, 128)]
            grads = []
            d_w = jnp.zeros((128, BOX_DIM), jnp.float32)
            for i in range(2):
                of_head = (head_lane < HEAD) == (i == 0)
                probs = hidden[:, lanes((slot * 2 + i) * page_len, page_len)]
                delta = jnp.sum(jnp.where(of_head, weighted, 0.0), axis=1, keepdims=True)
                d_probs = dot_t(jnp.where(of_head, d_o, jnp.zeros_like(d_o)), v)
                d_s = (probs.astype(jnp.float32) * (d_probs - delta)).astype(jnp.bfloat16)
                d_q = jnp.dot(d_s, k, preferred_element_type=jnp.float32)
                d_1 = jnp.dot(d_s, keys[0], preferred_element_type=jnp.float32)
                d_2 = jnp.dot(d_s, keys[1], preferred_element_type=jnp.float32)
                cosine, sine = table[0], table[1]
                d_sine = (d_1 * sine - d_2 * cosine).astype(jnp.bfloat16)
                d_cosine = (d_1 * cosine + d_2 * sine).astype(jnp.bfloat16)
                d_u = jnp.concatenate([d_sine, d_cosine], axis=1)
                d_q = d_q * (HEAD**-0.5) + dot_t(d_u, w)
                d_w = d_w + dot_n(jnp.where(of_head, q, jnp.zeros_like(q)), d_u)
                grads.append((d_q, dot_n(d_s, q) * (HEAD**-0.5), dot_n(probs, d_o)))
            first_head = head_lane < HEAD
            for n, (one, two) in enumerate(zip(*grads)):
                value = jnp.where(first_head, one, two).astype(jnp.bfloat16)
                slope[:, lanes(n * width + p * 128, 128)] = value
                if n == 0:
                    vec_g[:, lanes(BQ + p * 128, 128)] = total(value)
                if n == 2:
                    vec_g[:, lanes(BV + p * 128, 128)] = total(value)
            box_g[pl.ds(pl.multiple_of(p * 128, 128), 128), :] = d_w.astype(jnp.bfloat16)
            return carry

        lax.fori_loop(0, HEADS // 2, pair, 0)
        position[0] += len(BACK_TICKS)

        part = box_g[...]
        stored["box"][0] = jnp.concatenate(
            [part[:, :FREQ], part[:, 2 * FREQ : 3 * FREQ]], axis=1
        ).reshape(depth, 2, 2, -1, 384)
        stored["box"][1] = jnp.concatenate(
            [part[:, FREQ : 2 * FREQ], part[:, 3 * FREQ :]], axis=1
        ).reshape(depth, 2, 2, -1, 384)
        scatter.start(names.index("box"))
        for g in range(count):
            if names[g] == "down":
                scatter.left(g)

        height = stored["box"].shape[4]
        for t in range(3):
            def qkv_tile(h, carry, t=t):
                tile = dot_n(x_own[...], slope[:, lanes(h * 1152 + t * 384, 384)])
                stored["down"][h, :, :, :, t * height : (t + 1) * height, :] = tile.astype(
                    jnp.bfloat16
                ).reshape(depth, 2, 2, -1, 384)
                return carry

            lax.fori_loop(0, 2, qkv_tile, 0)
            scatter.start([g for g in range(count) if names[g] == "qkv"][t])

        for dz in range(depth):
            for dx in range(2):
                for dc in range(2):
                    for dy in range(2):
                        device = ((dz * 2 + dx) * 2 + dc) * 2 + dy
                        start = device * (VECTORS // (8 * depth)) // 128 * 128
                        pieces[dy, dz, dx, dc] = vec_g[:, start : start + 384]
        vector_c.start()
        fetch_weight("qkv", w_qkv).wait()

        def back_tile(h, carry):
            w = w_qkv.at[h][...].reshape(width, 1152)
            unit1[...] += dot_t(slope[:, lanes(h * 1152, 1152)], w)
            return carry

        lax.fori_loop(0, 2, back_tile, 0)
        dx_low[0] = unit1[rows(1 - y), :].astype(jnp.bfloat16)
        dx_swap.start()
        pltpu.make_async_copy(unit1.at[rows(y)], dx_out.at[y], out_sem.at[1]).start()

    vector_c = remote(pieces.at[:, :, :, 1 - c], pc_land, v_sems, (0,), place.c_peer)
    vector_y = remote(pieces.at[1 - y, :, :, c], py_land, v_sems, (1,), place.y_peer)
    vector_x = remote(pieces.at[y, :, 1 - x, c], px_land, v_sems, (2,), place.x_peer)

    def vector_z(k):
        there = lax.rem(z + k + 1, depth)
        return remote(
            pieces.at[y, there, x, c], pz_land.at[k], vz_sems, (k,), place.z_peers[k]
        )

    pl.run_scoped(with_qkv, pltpu.VMEM(w_in["qkv"].shape, jnp.bfloat16))

    vector_c.wait_recv()
    pieces[:, :, :, c] += pc_land[...]
    vector_y.start()
    tick()
    vector_y.wait_recv()
    pieces[y, :, :, c] += py_land[...]
    vector_x.start()
    tick()
    vector_x.wait_recv()
    pieces[y, :, x, c] += px_land[...]
    for k in range(depth - 1):
        vector_z(k).start()
    dx_swap.wait_recv()
    unit2[0:block, :] = dx_low[1].astype(jnp.float32)
    pltpu.make_async_copy(unit2.at[0:block], dx_out.at[1 - y], out_sem.at[2]).start()
    while position[0] < len(timeline):
        tick()
    for k in range(depth - 1):
        vector_z(k).wait_recv()
    piece_total = pieces[y, z, x, c]
    for k in range(depth - 1):
        piece_total = piece_total + pz_land[k]
    piece_sum[...] = piece_total
    finals = [pltpu.make_async_copy(piece_sum, piece_out, out_sem.at[3])]
    for i, name in enumerate(WEIGHTS):
        finals.append(pltpu.make_async_copy(summed[name], grad_out[name], out_sem.at[4 + i]))
    for copy in finals:
        copy.start()
    for g in range(count):
        scatter.left(g)
    for copy in (vector_c, vector_y, vector_x, out_swap, dx_swap):
        copy.wait_send()
    for k in range(depth - 1):
        vector_z(k).wait_send()
    out_swap.wait_recv()
    out_keep.wait()
    pltpu.make_async_copy(unit1.at[rows(y)], dx_out.at[y], out_sem.at[1]).wait()
    pltpu.make_async_copy(unit2.at[0:block], dx_out.at[1 - y], out_sem.at[2]).wait()
    for copy in finals:
        copy.wait()


BACK_TICKS = (0, 2, 4)


def backward_call(depth, full, kept, shards):
    low, single = jnp.bfloat16, jnp.float32
    page_len, width = kept["x"].shape
    heights = {n: s.shape[0] for n, s in zip(WEIGHTS, shards)}
    tall, short = heights["down"], heights["qkv"]

    def columns(name, first, left, right):
        pieces = by_columns(name, short, first, left, right)
        return (name, name) + pieces[1:] + (pieces[3],)

    def third(t, left):
        top = t * short
        return (
            "qkv",
            "down",
            (top, short, 0, left),
            (top, short, left, 384 - left),
            (top, short, 0, 384),
            (0, short, t * 384, 384),
        )

    def slab(first, size):
        pieces = by_rows("down", tall, first, size)
        return ("down", "down") + pieces[1:] + (pieces[3],)

    groups = [
        slab(0, 256),
        slab(256, 128),
        columns("up", 0, 384, 384),
        columns("up", 768, 384, 384),
        columns("out", 0, 256, 128),
        columns("box", 0, 128, 256),
        third(0, 256),
        third(1, 128),
        third(2, 256),
    ]
    count = len(groups)
    outs = [
        jax.ShapeDtypeStruct((2, page_len // 2, width), low),
        jax.ShapeDtypeStruct((2, page_len // 2, width), single),
    ]
    outs += [jax.ShapeDtypeStruct(s.shape, single) for s in shards]
    outs += [jax.ShapeDtypeStruct((1, 384), single)]
    by_name = dict(zip(WEIGHTS, shards))

    def vmem(*shape, kind=low):
        return pltpu.VMEM(shape, kind)

    size = lambda cut: (cut[1], cut[3])
    dma = pltpu.SemaphoreType.DMA
    scratch = [vmem(2, depth, 2, 2, *by_name[n].shape) for n in ("box", "out", "up", "down")]
    scratch += [vmem(2, depth, 2, *size(g[4])) for g in groups]
    scratch += [vmem(depth, 2, *size(g[2])) for g in groups]
    scratch += [vmem(2, depth, *size(g[3])) for g in groups]
    scratch += [vmem(depth, *size(g[2])) for g in groups]
    scratch += [vmem(depth, *size(g[3])) for g in groups]
    scratch += [vmem(depth - 1, *size(g[4])) for g in groups]
    scratch += [vmem(*s.shape, kind=single) for s in shards]
    scratch += [vmem(*full[n].shape) for n in ("box", "out")]
    scratch += [vmem(width, BOX_DIM), vmem(width, BOX_DIM)]
    scratch += [vmem(*kept[n].shape, kind=kept[n].dtype) for n in ("x", "ct", "qkv", "table")]
    scratch += [vmem(*kept["table"].shape)]
    scratch += [
        vmem(*kept[n].shape, kind=kept[n].dtype)
        for n in ("o", "unit1", "inv1", "g", "d", "unit2", "inv2", "vec")
    ]
    scratch += [vmem(page_len, width)] * 4
    scratch += [vmem(2, page_len // 2, width), vmem(1, VECTORS + 128, kind=single)]
    scratch += [
        vmem(2, depth, 2, 2, 1, 384, kind=single),
        vmem(2, depth, 2, 1, 384, kind=single),
        vmem(depth, 2, 1, 384, kind=single),
        vmem(depth, 1, 384, kind=single),
        vmem(depth - 1, 1, 384, kind=single),
        vmem(1, 384, kind=single),
    ]
    scratch += [dma((count,))] * 2 + [dma((count, 4))] * 2 + [dma((count, depth - 1))] * 2
    scratch += [dma((3,))] * 2 + [dma((depth - 1,))] * 2 + [dma((2,))] * 2
    scratch += [dma((17,)), dma((2, 2)), dma((9,))]
    anywhere = pl.BlockSpec(memory_space=pl.ANY)
    operands = [full[n] for n in WEIGHTS] + list(kept.values())
    plan = (depth, groups, page_len, width)
    results = pl.pallas_call(
        partial(backward_kernel, plan),
        out_shape=outs,
        in_specs=[anywhere] * len(operands),
        out_specs=[anywhere] * len(outs),
        scratch_shapes=scratch,
        compiler_params=pltpu.CompilerParams(
            collective_id=1, has_side_effects=True, vmem_limit_bytes=VMEM_BACK
        ),
    )(*operands)
    return results


VMEM_BACK = 63 * 2**20


def fast_layer(tokens, boxes, lengths, wqkv, wbox, wout, wup, wdown, vectors, cotangent):
    depth = lax.axis_size("dp") // 4
    device = lax.axis_index("dp") * 2 + lax.axis_index("blk")
    own = vectors.shape[0]
    offset = lax.rem(device * own, 128)
    piece = lax.dynamic_update_slice(
        jnp.zeros((384,), jnp.float32), vectors.astype(jnp.float32), (offset,)
    )[None, :]
    shards = (wqkv, wbox, wout, wup, wdown)
    full, kept = forward_call(depth, tokens, cotangent, boxes, lengths, piece, shards)
    results = backward_call(depth, full, kept, shards)
    d_vectors = lax.dynamic_slice(results[7][0], (offset,), (own,))
    return (*results[:7], d_vectors)


def on_device(*args):
    tokens, wqkv, wbox, wdown = args[0], args[3], args[4], args[7]
    blocks, groups = lax.axis_size("blk"), lax.axis_size("dp")
    fits = (
        blocks == 2
        and groups % 4 == 0
        and tokens.shape[0] == 2
        and wqkv.shape[0] % 16 == 0
        and wdown.shape[0] % 32 == 0
        and wbox.shape[1] == 2 * FREQ
    )
    return fast_layer(*args) if fits else general_layer(*args)


def solution(mesh):
    in_specs = (
        P("dp", "blk", None),
        P(None, "dp", "blk"),
        P("dp"),
        P("dp", "blk"),
        P("dp", "blk"),
        P("dp", "blk"),
        P("dp", "blk"),
        P("dp", "blk"),
        P(("dp", "blk")),
        P("dp", "blk", None),
    )
    out_specs = (
        P("dp", "blk", None),
        P("dp", "blk", None),
        P("dp", "blk"),
        P("dp", "blk"),
        P("dp", "blk"),
        P("dp", "blk"),
        P("dp", "blk"),
        P(("dp", "blk")),
    )
    return jax.shard_map(
        on_device, mesh=mesh, in_specs=in_specs, out_specs=out_specs, check_vma=False
    )
```

```python
from functools import partial
import math

import jax
import jax.numpy as jnp
import numpy as np
from jax import lax
from jax.experimental import pallas as pl
from jax.experimental.pallas import tpu as pltpu
from jax.sharding import PartitionSpec as P

HEADS = 12
HEAD = 64
FREQ = 192
BOX_DIM = 768

EPSILON = 1e-12
MASKED = -1e30


def box_table(boxes):
    frequency = jnp.exp(jnp.arange(FREQ, dtype=jnp.float32) * (-math.log(10000.0) / FREQ))
    across = boxes[0].astype(jnp.float32)[..., None] * frequency
    upward = boxes[1].astype(jnp.float32)[..., None] * frequency
    return jnp.concatenate(
        [jnp.cos(across), jnp.sin(across), jnp.cos(upward), jnp.sin(upward)], axis=-1
    )


def rotate(coeffs, own_table):
    cos_across, sin_across, cos_upward, sin_upward = jnp.split(own_table[..., None, :], 4, axis=-1)
    sa, ca, sb, cb = jnp.split(coeffs, 4, axis=-1)
    return jnp.concatenate(
        [
            sa * sin_across + ca * cos_across,
            ca * sin_across - sa * cos_across,
            sb * sin_upward + cb * cos_upward,
            cb * sin_upward - sb * cos_upward,
        ],
        axis=-1,
    )


def unrotate(grad_rows, own_table):
    cos_across, sin_across, cos_upward, sin_upward = jnp.split(own_table[..., None, :], 4, axis=-1)
    d1a, d2a, d1b, d2b = jnp.split(grad_rows, 4, axis=-1)
    return jnp.concatenate(
        [
            d1a * sin_across - d2a * cos_across,
            d1a * cos_across + d2a * sin_across,
            d1b * sin_upward - d2b * cos_upward,
            d1b * cos_upward + d2b * sin_upward,
        ],
        axis=-1,
    )


def normalize(hidden):
    row_mean = jnp.mean(hidden, axis=-1, keepdims=True)
    centered = hidden - row_mean
    inverse = lax.rsqrt(jnp.mean(centered * centered, axis=-1, keepdims=True) + EPSILON)
    return centered * inverse, inverse


def normalize_back(grad, unit, inverse, gain):
    scaled = grad * gain
    mean_grad = jnp.mean(scaled, axis=-1, keepdims=True)
    mean_unit = jnp.mean(scaled * unit, axis=-1, keepdims=True)
    d_hidden = inverse * (scaled - mean_grad - unit * mean_unit)
    return d_hidden, jnp.sum(grad * unit, axis=0), jnp.sum(grad, axis=0)


def unpack(vector_all, model_width, hidden_units):
    cuts = [model_width] * 5 + [hidden_units] + [model_width] * 3
    pieces = []
    offset = 0
    for length_here in cuts:
        pieces.append(vector_all[offset : offset + length_here])
        offset = offset + length_here
    return pieces


def dot32(a, b):
    return jnp.dot(a, b, preferred_element_type=jnp.float32)


def gather_weight(shard):
    part = lax.all_gather(shard, "blk", axis=1, tiled=True)
    return lax.all_gather(part, "dp", axis=0, tiled=True)


def scatter_weight(grad):
    part = lax.psum_scatter(grad.astype(jnp.bfloat16), "dp", scatter_dimension=0, tiled=True)
    return lax.psum_scatter(part, "blk", scatter_dimension=1, tiled=True).astype(jnp.float32)


def general_layer(tokens, boxes, lengths, wqkv, wbox, wout, wup, wdown, vectors, cotangent):
    blocks = lax.axis_size("blk")
    pages_here = tokens.shape[0] // blocks
    model_width = tokens.shape[2]
    to_pages = partial(
        lax.all_to_all, axis_name="blk", split_axis=0, concat_axis=1, tiled=True
    )
    from_pages = partial(
        lax.all_to_all, axis_name="blk", split_axis=1, concat_axis=0, tiled=True
    )
    page_tokens = to_pages(tokens)
    page_boxes = lax.all_to_all(boxes, "blk", split_axis=1, concat_axis=2, tiled=True)
    page_lengths = lax.dynamic_slice(lengths, (lax.axis_index("blk") * pages_here,), (pages_here,))
    full_qkv = gather_weight(wqkv)
    full_box = gather_weight(wbox)
    full_out = gather_weight(wout)
    full_up = gather_weight(wup)
    full_down = gather_weight(wdown)
    full_vec = lax.all_gather(vectors, ("dp", "blk"), axis=0, tiled=True).astype(jnp.float32)
    page_cotangent = to_pages(cotangent)
    hidden_units = full_up.shape[1]
    bq, bv, bo, g1, e1, b1, b2, g2, e2 = unpack(full_vec, model_width, hidden_units)
    page_len = page_tokens.shape[1]
    score_scale = HEAD ** (-0.5)

    x = page_tokens.reshape(-1, model_width)
    projected = dot32(x, full_qkv)
    head_shape = (pages_here, page_len, HEADS, HEAD)
    q = (projected[:, :model_width] + bq).astype(jnp.bfloat16).reshape(head_shape)
    k = projected[:, model_width : 2 * model_width].astype(jnp.bfloat16).reshape(head_shape)
    v = (projected[:, 2 * model_width :] + bv).astype(jnp.bfloat16).reshape(head_shape)
    table = box_table(page_boxes)
    box_heads = full_box.reshape(HEADS, HEAD, BOX_DIM)
    coeffs = jnp.einsum("pqhd,hdc->pqhc", q, box_heads, preferred_element_type=jnp.float32)
    box_query = rotate(coeffs, table).astype(jnp.bfloat16)
    box_keys = table.astype(jnp.bfloat16)
    scores = (
        jnp.einsum("pqhd,pkhd->phqk", q, k, preferred_element_type=jnp.float32)
        + jnp.einsum("pqhc,pkc->phqk", box_query, box_keys, preferred_element_type=jnp.float32)
    ) * score_scale
    is_valid = (jnp.arange(page_len)[None, :] < page_lengths[:, None])[:, None, None, :]
    masked = jnp.where(is_valid, scores, MASKED)
    probs = jax.nn.softmax(masked, axis=-1)
    probs_low = probs.astype(jnp.bfloat16)
    mixed = jnp.einsum("phqk,pkhd->pqhd", probs_low, v, preferred_element_type=jnp.float32)
    mixed_low = mixed.astype(jnp.bfloat16).reshape(-1, model_width)
    unit1, inv1 = normalize(x.astype(jnp.float32) + dot32(mixed_low, full_out) + bo)
    y1 = unit1 * g1 + e1
    y1_low = y1.astype(jnp.bfloat16)
    pre = dot32(y1_low, full_up) + b1
    hidden = jax.nn.gelu(pre, approximate=False).astype(jnp.bfloat16)
    unit2, inv2 = normalize(y1 + dot32(hidden, full_down) + b2)
    output = (unit2 * g2 + e2).astype(jnp.bfloat16)

    seed = page_cotangent.reshape(-1, model_width).astype(jnp.float32)
    d_h2, d_g2, d_e2 = normalize_back(seed, unit2, inv2, g2)
    d_f = d_h2.astype(jnp.bfloat16)
    d_hidden = dot32(d_f, full_down.T)
    d_pre = jax.vjp(partial(jax.nn.gelu, approximate=False), pre)[1](d_hidden)[0]
    d_pre = d_pre.astype(jnp.bfloat16)
    d_wdown = dot32(hidden.T, d_f)
    d_wup = dot32(y1_low.T, d_pre)
    d_y1 = dot32(d_pre, full_up.T) + d_h2
    d_h1, d_g1, d_e1 = normalize_back(d_y1, unit1, inv1, g1)
    d_a = d_h1.astype(jnp.bfloat16)
    d_wout = dot32(mixed_low.T, d_a)
    d_mixed = dot32(d_a, full_out.T).astype(jnp.bfloat16).reshape(head_shape)
    row_delta = jnp.einsum("pqhd,pqhd->phq", d_mixed.astype(jnp.float32), mixed)
    d_probs = jnp.einsum("pqhd,pkhd->phqk", d_mixed, v, preferred_element_type=jnp.float32)
    d_raw = (probs * (d_probs - row_delta[..., None])).astype(jnp.bfloat16)
    d_q = jnp.einsum("phqk,pkhd->pqhd", d_raw, k, preferred_element_type=jnp.float32)
    d_box_q = jnp.einsum("phqk,pkc->pqhc", d_raw, box_keys, preferred_element_type=jnp.float32)
    d_k = jnp.einsum("phqk,pqhd->pkhd", d_raw, q, preferred_element_type=jnp.float32)
    d_v = jnp.einsum("phqk,pqhd->pkhd", probs_low, d_mixed, preferred_element_type=jnp.float32)
    d_coeffs = unrotate(d_box_q * score_scale, table).astype(jnp.bfloat16)
    d_q = d_q * score_scale + jnp.einsum(
        "pqhc,hdc->pqhd", d_coeffs, box_heads, preferred_element_type=jnp.float32
    )
    d_wbox = jnp.einsum("pqhd,pqhc->hdc", q, d_coeffs, preferred_element_type=jnp.float32)
    flat = (-1, model_width)
    d_q = d_q.astype(jnp.bfloat16).reshape(flat)
    d_k = (d_k * score_scale).astype(jnp.bfloat16).reshape(flat)
    d_v = d_v.astype(jnp.bfloat16).reshape(flat)
    d_c = jnp.concatenate([d_q, d_k, d_v], axis=1)
    d_wqkv = dot32(x.T, d_c)
    d_x = dot32(d_c, full_qkv.T) + d_h1
    total = partial(jnp.sum, axis=0, dtype=jnp.float32)
    vector_grad = jnp.concatenate(
        [total(d_q), total(d_v), total(d_a), d_g1, d_e1, total(d_pre), total(d_f), d_g2, d_e2]
    )
    return (
        from_pages(output.reshape(page_tokens.shape)),
        from_pages(d_x.reshape(page_tokens.shape)),
        scatter_weight(d_wqkv),
        scatter_weight(d_wbox.reshape(model_width, BOX_DIM)),
        scatter_weight(d_wout),
        scatter_weight(d_wup),
        scatter_weight(d_wdown),
        lax.psum_scatter(vector_grad, ("dp", "blk"), scatter_dimension=0, tiled=True),
    )


GATHER_GROUPS = (
    ("qkv", (0, 48, 0, 384), (("zxy", (0, 48, 0, 384)),)),
    ("qkv", (0, 48, 384, 384), (("zyx", (0, 48, 384, 384)),)),
    ("qkv", (0, 48, 768, 384), (("zyx", (0, 48, 768, 256)), ("yxz", (0, 48, 1024, 128)),)),
    ("box", (0, 48, 0, 384), (("zxy", (0, 48, 0, 256)), ("yxz", (0, 48, 256, 128)),)),
    ("out", (0, 48, 0, 384), (("zxy", (0, 48, 0, 256)), ("yzx", (0, 48, 256, 128)),)),
    ("up", (0, 48, 0, 384), (("zyx", (0, 48, 0, 256)), ("yzx", (0, 48, 256, 128)),)),
    ("up", (0, 48, 384, 384), (("zxy", (0, 48, 384, 384)),)),
    ("up", (0, 48, 768, 384), (("zxy", (0, 48, 768, 128)), ("yxz", (0, 48, 896, 256)),)),
    ("up", (0, 48, 1152, 384), (("zyx", (0, 48, 1152, 384)),)),
    ("down", (0, 192, 0, 128), (("zyx", (0, 64, 0, 128)), ("yxz", (64, 128, 0, 128)),)),
    ("down", (0, 192, 128, 128), (("zxy", (0, 128, 128, 128)), ("zyx", (128, 64, 128, 128)),)),
    ("down", (0, 192, 256, 128), (("yxz", (0, 192, 256, 128)),)),
)
GATHER_EVENTS = (
    (4.0, 0, 0, 0),
    (4.0, 1, 0, 0),
    (4.0, 2, 0, 0),
    (4.0, 2, 1, 0),
    (4.0, 3, 0, 0),
    (4.0, 3, 1, 0),
    (4.0, 4, 1, 0),
    (4.0, 5, 1, 0),
    (8.2, 0, 0, 10),
    (10.1, 0, 0, 1),
    (10.1, 4, 0, 0),
    (10.5, 1, 0, 10),
    (12.3, 2, 0, 10),
    (12.5, 1, 0, 1),
    (12.5, 5, 0, 0),
    (13.8, 3, 0, 10),
    (14.1, 2, 0, 1),
    (14.1, 6, 0, 0),
    (14.9, 2, 1, 1),
    (14.9, 7, 1, 0),
    (15.2, 3, 1, 1),
    (15.2, 9, 1, 0),
    (15.4, 4, 0, 10),
    (15.4, 4, 1, 1),
    (15.4, 11, 0, 0),
    (15.5, 0, 0, 2),
    (15.7, 5, 1, 1),
    (15.8, 3, 0, 1),
    (15.8, 7, 0, 0),
    (17.3, 8, 0, 0),
    (17.3, 4, 0, 1),
    (17.6, 5, 0, 10),
    (18.3, 2, 1, 2),
    (18.8, 3, 1, 2),
    (19.1, 1, 0, 2),
    (20.0, 9, 0, 0),
    (20.0, 5, 0, 1),
    (20.1, 3, 0, 2),
    (20.3, 4, 1, 11),
    (21.4, 6, 0, 10),
    (21.9, 5, 1, 11),
    (22.1, 2, 0, 2),
    (23.9, 7, 1, 1),
    (24.2, 4, 1, 2),
    (24.3, 4, 0, 2),
    (24.6, 9, 1, 1),
    (25.2, 10, 0, 0),
    (25.2, 10, 1, 0),
    (25.2, 6, 0, 1),
    (25.6, 7, 0, 10),
    (26.1, 11, 0, 1),
    (26.4, 2, 1, 12),
    (27.5, 5, 1, 2),
    (28.5, 1, 0, 3),
    (28.7, 0, 0, 3),
    (29.0, 7, 0, 1),
    (30.4, 0, 0, 4),
    (30.6, 1, 0, 4),
    (30.9, 8, 0, 10),
    (31.1, 3, 1, 12),
    (31.7, 2, 1, 3),
    (32.8, 2, 1, 4),
    (33.4, 8, 0, 1),
    (33.7, 9, 0, 10),
    (34.0, 5, 0, 2),
    (35.0, 2, 0, 3),
    (35.1, 3, 0, 3),
    (35.1, 3, 1, 3),
    (35.3, 9, 0, 1),
    (35.6, 10, 0, 10),
    (35.9, 7, 1, 2),
    (36.4, 3, 1, 4),
    (36.5, 2, 0, 4),
    (36.6, 3, 0, 4),
    (36.9, 10, 1, 10),
    (37.8, 9, 1, 2),
    (38.1, 10, 0, 1),
    (39.1, 10, 1, 1),
    (39.2, 4, 1, 3),
    (40.3, 6, 0, 2),
    (40.4, 4, 0, 3),
    (40.4, 4, 1, 4),
    (40.9, 7, 1, 12),
    (41.0, 11, 0, 2),
    (41.8, 4, 0, 4),
    (42.7, 5, 1, 3),
    (43.4, 7, 0, 2),
    (43.5, 8, 0, 2),
    (43.8, 5, 1, 4),
    (44.9, 9, 0, 2),
    (47.9, 7, 1, 3),
    (48.5, 9, 1, 12),
    (49.3, 7, 1, 4),
    (50.0, 10, 1, 2),
    (50.5, 5, 0, 3),
    (51.9, 5, 0, 4),
    (52.4, 6, 0, 3),
    (53.3, 10, 0, 2),
    (54.2, 6, 0, 4),
    (54.9, -1, 0, 0),
    (54.9, 7, 0, 3),
    (56.1, 7, 0, 4),
    (58.7, 9, 1, 3),
    (59.6, 8, 0, 3),
    (60.5, 11, 0, 12),
    (60.6, 9, 1, 4),
    (61.3, 10, 0, 3),
    (61.3, 8, 0, 4),
    (62.4, 9, 0, 3),
    (63.0, 10, 0, 4),
    (63.8, 9, 0, 4),
    (65.2, 10, 1, 3),
    (66.7, 10, 1, 4),
    (69.4, 11, 0, 3),
    (71.5, 11, 0, 4),
)
SCATTER_GROUPS = (
    ("down", "down", (0, 192, 0, 128), (0, 192, 0, 128), (("xyz", (0, 128, 0, 128)), ("zyx", (128, 64, 0, 128)),)),
    ("down", "down", (0, 192, 128, 128), (0, 192, 128, 128), (("yxz", (0, 128, 128, 128)), ("xzy", (128, 64, 128, 128)),)),
    ("down", "down", (0, 192, 256, 128), (0, 192, 256, 128), (("xyz", (0, 128, 256, 128)), ("zxy", (128, 64, 256, 128)),)),
    ("up", "up", (0, 48, 0, 384), (0, 48, 0, 384), (("yxz", (0, 48, 0, 256)), ("xyz", (0, 48, 256, 128)),)),
    ("up", "up", (0, 48, 384, 384), (0, 48, 384, 384), (("xyz", (0, 48, 384, 256)), ("zxy", (0, 48, 640, 128)),)),
    ("up", "up", (0, 48, 768, 384), (0, 48, 768, 384), (("yxz", (0, 48, 768, 256)), ("zxy", (0, 48, 1024, 128)),)),
    ("up", "up", (0, 48, 1152, 384), (0, 48, 1152, 384), (("yxz", (0, 48, 1152, 256)), ("zyx", (0, 48, 1408, 128)),)),
    ("out", "out", (0, 48, 0, 384), (0, 48, 0, 384), (("xyz", (0, 48, 0, 256)), ("zyx", (0, 48, 256, 128)),)),
    ("box", "box", (0, 48, 0, 384), (0, 48, 0, 384), (("yxz", (0, 48, 0, 256)), ("zxy", (0, 48, 256, 128)),)),
    ("qkv", "down", (0, 48, 0, 384), (0, 48, 0, 384), (("yxz", (0, 48, 0, 128)), ("xzy", (0, 48, 128, 256)),)),
    ("qkv", "down", (48, 48, 0, 384), (0, 48, 384, 384), (("yxz", (48, 48, 0, 128)), ("xyz", (48, 48, 128, 128)), ("zyx", (48, 48, 256, 128)),)),
    ("qkv", "down", (96, 48, 0, 384), (0, 48, 768, 384), (("yxz", (96, 48, 0, 128)), ("xyz", (96, 48, 128, 128)), ("xzy", (96, 48, 256, 128)),)),
)
SCATTER_EVENTS = (
    (9.0, 0, 0, 0),
    (10.1, 1, 0, 0),
    (11.3, 2, 0, 0),
    (13.6, 0, 1, 10),
    (15.2, 3, 0, 0),
    (16.2, 4, 0, 0),
    (17.2, 5, 0, 0),
    (17.4, 0, 1, 1),
    (17.8, 0, 0, 1),
    (18.2, 6, 0, 0),
    (18.4, 2, 1, 10),
    (19.0, 1, 0, 1),
    (20.7, 1, 1, 1),
    (22.6, 4, 1, 10),
    (23.2, 2, 1, 1),
    (23.2, 3, 0, 1),
    (24.7, 7, 0, 0),
    (26.3, 2, 0, 1),
    (26.9, 5, 1, 10),
    (27.0, 4, 1, 1),
    (27.4, 0, 1, 2),
    (27.7, 5, 0, 1),
    (28.4, 3, 1, 1),
    (30.0, -1, 0, 0),
    (30.4, 5, 1, 1),
    (30.6, 0, 0, 2),
    (31.1, 6, 1, 10),
    (32.6, 4, 0, 1),
    (33.9, 1, 1, 11),
    (34.3, 6, 1, 1),
    (35.1, 6, 0, 1),
    (35.4, 1, 0, 2),
    (36.6, 1, 1, 2),
    (37.0, 7, 1, 10),
    (37.2, 2, 1, 2),
    (37.9, 3, 0, 2),
    (37.9, 2, 0, 2),
    (39.0, 3, 1, 2),
    (39.9, 0, 0, 12),
    (40.2, 7, 1, 1),
    (42.3, 0, 1, 3),
    (42.6, 7, 0, 1),
    (42.7, 1, 0, 12),
    (43.1, 0, 0, 3),
    (44.2, 4, 1, 2),
    (45.0, 5, 0, 2),
    (45.4, 3, 0, 12),
    (45.6, 1, 0, 3),
    (45.8, 5, 1, 2),
    (47.6, 2, 0, 12),
    (47.7, 8, 0, 0),
    (47.9, 3, 0, 3),
    (48.0, 6, 0, 2),
    (49.5, 4, 0, 2),
    (49.8, 3, 1, 12),
    (50.0, 6, 1, 2),
    (50.2, 2, 0, 3),
    (50.4, 1, 1, 3),
    (50.8, 2, 1, 3),
    (50.8, 5, 0, 12),
    (50.9, 9, 0, 0),
    (50.9, 10, 0, 0),
    (50.9, 11, 0, 0),
    (51.3, 7, 1, 2),
    (52.3, 3, 1, 3),
    (53.0, 6, 0, 12),
    (53.4, 7, 0, 2),
    (53.6, 4, 1, 3),
    (53.9, 5, 1, 3),
    (54.3, 5, 0, 3),
    (55.6, 8, 1, 10),
    (55.9, 6, 0, 3),
    (56.2, 9, 1, 1),
    (56.4, 6, 1, 3),
    (58.1, 8, 0, 1),
    (58.5, 10, 1, 1),
    (59.1, 8, 1, 1),
    (59.3, 4, 0, 12),
    (60.2, 9, 0, 1),
    (60.6, 11, 1, 1),
    (61.8, 4, 0, 3),
    (61.9, 10, 2, 10),
    (62.3, 10, 0, 1),
    (62.7, 11, 2, 1),
    (63.0, 7, 1, 3),
    (64.4, 11, 0, 1),
    (64.9, 7, 0, 12),
    (65.1, 8, 0, 2),
    (65.2, 10, 2, 1),
    (65.6, 8, 1, 2),
    (66.7, 9, 0, 2),
    (67.4, 7, 0, 3),
    (67.6, 9, 1, 11),
    (67.7, 10, 0, 2),
    (68.8, 11, 0, 2),
    (71.1, 9, 1, 2),
    (71.3, 11, 2, 11),
    (73.4, 8, 0, 12),
    (73.6, 11, 2, 2),
    (73.9, 10, 1, 2),
    (74.8, 9, 0, 12),
    (75.0, 11, 1, 2),
    (75.5, 8, 0, 3),
    (75.5, 8, 1, 3),
    (75.6, 10, 0, 12),
    (75.6, 10, 2, 2),
    (76.3, 9, 1, 3),
    (76.4, 11, 0, 12),
    (76.6, 9, 0, 3),
    (77.0, 11, 2, 3),
    (77.2, 10, 1, 12),
    (77.3, 10, 0, 3),
    (78.1, 11, 0, 3),
    (78.2, 11, 1, 12),
    (78.6, 10, 2, 3),
    (79.0, 10, 1, 3),
    (79.9, 11, 1, 3),
)


MESH = pl.DeviceIdType.MESH
WEIGHTS = ("qkv", "box", "out", "up", "down")
ROT = 4
ALL = slice(None)


def window(piece):
    return (pl.ds(piece[0], piece[1]), pl.ds(piece[2], piece[3]))


class Place:
    def __init__(self):
        dp = lax.axis_index("dp")
        self.y = lax.axis_index("blk")
        self.z = lax.div(dp, 4)
        self.x = lax.rem(lax.div(dp, 2), 2)
        self.c = lax.rem(dp, 2)
        x, y, z, c = self.x, self.y, self.z, self.c
        self.near = z + 1 - 2 * lax.rem(z, 2)
        self.far = lax.rem(z + 2, 4)
        self.mirror = 3 - z
        self.inner = jnp.logical_or(z == 1, z == 2)
        self.end = jnp.logical_or(z == 0, z == 3)
        at = lambda other: (other * 4 + x * 2 + c, y)
        self.near_peer, self.far_peer, self.mirror_peer = at(self.near), at(self.far), at(self.mirror)
        self.x_peer = (dp + 2 - 4 * x, y)
        self.y_peer = (dp, 1 - y)
        self.c_peer = (dp + 1 - 2 * c, y)

    def own(self):
        return dict(y=self.y, z=self.z, x=self.x)

    def vector_offset(self):
        device = ((self.z * 2 + self.x) * 2 + self.c) * 2 + self.y
        return lax.rem(device * (VECTORS // 32), 128)

    def greet(self):
        barrier = pltpu.get_barrier_semaphore()
        peers = [self.near_peer, self.far_peer, self.mirror_peer]
        peers += [self.x_peer, self.y_peer, self.c_peer]
        for peer in peers:
            pl.semaphore_signal(barrier, inc=1, device_id=peer, device_id_type=MESH)
        pl.semaphore_wait(barrier, len(peers))


def semaphore_table(groups):
    table = {}
    for g, group in enumerate(groups):
        for part, (path, _) in enumerate(group[-1]):
            for hop, axis in enumerate(path):
                for slot in range(4 if axis == "z" else 1):
                    table[g, part, hop, slot] = len(table)
    return table


def remote(src, dst, sems, at, peer):
    return pltpu.make_async_remote_copy(
        src, dst, sems[0].at[at], sems[1].at[at], device_id=peer, device_id_type=MESH
    )


class Gather:
    def __init__(self, place, groups, shards, full, sems, c_sems, own_sem):
        self.place, self.groups, self.shards, self.full = place, groups, shards, full
        self.sems, self.c_sems, self.own_sem = sems, c_sems, own_sem
        self.count = len(groups)
        self.table = semaphore_table(groups)
        self.owned = False

    def copy(self, g, part, hop, slot, arriving=False):
        p = self.place
        name, _, parts = self.groups[g]
        path, piece = parts[part]
        cut = window(piece)
        axis = path[hop]
        at = p.own()
        at.update({earlier: ALL for earlier in path[:hop]})
        if axis == "z":
            peer = (p.near_peer, p.far_peer, p.mirror_peer, p.near_peer)[slot]
            if slot == 3:
                at["z"] = p.mirror if arriving else p.far
            elif arriving:
                at["z"] = (p.near, p.far, p.mirror)[slot]
        else:
            peer = p.x_peer if axis == "x" else p.y_peer
            if arriving:
                at[axis] = 1 - at[axis]
        ref = self.full[name].at[(at["y"], at["z"], at["x"], p.c) + cut]
        source = self.shards[name].at[cut] if hop == 0 and slot < 3 else ref
        return remote(source, ref, self.sems, (self.table[g, part, hop, slot],), peer)

    def own_copy(self, g):
        p = self.place
        name, both, _ = self.groups[g]
        cut = window(both)
        return pltpu.make_async_copy(
            self.shards[name].at[cut],
            self.full[name].at[(p.y, p.z, p.x, p.c) + cut],
            self.own_sem.at[g],
        )

    def c_copy(self, g, part, arriving=False):
        p = self.place
        name, _, parts = self.groups[g]
        c = 1 - p.c if arriving else p.c
        ref = self.full[name].at[(ALL, ALL, ALL, c) + window(parts[part][1])]
        return remote(ref, ref, self.c_sems, (g, part), p.c_peer)

    def relay(self, g, part, hop):
        @pl.when(self.place.inner)
        def _():
            self.copy(g, part, hop, 1, True).wait_recv()
            self.copy(g, part, hop, 3).start()

    def start(self, g, part, hop):
        if self.groups[g][2][part][0][hop] != "z":
            self.copy(g, part, hop, 0).start()
            return
        self.copy(g, part, hop, 1).start()
        self.copy(g, part, hop, 0).start()

        @pl.when(self.place.inner)
        def _():
            self.copy(g, part, hop, 2).start()

    def finish(self, g, part, hop):
        self.copy(g, part, hop, 0, True).wait_recv()
        if self.groups[g][2][part][0][hop] != "z":
            return

        @pl.when(self.place.inner)
        def _():
            self.copy(g, part, hop, 2, True).wait_recv()

        @pl.when(self.place.end)
        def _():
            self.copy(g, part, hop, 1, True).wait_recv()
            self.copy(g, part, hop, 3, True).wait_recv()

    def own(self):
        for g in range(self.count):
            self.own_copy(g).start()

    def step(self, g, part, step):
        if step >= 10:
            self.relay(g, part, step - 10)
            return
        if step >= 1 and not self.owned:
            self.owned = True
            for other in range(self.count):
                self.own_copy(other).wait()
        if 1 <= step <= 3:
            self.finish(g, part, step - 1)
        if step <= 2:
            self.start(g, part, step)
        if step == 3:
            self.c_copy(g, part).start()
        if step == 4:
            self.c_copy(g, part, True).wait_recv()

    def drain(self):
        for (g, part, hop, slot), _ in self.table.items():
            copy = self.copy(g, part, hop, slot)
            if slot < 2:
                copy.wait_send()
            else:
                pl.when(self.place.inner)(copy.wait_send)
        for g, (_, _, parts) in enumerate(self.groups):
            for part in range(len(parts)):
                self.c_copy(g, part).wait_send()


class Clock:
    def __init__(self, events, run, now, begun=None):
        self.events, self.run, self.now, self.at, self.begun = events, run, now, 0, begun

    def may(self, event):
        return self.begun is None or event[1] < 0 or event[1] in self.begun

    def take(self, until):
        first = self.at
        while self.at < len(self.events):
            event = self.events[self.at]
            if event[0] > until or not self.may(event):
                break
            self.at += 1
        return self.events[first : self.at]

    def catch_up(self):
        for _, *event in self.take(self.now):
            self.run(*event)

    def spend(self, time):
        self.now += time
        self.catch_up()

    def upto(self, *wanted):
        last = max(i for i, (_, *event) in enumerate(self.events) if tuple(event) in wanted)
        self.now = max(self.now, self.events[last][0])
        while self.at <= last:
            assert self.may(self.events[self.at])
            _, *event = self.events[self.at]
            self.at += 1
            self.run(*event)

    def loop(self, count, each, body, points=1):
        due = [
            [self.take(self.now + each * (i + k / points)) for k in range(points)]
            for i in range(count)
        ]
        self.now += count * each

        def wrapped(i, carry):
            point = iter(range(points))

            def serve():
                k = next(point)
                for n in range(count):
                    if due[n][k]:

                        @pl.when(i == n)
                        def _():
                            for _, *event in due[n][k]:
                                self.run(*event)

            serve()
            return body(i, carry, serve)

        lax.fori_loop(0, count, wrapped, 0)
        self.catch_up()


def sine_cosine(angle):
    turns = jnp.floor(angle * (2.0 / math.pi) + 0.5)
    rest = angle - turns * 1.5703125
    rest = rest - turns * 4.837512969970703125e-4
    rest = rest - turns * 7.54978995489188216e-8
    square = rest * rest
    sine = rest + rest * square * (
        -1.6666654611e-1 + square * (8.3321608736e-3 + square * -1.9515295891e-4)
    )
    cosine = (
        1.0
        - 0.5 * square
        + square
        * square
        * (
            4.166664568298827e-2
            + square * (-1.388731625493765e-3 + square * 2.443315711809948e-5)
        )
    )
    quarter = turns.astype(jnp.int32)
    odd = (quarter & 1) == 1
    sine_sign = jnp.where((quarter & 2) == 2, -1.0, 1.0)
    cosine_sign = jnp.where(((quarter + 1) & 2) == 2, -1.0, 1.0)
    return (
        sine_sign * jnp.where(odd, cosine, sine),
        cosine_sign * jnp.where(odd, sine, cosine),
    )


def dot_t(a, b):
    return lax.dot_general(a, b, (((1,), (1,)), ((), ())), preferred_element_type=jnp.float32)


def dot_n(a, b):
    return lax.dot_general(a, b, (((0,), (0,)), ((), ())), preferred_element_type=jnp.float32)


def lanes(start, size):
    return pl.ds(pl.multiple_of(start, 128), size)


BQ, BV, BO, G1, E1, B1, B2, G2, E2 = 0, 768, 1536, 2304, 3072, 3840, 6912, 7680, 8448
VECTORS = 9216


def forward_kernel(plan, *refs):
    groups, page_len, width = plan
    block = page_len // 2
    refs = iter(refs)
    take = lambda n: [next(refs) for _ in range(n)]
    tokens, cotangent, boxes, lengths, vectors = take(5)
    shards = dict(zip(WEIGHTS, take(5)))
    full_out = dict(zip(WEIGHTS, take(5)))
    (x_out, ct_out, qkv_out, table_out, p_out, o_out, unit1_out, inv1_out) = take(8)
    (g_out, d_out, unit2_out, inv2_out, vec_out) = take(5)
    full = dict(zip(WEIGHTS, take(5)))
    (x_own, boxes_peer, pieces, vec, qkv, table, keys, box_w, p_slots, o_own, o_low) = take(11)
    (unit1, inv1, y1_low, hidden, slope, unit2, inv2) = take(7)
    w_sems, c_sems = take(2), take(2)
    (own_sem,) = take(1)
    vz_sems, vxy_sems, vc_sems = take(2), take(2), take(2)
    ex_sems = take(2)
    (local_sem, p_sem, out_sem) = take(3)
    bias_qkv, piece = take(2)

    place = Place()
    y, z, x, c = place.y, place.z, place.x, place.c
    gather = Gather(place, groups, shards, full, w_sems, c_sems, own_sem)

    def swap(i, source, target, arriving=False):
        at = (1 - y) if arriving else y
        return remote(
            source.at[1 - y], target.at[pl.ds(pl.multiple_of(at * block, block), block)],
            ex_sems, (i,), place.y_peer,
        )

    def keep(i, source, target):
        return pltpu.make_async_copy(
            source.at[y], target.at[pl.ds(pl.multiple_of(y * block, block), block)],
            local_sem.at[i],
        )

    box_swap = remote(boxes, boxes_peer, ex_sems, (2,), place.y_peer)

    def vector_z(k, arriving=False):
        at = lax.rem(z + 4 - k, 4) if arriving else z
        peer = (lax.rem(z + k, 4) * 4 + x * 2 + c, y)
        return remote(piece, pieces.at[y, at, x, c], vz_sems, (k - 1,), peer)

    def vector_xy(i, arriving=False):
        at_x = 1 - x if arriving else x
        at_y = 1 - y if arriving else y
        index = ((y, ALL, at_x, c), (at_y, ALL, ALL, c))[i]
        ref = pieces.at[index]
        return remote(ref, ref, vxy_sems, (i,), (place.x_peer, place.y_peer)[i])

    def vector_c(arriving=False):
        ref = pieces.at[:, :, :, 1 - c if arriving else c]
        return remote(ref, ref, vc_sems, (0,), place.c_peer)

    vector_own = pltpu.make_async_copy(piece, pieces.at[y, z, x, c], local_sem.at[2])

    def event(g, part, step):
        if g < 0:
            swap(1, cotangent, ct_out).start()
        else:
            gather.step(g, part, step)

    clock = Clock(GATHER_EVENTS, event, 4.0)

    def need(g):
        clock.upto(*((g, part, 4) for part in range(len(groups[g][2]))))

    outgoing = []

    def send_out(ref, out):
        copy = pltpu.make_async_copy(ref, out, out_sem.at[len(outgoing)])
        copy.start()
        outgoing.append(copy)

    own_vector = vectors[...].astype(jnp.float32).reshape(1, -1)
    own_vector = jnp.concatenate(
        [own_vector, jnp.zeros((1, 384 - own_vector.shape[1]), jnp.float32)], axis=1
    )
    own_vector = jnp.broadcast_to(own_vector, (8, 384))
    piece[...] = pltpu.roll(own_vector, place.vector_offset(), 1)[0:1, :]
    place.greet()
    gather.own()
    box_swap.start()
    for k in range(1, 4):
        vector_z(k).start()
    vector_own.start()
    swap(0, tokens, x_own).start()
    clock.catch_up()
    keep(0, tokens, x_own).start()
    keep(1, cotangent, ct_out).start()
    clock.spend(3.0)
    vector_own.wait()
    for k in range(1, 4):
        vector_z(k, True).wait_recv()
    vector_xy(0).start()
    clock.spend(3.0)
    vector_xy(0, True).wait_recv()
    vector_xy(1).start()

    box_swap.wait_recv()
    mine, other = boxes[...], boxes_peer[...]
    first_block = y == 0
    mine = jnp.where(first_block, mine[:, 0, :], mine[:, 1, :])
    other = jnp.where(first_block, other[:, 0, :], other[:, 1, :])
    both = jnp.concatenate(
        [jnp.where(first_block, mine, other), jnp.where(first_block, other, mine)], axis=1
    ).astype(jnp.float32)
    both = jnp.concatenate([both, jnp.zeros((6, page_len), jnp.float32)], axis=0)
    across_up = both.T
    lane = lax.broadcasted_iota(jnp.int32, (1, 2 * FREQ), 1)
    step = jnp.where(lane < FREQ, lane, lane - FREQ).astype(jnp.float32)
    frequency = jnp.exp(step * (-math.log(10000.0) / FREQ))
    angle = jnp.where(lane < FREQ, across_up[:, 0:1], across_up[:, 1:2]) * frequency
    sine, cosine = sine_cosine(angle)
    table[0], table[1] = cosine, sine
    keys[0], keys[1] = cosine.astype(jnp.bfloat16), sine.astype(jnp.bfloat16)
    send_out(table, table_out)
    clock.spend(3.0)
    vector_xy(1, True).wait_recv()
    vector_c().start()

    keep(0, tokens, x_own).wait()
    swap(0, tokens, x_own, True).wait_recv()
    send_out(x_own, x_out)
    clock.catch_up()
    vector_c(True).wait_recv()
    vec[...] = jnp.zeros_like(vec)
    for dz in range(4):
        for dx in range(2):
            for dc in range(2):
                for dy in range(2):
                    device = ((dz * 2 + dx) * 2 + dc) * 2 + dy
                    start = device * (VECTORS // 32) // 128 * 128
                    vec[:, start : start + 384] += pieces[dy, dz, dx, dc]
    send_out(vec, vec_out)

    def vector(start, size=width):
        return vec[:, start : start + size]

    def project(first, count):
        def project_tile(h, carry):
            w = full["qkv"].at[h][:, :, :, :, first : first + count].reshape(width, count)
            out = jnp.dot(x_own[...], w, preferred_element_type=jnp.float32)
            start = pl.multiple_of(h * 1152 + first, 128)
            column = start + lax.broadcasted_iota(jnp.int32, (1, count), 1)
            bias = bias_qkv[:, lanes(start, count)]
            qkv[:, lanes(start, count)] = (out + bias).astype(jnp.bfloat16)
            return carry

        lax.fori_loop(0, 2, project_tile, 0)

    bias_qkv[:, 0:width] = vector(BQ)
    bias_qkv[:, width : 2 * width] = jnp.zeros((1, width), jnp.float32)
    bias_qkv[:, 2 * width : 3 * width] = vector(BV)
    for g, (name, cut, _) in enumerate(groups):
        if name == "qkv":
            need(g)
            project(cut[2], cut[3])
            clock.spend(1.3)
    send_out(qkv, qkv_out)

    box_group = [g for g, group in enumerate(groups) if group[0] == "box"][-1]
    need(box_group)
    low = full["box"].at[0][...].reshape(width, 2 * FREQ)
    high = full["box"].at[1][...].reshape(width, 2 * FREQ)
    box_w[...] = jnp.concatenate(
        [low[:, :FREQ], high[:, :FREQ], low[:, FREQ:], high[:, FREQ:]], axis=1
    )
    page_length = jnp.where(first_block, lengths[0], lengths[1])
    valid = lax.broadcasted_iota(jnp.int32, (1, page_len), 1) < page_length
    head_lane = lax.broadcasted_iota(jnp.int32, (1, 128), 1)

    def p_copy(p, slot):
        return pltpu.make_async_copy(p_slots.at[slot], p_out.at[p], p_sem.at[slot])

    def pair(p, carry, serve):
        slot = lax.rem(p, 2)

        @pl.when(p >= 2)
        def _():
            p_copy(p - 2, slot).wait()

        q = qkv[:, lanes(p * 128, 128)]
        k = qkv[:, lanes(width + p * 128, 128)]
        v = qkv[:, lanes(2 * width + p * 128, 128)]
        w = box_w[pl.ds(pl.multiple_of(p * 128, 128), 128), :]
        outs = []
        for i in range(2):
            if i:
                serve()
            of_head = (head_lane < HEAD) == (i == 0)
            q_head = jnp.where(of_head, q, jnp.zeros_like(q))
            u = jnp.dot(q_head, w, preferred_element_type=jnp.float32)
            on_sine, on_cosine = u[:, : 2 * FREQ], u[:, 2 * FREQ :]
            cosine, sine = table[0], table[1]
            b_cosine = (on_sine * sine + on_cosine * cosine).astype(jnp.bfloat16)
            b_sine = (on_cosine * sine - on_sine * cosine).astype(jnp.bfloat16)
            s = dot_t(q_head, k) + dot_t(b_cosine, keys[0]) + dot_t(b_sine, keys[1])
            s = jnp.where(valid, s, MASKED)
            top = jnp.max(s, axis=1, keepdims=True)
            e = jnp.exp((s - top) * (HEAD**-0.5))
            probs = (e * (1.0 / jnp.sum(e, axis=1, keepdims=True))).astype(jnp.bfloat16)
            p_slots[slot, i] = probs
            outs.append(jnp.dot(probs, v, preferred_element_type=jnp.float32))
        mixed = jnp.where(head_lane < HEAD, outs[0], outs[1])
        o_own[:, lanes(p * 128, 128)] = mixed
        o_low[:, lanes(p * 128, 128)] = mixed.astype(jnp.bfloat16)
        p_copy(p, slot).start()
        return carry

    clock.loop(HEADS // 2, PAIR_TIME, pair, 2)
    p_copy(4, 0).wait()
    p_copy(5, 1).wait()
    send_out(o_own, o_out)

    def last_of(name):
        return [g for g, group in enumerate(groups) if group[0] == name][-1]

    def weight_out(name):
        send_out(full[name], full_out[name])

    weight_out("qkv")
    weight_out("box")
    need(last_of("out"))
    weight_out("out")
    for h in range(2):
        w = full["out"].at[h][...].reshape(width, 384)
        cut = slice(h * 384, (h + 1) * 384)
        o_own_part = jnp.dot(o_low[...], w, preferred_element_type=jnp.float32)
        unit2[:, cut] = x_own[:, cut].astype(jnp.float32) + o_own_part + vec[:, BO + h * 384 : BO + (h + 1) * 384]

    def norm(hidden_sum):
        mean = jnp.mean(hidden_sum, axis=1, keepdims=True)
        centered = hidden_sum - mean
        inverse = lax.rsqrt(jnp.mean(centered * centered, axis=1, keepdims=True) + EPSILON)
        return centered * inverse, inverse

    unit, inverse = norm(unit2[...])
    unit1[...] = unit
    inv1[...] = jnp.broadcast_to(inverse, (page_len, 128))
    y1 = unit * vector(G1) + vector(E1)
    y1_low[...] = y1.astype(jnp.bfloat16)
    unit2[...] = y1 + vector(B2)
    send_out(unit1, unit1_out)
    send_out(inv1, inv1_out)

    def up_tile(first, h, t):
        start = pl.multiple_of(first + t * UP_TILE, 128)
        w = full["up"].at[h][:, :, :, :, pl.ds(start, UP_TILE)].reshape(width, UP_TILE)
        at = lanes(h * 1536 + start, UP_TILE)
        pre = jnp.dot(y1_low[...], w, preferred_element_type=jnp.float32)
        pre = pre + vec[:, lanes(B1 + h * 1536 + start, UP_TILE)]
        half = 0.5 + 0.5 * lax.erf(pre * (2.0**-0.5))
        hidden[:, at] = (pre * half).astype(jnp.bfloat16)
        bell = jnp.exp(pre * pre * -0.5) * ((2.0 * math.pi) ** -0.5)
        slope[:, at] = (half + pre * bell).astype(jnp.bfloat16)

    clock.spend(2.0)
    for g, (name, cut, _) in enumerate(groups):
        if name == "up":
            need(g)
            tiles = cut[3] // UP_TILE

            def up_body(i, carry, first=cut[2], tiles=tiles):
                up_tile(first, lax.div(i, tiles), lax.rem(i, tiles))
                return carry

            lax.fori_loop(0, 2 * tiles, up_body, 0)
            clock.spend(1.7)
    send_out(hidden, g_out)
    send_out(slope, d_out)
    weight_out("up")

    for g, (name, cut, _) in enumerate(groups):
        if name == "down":
            need(g)
            first, count = cut[2], cut[3]

            def down_body(h, carry, first=first, count=count):
                w = full["down"].at[h][:, :, :, :, first : first + count].reshape(4 * width, count)
                at = lanes(h * 384 + first, count)
                unit2[:, at] += jnp.dot(hidden[...], w, preferred_element_type=jnp.float32)
                return carry

            lax.fori_loop(0, 2, down_body, 0)
            clock.spend(1.0)
    clock.upto(*(tuple(event) for _, *event in GATHER_EVENTS))
    weight_out("down")
    unit, inverse = norm(unit2[...])
    unit2[...] = unit
    inv2[...] = jnp.broadcast_to(inverse, (page_len, 128))
    send_out(unit2, unit2_out)
    send_out(inv2, inv2_out)

    gather.drain()
    for k in range(1, 4):
        vector_z(k).wait_send()
    vector_xy(0).wait_send()
    vector_xy(1).wait_send()
    vector_c().wait_send()
    box_swap.wait_send()
    swap(0, tokens, x_own).wait_send()
    swap(1, cotangent, ct_out).wait_send()
    swap(1, cotangent, ct_out, True).wait_recv()
    keep(1, cotangent, ct_out).wait()
    for copy in outgoing:
        copy.wait()


PAIR_TIME = 3.3
UP_TILE = 384


def forward_call(tokens, cotangent, boxes, lengths, vectors, shards):
    page_len = tokens.shape[1] * 2
    width = tokens.shape[2]
    groups = GATHER_GROUPS
    count = len(groups)
    full = [jax.ShapeDtypeStruct((2, 4, 2, 2) + s.shape, jnp.bfloat16) for s in shards]
    low, single = jnp.bfloat16, jnp.float32
    kinds = dict(
        x=((page_len, width), low),
        ct=((page_len, width), low),
        qkv=((page_len, 3 * width), low),
        table=((2, page_len, 2 * FREQ), single),
        p=((HEADS // 2, 2, page_len, page_len), low),
        o=((page_len, width), single),
        unit1=((page_len, width), single),
        inv1=((page_len, 128), single),
        g=((page_len, 4 * width), low),
        d=((page_len, 4 * width), low),
        unit2=((page_len, width), single),
        inv2=((page_len, 128), single),
        vec=((1, VECTORS + 128), single),
    )
    outs = full + [jax.ShapeDtypeStruct(*kinds[k]) for k in kinds]
    anywhere = pl.BlockSpec(memory_space=pl.ANY)
    vmem = pl.BlockSpec(memory_space=pltpu.VMEM)
    smem = pl.BlockSpec(memory_space=pltpu.SMEM)
    dma = pltpu.SemaphoreType.DMA
    scratch = [pltpu.VMEM(f.shape, f.dtype) for f in full]
    scratch += [
        pltpu.VMEM((page_len, width), low),
        pltpu.VMEM(boxes.shape, jnp.int32),
        pltpu.VMEM((2, 4, 2, 2, 1, 384), single),
        pltpu.VMEM((1, VECTORS + 128), single),
        pltpu.VMEM((page_len, 3 * width), low),
        pltpu.VMEM((2, page_len, 2 * FREQ), single),
        pltpu.VMEM((2, page_len, 2 * FREQ), low),
        pltpu.VMEM((width, BOX_DIM), low),
        pltpu.VMEM((2, 2, page_len, page_len), low),
        pltpu.VMEM((page_len, width), single),
        pltpu.VMEM((page_len, width), low),
        pltpu.VMEM((page_len, width), single),
        pltpu.VMEM((page_len, 128), single),
        pltpu.VMEM((page_len, width), low),
        pltpu.VMEM((page_len, 4 * width), low),
        pltpu.VMEM((page_len, 4 * width), low),
        pltpu.VMEM((page_len, width), single),
        pltpu.VMEM((page_len, 128), single),
    ]
    scratch += [dma((len(semaphore_table(groups)),))] * 2 + [dma((count, 3))] * 2
    scratch += [dma((count,))]
    scratch += [dma((3,))] * 2 + [dma((2,))] * 2 + [dma((1,))] * 2
    scratch += [dma((3,))] * 2 + [dma((3,)), dma((2,)), dma((18,))]
    scratch += [pltpu.VMEM((1, 3 * width), single), pltpu.VMEM((1, 384), single)]
    plan = (groups, page_len, width)
    results = pl.pallas_call(
        partial(forward_kernel, plan),
        out_shape=outs,
        in_specs=[anywhere, anywhere, vmem, smem, vmem] + [anywhere] * 5,
        out_specs=[anywhere] * len(outs),
        scratch_shapes=scratch,
        compiler_params=pltpu.CompilerParams(
            collective_id=0, has_side_effects=True, vmem_limit_bytes=VMEM_LIMIT
        ),
    )(tokens, cotangent, boxes, lengths, vectors, *shards)
    return dict(zip(WEIGHTS, results[:5])), dict(zip(kinds, results[5:]))


VMEM_LIMIT = 60 * 2**20


def landing_shape(path, hop, piece):
    sizes = dict(y=2, z=4, x=2)
    to_come = [sizes[axis] for axis in "yzx" if axis in path[hop + 1 :]]
    return (4 if path[hop] == "z" else 1, *to_come, piece[1], piece[3])


class Scatter:
    def __init__(self, place, groups, stored, c_land, landing, summed, sems, c_sems):
        self.place, self.groups, self.stored, self.summed = place, groups, stored, summed
        self.c_land, self.landing = c_land, landing
        self.sems, self.c_sems = sems, c_sems
        self.table = semaphore_table(groups)
        self.sent = set()

    def c_copy(self, g):
        p = self.place
        store, both = self.groups[g][1], self.groups[g][2]
        ref = self.stored[store].at[(ALL, ALL, ALL, 1 - p.c) + window(both)]
        return remote(ref, self.c_land[g], self.c_sems, (g,), p.c_peer)

    def copy(self, g, part, hop, slot):
        p = self.place
        path, piece = self.groups[g][-1][part]
        axis = path[hop]
        at = p.own()
        at.update({later: ALL for later in path[hop + 1 :]})
        if axis == "z":
            at["z"] = (p.near, p.far, p.mirror, p.mirror)[slot]
            peer = (p.near_peer, p.far_peer, p.mirror_peer, p.near_peer)[slot]
        else:
            at[axis] = 1 - at[axis]
            peer = p.x_peer if axis == "x" else p.y_peer
        ref = self.stored[self.groups[g][1]].at[(at["y"], at["z"], at["x"], p.c) + window(piece)]
        land = self.landing[g][part][hop].at[slot]
        return remote(ref, land, self.sems, (self.table[g, part, hop, slot],), peer)

    def add(self, g, part, hop, slots, place_z=None):
        p = self.place
        name, store, both, result, parts = self.groups[g]
        store = self.stored[store]
        path, piece = ("yzx", both) if hop < 0 else parts[part]
        cut = window(piece)
        sizes = dict(y=2, z=4, x=2)
        to_come = [axis for axis in "yzx" if axis in path[hop + 1 :]]
        count = math.prod(sizes[axis] for axis in to_come)
        land = self.c_land[g] if hop < 0 else self.landing[g][part][hop]

        def block(i):
            at = p.own()
            if place_z is not None:
                at["z"] = place_z
            inner = []
            for axis in to_come[::-1]:
                at[axis] = lax.rem(i, sizes[axis])
                i = lax.div(i, sizes[axis])
                inner.insert(0, at[axis])
            here = (at["y"], at["z"], at["x"], p.c) + cut
            value = store[here].astype(jnp.float32)
            for slot in slots:
                arrived = land[tuple(inner)] if hop < 0 else land[(slot, *inner)]
                value = value + arrived.astype(jnp.float32)
            return here, value

        if hop == 2 and place_z is None:
            _, value = block(0)
            top, height, first, size = piece
            top, first = top - both[0] + result[0], first - both[2] + result[2]
            self.summed[name][top : top + height, first : first + size] = value
            return

        def body(i, carry):
            here, value = block(i)
            store[here] = value.astype(jnp.bfloat16)
            return carry

        lax.fori_loop(0, count, body, 0)

    def begin(self, g):
        self.c_copy(g).start()

    def start(self, g, part, hop):
        p = self.place
        if self.groups[g][-1][part][0][hop] != "z":
            self.copy(g, part, hop, 0).start()
            return

        @pl.when(p.end)
        def _():
            self.copy(g, part, hop, 3).start()
            self.copy(g, part, hop, 1).start()

        self.copy(g, part, hop, 0).start()

        @pl.when(p.inner)
        def _():
            self.copy(g, part, hop, 2).start()

    def relay(self, g, part, hop):
        p = self.place

        @pl.when(p.inner)
        def _():
            self.copy(g, part, hop, 3).wait_recv()
            self.add(g, part, hop, (3,), p.far)
            self.copy(g, part, hop, 1).start()

    def finish(self, g, part, hop):
        p = self.place
        self.copy(g, part, hop, 0).wait_recv()
        if self.groups[g][-1][part][0][hop] != "z":
            self.add(g, part, hop, (0,))
            return
        self.copy(g, part, hop, 1).wait_recv()

        @pl.when(p.inner)
        def _():
            self.copy(g, part, hop, 2).wait_recv()
            self.add(g, part, hop, (0, 1, 2))

        @pl.when(p.end)
        def _():
            self.add(g, part, hop, (0, 1))

    def step(self, g, part, step):
        if step >= 10:
            self.relay(g, part, step - 10)
            return
        if step == 0:
            self.c_copy(g).wait_recv()
            self.add(g, 0, -1, (0,))
            for part in range(len(self.groups[g][-1])):
                self.start(g, part, 0)
            return
        self.finish(g, part, step - 1)
        if step < 3:
            self.start(g, part, step)

    def left(self, g):
        if g in self.sent:
            return
        self.sent.add(g)
        p = self.place
        self.c_copy(g).wait_send()
        for (group, part, hop, slot), _ in self.table.items():
            if group == g:
                wait = self.copy(g, part, hop, slot).wait_send
                if slot < 2:
                    wait()
                else:
                    pl.when(p.inner if slot == 2 else p.end)(wait)


def backward_kernel(plan, *refs):
    groups, page_len, width = plan
    block = page_len // 2
    refs = iter(refs)
    take = lambda n: [next(refs) for _ in range(n)]
    w_in = dict(zip(WEIGHTS, take(5)))
    (x_in, ct_in, qkv_in, table_in, p_in, o_in, unit1_in, inv1_in) = take(8)
    (g_in, d_in, unit2_in, inv2_in, vec_in) = take(5)
    out_out, dx_out = take(2)
    grad_out = dict(zip(WEIGHTS, take(5)))
    (piece_out,) = take(1)
    stored = dict(zip(("box", "out", "up", "down"), take(4)))
    count = len(groups)
    c_land = take(count)
    landing = [[take(3) for _ in group[-1]] for group in groups]
    summed = dict(zip(WEIGHTS, take(5)))
    w_box, w_out, box_w, box_g = take(4)
    (x_own, ct, qkv, table, keys, o_own, unit1, inv1, hidden, slope, unit2, inv2, vec) = take(13)
    (y1_low, d_a, d_mixed, out_low, dx_low, vec_g) = take(6)
    pieces, pc_land, py_land, px_land, pz_land, piece_sum = take(6)
    w_sems, c_sems = take(2), take(2)
    v_sems, vz_sems, ex_sems = take(2), take(2), take(2)
    in_sem, p_sem, out_sem = take(3)

    place = Place()
    y, z, x, c = place.y, place.z, place.x, place.c
    scatter = Scatter(place, groups, stored, c_land, landing, summed, w_sems, c_sems)

    sources = dict(
        unit2=(unit2_in, unit2),
        ct=(ct_in, ct),
        inv2=(inv2_in, inv2),
        vec=(vec_in, vec),
        g=(g_in, hidden),
        d=(d_in, slope),
        unit1=(unit1_in, unit1),
        inv1=(inv1_in, inv1),
        w_out=(w_in["out"], w_out),
        w_box=(w_in["box"], w_box),
        o=(o_in, o_own),
        qkv=(qkv_in, qkv),
        table=(table_in, table),
        x=(x_in, x_own),
    )
    order = list(sources)

    def fetch(name):
        source, target = sources[name]
        return pltpu.make_async_copy(source, target, in_sem.at[order.index(name)])

    def fetch_weight(name, target):
        at = len(order) + ("down", "up", "qkv").index(name)
        return pltpu.make_async_copy(w_in[name], target, in_sem.at[at])

    def vector(start, size=width):
        return vec[:, start : start + size]

    def total(value):
        return jnp.sum(value.astype(jnp.float32), axis=0, keepdims=True)

    def norm_back(grad, unit, inverse, gain):
        scaled = grad * gain
        mean_grad = jnp.mean(scaled, axis=1, keepdims=True)
        mean_unit = jnp.mean(scaled * unit, axis=1, keepdims=True)
        return inverse * (scaled - mean_grad - unit * mean_unit)

    names = [group[0] for group in groups]

    def event(g, part, step):
        if g < 0:
            out_swap.start()
        else:
            scatter.step(g, part, step)

    clock = Clock(SCATTER_EVENTS, event, 0.0, set())

    def begin(g):
        clock.begun.add(g)
        scatter.begin(g)

    for name in ("unit2", "ct", "inv2", "vec", "g"):
        fetch(name).start()
    place.greet()

    fetch("unit2").wait()
    fetch("ct").wait()
    fetch("inv2").wait()
    fetch("vec").wait()
    unit = unit2[...]
    out_low[...] = (unit * vector(G2) + vector(E2)).astype(jnp.bfloat16)
    seed = ct[...].astype(jnp.float32)
    vec_g[:, G2 : G2 + width] = total(seed * unit)
    vec_g[:, E2 : E2 + width] = total(seed)
    d_h2 = norm_back(seed, unit, inv2[:, 0:1], vector(G2))
    unit2[...] = d_h2
    ct[...] = d_h2.astype(jnp.bfloat16)
    d_f = ct
    vec_g[:, B2 : B2 + width] = total(d_f[...])

    def rows(at):
        return pl.ds(pl.multiple_of(at * block, block), block)

    out_swap = remote(out_low.at[rows(1 - y)], out_out.at[y], ex_sems, (0,), place.y_peer)
    out_keep = pltpu.make_async_copy(out_low.at[rows(y)], out_out.at[y], out_sem.at[0])
    dx_swap = remote(dx_low.at[0], dx_low.at[1], ex_sems, (1,), place.y_peer)

    def with_down(w_down):
        fetch_weight("down", w_down).start()
        fetch("g").wait()

        for name in ("d", "unit1", "inv1", "w_out", "o", "w_box", "qkv", "table", "x"):
            fetch(name).start()

        def down_grads(first, size):
            left = d_f[:, first : first + size]
            right = d_f[:, 384 + first : 384 + first + size]
            both = jnp.concatenate([left, right], axis=1)

            def grad_tile(t, carry):
                part = dot_n(hidden[:, lanes(t * width, width)], both).astype(jnp.bfloat16)
                for h in range(2):
                    stored["down"][h, t, :, :, :, first : first + size] = part[
                        :, h * size : (h + 1) * size
                    ].reshape(2, 2, -1, size)
                return carry

            lax.fori_loop(0, 4, grad_tile, 0)
            for g, group in enumerate(groups):
                if group[0] == "down" and first <= group[2][2] < first + size:
                    begin(g)
            clock.spend(DOWN_TIME)

        clock.now = START_TIME
        down_grads(0, 128)
        down_grads(128, 256)
        out_keep.start()
        fetch_weight("down", w_down).wait()
        fetch("d").wait()

        def slope_tile(t, carry, serve):
            w0 = w_down.at[0, t][...].reshape(width, 384)
            w1 = w_down.at[1, t][...].reshape(width, 384)
            d_hidden = dot_t(d_f[:, :384], w0) + dot_t(d_f[:, 384:], w1)
            at = lanes(t * width, width)
            d_pre = (d_hidden * slope[:, at].astype(jnp.float32)).astype(jnp.bfloat16)
            slope[:, at] = d_pre
            vec_g[:, lanes(B1 + t * width, width)] = total(d_pre)
            return carry

        clock.loop(4, SLOPE_TIME, slope_tile)

    pl.run_scoped(with_down, pltpu.VMEM(w_in["down"].shape, jnp.bfloat16))

    fetch("unit1").wait()
    fetch("inv1").wait()
    y1_low[...] = (unit1[...] * vector(G1) + vector(E1)).astype(jnp.bfloat16)

    def with_up(w_up):
        fetch_weight("up", w_up).start()

        def up_tile(i, carry, serve, part):
            tile = dot_n(y1_low[...], slope[:, lanes(i * 1536 + part * width, width)])
            stored["up"][i, :, :, :, :, part * width : (part + 1) * width] = tile.astype(
                jnp.bfloat16
            ).reshape(4, 2, 2, -1, width)
            return carry

        for part in range(2):
            clock.loop(2, UP_TIME, partial(up_tile, part=part))
            for g, group in enumerate(groups):
                if group[0] == "up" and group[2][2] // width == part:
                    begin(g)
        fetch_weight("up", w_up).wait()

        def back_tile(h, carry, serve):
            w = w_up.at[h][...].reshape(width, 1536)
            unit2[...] += dot_t(slope[:, lanes(h * 1536, 1536)], w)
            return carry

        clock.loop(2, UP_BACK_TIME, back_tile)

    pl.run_scoped(with_up, pltpu.VMEM(w_in["up"].shape, jnp.bfloat16))

    unit = unit1[...]
    d_y1 = unit2[...]
    vec_g[:, G1 : G1 + width] = total(d_y1 * unit)
    vec_g[:, E1 : E1 + width] = total(d_y1)
    d_h1 = norm_back(d_y1, unit, inv1[:, 0:1], vector(G1))
    unit1[...] = d_h1
    d_a[...] = d_h1.astype(jnp.bfloat16)
    vec_g[:, BO : BO + width] = total(d_a[...])
    fetch("w_out").wait()
    fetch("o").wait()
    d_mixed[...] = (
        dot_t(d_a[:, :384], w_out.at[0][...].reshape(width, 384))
        + dot_t(d_a[:, 384:], w_out.at[1][...].reshape(width, 384))
    ).astype(jnp.bfloat16)
    part = dot_n(o_own[...].astype(jnp.bfloat16), d_a[...]).astype(jnp.bfloat16)
    for h in range(2):
        stored["out"][h] = part[:, h * 384 : (h + 1) * 384].reshape(4, 2, 2, -1, 384)
    begin(names.index("out"))
    clock.spend(NORM_TIME)

    for name in ("w_box", "qkv", "table", "x"):
        fetch(name).wait()
    low = w_box.at[0][...].reshape(width, 2 * FREQ)
    high = w_box.at[1][...].reshape(width, 2 * FREQ)
    box_w[...] = jnp.concatenate(
        [low[:, :FREQ], high[:, :FREQ], low[:, FREQ:], high[:, FREQ:]], axis=1
    )
    keys[...] = table[...].astype(jnp.bfloat16)
    table[...] = table[...] * (HEAD**-0.5)
    head_lane = lax.broadcasted_iota(jnp.int32, (1, 128), 1)

    def p_copy(p, slot, i):
        at = lanes((slot * 2 + i) * page_len, page_len)
        return pltpu.make_async_copy(p_in.at[p, i], hidden.at[:, at], p_sem.at[slot, i])

    p_copy(0, 0, 0).start()
    p_copy(0, 0, 1).start()

    def with_qkv(w_qkv):
        fetch_weight("qkv", w_qkv).start()

        def pair(p, carry, serve):
            slot = lax.rem(p, 2)

            @pl.when(p < HEADS // 2 - 1)
            def _():
                p_copy(p + 1, 1 - slot, 0).start()
                p_copy(p + 1, 1 - slot, 1).start()

            p_copy(p, slot, 0).wait()
            p_copy(p, slot, 1).wait()
            q = qkv[:, lanes(p * 128, 128)]
            k = qkv[:, lanes(width + p * 128, 128)]
            v = qkv[:, lanes(2 * width + p * 128, 128)]
            w = box_w[pl.ds(pl.multiple_of(p * 128, 128), 128), :]
            d_o = d_mixed[:, lanes(p * 128, 128)]
            weighted = d_o.astype(jnp.float32) * o_own[:, lanes(p * 128, 128)]
            grads = []
            d_w = jnp.zeros((128, BOX_DIM), jnp.float32)
            for i in range(2):
                if i:
                    serve()
                of_head = (head_lane < HEAD) == (i == 0)
                probs = hidden[:, lanes((slot * 2 + i) * page_len, page_len)]
                delta = jnp.sum(jnp.where(of_head, weighted, 0.0), axis=1, keepdims=True)
                d_probs = dot_t(jnp.where(of_head, d_o, jnp.zeros_like(d_o)), v)
                d_s = (probs.astype(jnp.float32) * (d_probs - delta)).astype(jnp.bfloat16)
                d_q = jnp.dot(d_s, k, preferred_element_type=jnp.float32)
                d_1 = jnp.dot(d_s, keys[0], preferred_element_type=jnp.float32)
                d_2 = jnp.dot(d_s, keys[1], preferred_element_type=jnp.float32)
                cosine, sine = table[0], table[1]
                d_sine = (d_1 * sine - d_2 * cosine).astype(jnp.bfloat16)
                d_cosine = (d_1 * cosine + d_2 * sine).astype(jnp.bfloat16)
                d_u = jnp.concatenate([d_sine, d_cosine], axis=1)
                d_q = d_q * (HEAD**-0.5) + dot_t(d_u, w)
                d_w = d_w + dot_n(jnp.where(of_head, q, jnp.zeros_like(q)), d_u)
                grads.append((d_q, dot_n(d_s, q) * (HEAD**-0.5), dot_n(probs, d_o)))
            first_head = head_lane < HEAD
            for n, (one, two) in enumerate(zip(*grads)):
                value = jnp.where(first_head, one, two).astype(jnp.bfloat16)
                slope[:, lanes(n * width + p * 128, 128)] = value
                if n == 0:
                    vec_g[:, lanes(BQ + p * 128, 128)] = total(value)
                if n == 2:
                    vec_g[:, lanes(BV + p * 128, 128)] = total(value)
            box_g[pl.ds(pl.multiple_of(p * 128, 128), 128), :] = d_w.astype(jnp.bfloat16)
            return carry

        clock.loop(HEADS // 2, PAIR_BACK_TIME, pair, 2)

        part = box_g[...]
        stored["box"][0] = jnp.concatenate(
            [part[:, :FREQ], part[:, 2 * FREQ : 3 * FREQ]], axis=1
        ).reshape(4, 2, 2, -1, 384)
        stored["box"][1] = jnp.concatenate(
            [part[:, FREQ : 2 * FREQ], part[:, 3 * FREQ :]], axis=1
        ).reshape(4, 2, 2, -1, 384)
        begin(names.index("box"))
        clock.spend(0.5)
        clock.upto(*[
            (g, part, 3)
            for g, group in enumerate(groups)
            if names[g] == "down"
            for part in range(len(group[-1]))
        ])
        for g in range(count):
            if names[g] == "down":
                scatter.left(g)

        height = stored["box"].shape[4]
        for t in range(3):
            def qkv_tile(h, carry, t=t):
                tile = dot_n(x_own[...], slope[:, lanes(h * 1152 + t * 384, 384)])
                stored["down"][h, :, :, :, t * height : (t + 1) * height, :] = tile.astype(
                    jnp.bfloat16
                ).reshape(4, 2, 2, -1, 384)
                return carry

            lax.fori_loop(0, 2, qkv_tile, 0)
            begin([g for g in range(count) if names[g] == "qkv"][t])
            clock.spend(1.0)

        for dz in range(4):
            for dx in range(2):
                for dc in range(2):
                    for dy in range(2):
                        device = ((dz * 2 + dx) * 2 + dc) * 2 + dy
                        start = device * (VECTORS // 32) // 128 * 128
                        pieces[dy, dz, dx, dc] = vec_g[:, start : start + 384]
        vector_c.start()
        fetch_weight("qkv", w_qkv).wait()

        def back_tile(h, carry, serve):
            w = w_qkv.at[h][...].reshape(width, 1152)
            unit1[...] += dot_t(slope[:, lanes(h * 1152, 1152)], w)
            return carry

        clock.loop(2, 1.0, back_tile)
        dx_low[0] = unit1[rows(1 - y), :].astype(jnp.bfloat16)
        dx_swap.start()
        pltpu.make_async_copy(unit1.at[rows(y)], dx_out.at[y], out_sem.at[1]).start()

    vector_c = remote(pieces.at[:, :, :, 1 - c], pc_land, v_sems, (0,), place.c_peer)
    vector_y = remote(pieces.at[1 - y, :, :, c], py_land, v_sems, (1,), place.y_peer)
    vector_x = remote(pieces.at[y, :, 1 - x, c], px_land, v_sems, (2,), place.x_peer)

    def vector_z(k):
        there = lax.rem(z + k + 1, 4)
        peer = (there * 4 + x * 2 + c, y)
        return remote(pieces.at[y, there, x, c], pz_land.at[k], vz_sems, (k,), peer)

    pl.run_scoped(with_qkv, pltpu.VMEM(w_in["qkv"].shape, jnp.bfloat16))

    vector_c.wait_recv()
    pieces[:, :, :, c] += pc_land[...]
    vector_y.start()
    clock.spend(3.0)
    vector_y.wait_recv()
    pieces[y, :, :, c] += py_land[...]
    vector_x.start()
    clock.spend(3.0)
    vector_x.wait_recv()
    pieces[y, :, x, c] += px_land[...]
    for k in range(3):
        vector_z(k).start()
    clock.upto(*(tuple(event) for _, *event in SCATTER_EVENTS))
    dx_swap.wait_recv()
    unit2[0:block, :] = dx_low[1].astype(jnp.float32)
    pltpu.make_async_copy(unit2.at[0:block], dx_out.at[1 - y], out_sem.at[2]).start()
    for k in range(3):
        vector_z(k).wait_recv()
    piece_total = pieces[y, z, x, c]
    for k in range(3):
        piece_total = piece_total + pz_land[k]
    piece_sum[...] = piece_total
    finals = [pltpu.make_async_copy(piece_sum, piece_out, out_sem.at[3])]
    for i, name in enumerate(WEIGHTS):
        finals.append(pltpu.make_async_copy(summed[name], grad_out[name], out_sem.at[4 + i]))
    for copy in finals:
        copy.start()
    for g in range(count):
        scatter.left(g)
    for copy in (vector_c, vector_y, vector_x, out_swap, dx_swap):
        copy.wait_send()
    for k in range(3):
        vector_z(k).wait_send()
    out_swap.wait_recv()
    out_keep.wait()
    pltpu.make_async_copy(unit1.at[rows(y)], dx_out.at[y], out_sem.at[1]).wait()
    pltpu.make_async_copy(unit2.at[0:block], dx_out.at[1 - y], out_sem.at[2]).wait()
    for copy in finals:
        copy.wait()


START_TIME = 6.0
DOWN_TIME = 1.0
SLOPE_TIME = 1.0
UP_TIME = 0.8
UP_BACK_TIME = 1.4
NORM_TIME = 4.5
PAIR_BACK_TIME = 3.4


def backward_call(full, kept, shards):
    low, single = jnp.bfloat16, jnp.float32
    page_len, width = kept["x"].shape
    groups = SCATTER_GROUPS
    count = len(groups)
    outs = [
        jax.ShapeDtypeStruct((2, page_len // 2, width), low),
        jax.ShapeDtypeStruct((2, page_len // 2, width), single),
    ]
    outs += [jax.ShapeDtypeStruct(s.shape, single) for s in shards]
    outs += [jax.ShapeDtypeStruct((1, 384), single)]
    by_name = dict(zip(WEIGHTS, shards))

    def vmem(*shape, kind=low):
        return pltpu.VMEM(shape, kind)

    size = lambda cut: (cut[1], cut[3])
    dma = pltpu.SemaphoreType.DMA
    scratch = [vmem(2, 4, 2, 2, *by_name[n].shape) for n in ("box", "out", "up", "down")]
    scratch += [vmem(2, 4, 2, *size(g[2])) for g in groups]
    for group in groups:
        for path, piece in group[-1]:
            scratch += [vmem(*landing_shape(path, hop, piece)) for hop in range(3)]
    scratch += [vmem(*s.shape, kind=single) for s in shards]
    scratch += [vmem(*full[n].shape) for n in ("box", "out")]
    scratch += [vmem(width, BOX_DIM), vmem(width, BOX_DIM)]
    scratch += [vmem(*kept[n].shape, kind=kept[n].dtype) for n in ("x", "ct", "qkv", "table")]
    scratch += [vmem(*kept["table"].shape)]
    scratch += [
        vmem(*kept[n].shape, kind=kept[n].dtype)
        for n in ("o", "unit1", "inv1", "g", "d", "unit2", "inv2", "vec")
    ]
    scratch += [vmem(page_len, width)] * 4
    scratch += [vmem(2, page_len // 2, width), vmem(1, VECTORS + 128, kind=single)]
    scratch += [
        vmem(2, 4, 2, 2, 1, 384, kind=single),
        vmem(2, 4, 2, 1, 384, kind=single),
        vmem(4, 2, 1, 384, kind=single),
        vmem(4, 1, 384, kind=single),
        vmem(3, 1, 384, kind=single),
        vmem(1, 384, kind=single),
    ]
    scratch += [dma((len(semaphore_table(groups)),))] * 2 + [dma((count,))] * 2
    scratch += [dma((3,))] * 2 + [dma((3,))] * 2 + [dma((2,))] * 2
    scratch += [dma((17,)), dma((2, 2)), dma((9,))]
    anywhere = pl.BlockSpec(memory_space=pl.ANY)
    operands = [full[n] for n in WEIGHTS] + list(kept.values())
    plan = (groups, page_len, width)
    results = pl.pallas_call(
        partial(backward_kernel, plan),
        out_shape=outs,
        in_specs=[anywhere] * len(operands),
        out_specs=[anywhere] * len(outs),
        scratch_shapes=scratch,
        compiler_params=pltpu.CompilerParams(
            collective_id=1, has_side_effects=True, vmem_limit_bytes=VMEM_BACK
        ),
    )(*operands)
    return results


VMEM_BACK = 63 * 2**20


def finish_kernel(*refs):
    count = len(refs) // 2
    ins, outs = refs[:count], refs[count:]
    for i in range(count - 1):
        outs[i][...] = ins[i][...]
    rows = jnp.broadcast_to(ins[-1][...], (8, 384))
    rows = pltpu.roll(rows, 384 - Place().vector_offset(), 1)
    outs[-1][...] = rows[0:1, : VECTORS // 32].reshape(VECTORS // 32)


def finish_call(results):
    vmem = pl.BlockSpec(memory_space=pltpu.VMEM)
    outs = [jax.ShapeDtypeStruct(r.shape, r.dtype) for r in results[:-1]]
    outs += [jax.ShapeDtypeStruct((VECTORS // 32,), jnp.float32)]
    return pl.pallas_call(
        finish_kernel,
        out_shape=outs,
        in_specs=[vmem] * len(outs),
        out_specs=[vmem] * len(outs),
        compiler_params=pltpu.CompilerParams(vmem_limit_bytes=VMEM_BACK),
    )(*results)


def fast_layer(tokens, boxes, lengths, wqkv, wbox, wout, wup, wdown, vectors, cotangent):
    shards = (wqkv, wbox, wout, wup, wdown)
    full, kept = forward_call(tokens, cotangent, boxes, lengths, vectors, shards)
    return tuple(finish_call(backward_call(full, kept, shards)))


def on_device(*args):
    tokens, wqkv, wbox, wdown = args[0], args[3], args[4], args[7]
    blocks, groups = lax.axis_size("blk"), lax.axis_size("dp")
    fits = (
        blocks == 2
        and groups == 16
        and tokens.shape[0] == 2
        and wqkv.shape == (48, 1152)
        and wdown.shape == (192, 384)
        and wbox.shape == (48, 2 * FREQ)
    )
    return fast_layer(*args) if fits else general_layer(*args)


def solution(mesh):
    in_specs = (
        P("dp", "blk", None),
        P(None, "dp", "blk"),
        P("dp"),
        P("dp", "blk"),
        P("dp", "blk"),
        P("dp", "blk"),
        P("dp", "blk"),
        P("dp", "blk"),
        P(("dp", "blk")),
        P("dp", "blk", None),
    )
    out_specs = (
        P("dp", "blk", None),
        P("dp", "blk", None),
        P("dp", "blk"),
        P("dp", "blk"),
        P("dp", "blk"),
        P("dp", "blk"),
        P("dp", "blk"),
        P(("dp", "blk")),
    )
    return jax.shard_map(
        on_device, mesh=mesh, in_specs=in_specs, out_specs=out_specs, check_vma=False
    )
```

```python
from functools import partial
import math

import jax
import jax.numpy as jnp
import numpy as np
from jax import lax
from jax.experimental import pallas as pl
from jax.experimental.pallas import tpu as pltpu
from jax.sharding import PartitionSpec as P

HEADS = 12
HEAD = 64
FREQ = 192
BOX_DIM = 768

EPSILON = 1e-12
MASKED = -1e30


def box_table(boxes):
    frequency = jnp.exp(jnp.arange(FREQ, dtype=jnp.float32) * (-math.log(10000.0) / FREQ))
    across = boxes[0].astype(jnp.float32)[..., None] * frequency
    upward = boxes[1].astype(jnp.float32)[..., None] * frequency
    return jnp.concatenate(
        [jnp.cos(across), jnp.sin(across), jnp.cos(upward), jnp.sin(upward)], axis=-1
    )


def rotate(coeffs, own_table):
    cos_across, sin_across, cos_upward, sin_upward = jnp.split(own_table[..., None, :], 4, axis=-1)
    sa, ca, sb, cb = jnp.split(coeffs, 4, axis=-1)
    return jnp.concatenate(
        [
            sa * sin_across + ca * cos_across,
            ca * sin_across - sa * cos_across,
            sb * sin_upward + cb * cos_upward,
            cb * sin_upward - sb * cos_upward,
        ],
        axis=-1,
    )


def unrotate(grad_rows, own_table):
    cos_across, sin_across, cos_upward, sin_upward = jnp.split(own_table[..., None, :], 4, axis=-1)
    d1a, d2a, d1b, d2b = jnp.split(grad_rows, 4, axis=-1)
    return jnp.concatenate(
        [
            d1a * sin_across - d2a * cos_across,
            d1a * cos_across + d2a * sin_across,
            d1b * sin_upward - d2b * cos_upward,
            d1b * cos_upward + d2b * sin_upward,
        ],
        axis=-1,
    )


def normalize(hidden):
    row_mean = jnp.mean(hidden, axis=-1, keepdims=True)
    centered = hidden - row_mean
    inverse = lax.rsqrt(jnp.mean(centered * centered, axis=-1, keepdims=True) + EPSILON)
    return centered * inverse, inverse


def normalize_back(grad, unit, inverse, gain):
    scaled = grad * gain
    mean_grad = jnp.mean(scaled, axis=-1, keepdims=True)
    mean_unit = jnp.mean(scaled * unit, axis=-1, keepdims=True)
    d_hidden = inverse * (scaled - mean_grad - unit * mean_unit)
    return d_hidden, jnp.sum(grad * unit, axis=0), jnp.sum(grad, axis=0)


def unpack(vector_all, model_width, hidden_units):
    cuts = [model_width] * 5 + [hidden_units] + [model_width] * 3
    pieces = []
    offset = 0
    for length_here in cuts:
        pieces.append(vector_all[offset : offset + length_here])
        offset = offset + length_here
    return pieces


def dot32(a, b):
    return jnp.dot(a, b, preferred_element_type=jnp.float32)


def gather_weight(shard):
    part = lax.all_gather(shard, "blk", axis=1, tiled=True)
    return lax.all_gather(part, "dp", axis=0, tiled=True)


def scatter_weight(grad):
    part = lax.psum_scatter(grad.astype(jnp.bfloat16), "dp", scatter_dimension=0, tiled=True)
    return lax.psum_scatter(part, "blk", scatter_dimension=1, tiled=True).astype(jnp.float32)


def general_layer(tokens, boxes, lengths, wqkv, wbox, wout, wup, wdown, vectors, cotangent):
    blocks = lax.axis_size("blk")
    pages_here = tokens.shape[0] // blocks
    model_width = tokens.shape[2]
    to_pages = partial(
        lax.all_to_all, axis_name="blk", split_axis=0, concat_axis=1, tiled=True
    )
    from_pages = partial(
        lax.all_to_all, axis_name="blk", split_axis=1, concat_axis=0, tiled=True
    )
    page_tokens = to_pages(tokens)
    page_boxes = lax.all_to_all(boxes, "blk", split_axis=1, concat_axis=2, tiled=True)
    page_lengths = lax.dynamic_slice(lengths, (lax.axis_index("blk") * pages_here,), (pages_here,))
    full_qkv = gather_weight(wqkv)
    full_box = gather_weight(wbox)
    full_out = gather_weight(wout)
    full_up = gather_weight(wup)
    full_down = gather_weight(wdown)
    full_vec = lax.all_gather(vectors, ("dp", "blk"), axis=0, tiled=True).astype(jnp.float32)
    page_cotangent = to_pages(cotangent)
    hidden_units = full_up.shape[1]
    bq, bv, bo, g1, e1, b1, b2, g2, e2 = unpack(full_vec, model_width, hidden_units)
    page_len = page_tokens.shape[1]
    score_scale = HEAD ** (-0.5)

    x = page_tokens.reshape(-1, model_width)
    projected = dot32(x, full_qkv)
    head_shape = (pages_here, page_len, HEADS, HEAD)
    q = (projected[:, :model_width] + bq).astype(jnp.bfloat16).reshape(head_shape)
    k = projected[:, model_width : 2 * model_width].astype(jnp.bfloat16).reshape(head_shape)
    v = (projected[:, 2 * model_width :] + bv).astype(jnp.bfloat16).reshape(head_shape)
    table = box_table(page_boxes)
    box_heads = full_box.reshape(HEADS, HEAD, BOX_DIM)
    coeffs = jnp.einsum("pqhd,hdc->pqhc", q, box_heads, preferred_element_type=jnp.float32)
    box_query = rotate(coeffs, table).astype(jnp.bfloat16)
    box_keys = table.astype(jnp.bfloat16)
    scores = (
        jnp.einsum("pqhd,pkhd->phqk", q, k, preferred_element_type=jnp.float32)
        + jnp.einsum("pqhc,pkc->phqk", box_query, box_keys, preferred_element_type=jnp.float32)
    ) * score_scale
    is_valid = (jnp.arange(page_len)[None, :] < page_lengths[:, None])[:, None, None, :]
    masked = jnp.where(is_valid, scores, MASKED)
    probs = jax.nn.softmax(masked, axis=-1)
    probs_low = probs.astype(jnp.bfloat16)
    mixed = jnp.einsum("phqk,pkhd->pqhd", probs_low, v, preferred_element_type=jnp.float32)
    mixed_low = mixed.astype(jnp.bfloat16).reshape(-1, model_width)
    unit1, inv1 = normalize(x.astype(jnp.float32) + dot32(mixed_low, full_out) + bo)
    y1 = unit1 * g1 + e1
    y1_low = y1.astype(jnp.bfloat16)
    pre = dot32(y1_low, full_up) + b1
    hidden = jax.nn.gelu(pre, approximate=False).astype(jnp.bfloat16)
    unit2, inv2 = normalize(y1 + dot32(hidden, full_down) + b2)
    output = (unit2 * g2 + e2).astype(jnp.bfloat16)

    seed = page_cotangent.reshape(-1, model_width).astype(jnp.float32)
    d_h2, d_g2, d_e2 = normalize_back(seed, unit2, inv2, g2)
    d_f = d_h2.astype(jnp.bfloat16)
    d_hidden = dot32(d_f, full_down.T)
    d_pre = jax.vjp(partial(jax.nn.gelu, approximate=False), pre)[1](d_hidden)[0]
    d_pre = d_pre.astype(jnp.bfloat16)
    d_wdown = dot32(hidden.T, d_f)
    d_wup = dot32(y1_low.T, d_pre)
    d_y1 = dot32(d_pre, full_up.T) + d_h2
    d_h1, d_g1, d_e1 = normalize_back(d_y1, unit1, inv1, g1)
    d_a = d_h1.astype(jnp.bfloat16)
    d_wout = dot32(mixed_low.T, d_a)
    d_mixed = dot32(d_a, full_out.T).astype(jnp.bfloat16).reshape(head_shape)
    row_delta = jnp.einsum("pqhd,pqhd->phq", d_mixed.astype(jnp.float32), mixed)
    d_probs = jnp.einsum("pqhd,pkhd->phqk", d_mixed, v, preferred_element_type=jnp.float32)
    d_raw = (probs * (d_probs - row_delta[..., None])).astype(jnp.bfloat16)
    d_q = jnp.einsum("phqk,pkhd->pqhd", d_raw, k, preferred_element_type=jnp.float32)
    d_box_q = jnp.einsum("phqk,pkc->pqhc", d_raw, box_keys, preferred_element_type=jnp.float32)
    d_k = jnp.einsum("phqk,pqhd->pkhd", d_raw, q, preferred_element_type=jnp.float32)
    d_v = jnp.einsum("phqk,pqhd->pkhd", probs_low, d_mixed, preferred_element_type=jnp.float32)
    d_coeffs = unrotate(d_box_q * score_scale, table).astype(jnp.bfloat16)
    d_q = d_q * score_scale + jnp.einsum(
        "pqhc,hdc->pqhd", d_coeffs, box_heads, preferred_element_type=jnp.float32
    )
    d_wbox = jnp.einsum("pqhd,pqhc->hdc", q, d_coeffs, preferred_element_type=jnp.float32)
    flat = (-1, model_width)
    d_q = d_q.astype(jnp.bfloat16).reshape(flat)
    d_k = (d_k * score_scale).astype(jnp.bfloat16).reshape(flat)
    d_v = d_v.astype(jnp.bfloat16).reshape(flat)
    d_c = jnp.concatenate([d_q, d_k, d_v], axis=1)
    d_wqkv = dot32(x.T, d_c)
    d_x = dot32(d_c, full_qkv.T) + d_h1
    total = partial(jnp.sum, axis=0, dtype=jnp.float32)
    vector_grad = jnp.concatenate(
        [total(d_q), total(d_v), total(d_a), d_g1, d_e1, total(d_pre), total(d_f), d_g2, d_e2]
    )
    return (
        from_pages(output.reshape(page_tokens.shape)),
        from_pages(d_x.reshape(page_tokens.shape)),
        scatter_weight(d_wqkv),
        scatter_weight(d_wbox.reshape(model_width, BOX_DIM)),
        scatter_weight(d_wout),
        scatter_weight(d_wup),
        scatter_weight(d_wdown),
        lax.psum_scatter(vector_grad, ("dp", "blk"), scatter_dimension=0, tiled=True),
    )


GATHER_GROUPS = (
    ("qkv", (0, 48, 0, 384), (("zxy", (0, 48, 0, 256)), ("zyx", (0, 48, 256, 128)),)),
    ("qkv", (0, 48, 384, 384), (("zyx", (0, 48, 384, 256)), ("yzx", (0, 48, 640, 128)),)),
    ("qkv", (0, 48, 768, 384), (("zxy", (0, 48, 768, 384)),)),
    ("box", (0, 48, 0, 384), (("zxy", (0, 48, 0, 256)), ("yzx", (0, 48, 256, 128)),)),
    ("out", (0, 48, 0, 384), (("zxy", (0, 48, 0, 256)), ("yxz", (0, 48, 256, 128)),)),
    ("up", (0, 48, 0, 384), (("zxy", (0, 48, 0, 256)), ("yzx", (0, 48, 256, 128)),)),
    ("up", (0, 48, 384, 384), (("yxz", (0, 48, 384, 384)),)),
    ("up", (0, 48, 768, 384), (("yxz", (0, 48, 768, 384)),)),
    ("up", (0, 48, 1152, 384), (("zxy", (0, 48, 1152, 256)), ("zyx", (0, 48, 1408, 128)),)),
    ("down", (0, 192, 0, 128), (("zxy", (0, 64, 0, 128)), ("yxz", (64, 128, 0, 128)),)),
    ("down", (0, 192, 128, 128), (("zxy", (0, 128, 128, 128)), ("yzx", (128, 64, 128, 128)),)),
    ("down", (0, 192, 256, 128), (("zyx", (0, 192, 256, 128)),)),
)
GATHER_EVENTS = (
    (1, 0, 0, 0),
    (1, 2, 0, 0),
    (1, 9, 1, 0),
    (1, 10, 1, 0),
    (2, 0, 1, 0),
    (2, 1, 1, 0),
    (2, 7, 0, 0),
    (3, 5, 1, 0),
    (4, 1, 0, 0),
    (4, 8, 0, 0),
    (4, 0, 0, 10),
    (4, 3, 1, 0),
    (4, 6, 0, 0),
    (5, 4, 1, 0),
    (5, 5, 0, 0),
    (5, 0, 0, 1),
    (5, 3, 0, 0),
    (5, 0, 1, 10),
    (5, 8, 1, 0),
    (5, 2, 0, 10),
    (6, 1, 0, 10),
    (6, 0, 1, 1),
    (6, 4, 0, 0),
    (6, 1, 0, 1),
    (6, 0, 0, 2),
    (6, 3, 0, 10),
    (6, 2, 0, 1),
    (6, 1, 1, 1),
    (6, 3, 1, 1),
    (6, 4, 1, 1),
    (6, 4, 0, 10),
    (6, 5, 1, 1),
    (6, 3, 0, 1),
    (6, 0, 1, 2),
    (6, 5, 0, 10),
    (6, 4, 0, 1),
    (6, 1, 1, 11),
    (6, 1, 0, 2),
    (6, 5, 0, 1),
    (6, 3, 1, 11),
    (6, 1, 1, 2),
    (6, 6, 0, 1),
    (6, 8, 1, 10),
    (6, 5, 1, 11),
    (6, 3, 1, 2),
    (6, 10, 0, 0),
    (6, 9, 1, 1),
    (6, 2, 0, 2),
    (7, 9, 0, 0),
    (7, 0, 1, 3),
    (7, 0, 1, 4),
    (7, 3, 0, 2),
    (7, 4, 0, 2),
    (7, 0, 0, 3),
    (7, 8, 1, 1),
    (7, 4, 1, 2),
    (7, 10, 1, 1),
    (7, 0, 0, 4),
    (7, 11, 0, 0),
    (7, 2, 0, 3),
    (7, 5, 1, 2),
    (7, 7, 0, 1),
    (8, 8, 0, 10),
    (8, 2, 0, 4),
    (8, 9, 0, 10),
    (8, 11, 0, 10),
    (8, 10, 0, 10),
    (8, 1, 1, 3),
    (8, 3, 0, 3),
    (8, 1, 1, 4),
    (8, 9, 0, 1),
    (9, 5, 0, 2),
    (9, 8, 0, 1),
    (9, 4, 1, 12),
    (9, 6, 0, 2),
    (9, 1, 0, 3),
    (11, 3, 1, 3),
    (11, 1, 0, 4),
    (12, 3, 0, 4),
    (13, 11, 0, 1),
    (14, 4, 0, 3),
    (15, 4, 1, 3),
    (15, 10, 1, 11),
    (17, 10, 0, 1),
    (18, 3, 1, 4),
    (18, 6, 0, 12),
    (18, 7, 0, 2),
    (18, 8, 1, 2),
    (19, 10, 1, 2),
    (19, 8, 0, 2),
    (20, 4, 1, 4),
    (21, 5, 1, 3),
    (22, 5, 0, 3),
    (22, 9, 0, 2),
    (23, 11, 0, 2),
    (23, 9, 1, 2),
    (24, 8, 1, 3),
    (24, 10, 0, 2),
    (28, 5, 1, 4),
    (28, 8, 1, 4),
    (29, 5, 0, 4),
    (30, 7, 0, 12),
    (31, 6, 0, 3),
    (32, 8, 0, 3),
    (32, 10, 1, 3),
    (33, 6, 0, 4),
    (35, 9, 0, 3),
    (37, 8, 0, 4),
    (38, 10, 0, 3),
    (39, 10, 1, 4),
    (39, 11, 0, 3),
    (40, 9, 0, 4),
    (40, 9, 1, 12),
    (40, -1, 0, 0),
    (41, 4, 0, 4),
    (41, 7, 0, 3),
    (49, 11, 0, 4),
    (52, 10, 0, 4),
    (53, 9, 1, 3),
    (59, 7, 0, 4),
    (64, 9, 1, 4),
)
SCATTER_GROUPS = (
    ("down", "down", (0, 192, 0, 128), (0, 192, 0, 128), (("zxy", (0, 192, 0, 128)),)),
    ("down", "down", (0, 192, 128, 128), (0, 192, 128, 128), (("xzy", (0, 192, 128, 128)),)),
    ("down", "down", (0, 192, 256, 128), (0, 192, 256, 128), (("yxz", (0, 192, 256, 128)),)),
    ("up", "up", (0, 48, 0, 384), (0, 48, 0, 384), (("yxz", (0, 48, 0, 128)), ("zxy", (0, 48, 128, 128)), ("xyz", (0, 48, 256, 128)),)),
    ("up", "up", (0, 48, 384, 384), (0, 48, 384, 384), (("yxz", (0, 48, 384, 128)), ("xzy", (0, 48, 512, 256)),)),
    ("up", "up", (0, 48, 768, 384), (0, 48, 768, 384), (("zyx", (0, 48, 768, 128)), ("yxz", (0, 48, 896, 128)), ("yzx", (0, 48, 1024, 128)),)),
    ("up", "up", (0, 48, 1152, 384), (0, 48, 1152, 384), (("xyz", (0, 48, 1152, 384)),)),
    ("out", "out", (0, 48, 0, 384), (0, 48, 0, 384), (("yzx", (0, 48, 0, 384)),)),
    ("qkv", "early", (0, 48, 0, 384), 0, (("yxz", (0, 48, 0, 128)), ("xzy", (0, 48, 128, 256)),)),
    ("box", "box", (0, 48, 0, 384), (0, 48, 0, 384), (("yxz", (0, 48, 0, 128)), ("xzy", (0, 48, 128, 256)),)),
    ("qkv", "down", (0, 48, 0, 384), 1, (("yxz", (0, 48, 0, 256)), ("xyz", (0, 48, 256, 128)),)),
    ("qkv", "down", (48, 48, 0, 384), 2, (("xyz", (48, 48, 0, 256)), ("xzy", (48, 48, 256, 128)),)),
)
SCATTER_EVENTS = (
    (1, -1, 0, 0),
    (4, 0, 0, 0),
    (10, 2, 0, 0),
    (11, 1, 0, 0),
    (13, 0, 0, 10),
    (15, 3, 0, 0),
    (17, 4, 0, 0),
    (18, 5, 0, 0),
    (19, 2, 0, 1),
    (20, 7, 0, 0),
    (21, 1, 0, 1),
    (23, 0, 0, 1),
    (23, 6, 0, 0),
    (25, 1, 0, 11),
    (30, 2, 0, 2),
    (30, 3, 0, 1),
    (32, 3, 1, 10),
    (34, 2, 0, 12),
    (34, 5, 2, 1),
    (35, 4, 0, 1),
    (36, 4, 1, 1),
    (36, 5, 0, 10),
    (36, 8, 0, 0),
    (38, 0, 0, 2),
    (39, 3, 1, 1),
    (39, 4, 1, 11),
    (40, 1, 0, 2),
    (40, 3, 2, 1),
    (41, 5, 0, 1),
    (41, 5, 1, 1),
    (41, 5, 2, 11),
    (42, 4, 0, 2),
    (43, 3, 0, 2),
    (44, 3, 2, 2),
    (44, 7, 0, 1),
    (44, 3, 0, 12),
    (45, 5, 1, 2),
    (45, 6, 0, 1),
    (46, 8, 0, 1),
    (46, 3, 2, 12),
    (46, 5, 2, 2),
    (47, 2, 0, 3),
    (48, 4, 0, 12),
    (48, 1, 0, 3),
    (48, 9, 0, 0),
    (49, 0, 0, 3),
    (49, 4, 1, 2),
    (50, 8, 1, 1),
    (50, 3, 1, 2),
    (50, 10, 0, 0),
    (51, 11, 0, 0),
    (57, 4, 1, 3),
    (59, 5, 0, 2),
    (60, 3, 1, 3),
    (67, 5, 1, 12),
    (68, 3, 0, 3),
    (107, 3, 2, 3),
    (965, 9, 1, 1),
    (973, 5, 1, 3),
    (984, 9, 1, 11),
    (985, 10, 1, 1),
    (985, 4, 0, 3),
    (989, 6, 0, 2),
    (992, 8, 1, 11),
    (993, 7, 0, 11),
    (995, 9, 0, 1),
    (995, 5, 2, 3),
    (995, 10, 0, 1),
    (996, 11, 1, 1),
    (997, 11, 0, 1),
    (998, 6, 0, 12),
    (998, 9, 0, 2),
    (998, 9, 1, 2),
    (999, 10, 0, 2),
    (999, 8, 1, 2),
    (999, 11, 1, 11),
    (999, 10, 1, 2),
    (1000, 9, 0, 12),
    (1000, 10, 0, 12),
    (1001, 5, 0, 3),
    (1001, 8, 0, 2),
    (1003, 7, 0, 2),
    (1003, 10, 1, 12),
    (1004, 11, 0, 2),
    (1005, 8, 0, 12),
    (1006, 11, 1, 2),
    (1008, 9, 0, 3),
    (1008, 8, 1, 3),
    (1010, 10, 0, 3),
    (1012, 11, 0, 12),
    (1016, 6, 0, 3),
    (1016, 8, 0, 3),
    (1016, 7, 0, 3),
    (1018, 10, 1, 3),
    (1021, 11, 1, 3),
    (1025, 9, 1, 3),
    (1026, 11, 0, 3),
)


MESH = pl.DeviceIdType.MESH
WEIGHTS = ("qkv", "box", "out", "up", "down")
ROT = 4
ALL = slice(None)


def window(piece):
    return (pl.ds(piece[0], piece[1]), pl.ds(piece[2], piece[3]))


class Place:
    def __init__(self):
        dp = lax.axis_index("dp")
        self.y = lax.axis_index("blk")
        self.z = lax.div(dp, 4)
        self.x = lax.rem(lax.div(dp, 2), 2)
        self.c = lax.rem(dp, 2)
        x, y, z, c = self.x, self.y, self.z, self.c
        self.near = z + 1 - 2 * lax.rem(z, 2)
        self.far = lax.rem(z + 2, 4)
        self.mirror = 3 - z
        self.inner = jnp.logical_or(z == 1, z == 2)
        self.end = jnp.logical_or(z == 0, z == 3)
        at = lambda other: (other * 4 + x * 2 + c, y)
        self.near_peer, self.far_peer, self.mirror_peer = at(self.near), at(self.far), at(self.mirror)
        self.x_peer = (dp + 2 - 4 * x, y)
        self.y_peer = (dp, 1 - y)
        self.c_peer = (dp + 1 - 2 * c, y)

    def own(self):
        return dict(y=self.y, z=self.z, x=self.x)

    def vector_offset(self):
        device = ((self.z * 2 + self.x) * 2 + self.c) * 2 + self.y
        return lax.rem(device * (VECTORS // 32), 128)

    def greet(self):
        barrier = pltpu.get_barrier_semaphore()
        peers = [self.near_peer, self.far_peer, self.mirror_peer]
        peers += [self.x_peer, self.y_peer, self.c_peer]
        for peer in peers:
            pl.semaphore_signal(barrier, inc=1, device_id=peer, device_id_type=MESH)
        pl.semaphore_wait(barrier, len(peers))


def semaphore_table(groups, slots):
    table = {}
    for g, group in enumerate(groups):
        for part, (path, _) in enumerate(group[-1]):
            for hop, axis in enumerate(path):
                for slot in range(slots if axis == "z" else 1):
                    table[g, part, hop, slot] = len(table)
    return table


SEND_RINGS = dict(all=(0, 24), inner=(24, 12), end=(36, 12))
SENDS = 48


class Sends:
    def __init__(self, place, events, started):
        self.place = place
        self.index, self.before, self.kind, self.after = {}, {}, {}, {}
        turns = {kind: [] for kind in SEND_RINGS}
        for at, (_, *event) in enumerate(events):
            for key, kind in started(*event):
                base, size = SEND_RINGS[kind]
                turn = turns[kind]
                self.index[key], self.kind[key] = base + len(turn) % size, kind
                if len(turn) >= size:
                    self.before[key] = turn[-size]
                    self.after[turn[-size]] = at
                turn.append(key)
        self.done = set()

    def when(self, key, act):
        kind = self.kind[key]
        if kind == "all":
            act()
        else:
            pl.when(self.place.inner if kind == "inner" else self.place.end)(act)

    def start(self, copy, *key):
        before = self.before.get(key)
        if before is not None and before not in self.done:
            copy(*before).wait_send()
        copy(*key).start()

    def left(self, copy, now=None, chosen=lambda key: True):
        for key in self.index:
            at = self.after.get(key)
            if key in self.done or not chosen(key) or (at is not None and (now is None or at < now)):
                continue
            self.done.add(key)
            self.when(key, copy(*key).wait_send)


def remote(src, dst, sems, at, peer, send=None):
    return pltpu.make_async_remote_copy(
        src,
        dst,
        sems[0].at[at if send is None else send],
        sems[1].at[at],
        device_id=peer,
        device_id_type=MESH,
    )


def core_table(groups):
    keys = [(g, part) for g, group in enumerate(groups) for part in range(len(group[-1]))]
    return {key: n for n, key in enumerate(keys)}


class Gather:
    def __init__(self, place, groups, shards, full, sems, own_sem):
        self.place, self.groups, self.shards, self.full = place, groups, shards, full
        self.sems, self.own_sem = sems, own_sem
        self.count = len(groups)
        self.table = semaphore_table(groups, 3)
        self.c_table = core_table(groups)
        self.sends = Sends(place, GATHER_EVENTS, self.started)
        self.owned = False

    def started(self, g, part, step):
        if g < 0 or step == 4:
            return []
        if step == 3:
            return [((g, part, 3, 0), "all")]
        if step >= 10:
            return [((g, part, step - 10, 3), "inner")]
        if self.groups[g][2][part][0][step] != "z":
            return [((g, part, step, 0), "all")]
        return [
            ((g, part, step, 1), "all"),
            ((g, part, step, 0), "all"),
            ((g, part, step, 2), "inner"),
        ]

    def copy(self, g, part, hop, slot, arriving=False):
        p = self.place
        name, _, parts = self.groups[g]
        path, piece = parts[part]
        cut = window(piece)
        send = self.sends.index[g, part, hop, slot]
        if hop == 3:
            c = 1 - p.c if arriving else p.c
            ref = self.full[name].at[(ALL, ALL, ALL, c) + cut]
            at = len(self.table) + self.c_table[g, part]
            return remote(ref, ref, self.sems, (at,), p.c_peer, (send,))
        axis = path[hop]
        at = p.own()
        at.update({earlier: ALL for earlier in path[:hop]})
        if axis == "z":
            peer = (p.near_peer, p.far_peer, p.mirror_peer, p.near_peer)[slot]
            if slot == 3:
                at["z"] = p.mirror if arriving else p.far
            elif arriving:
                at["z"] = (p.near, p.far, p.mirror)[slot]
        else:
            peer = p.x_peer if axis == "x" else p.y_peer
            if arriving:
                at[axis] = 1 - at[axis]
        ref = self.full[name].at[(at["y"], at["z"], at["x"], p.c) + cut]
        source = self.shards[name].at[cut] if hop == 0 and slot < 3 else ref
        at = self.table[g, part, hop, min(slot, 2)]
        return remote(source, ref, self.sems, (at,), peer, (send,))

    def own_copy(self, g):
        p = self.place
        name, both, _ = self.groups[g]
        cut = window(both)
        return pltpu.make_async_copy(
            self.shards[name].at[cut],
            self.full[name].at[(p.y, p.z, p.x, p.c) + cut],
            self.own_sem.at[g],
        )

    def relay(self, g, part, hop):
        @pl.when(self.place.inner)
        def _():
            self.copy(g, part, hop, 1, True).wait_recv()
            self.sends.start(self.copy, g, part, hop, 3)

    def start(self, g, part, hop):
        if self.groups[g][2][part][0][hop] != "z":
            self.sends.start(self.copy, g, part, hop, 0)
            return
        self.sends.start(self.copy, g, part, hop, 1)
        self.sends.start(self.copy, g, part, hop, 0)

        @pl.when(self.place.inner)
        def _():
            self.sends.start(self.copy, g, part, hop, 2)

    def finish(self, g, part, hop):
        self.copy(g, part, hop, 0, True).wait_recv()
        if self.groups[g][2][part][0][hop] != "z":
            return

        @pl.when(self.place.inner)
        def _():
            self.copy(g, part, hop, 2, True).wait_recv()

        @pl.when(self.place.end)
        def _():
            self.copy(g, part, hop, 1, True).wait_recv()
            self.copy(g, part, hop, 3, True).wait_recv()

    def own(self):
        for g in range(self.count):
            self.own_copy(g).start()

    def step(self, g, part, step):
        if step >= 10:
            self.relay(g, part, step - 10)
            return
        if step >= 1 and not self.owned:
            self.owned = True
            for other in range(self.count):
                self.own_copy(other).wait()
        if 1 <= step <= 3:
            self.finish(g, part, step - 1)
        if step <= 2:
            self.start(g, part, step)
        if step == 3:
            self.sends.start(self.copy, g, part, 3, 0)
        if step == 4:
            self.copy(g, part, 3, 0, True).wait_recv()


class Clock:
    def __init__(self, events, run, begun=None):
        self.events, self.run, self.now, self.at, self.begun = events, run, 0, 0, begun

    def may(self, event):
        return self.begun is None or event[1] < 0 or event[1] in self.begun

    def take(self):
        self.now += 1
        first = self.at
        while self.at < len(self.events):
            event = self.events[self.at]
            if event[0] > self.now or not self.may(event):
                break
            self.at += 1
        return self.events[first : self.at]

    def point(self):
        for _, *event in self.take():
            self.run(*event)

    def upto(self, *wanted):
        self.now += 1
        last = max(i for i, (_, *event) in enumerate(self.events) if tuple(event) in wanted)
        while self.at <= last:
            assert self.may(self.events[self.at])
            _, *event = self.events[self.at]
            self.at += 1
            self.run(*event)

    def loop(self, count, body, points=1):
        due = [[self.take() for _ in range(points)] for _ in range(count)]

        def wrapped(i, carry):
            point = iter(range(points))

            def serve():
                k = next(point)
                for n in range(count):
                    if due[n][k]:

                        @pl.when(i == n)
                        def _():
                            for _, *event in due[n][k]:
                                self.run(*event)

            serve()
            return body(i, carry, serve)

        lax.fori_loop(0, count, wrapped, 0)
        self.point()


def sine_cosine(angle):
    turns = jnp.floor(angle * (2.0 / math.pi) + 0.5)
    rest = angle - turns * 1.5703125
    rest = rest - turns * 4.837512969970703125e-4
    rest = rest - turns * 7.54978995489188216e-8
    square = rest * rest
    sine = rest + rest * square * (
        -1.6666654611e-1 + square * (8.3321608736e-3 + square * -1.9515295891e-4)
    )
    cosine = (
        1.0
        - 0.5 * square
        + square
        * square
        * (
            4.166664568298827e-2
            + square * (-1.388731625493765e-3 + square * 2.443315711809948e-5)
        )
    )
    quarter = turns.astype(jnp.int32)
    odd = (quarter & 1) == 1
    sine_sign = jnp.where((quarter & 2) == 2, -1.0, 1.0)
    cosine_sign = jnp.where(((quarter + 1) & 2) == 2, -1.0, 1.0)
    return (
        sine_sign * jnp.where(odd, cosine, sine),
        cosine_sign * jnp.where(odd, sine, cosine),
    )


def dot_t(a, b):
    return lax.dot_general(a, b, (((1,), (1,)), ((), ())), preferred_element_type=jnp.float32)


def dot_n(a, b):
    return lax.dot_general(a, b, (((0,), (0,)), ((), ())), preferred_element_type=jnp.float32)


def lanes(start, size):
    return pl.ds(pl.multiple_of(start, 128), size)


BQ, BV, BO, G1, E1, B1, B2, G2, E2 = 0, 768, 1536, 2304, 3072, 3840, 6912, 7680, 8448
VECTORS = 9216


def forward_kernel(plan, *refs):
    groups, page_len, width = plan
    block = page_len // 2
    refs = iter(refs)
    take = lambda n: [next(refs) for _ in range(n)]
    tokens, cotangent, boxes, lengths, vectors = take(5)
    shards = dict(zip(WEIGHTS, take(5)))
    full_out = dict(zip(WEIGHTS, take(5)))
    (x_out, ct_out, qkv_out, table_out, p_out, o_out, unit1_out, inv1_out) = take(8)
    (g_out, d_out, unit2_out, inv2_out, vec_out) = take(5)
    full = dict(zip(WEIGHTS, take(5)))
    (x_own, boxes_peer, pieces, vec, qkv, table, keys, box_w, p_slots, o_own, o_low) = take(11)
    (unit1, inv1, y1_low, hidden, slope, unit2, inv2) = take(7)
    w_sems = take(2)
    (own_sem,) = take(1)
    vz_sems, vxy_sems, vc_sems = take(2), take(2), take(2)
    ex_sems = take(2)
    (local_sem, p_sem, out_sem) = take(3)
    bias_qkv, piece = take(2)

    place = Place()
    y, z, x, c = place.y, place.z, place.x, place.c
    gather = Gather(place, groups, shards, full, w_sems, own_sem)

    def swap(i, source, target, arriving=False):
        at = (1 - y) if arriving else y
        return remote(
            source.at[1 - y], target.at[pl.ds(pl.multiple_of(at * block, block), block)],
            ex_sems, (i,), place.y_peer,
        )

    def keep(i, source, target):
        return pltpu.make_async_copy(
            source.at[y], target.at[pl.ds(pl.multiple_of(y * block, block), block)],
            local_sem.at[i],
        )

    box_swap = remote(boxes, boxes_peer, ex_sems, (2,), place.y_peer)

    def vector_y(arriving=False):
        at = 1 - y if arriving else y
        return remote(piece, pieces.at[at, z, x, c], vxy_sems, (0,), place.y_peer)

    def vector_x(arriving=False):
        ref = pieces.at[:, z, 1 - x if arriving else x, c]
        return remote(ref, ref, vxy_sems, (1,), place.x_peer)

    def vector_z(k, arriving=False):
        ref = pieces.at[:, lax.rem(z + 4 - k, 4) if arriving else z, :, c]
        peer = (lax.rem(z + k, 4) * 4 + x * 2 + c, y)
        return remote(ref, ref, vz_sems, (k - 1,), peer)

    def vector_c(arriving=False):
        ref = pieces.at[:, :, :, 1 - c if arriving else c]
        return remote(ref, ref, vc_sems, (0,), place.c_peer)

    vector_own = pltpu.make_async_copy(piece, pieces.at[y, z, x, c], local_sem.at[2])

    def event(g, part, step):
        if g < 0:
            swap(1, cotangent, ct_out).start()
        else:
            gather.step(g, part, step)

    clock = Clock(GATHER_EVENTS, event)

    def need(g):
        clock.upto(*((g, part, 4) for part in range(len(groups[g][2]))))

    outgoing = []

    def send_out(ref, out):
        copy = pltpu.make_async_copy(ref, out, out_sem.at[len(outgoing)])
        copy.start()
        outgoing.append(copy)

    own_vector = vectors[...].astype(jnp.float32).reshape(1, -1)
    own_vector = jnp.concatenate(
        [own_vector, jnp.zeros((1, 384 - own_vector.shape[1]), jnp.float32)], axis=1
    )
    own_vector = jnp.broadcast_to(own_vector, (8, 384))
    piece[...] = pltpu.roll(own_vector, place.vector_offset(), 1)[0:1, :]
    place.greet()
    gather.own()
    box_swap.start()
    vector_y().start()
    vector_own.start()
    swap(0, tokens, x_own).start()
    clock.point()
    keep(0, tokens, x_own).start()
    keep(1, cotangent, ct_out).start()

    box_swap.wait_recv()
    mine, other = boxes[...], boxes_peer[...]
    first_block = y == 0
    mine = jnp.where(first_block, mine[:, 0, :], mine[:, 1, :])
    other = jnp.where(first_block, other[:, 0, :], other[:, 1, :])
    both = jnp.concatenate(
        [jnp.where(first_block, mine, other), jnp.where(first_block, other, mine)], axis=1
    ).astype(jnp.float32)
    both = jnp.concatenate([both, jnp.zeros((6, page_len), jnp.float32)], axis=0)
    across_up = both.T
    lane = lax.broadcasted_iota(jnp.int32, (1, 2 * FREQ), 1)
    step = jnp.where(lane < FREQ, lane, lane - FREQ).astype(jnp.float32)
    frequency = jnp.exp(step * (-math.log(10000.0) / FREQ))
    angle = jnp.where(lane < FREQ, across_up[:, 0:1], across_up[:, 1:2]) * frequency
    sine, cosine = sine_cosine(angle)
    table[0], table[1] = cosine, sine
    keys[0 : 2 * FREQ, :] = cosine.astype(jnp.bfloat16).T
    keys[2 * FREQ :, :] = sine.astype(jnp.bfloat16).T
    send_out(table, table_out)
    clock.point()
    vector_own.wait()
    vector_y(True).wait_recv()
    vector_x().start()
    clock.point()
    vector_x(True).wait_recv()
    for k in range(1, 4):
        vector_z(k).start()
    clock.point()
    clock.upto(*((0, part, 3) for part in range(len(groups[0][2]))))
    for k in range(1, 4):
        vector_z(k, True).wait_recv()
    vector_c().start()
    need(0)
    vector_c(True).wait_recv()
    vec[...] = jnp.zeros_like(vec)
    for dz in range(4):
        for dx in range(2):
            for dc in range(2):
                for dy in range(2):
                    device = ((dz * 2 + dx) * 2 + dc) * 2 + dy
                    start = device * (VECTORS // 32) // 128 * 128
                    vec[:, start : start + 384] += pieces[dy, dz, dx, dc]
    send_out(vec, vec_out)

    def vector(start, size=width):
        return vec[:, start : start + size]

    def project(first, count):
        def project_tile(h, carry):
            w = full["qkv"].at[h][:, :, :, :, first : first + count].reshape(width, count)
            out = jnp.dot(x_own[...], w, preferred_element_type=jnp.float32)
            start = pl.multiple_of(h * 1152 + first, 128)
            column = start + lax.broadcasted_iota(jnp.int32, (1, count), 1)
            bias = bias_qkv[:, lanes(start, count)]
            qkv[:, lanes(start, count)] = (out + bias).astype(jnp.bfloat16)
            return carry

        lax.fori_loop(0, 2, project_tile, 0)

    bias_qkv[:, 0:width] = vector(BQ)
    bias_qkv[:, width : 2 * width] = jnp.zeros((1, width), jnp.float32)
    bias_qkv[:, 2 * width : 3 * width] = vector(BV)
    for g, (name, cut, _) in enumerate(groups):
        if name == "qkv":
            if g == 0:
                keep(0, tokens, x_own).wait()
                swap(0, tokens, x_own, True).wait_recv()
                send_out(x_own, x_out)
            else:
                need(g)
            project(cut[2], cut[3])
            clock.point()
    send_out(qkv, qkv_out)

    box_group = [g for g, group in enumerate(groups) if group[0] == "box"][-1]
    need(box_group)
    low = full["box"].at[0][...].reshape(width, 2 * FREQ)
    high = full["box"].at[1][...].reshape(width, 2 * FREQ)
    box_w[...] = jnp.concatenate(
        [low[:, :FREQ], high[:, :FREQ], low[:, FREQ:], high[:, FREQ:]], axis=1
    )
    page_length = jnp.where(first_block, lengths[0], lengths[1])
    valid = lax.broadcasted_iota(jnp.int32, (1, page_len), 1) < page_length
    head_lane = lax.broadcasted_iota(jnp.int32, (1, 128), 1)

    def p_copy(p, slot):
        return pltpu.make_async_copy(p_slots.at[slot], p_out.at[p], p_sem.at[slot])

    def pair(p, carry, serve):
        slot = lax.rem(p, 2)

        @pl.when(p >= 2)
        def _():
            p_copy(p - 2, slot).wait()

        q = qkv[:, lanes(p * 128, 128)]
        k = qkv[:, lanes(width + p * 128, 128)].T
        v = qkv[:, lanes(2 * width + p * 128, 128)]
        w = box_w[pl.ds(pl.multiple_of(p * 128, 128), 128), :]
        outs = []
        for i in range(2):
            if i:
                serve()
            of_head = (head_lane < HEAD) == (i == 0)
            q_head = jnp.where(of_head, q, jnp.zeros_like(q))
            u = jnp.dot(q_head, w, preferred_element_type=jnp.float32)
            on_sine, on_cosine = u[:, : 2 * FREQ], u[:, 2 * FREQ :]
            cosine, sine = table[0], table[1]
            b_cosine = (on_sine * sine + on_cosine * cosine).astype(jnp.bfloat16)
            b_sine = (on_cosine * sine - on_sine * cosine).astype(jnp.bfloat16)
            serve()
            b = jnp.concatenate([q_head, b_cosine, b_sine], axis=1)
            s = jnp.dot(b, jnp.concatenate([k, keys[...]], axis=0), preferred_element_type=jnp.float32)
            s = jnp.where(valid, s, MASKED)
            top = jnp.max(s, axis=1, keepdims=True)
            e = jnp.exp((s - top) * (HEAD**-0.5))
            probs = (e * (1.0 / jnp.sum(e, axis=1, keepdims=True))).astype(jnp.bfloat16)
            p_slots[slot, i] = probs
            outs.append(jnp.dot(probs, v, preferred_element_type=jnp.float32))
        mixed = jnp.where(head_lane < HEAD, outs[0], outs[1])
        o_own[:, lanes(p * 128, 128)] = mixed
        o_low[:, lanes(p * 128, 128)] = mixed.astype(jnp.bfloat16)
        p_copy(p, slot).start()
        return carry

    clock.loop(HEADS // 2, pair, 4)
    p_copy(4, 0).wait()
    p_copy(5, 1).wait()
    send_out(o_own, o_out)

    def last_of(name):
        return [g for g, group in enumerate(groups) if group[0] == name][-1]

    def weight_out(name):
        send_out(full[name], full_out[name])

    weight_out("qkv")
    weight_out("box")
    need(last_of("out"))
    weight_out("out")
    for h in range(2):
        w = full["out"].at[h][...].reshape(width, 384)
        cut = slice(h * 384, (h + 1) * 384)
        o_own_part = jnp.dot(o_low[...], w, preferred_element_type=jnp.float32)
        unit2[:, cut] = x_own[:, cut].astype(jnp.float32) + o_own_part + vec[:, BO + h * 384 : BO + (h + 1) * 384]

    def norm(hidden_sum):
        mean = jnp.mean(hidden_sum, axis=1, keepdims=True)
        centered = hidden_sum - mean
        inverse = lax.rsqrt(jnp.mean(centered * centered, axis=1, keepdims=True) + EPSILON)
        return centered * inverse, inverse

    unit, inverse = norm(unit2[...])
    unit1[...] = unit
    inv1[...] = jnp.broadcast_to(inverse, (page_len, 128))
    y1 = unit * vector(G1) + vector(E1)
    y1_low[...] = y1.astype(jnp.bfloat16)
    unit2[...] = y1 + vector(B2)
    send_out(unit1, unit1_out)
    send_out(inv1, inv1_out)

    def up_tile(first, h, t):
        start = pl.multiple_of(first + t * UP_TILE, 128)
        w = full["up"].at[h][:, :, :, :, pl.ds(start, UP_TILE)].reshape(width, UP_TILE)
        at = lanes(h * 1536 + start, UP_TILE)
        pre = jnp.dot(y1_low[...], w, preferred_element_type=jnp.float32)
        pre = pre + vec[:, lanes(B1 + h * 1536 + start, UP_TILE)]
        half = 0.5 + 0.5 * lax.erf(pre * (2.0**-0.5))
        hidden[:, at] = (pre * half).astype(jnp.bfloat16)
        bell = jnp.exp(pre * pre * -0.5) * ((2.0 * math.pi) ** -0.5)
        slope[:, at] = (half + pre * bell).astype(jnp.bfloat16)

    clock.point()
    for g, (name, cut, _) in enumerate(groups):
        if name == "up":
            need(g)
            tiles = cut[3] // UP_TILE

            def up_body(i, carry, first=cut[2], tiles=tiles):
                up_tile(first, lax.div(i, tiles), lax.rem(i, tiles))
                return carry

            lax.fori_loop(0, 2 * tiles, up_body, 0)
            clock.point()
    send_out(hidden, g_out)
    send_out(slope, d_out)
    weight_out("up")

    for g, (name, cut, _) in enumerate(groups):
        if name == "down":
            need(g)
            first, count = cut[2], cut[3]

            def down_body(h, carry, first=first, count=count):
                w = full["down"].at[h][:, :, :, :, first : first + count].reshape(4 * width, count)
                at = lanes(h * 384 + first, count)
                unit2[:, at] += jnp.dot(hidden[...], w, preferred_element_type=jnp.float32)
                return carry

            lax.fori_loop(0, 2, down_body, 0)
            clock.point()
    clock.upto(*(tuple(event) for _, *event in GATHER_EVENTS))
    weight_out("down")
    unit, inverse = norm(unit2[...])
    unit2[...] = unit
    inv2[...] = jnp.broadcast_to(inverse, (page_len, 128))
    send_out(unit2, unit2_out)
    send_out(inv2, inv2_out)

    gather.sends.left(gather.copy)
    for k in range(1, 4):
        vector_z(k).wait_send()
    vector_y().wait_send()
    vector_x().wait_send()
    vector_c().wait_send()
    box_swap.wait_send()
    swap(0, tokens, x_own).wait_send()
    swap(1, cotangent, ct_out).wait_send()
    swap(1, cotangent, ct_out, True).wait_recv()
    keep(1, cotangent, ct_out).wait()
    for copy in outgoing:
        copy.wait()


UP_TILE = 384


def forward_call(tokens, cotangent, boxes, lengths, vectors, shards):
    page_len = tokens.shape[1] * 2
    width = tokens.shape[2]
    groups = GATHER_GROUPS
    count = len(groups)
    full = [jax.ShapeDtypeStruct((2, 4, 2, 2) + s.shape, jnp.bfloat16) for s in shards]
    low, single = jnp.bfloat16, jnp.float32
    kinds = dict(
        x=((page_len, width), low),
        ct=((page_len, width), low),
        qkv=((page_len, 3 * width), low),
        table=((2, page_len, 2 * FREQ), single),
        p=((HEADS // 2, 2, page_len, page_len), low),
        o=((page_len, width), single),
        unit1=((page_len, width), single),
        inv1=((page_len, 128), single),
        g=((page_len, 4 * width), low),
        d=((page_len, 4 * width), low),
        unit2=((page_len, width), single),
        inv2=((page_len, 128), single),
        vec=((1, VECTORS + 128), single),
    )
    outs = full + [jax.ShapeDtypeStruct(*kinds[k]) for k in kinds]
    anywhere = pl.BlockSpec(memory_space=pl.ANY)
    vmem = pl.BlockSpec(memory_space=pltpu.VMEM)
    smem = pl.BlockSpec(memory_space=pltpu.SMEM)
    dma = pltpu.SemaphoreType.DMA
    scratch = [pltpu.VMEM(f.shape, f.dtype) for f in full]
    scratch += [
        pltpu.VMEM((page_len, width), low),
        pltpu.VMEM(boxes.shape, jnp.int32),
        pltpu.VMEM((2, 4, 2, 2, 1, 384), single),
        pltpu.VMEM((1, VECTORS + 128), single),
        pltpu.VMEM((page_len, 3 * width), low),
        pltpu.VMEM((2, page_len, 2 * FREQ), single),
        pltpu.VMEM((BOX_DIM, page_len), low),
        pltpu.VMEM((width, BOX_DIM), low),
        pltpu.VMEM((2, 2, page_len, page_len), low),
        pltpu.VMEM((page_len, width), single),
        pltpu.VMEM((page_len, width), low),
        pltpu.VMEM((page_len, width), single),
        pltpu.VMEM((page_len, 128), single),
        pltpu.VMEM((page_len, width), low),
        pltpu.VMEM((page_len, 4 * width), low),
        pltpu.VMEM((page_len, 4 * width), low),
        pltpu.VMEM((page_len, width), single),
        pltpu.VMEM((page_len, 128), single),
    ]
    arrivals = len(semaphore_table(groups, 3)) + len(core_table(groups))
    scratch += [dma((SENDS,)), dma((arrivals,))]
    scratch += [dma((count,))]
    scratch += [dma((3,))] * 2 + [dma((2,))] * 2 + [dma((1,))] * 2
    scratch += [dma((3,))] * 2 + [dma((3,)), dma((2,)), dma((18,))]
    scratch += [pltpu.VMEM((1, 3 * width), single), pltpu.VMEM((1, 384), single)]
    plan = (groups, page_len, width)
    results = pl.pallas_call(
        partial(forward_kernel, plan),
        out_shape=outs,
        in_specs=[anywhere, anywhere, vmem, smem, vmem] + [anywhere] * 5,
        out_specs=[anywhere] * len(outs),
        scratch_shapes=scratch,
        compiler_params=pltpu.CompilerParams(
            collective_id=0, has_side_effects=True, vmem_limit_bytes=VMEM_LIMIT
        ),
    )(tokens, cotangent, boxes, lengths, vectors, *shards)
    return dict(zip(WEIGHTS, results[:5])), dict(zip(kinds, results[5:]))


VMEM_LIMIT = 60 * 2**20


def landing_shape(path, hop, piece):
    sizes = dict(y=2, z=4, x=2)
    to_come = [sizes[axis] for axis in "yzx" if axis in path[hop + 1 :]]
    return (4 if path[hop] == "z" else 1, *to_come, piece[1], piece[3])


THIRDS = ((0, 1, 2), (1, 0, 2))


class Scatter:
    def __init__(self, place, groups, stored, c_land, landing, summed, sems, c_sems):
        self.place, self.groups, self.stored, self.summed = place, groups, stored, summed
        self.c_land, self.landing = c_land, landing
        self.sems, self.c_sems = sems, c_sems
        self.table = semaphore_table(groups, 4)
        self.sends = Sends(place, SCATTER_EVENTS, self.started)
        self.sent = set()

    def started(self, g, part, step):
        if g < 0 or step == 3:
            return []
        if step >= 10:
            return [((g, part, step - 10, 1), "inner")]
        out = []
        for other in range(len(self.groups[g][-1])) if step == 0 else (part,):
            if self.groups[g][-1][other][0][step] != "z":
                out.append(((g, other, step, 0), "all"))
                continue
            out.append(((g, other, step, 3), "end"))
            out.append(((g, other, step, "end"), "end"))
            out.append(((g, other, step, 0), "all"))
            out.append(((g, other, step, 2), "inner"))
        return out

    def c_copy(self, g):
        p = self.place
        store, both = self.groups[g][1], self.groups[g][2]
        ref = self.stored[store].at[(ALL, ALL, ALL, 1 - p.c) + window(both)]
        return remote(ref, self.c_land[g], self.c_sems, (g,), p.c_peer)

    def copy(self, g, part, hop, slot):
        p = self.place
        send = self.sends.index[g, part, hop, slot]
        slot = 1 if slot == "end" else slot
        path, piece = self.groups[g][-1][part]
        axis = path[hop]
        at = p.own()
        at.update({later: ALL for later in path[hop + 1 :]})
        if axis == "z":
            at["z"] = (p.near, p.far, p.mirror, p.mirror)[slot]
            peer = (p.near_peer, p.far_peer, p.mirror_peer, p.near_peer)[slot]
        else:
            at[axis] = 1 - at[axis]
            peer = p.x_peer if axis == "x" else p.y_peer
        ref = self.stored[self.groups[g][1]].at[(at["y"], at["z"], at["x"], p.c) + window(piece)]
        land = self.landing[g][part][hop].at[slot]
        at = self.table[g, part, hop, slot]
        return remote(ref, land, self.sems, (at,), peer, (send,))

    def add(self, g, part, hop, slots, place_z=None):
        p = self.place
        name, store, both, result, parts = self.groups[g]
        store = self.stored[store]
        path, piece = ("yzx", both) if hop < 0 else parts[part]
        cut = window(piece)
        sizes = dict(y=2, z=4, x=2)
        to_come = [axis for axis in "yzx" if axis in path[hop + 1 :]]
        count = math.prod(sizes[axis] for axis in to_come)
        land = self.c_land[g] if hop < 0 else self.landing[g][part][hop]

        def block(i):
            at = p.own()
            if place_z is not None:
                at["z"] = place_z
            inner = []
            for axis in to_come[::-1]:
                at[axis] = lax.rem(i, sizes[axis])
                i = lax.div(i, sizes[axis])
                inner.insert(0, at[axis])
            here = (at["y"], at["z"], at["x"], p.c) + cut
            value = store[here].astype(jnp.float32)
            for slot in slots:
                arrived = land[tuple(inner)] if hop < 0 else land[(slot, *inner)]
                value = value + arrived.astype(jnp.float32)
            return here, value

        if hop == 2 and place_z is None:
            _, value = block(0)
            top, height, first, size = piece
            if name == "qkv":
                third = jnp.where(p.y == 0, THIRDS[0][result], THIRDS[1][result])
                self.summed[name][:, lanes(first + 384 * third, size)] = value
                return
            top, first = top - both[0] + result[0], first - both[2] + result[2]
            self.summed[name][top : top + height, first : first + size] = value
            return

        together = min(count, 4)

        def body(i, carry):
            for k in range(together):
                here, value = block(i * together + k)
                store[here] = value.astype(jnp.bfloat16)
            return carry

        lax.fori_loop(0, count // together, body, 0)

    def begin(self, g):
        self.c_copy(g).start()

    def start(self, g, part, hop):
        p = self.place
        if self.groups[g][-1][part][0][hop] != "z":
            self.sends.start(self.copy, g, part, hop, 0)
            return

        @pl.when(p.end)
        def _():
            self.sends.start(self.copy, g, part, hop, 3)
            self.sends.start(self.copy, g, part, hop, "end")

        self.sends.start(self.copy, g, part, hop, 0)

        @pl.when(p.inner)
        def _():
            self.sends.start(self.copy, g, part, hop, 2)

    def relay(self, g, part, hop):
        p = self.place

        @pl.when(p.inner)
        def _():
            self.copy(g, part, hop, 3).wait_recv()
            self.add(g, part, hop, (3,), p.far)
            self.sends.start(self.copy, g, part, hop, 1)

    def finish(self, g, part, hop):
        p = self.place
        self.copy(g, part, hop, 0).wait_recv()
        if self.groups[g][-1][part][0][hop] != "z":
            self.add(g, part, hop, (0,))
            return
        self.copy(g, part, hop, 1).wait_recv()

        @pl.when(p.inner)
        def _():
            self.copy(g, part, hop, 2).wait_recv()
            self.add(g, part, hop, (0, 1, 2))

        @pl.when(p.end)
        def _():
            self.add(g, part, hop, (0, 1))

    def step(self, g, part, step):
        if step >= 10:
            self.relay(g, part, step - 10)
            return
        if step == 0:
            self.c_copy(g).wait_recv()
            self.add(g, 0, -1, (0,))
            for part in range(len(self.groups[g][-1])):
                self.start(g, part, 0)
            return
        self.finish(g, part, step - 1)
        if step < 3:
            self.start(g, part, step)

    def left(self, chosen, now=None):
        for g in chosen:
            if g not in self.sent:
                self.sent.add(g)
                self.c_copy(g).wait_send()
        self.sends.left(self.copy, now, lambda key: key[0] in chosen)


def backward_kernel(plan, *refs):
    groups, page_len, width = plan
    block = page_len // 2
    refs = iter(refs)
    take = lambda n: [next(refs) for _ in range(n)]
    w_in = dict(zip(WEIGHTS, take(5)))
    (x_in, ct_in, qkv_in, table_in, p_in, o_in, unit1_in, inv1_in) = take(8)
    (g_in, d_in, unit2_in, inv2_in, vec_in) = take(5)
    out_out, dx_out = take(2)
    grad_out = dict(zip(WEIGHTS, take(5)))
    (piece_out,) = take(1)
    stored = dict(zip(("box", "out", "up", "down"), take(4)))
    count = len(groups)
    c_land = take(count)
    landing = [[take(3) for _ in group[-1]] for group in groups]
    summed = dict(zip(WEIGHTS, take(5)))
    w_box, w_out, box_w, box_g = take(4)
    (ct, qkv, table, keys, o_own, unit1, inv1, hidden, slope, unit2, inv2, vec) = take(12)
    (y1_low, d_a, d_mixed, out_low, dx_low, vec_g) = take(6)
    pieces, pc_land, py_land, px_land, pz_land, piece_sum = take(6)
    w_sems, c_sems = take(2), take(2)
    v_sems, vz_sems, ex_sems = take(2), take(2), take(2)
    in_sem, p_sem, out_sem = take(3)

    place = Place()
    y, z, x, c = place.y, place.z, place.x, place.c
    scatter = Scatter(place, groups, stored, c_land, landing, summed, w_sems, c_sems)

    sources = dict(
        unit2=(unit2_in, unit2),
        ct=(ct_in, ct),
        inv2=(inv2_in, inv2),
        vec=(vec_in, vec),
        g=(g_in, hidden),
        d=(d_in, slope),
        unit1=(unit1_in, unit1),
        inv1=(inv1_in, inv1),
        w_out=(w_in["out"], w_out),
        w_box=(w_in["box"], w_box),
        o=(o_in, o_own),
        qkv=(qkv_in, qkv),
        table=(table_in, table),
        x=(x_in, y1_low),
    )
    order = list(sources)

    def fetch(name):
        source, target = sources[name]
        return pltpu.make_async_copy(source, target, in_sem.at[order.index(name)])

    def fetch_weight(name, target):
        at = len(order) + ("down", "up", "qkv").index(name)
        return pltpu.make_async_copy(w_in[name], target, in_sem.at[at])

    def vector(start, size=width):
        return vec[:, start : start + size]

    def total(value):
        return jnp.sum(value.astype(jnp.float32), axis=0, keepdims=True)

    def norm_back(grad, unit, inverse, gain):
        scaled = grad * gain
        mean_grad = jnp.mean(scaled, axis=1, keepdims=True)
        mean_unit = jnp.mean(scaled * unit, axis=1, keepdims=True)
        return inverse * (scaled - mean_grad - unit * mean_unit)

    names = [group[0] for group in groups]

    def event(g, part, step):
        if g < 0:
            out_swap.start()
        else:
            scatter.step(g, part, step)

    clock = Clock(SCATTER_EVENTS, event, set())

    def begin(g):
        clock.begun.add(g)
        scatter.begin(g)

    for name in ("unit2", "ct", "inv2", "vec", "g"):
        fetch(name).start()
    place.greet()

    fetch("unit2").wait()
    fetch("ct").wait()
    fetch("inv2").wait()
    fetch("vec").wait()
    unit = unit2[...]
    out_low[...] = (unit * vector(G2) + vector(E2)).astype(jnp.bfloat16)
    seed = ct[...].astype(jnp.float32)
    vec_g[:, G2 : G2 + width] = total(seed * unit)
    vec_g[:, E2 : E2 + width] = total(seed)
    d_h2 = norm_back(seed, unit, inv2[:, 0:1], vector(G2))
    unit2[...] = d_h2
    ct[...] = d_h2.astype(jnp.bfloat16)
    d_f = ct
    vec_g[:, B2 : B2 + width] = total(d_f[...])

    def rows(at):
        return pl.ds(pl.multiple_of(at * block, block), block)

    out_swap = remote(out_low.at[rows(1 - y)], out_out.at[y], ex_sems, (0,), place.y_peer)
    out_keep = pltpu.make_async_copy(out_low.at[rows(y)], out_out.at[y], out_sem.at[0])
    dx_swap = remote(dx_low.at[0], dx_low.at[1], ex_sems, (1,), place.y_peer)

    def with_down(w_down):
        fetch_weight("down", w_down).start()
        fetch("g").wait()

        for name in ("d", "unit1", "inv1", "w_out", "o", "w_box", "qkv", "table"):
            fetch(name).start()

        def down_grads(first, size):
            left = d_f[:, first : first + size]
            right = d_f[:, 384 + first : 384 + first + size]
            both = jnp.concatenate([left, right], axis=1)

            def grad_tile(t, carry):
                part = dot_n(hidden[:, lanes(t * width, width)], both).astype(jnp.bfloat16)
                for h in range(2):
                    stored["down"][h, t, :, :, :, first : first + size] = part[
                        :, h * size : (h + 1) * size
                    ].reshape(2, 2, -1, size)
                return carry

            lax.fori_loop(0, 4, grad_tile, 0)
            for g, group in enumerate(groups):
                if group[0] == "down" and first <= group[2][2] < first + size:
                    begin(g)
            clock.point()

        down_grads(0, 128)
        down_grads(128, 256)
        out_keep.start()
        fetch_weight("down", w_down).wait()
        fetch("d").wait()

        def slope_tile(t, carry, serve):
            w0 = w_down.at[0, t][...].reshape(width, 384)
            w1 = w_down.at[1, t][...].reshape(width, 384)
            d_hidden = dot_t(d_f[...], jnp.concatenate([w0, w1], axis=1))
            at = lanes(t * width, width)
            d_pre = (d_hidden * slope[:, at].astype(jnp.float32)).astype(jnp.bfloat16)
            slope[:, at] = d_pre
            vec_g[:, lanes(B1 + t * width, width)] = total(d_pre)
            return carry

        clock.loop(4, slope_tile)

    pl.run_scoped(with_down, pltpu.VMEM(w_in["down"].shape, jnp.bfloat16))

    fetch("unit1").wait()
    fetch("inv1").wait()
    y1_low[...] = (unit1[...] * vector(G1) + vector(E1)).astype(jnp.bfloat16)

    def with_up(w_up):
        fetch_weight("up", w_up).start()

        def up_tile(i, carry, serve, part):
            tile = dot_n(y1_low[...], slope[:, lanes(i * 1536 + part * width, width)])
            stored["up"][i, :, :, :, :, part * width : (part + 1) * width] = tile.astype(
                jnp.bfloat16
            ).reshape(4, 2, 2, -1, width)
            return carry

        for part in range(2):
            clock.loop(2, partial(up_tile, part=part))
            for g, group in enumerate(groups):
                if group[0] == "up" and group[2][2] // width == part:
                    begin(g)
        fetch_weight("up", w_up).wait()

        def back_tile(h, carry, serve):
            w = w_up.at[h][...].reshape(width, 1536)
            unit2[...] += dot_t(slope[:, lanes(h * 1536, 1536)], w)
            return carry

        clock.loop(2, back_tile)

    pl.run_scoped(with_up, pltpu.VMEM(w_in["up"].shape, jnp.bfloat16))

    x_own = y1_low
    fetch("x").start()
    unit = unit1[...]
    d_y1 = unit2[...]
    vec_g[:, G1 : G1 + width] = total(d_y1 * unit)
    vec_g[:, E1 : E1 + width] = total(d_y1)
    d_h1 = norm_back(d_y1, unit, inv1[:, 0:1], vector(G1))
    unit1[...] = d_h1
    d_a[...] = d_h1.astype(jnp.bfloat16)
    vec_g[:, BO : BO + width] = total(d_a[...])
    fetch("w_out").wait()
    fetch("o").wait()
    both = jnp.concatenate([w_out.at[h][...].reshape(width, 384) for h in range(2)], axis=1)
    d_mixed[...] = dot_t(d_a[...], both).astype(jnp.bfloat16)
    part = dot_n(o_own[...].astype(jnp.bfloat16), d_a[...]).astype(jnp.bfloat16)
    for h in range(2):
        stored["out"][h] = part[:, h * 384 : (h + 1) * 384].reshape(4, 2, 2, -1, 384)
    begin(names.index("out"))
    clock.point()

    for name in ("w_box", "qkv", "table", "x"):
        fetch(name).wait()
    low = w_box.at[0][...].reshape(width, 2 * FREQ)
    high = w_box.at[1][...].reshape(width, 2 * FREQ)
    box_w[...] = jnp.concatenate(
        [low[:, :FREQ], high[:, :FREQ], low[:, FREQ:], high[:, FREQ:]], axis=1
    ).T
    keys[:, : 2 * FREQ] = table[0].astype(jnp.bfloat16)
    keys[:, 2 * FREQ :] = table[1].astype(jnp.bfloat16)
    table[...] = table[...] * (HEAD**-0.5)
    head_lane = lax.broadcasted_iota(jnp.int32, (1, 128), 1)

    def p_copy(p, slot, i):
        at = lanes((slot * 2 + i) * page_len, page_len)
        return pltpu.make_async_copy(p_in.at[p, i], hidden.at[:, at], p_sem.at[slot, i])

    p_copy(0, 0, 0).start()
    p_copy(0, 0, 1).start()

    vector_c = remote(pieces.at[:, :, :, 1 - c], pc_land, v_sems, (0,), place.c_peer)
    vector_y = remote(pieces.at[1 - y, :, :, c], py_land, v_sems, (1,), place.y_peer)
    vector_x = remote(pieces.at[y, :, 1 - x, c], px_land, v_sems, (2,), place.x_peer)

    def vector_z(k):
        there = lax.rem(z + k + 1, 4)
        peer = (there * 4 + x * 2 + c, y)
        return remote(pieces.at[y, there, x, c], pz_land.at[k], vz_sems, (k,), peer)

    def with_qkv(w_qkv, early):
        stored["early"] = early
        fetch_weight("qkv", w_qkv).start()

        def pair(p, carry, serve):
            slot = lax.rem(p, 2)

            @pl.when(p < HEADS // 2 - 1)
            def _():
                p_copy(p + 1, 1 - slot, 0).start()
                p_copy(p + 1, 1 - slot, 1).start()

            p_copy(p, slot, 0).wait()
            p_copy(p, slot, 1).wait()
            q_t = qkv[:, lanes(p * 128, 128)].T
            k = qkv[:, lanes(width + p * 128, 128)]
            v_t = qkv[:, lanes(2 * width + p * 128, 128)].T
            w_t = box_w[:, lanes(p * 128, 128)]
            d_o = d_mixed[:, lanes(p * 128, 128)]
            d_o_t = d_o.T
            weighted = d_o.astype(jnp.float32) * o_own[:, lanes(p * 128, 128)]
            keys_k = jnp.concatenate([keys[...], k], axis=1)
            grads = []
            for i in range(2):
                if i:
                    serve()
                of_head = (head_lane < HEAD) == (i == 0)
                rows_head = slice(i * HEAD, (i + 1) * HEAD)
                probs = hidden[:, lanes((slot * 2 + i) * page_len, page_len)]
                delta = jnp.sum(jnp.where(of_head, weighted, 0.0), axis=1, keepdims=True)
                d_probs = jnp.dot(
                    jnp.where(of_head, d_o, jnp.zeros_like(d_o)),
                    v_t,
                    preferred_element_type=jnp.float32,
                )
                d_s = (probs.astype(jnp.float32) * (d_probs - delta)).astype(jnp.bfloat16)
                serve()
                d_b = jnp.dot(d_s, keys_k, preferred_element_type=jnp.float32)
                d_1, d_2 = d_b[:, : 2 * FREQ], d_b[:, 2 * FREQ : 4 * FREQ]
                cosine, sine = table[0], table[1]
                d_sine = (d_1 * sine - d_2 * cosine).astype(jnp.bfloat16)
                d_cosine = (d_1 * cosine + d_2 * sine).astype(jnp.bfloat16)
                d_u = jnp.concatenate([d_sine, d_cosine], axis=1)
                d_q = d_b[:, 4 * FREQ :] * (HEAD**-0.5) + jnp.dot(
                    d_u, w_t, preferred_element_type=jnp.float32
                )
                d_w = jnp.dot(q_t[rows_head], d_u, preferred_element_type=jnp.float32)
                box_g[pl.ds(pl.multiple_of(p * 128 + i * HEAD, HEAD), HEAD), :] = d_w.astype(
                    jnp.bfloat16
                )
                d_k = jnp.dot(q_t[rows_head], d_s, preferred_element_type=jnp.float32)
                d_v = jnp.dot(d_o_t[rows_head], probs, preferred_element_type=jnp.float32)
                grads.append((d_q, d_k * (HEAD**-0.5), d_v))
            (q_one, k_one, v_one), (q_two, k_two, v_two) = grads
            d_q = jnp.where(head_lane < HEAD, q_one, q_two).astype(jnp.bfloat16)
            d_k = jnp.concatenate([k_one, k_two], axis=0).astype(jnp.bfloat16).T
            d_v = jnp.concatenate([v_one, v_two], axis=0).astype(jnp.bfloat16).T
            for n, value in enumerate((d_q, d_k, d_v)):
                slope[:, lanes(n * width + p * 128, 128)] = value
            vec_g[:, lanes(BQ + p * 128, 128)] = total(d_q)
            vec_g[:, lanes(BV + p * 128, 128)] = total(d_v)
            return carry

        def qkv_grads(slot):
            store, top = ("early", 0) if slot == 0 else ("down", (slot - 1) * 48)
            for h in range(2):
                first = h * 1152 + THIRDS[h][slot] * 384
                tile = dot_n(x_own[...], slope[:, first : first + 384])
                stored[store][h, :, :, :, top : top + 48, :] = tile.astype(
                    jnp.bfloat16
                ).reshape(4, 2, 2, -1, 384)
            begin([g for g in range(count) if names[g] == "qkv"][slot])

        half = HEADS // 4
        clock.loop(half, pair, 4)
        qkv_grads(0)
        clock.point()
        clock.loop(half, lambda p, carry, serve: pair(p + half, carry, serve), 4)

        part = box_g[...]
        stored["box"][0] = jnp.concatenate(
            [part[:, :FREQ], part[:, 2 * FREQ : 3 * FREQ]], axis=1
        ).reshape(4, 2, 2, -1, 384)
        stored["box"][1] = jnp.concatenate(
            [part[:, FREQ : 2 * FREQ], part[:, 3 * FREQ :]], axis=1
        ).reshape(4, 2, 2, -1, 384)
        begin(names.index("box"))
        clock.point()
        clock.upto(*[
            (g, part, 3)
            for g, group in enumerate(groups)
            if names[g] == "down"
            for part in range(len(group[-1]))
        ])
        scatter.left([g for g in range(count) if names[g] == "down"], clock.at)

        for slot in (1, 2):
            qkv_grads(slot)
            clock.point()

        for dz in range(4):
            for dx in range(2):
                for dc in range(2):
                    for dy in range(2):
                        device = ((dz * 2 + dx) * 2 + dc) * 2 + dy
                        start = device * (VECTORS // 32) // 128 * 128
                        pieces[dy, dz, dx, dc] = vec_g[:, start : start + 384]
        vector_c.start()
        fetch_weight("qkv", w_qkv).wait()

        def back_tile(h, carry, serve):
            w = w_qkv.at[h][...].reshape(width, 1152)
            unit1[...] += dot_t(slope[:, lanes(h * 1152, 1152)], w)
            return carry

        clock.loop(2, back_tile)
        dx_low[0] = unit1[rows(1 - y), :].astype(jnp.bfloat16)
        dx_swap.start()
        pltpu.make_async_copy(unit1.at[rows(y)], dx_out.at[y], out_sem.at[1]).start()

        vector_c.wait_recv()
        pieces[:, :, :, c] += pc_land[...]
        vector_y.start()
        clock.point()
        vector_y.wait_recv()
        pieces[y, :, :, c] += py_land[...]
        vector_x.start()
        clock.point()
        vector_x.wait_recv()
        pieces[y, :, x, c] += px_land[...]
        for k in range(3):
            vector_z(k).start()
        clock.upto(*(tuple(event) for _, *event in SCATTER_EVENTS))
        dx_swap.wait_recv()
        unit2[0:block, :] = dx_low[1].astype(jnp.float32)
        pltpu.make_async_copy(unit2.at[0:block], dx_out.at[1 - y], out_sem.at[2]).start()
        for k in range(3):
            vector_z(k).wait_recv()
        piece_total = pieces[y, z, x, c]
        for k in range(3):
            piece_total = piece_total + pz_land[k]
        piece_sum[...] = piece_total
        finals = [pltpu.make_async_copy(piece_sum, piece_out, out_sem.at[3])]
        for i, name in enumerate(WEIGHTS):
            finals.append(pltpu.make_async_copy(summed[name], grad_out[name], out_sem.at[4 + i]))
        for copy in finals:
            copy.start()
        scatter.left(range(count))
        for copy in (vector_c, vector_y, vector_x, out_swap, dx_swap):
            copy.wait_send()
        for k in range(3):
            vector_z(k).wait_send()
        out_swap.wait_recv()
        out_keep.wait()
        pltpu.make_async_copy(unit1.at[rows(y)], dx_out.at[y], out_sem.at[1]).wait()
        pltpu.make_async_copy(unit2.at[0:block], dx_out.at[1 - y], out_sem.at[2]).wait()
        for copy in finals:
            copy.wait()

    pl.run_scoped(
        with_qkv,
        pltpu.VMEM(w_in["qkv"].shape, jnp.bfloat16),
        pltpu.VMEM(stored["box"].shape, jnp.bfloat16),
    )


def backward_call(full, kept, shards):
    low, single = jnp.bfloat16, jnp.float32
    page_len, width = kept["x"].shape
    groups = SCATTER_GROUPS
    count = len(groups)
    outs = [
        jax.ShapeDtypeStruct((2, page_len // 2, width), low),
        jax.ShapeDtypeStruct((2, page_len // 2, width), single),
    ]
    outs += [jax.ShapeDtypeStruct(s.shape, single) for s in shards]
    outs += [jax.ShapeDtypeStruct((1, 384), single)]
    by_name = dict(zip(WEIGHTS, shards))

    def vmem(*shape, kind=low):
        return pltpu.VMEM(shape, kind)

    size = lambda cut: (cut[1], cut[3])
    dma = pltpu.SemaphoreType.DMA
    scratch = [vmem(2, 4, 2, 2, *by_name[n].shape) for n in ("box", "out", "up", "down")]
    scratch += [vmem(2, 4, 2, *size(g[2])) for g in groups]
    for group in groups:
        for path, piece in group[-1]:
            scratch += [vmem(*landing_shape(path, hop, piece)) for hop in range(3)]
    scratch += [vmem(*s.shape, kind=single) for s in shards]
    scratch += [vmem(*full[n].shape) for n in ("box", "out")]
    scratch += [vmem(width, BOX_DIM), vmem(width, BOX_DIM)]
    scratch += [vmem(*kept[n].shape, kind=kept[n].dtype) for n in ("ct", "qkv", "table")]
    scratch += [vmem(page_len, BOX_DIM)]
    scratch += [
        vmem(*kept[n].shape, kind=kept[n].dtype)
        for n in ("o", "unit1", "inv1", "g", "d", "unit2", "inv2", "vec")
    ]
    scratch += [vmem(page_len, width)] * 4
    scratch += [vmem(2, page_len // 2, width), vmem(1, VECTORS + 128, kind=single)]
    scratch += [
        vmem(2, 4, 2, 2, 1, 384, kind=single),
        vmem(2, 4, 2, 1, 384, kind=single),
        vmem(4, 2, 1, 384, kind=single),
        vmem(4, 1, 384, kind=single),
        vmem(3, 1, 384, kind=single),
        vmem(1, 384, kind=single),
    ]
    scratch += [dma((SENDS,)), dma((len(semaphore_table(groups, 4)),))] + [dma((count,))] * 2
    scratch += [dma((3,))] * 2 + [dma((3,))] * 2 + [dma((2,))] * 2
    scratch += [dma((17,)), dma((2, 2)), dma((9,))]
    anywhere = pl.BlockSpec(memory_space=pl.ANY)
    operands = [full[n] for n in WEIGHTS] + list(kept.values())
    plan = (groups, page_len, width)
    results = pl.pallas_call(
        partial(backward_kernel, plan),
        out_shape=outs,
        in_specs=[anywhere] * len(operands),
        out_specs=[anywhere] * len(outs),
        scratch_shapes=scratch,
        compiler_params=pltpu.CompilerParams(
            collective_id=1, has_side_effects=True, vmem_limit_bytes=VMEM_BACK
        ),
    )(*operands)
    return results


VMEM_BACK = 63 * 2**20


def finish_kernel(*refs):
    count = len(refs) // 2
    ins, outs = refs[:count], refs[count:]
    for i in range(count - 1):
        outs[i][...] = ins[i][...]
    rows = jnp.broadcast_to(ins[-1][...], (8, 384))
    rows = pltpu.roll(rows, 384 - Place().vector_offset(), 1)
    outs[-1][...] = rows[0:1, : VECTORS // 32].reshape(VECTORS // 32)


def finish_call(results):
    vmem = pl.BlockSpec(memory_space=pltpu.VMEM)
    outs = [jax.ShapeDtypeStruct(r.shape, r.dtype) for r in results[:-1]]
    outs += [jax.ShapeDtypeStruct((VECTORS // 32,), jnp.float32)]
    return pl.pallas_call(
        finish_kernel,
        out_shape=outs,
        in_specs=[vmem] * len(outs),
        out_specs=[vmem] * len(outs),
        compiler_params=pltpu.CompilerParams(vmem_limit_bytes=VMEM_BACK),
    )(*results)


def fast_layer(tokens, boxes, lengths, wqkv, wbox, wout, wup, wdown, vectors, cotangent):
    shards = (wqkv, wbox, wout, wup, wdown)
    full, kept = forward_call(tokens, cotangent, boxes, lengths, vectors, shards)
    return tuple(finish_call(backward_call(full, kept, shards)))


def on_device(*args):
    tokens, wqkv, wbox, wdown = args[0], args[3], args[4], args[7]
    blocks, groups = lax.axis_size("blk"), lax.axis_size("dp")
    fits = (
        blocks == 2
        and groups == 16
        and tokens.shape[0] == 2
        and wqkv.shape == (48, 1152)
        and wdown.shape == (192, 384)
        and wbox.shape == (48, 2 * FREQ)
    )
    return fast_layer(*args) if fits else general_layer(*args)


def solution(mesh):
    in_specs = (
        P("dp", "blk", None),
        P(None, "dp", "blk"),
        P("dp"),
        P("dp", "blk"),
        P("dp", "blk"),
        P("dp", "blk"),
        P("dp", "blk"),
        P("dp", "blk"),
        P(("dp", "blk")),
        P("dp", "blk", None),
    )
    out_specs = (
        P("dp", "blk", None),
        P("dp", "blk", None),
        P("dp", "blk"),
        P("dp", "blk"),
        P("dp", "blk"),
        P("dp", "blk"),
        P("dp", "blk"),
        P(("dp", "blk")),
    )
    return jax.shard_map(
        on_device, mesh=mesh, in_specs=in_specs, out_specs=out_specs, check_vma=False
    )
```

```python
from functools import partial
import math

import jax
import jax.numpy as jnp
import numpy as np
from jax import lax
from jax.experimental import pallas as pl
from jax.experimental.pallas import tpu as pltpu
from jax.sharding import PartitionSpec as P

HEADS = 12
HEAD = 64
FREQ = 192
BOX_DIM = 768

EPSILON = 1e-12
MASKED = -1e30


def box_table(boxes):
    frequency = jnp.exp(jnp.arange(FREQ, dtype=jnp.float32) * (-math.log(10000.0) / FREQ))
    across = boxes[0].astype(jnp.float32)[..., None] * frequency
    upward = boxes[1].astype(jnp.float32)[..., None] * frequency
    return jnp.concatenate(
        [jnp.cos(across), jnp.sin(across), jnp.cos(upward), jnp.sin(upward)], axis=-1
    )


def rotate(coeffs, own_table):
    cos_across, sin_across, cos_upward, sin_upward = jnp.split(own_table[..., None, :], 4, axis=-1)
    sa, ca, sb, cb = jnp.split(coeffs, 4, axis=-1)
    return jnp.concatenate(
        [
            sa * sin_across + ca * cos_across,
            ca * sin_across - sa * cos_across,
            sb * sin_upward + cb * cos_upward,
            cb * sin_upward - sb * cos_upward,
        ],
        axis=-1,
    )


def unrotate(grad_rows, own_table):
    cos_across, sin_across, cos_upward, sin_upward = jnp.split(own_table[..., None, :], 4, axis=-1)
    d1a, d2a, d1b, d2b = jnp.split(grad_rows, 4, axis=-1)
    return jnp.concatenate(
        [
            d1a * sin_across - d2a * cos_across,
            d1a * cos_across + d2a * sin_across,
            d1b * sin_upward - d2b * cos_upward,
            d1b * cos_upward + d2b * sin_upward,
        ],
        axis=-1,
    )


def normalize(hidden):
    row_mean = jnp.mean(hidden, axis=-1, keepdims=True)
    centered = hidden - row_mean
    inverse = lax.rsqrt(jnp.mean(centered * centered, axis=-1, keepdims=True) + EPSILON)
    return centered * inverse, inverse


def normalize_back(grad, unit, inverse, gain):
    scaled = grad * gain
    mean_grad = jnp.mean(scaled, axis=-1, keepdims=True)
    mean_unit = jnp.mean(scaled * unit, axis=-1, keepdims=True)
    d_hidden = inverse * (scaled - mean_grad - unit * mean_unit)
    return d_hidden, jnp.sum(grad * unit, axis=0), jnp.sum(grad, axis=0)


def unpack(vector_all, model_width, hidden_units):
    cuts = [model_width] * 5 + [hidden_units] + [model_width] * 3
    pieces = []
    offset = 0
    for length_here in cuts:
        pieces.append(vector_all[offset : offset + length_here])
        offset = offset + length_here
    return pieces


def dot32(a, b):
    return jnp.dot(a, b, preferred_element_type=jnp.float32)


def gather_weight(shard):
    part = lax.all_gather(shard, "blk", axis=1, tiled=True)
    return lax.all_gather(part, "dp", axis=0, tiled=True)


def scatter_weight(grad):
    part = lax.psum_scatter(grad.astype(jnp.bfloat16), "dp", scatter_dimension=0, tiled=True)
    return lax.psum_scatter(part, "blk", scatter_dimension=1, tiled=True).astype(jnp.float32)


def general_layer(tokens, boxes, lengths, wqkv, wbox, wout, wup, wdown, vectors, cotangent):
    blocks = lax.axis_size("blk")
    pages_here = tokens.shape[0] // blocks
    model_width = tokens.shape[2]
    to_pages = partial(
        lax.all_to_all, axis_name="blk", split_axis=0, concat_axis=1, tiled=True
    )
    from_pages = partial(
        lax.all_to_all, axis_name="blk", split_axis=1, concat_axis=0, tiled=True
    )
    page_tokens = to_pages(tokens)
    page_boxes = lax.all_to_all(boxes, "blk", split_axis=1, concat_axis=2, tiled=True)
    page_lengths = lax.dynamic_slice(lengths, (lax.axis_index("blk") * pages_here,), (pages_here,))
    full_qkv = gather_weight(wqkv)
    full_box = gather_weight(wbox)
    full_out = gather_weight(wout)
    full_up = gather_weight(wup)
    full_down = gather_weight(wdown)
    full_vec = lax.all_gather(vectors, ("dp", "blk"), axis=0, tiled=True).astype(jnp.float32)
    page_cotangent = to_pages(cotangent)
    hidden_units = full_up.shape[1]
    bq, bv, bo, g1, e1, b1, b2, g2, e2 = unpack(full_vec, model_width, hidden_units)
    page_len = page_tokens.shape[1]
    score_scale = HEAD ** (-0.5)

    x = page_tokens.reshape(-1, model_width)
    projected = dot32(x, full_qkv)
    head_shape = (pages_here, page_len, HEADS, HEAD)
    q = (projected[:, :model_width] + bq).astype(jnp.bfloat16).reshape(head_shape)
    k = projected[:, model_width : 2 * model_width].astype(jnp.bfloat16).reshape(head_shape)
    v = (projected[:, 2 * model_width :] + bv).astype(jnp.bfloat16).reshape(head_shape)
    table = box_table(page_boxes)
    box_heads = full_box.reshape(HEADS, HEAD, BOX_DIM)
    coeffs = jnp.einsum("pqhd,hdc->pqhc", q, box_heads, preferred_element_type=jnp.float32)
    box_query = rotate(coeffs, table).astype(jnp.bfloat16)
    box_keys = table.astype(jnp.bfloat16)
    scores = (
        jnp.einsum("pqhd,pkhd->phqk", q, k, preferred_element_type=jnp.float32)
        + jnp.einsum("pqhc,pkc->phqk", box_query, box_keys, preferred_element_type=jnp.float32)
    ) * score_scale
    is_valid = (jnp.arange(page_len)[None, :] < page_lengths[:, None])[:, None, None, :]
    masked = jnp.where(is_valid, scores, MASKED)
    probs = jax.nn.softmax(masked, axis=-1)
    probs_low = probs.astype(jnp.bfloat16)
    mixed = jnp.einsum("phqk,pkhd->pqhd", probs_low, v, preferred_element_type=jnp.float32)
    mixed_low = mixed.astype(jnp.bfloat16).reshape(-1, model_width)
    unit1, inv1 = normalize(x.astype(jnp.float32) + dot32(mixed_low, full_out) + bo)
    y1 = unit1 * g1 + e1
    y1_low = y1.astype(jnp.bfloat16)
    pre = dot32(y1_low, full_up) + b1
    hidden = jax.nn.gelu(pre, approximate=False).astype(jnp.bfloat16)
    unit2, inv2 = normalize(y1 + dot32(hidden, full_down) + b2)
    output = (unit2 * g2 + e2).astype(jnp.bfloat16)

    seed = page_cotangent.reshape(-1, model_width).astype(jnp.float32)
    d_h2, d_g2, d_e2 = normalize_back(seed, unit2, inv2, g2)
    d_f = d_h2.astype(jnp.bfloat16)
    d_hidden = dot32(d_f, full_down.T)
    d_pre = jax.vjp(partial(jax.nn.gelu, approximate=False), pre)[1](d_hidden)[0]
    d_pre = d_pre.astype(jnp.bfloat16)
    d_wdown = dot32(hidden.T, d_f)
    d_wup = dot32(y1_low.T, d_pre)
    d_y1 = dot32(d_pre, full_up.T) + d_h2
    d_h1, d_g1, d_e1 = normalize_back(d_y1, unit1, inv1, g1)
    d_a = d_h1.astype(jnp.bfloat16)
    d_wout = dot32(mixed_low.T, d_a)
    d_mixed = dot32(d_a, full_out.T).astype(jnp.bfloat16).reshape(head_shape)
    row_delta = jnp.einsum("pqhd,pqhd->phq", d_mixed.astype(jnp.float32), mixed)
    d_probs = jnp.einsum("pqhd,pkhd->phqk", d_mixed, v, preferred_element_type=jnp.float32)
    d_raw = (probs * (d_probs - row_delta[..., None])).astype(jnp.bfloat16)
    d_q = jnp.einsum("phqk,pkhd->pqhd", d_raw, k, preferred_element_type=jnp.float32)
    d_box_q = jnp.einsum("phqk,pkc->pqhc", d_raw, box_keys, preferred_element_type=jnp.float32)
    d_k = jnp.einsum("phqk,pqhd->pkhd", d_raw, q, preferred_element_type=jnp.float32)
    d_v = jnp.einsum("phqk,pqhd->pkhd", probs_low, d_mixed, preferred_element_type=jnp.float32)
    d_coeffs = unrotate(d_box_q * score_scale, table).astype(jnp.bfloat16)
    d_q = d_q * score_scale + jnp.einsum(
        "pqhc,hdc->pqhd", d_coeffs, box_heads, preferred_element_type=jnp.float32
    )
    d_wbox = jnp.einsum("pqhd,pqhc->hdc", q, d_coeffs, preferred_element_type=jnp.float32)
    flat = (-1, model_width)
    d_q = d_q.astype(jnp.bfloat16).reshape(flat)
    d_k = (d_k * score_scale).astype(jnp.bfloat16).reshape(flat)
    d_v = d_v.astype(jnp.bfloat16).reshape(flat)
    d_c = jnp.concatenate([d_q, d_k, d_v], axis=1)
    d_wqkv = dot32(x.T, d_c)
    d_x = dot32(d_c, full_qkv.T) + d_h1
    total = partial(jnp.sum, axis=0, dtype=jnp.float32)
    vector_grad = jnp.concatenate(
        [total(d_q), total(d_v), total(d_a), d_g1, d_e1, total(d_pre), total(d_f), d_g2, d_e2]
    )
    return (
        from_pages(output.reshape(page_tokens.shape)),
        from_pages(d_x.reshape(page_tokens.shape)),
        scatter_weight(d_wqkv),
        scatter_weight(d_wbox.reshape(model_width, BOX_DIM)),
        scatter_weight(d_wout),
        scatter_weight(d_wup),
        scatter_weight(d_wdown),
        lax.psum_scatter(vector_grad, ("dp", "blk"), scatter_dimension=0, tiled=True),
    )


GATHER_GROUPS = (
    ("qkv", (0, 48, 0, 384), (("zxy", (0, 48, 0, 384)),)),
    ("qkv", (0, 48, 384, 384), (("yzx", (0, 48, 384, 256)), ("yzx", (0, 48, 640, 128)),)),
    ("qkv", (0, 48, 768, 384), (("zxy", (0, 48, 768, 384)),)),
    ("box", (0, 48, 0, 384), (("zxy", (0, 48, 0, 256)), ("yzx", (0, 48, 256, 128)),)),
    ("out", (0, 48, 0, 384), (("yxz", (0, 48, 0, 128)), ("xzy", (0, 48, 128, 256)),)),
    ("up", (0, 48, 0, 384), (("yxz", (0, 48, 0, 256)), ("zyx", (0, 48, 256, 128)),)),
    ("up", (0, 48, 384, 384), (("zyx", (0, 48, 384, 384)),)),
    ("up", (0, 48, 768, 384), (("yxz", (0, 48, 768, 384)),)),
    ("up", (0, 48, 1152, 384), (("zyx", (0, 48, 1152, 256)), ("zyx", (0, 48, 1408, 128)),)),
    ("down", (0, 192, 0, 128), (("zxy", (0, 64, 0, 128)), ("yxz", (64, 128, 0, 128)),)),
    ("down", (0, 192, 128, 128), (("zyx", (0, 64, 128, 128)), ("xzy", (64, 128, 128, 128)),)),
    ("down", (0, 192, 256, 128), (("zxy", (0, 192, 256, 128)),)),
)
GATHER_EVENTS = (
    (1, 0, 0, 0),
    (1, 1, 1, 0),
    (1, 2, 0, 0),
    (1, 3, 0, 0),
    (1, 0, 0, 10),
    (1, 0, 0, 1),
    (1, 6, 0, 0),
    (1, 3, 1, 0),
    (1, 5, 0, 0),
    (1, 8, 1, 0),
    (1, 2, 0, 10),
    (1, 4, 0, 0),
    (1, 1, 0, 0),
    (2, 9, 0, 0),
    (2, 3, 0, 10),
    (2, 7, 0, 0),
    (2, 2, 0, 1),
    (2, 9, 1, 0),
    (2, 1, 1, 1),
    (2, 8, 0, 0),
    (2, 0, 0, 2),
    (3, 1, 0, 1),
    (3, 3, 0, 1),
    (4, 7, 0, 1),
    (4, 1, 1, 11),
    (4, 3, 1, 1),
    (4, 4, 0, 1),
    (4, 2, 0, 2),
    (4, 9, 0, 10),
    (5, 5, 1, 0),
    (5, 10, 1, 0),
    (6, 4, 1, 0),
    (7, 1, 1, 2),
    (7, 6, 0, 10),
    (7, 1, 0, 11),
    (8, 3, 0, 2),
    (8, 9, 0, 1),
    (8, 3, 1, 11),
    (8, 11, 0, 0),
    (8, 10, 1, 1),
    (9, 8, 0, 10),
    (9, 8, 1, 10),
    (9, 1, 0, 2),
    (9, 6, 0, 1),
    (10, 0, 0, 3),
    (10, 1, 1, 3),
    (10, 0, 0, 4),
    (11, 5, 1, 10),
    (12, 10, 0, 0),
    (12, 3, 1, 2),
    (12, 2, 0, 3),
    (12, 9, 1, 1),
    (13, 5, 0, 1),
    (13, 11, 0, 10),
    (13, 10, 1, 11),
    (13, 4, 1, 1),
    (13, 8, 0, 1),
    (14, 1, 0, 3),
    (14, 4, 0, 2),
    (15, 5, 1, 1),
    (16, 8, 1, 1),
    (18, 1, 1, 4),
    (18, 2, 0, 4),
    (18, 9, 0, 2),
    (18, 1, 0, 4),
    (18, 11, 0, 1),
    (20, 3, 1, 3),
    (20, 10, 1, 2),
    (21, 3, 0, 3),
    (21, 4, 1, 11),
    (21, 5, 0, 2),
    (21, 7, 0, 2),
    (22, 10, 0, 10),
    (22, 3, 1, 4),
    (22, 9, 1, 2),
    (22, 6, 0, 2),
    (23, 3, 0, 4),
    (23, 8, 0, 2),
    (26, 4, 0, 12),
    (27, 5, 1, 2),
    (27, 10, 0, 1),
    (28, 4, 1, 2),
    (31, 11, 0, 2),
    (32, 10, 0, 2),
    (32, 5, 0, 12),
    (33, 7, 0, 12),
    (33, 4, 0, 3),
    (34, 6, 0, 3),
    (35, 9, 0, 3),
    (36, 8, 1, 2),
    (37, 4, 1, 3),
    (39, 10, 1, 3),
    (42, 8, 0, 3),
    (44, 6, 0, 4),
    (46, 5, 1, 3),
    (46, 9, 0, 4),
    (49, 4, 0, 4),
    (54, 10, 0, 3),
    (55, 5, 0, 3),
    (56, 4, 1, 4),
    (56, 7, 0, 3),
    (57, 10, 1, 4),
    (61, 5, 1, 4),
    (62, 8, 1, 3),
    (63, 10, 0, 4),
    (64, 9, 1, 12),
    (79, -1, 0, 0),
    (80, 5, 0, 4),
    (81, 11, 0, 3),
    (93, 7, 0, 4),
    (93, 8, 1, 4),
    (95, 9, 1, 3),
    (102, 8, 0, 4),
    (124, 9, 1, 4),
    (131, 11, 0, 4),
)
SCATTER_GROUPS = (
    ("down", "down", (0, 192, 0, 128), (0, 192, 0, 128), (("zxy", (0, 64, 0, 128)), ("xzy", (64, 128, 0, 128)),)),
    ("down", "down", (0, 192, 128, 128), (0, 192, 128, 128), (("zxy", (0, 64, 128, 128)), ("yxz", (64, 128, 128, 128)),)),
    ("down", "down", (0, 192, 256, 128), (0, 192, 256, 128), (("yzx", (0, 192, 256, 128)),)),
    ("up", "up", (0, 48, 0, 384), (0, 48, 0, 384), (("xyz", (0, 48, 0, 128)), ("yxz", (0, 48, 128, 256)),)),
    ("up", "up", (0, 48, 384, 384), (0, 48, 384, 384), (("xyz", (0, 48, 384, 384)),)),
    ("up", "up", (0, 48, 768, 384), (0, 48, 768, 384), (("xyz", (0, 48, 768, 384)),)),
    ("up", "up", (0, 48, 1152, 384), (0, 48, 1152, 384), (("xyz", (0, 48, 1152, 384)),)),
    ("out", "out", (0, 48, 0, 384), (0, 48, 0, 384), (("zyx", (0, 48, 0, 256)), ("yxz", (0, 48, 256, 128)),)),
    ("qkv", "early", (0, 48, 0, 384), 0, (("zxy", (0, 48, 0, 384)),)),
    ("box", "box", (0, 48, 0, 384), (0, 48, 0, 384), (("yxz", (0, 48, 0, 128)), ("xyz", (0, 48, 128, 256)),)),
    ("qkv", "down", (0, 48, 0, 384), 1, (("yxz", (0, 48, 0, 128)), ("yxz", (0, 48, 128, 256)),)),
    ("qkv", "down", (48, 48, 0, 384), 2, (("yxz", (48, 48, 0, 128)), ("xzy", (48, 48, 128, 256)),)),
)
SCATTER_EVENTS = (
    (4, 0, 0, 0),
    (6, 1, 0, 0),
    (12, 0, 0, 10),
    (12, 2, 0, 0),
    (15, 0, 1, 1),
    (15, 5, 0, 0),
    (16, 1, 0, 10),
    (17, 0, 1, 11),
    (17, 4, 0, 0),
    (18, 3, 0, 0),
    (19, 7, 0, 0),
    (19, -1, 0, 0),
    (22, 1, 0, 1),
    (24, 0, 0, 1),
    (24, 2, 0, 1),
    (24, 7, 0, 10),
    (25, 1, 1, 1),
    (27, 4, 0, 1),
    (31, 6, 0, 0),
    (32, 3, 1, 1),
    (32, 2, 0, 11),
    (34, 1, 1, 2),
    (35, 8, 0, 0),
    (35, 1, 0, 2),
    (36, 5, 0, 1),
    (38, 0, 1, 2),
    (39, 1, 1, 12),
    (41, 0, 0, 2),
    (41, 6, 0, 1),
    (41, 2, 0, 2),
    (45, 4, 0, 2),
    (45, 0, 1, 3),
    (46, 1, 1, 3),
    (46, 8, 0, 10),
    (46, 3, 0, 1),
    (47, 7, 0, 1),
    (47, 9, 0, 0),
    (47, 1, 0, 3),
    (47, 0, 0, 3),
    (47, 2, 0, 3),
    (48, 3, 1, 2),
    (48, -2, 0, 0),
    (48, 7, 1, 1),
    (48, 10, 0, 0),
    (49, 4, 0, 12),
    (49, 6, 0, 2),
    (49, 11, 0, 0),
    (50, 9, 1, 1),
    (51, 3, 0, 2),
    (62, 5, 0, 2),
    (64, 9, 0, 1),
    (67, -2, 0, 1),
    (68, 7, 0, 2),
    (71, 3, 0, 12),
    (78, 7, 1, 2),
    (89, 11, 1, 1),
    (98, 10, 1, 1),
    (100, 4, 0, 3),
    (117, -2, 0, 2),
    (128, 3, 0, 3),
    (183, 8, 0, 1),
    (521, 6, 0, 12),
    (525, 3, 1, 12),
    (544, 11, 1, 11),
    (563, 5, 0, 12),
    (615, 7, 1, 12),
    (874, 10, 0, 1),
    (912, 9, 0, 2),
    (918, 9, 1, 2),
    (959, 11, 0, 1),
    (959, 10, 0, 2),
    (975, 9, 1, 12),
    (978, 11, 0, 2),
    (979, 10, 1, 2),
    (979, 8, 0, 2),
    (999, 10, 0, 12),
    (1000, 11, 1, 2),
    (1002, 9, 0, 12),
    (1010, 3, 1, 3),
    (1020, 11, 0, 12),
    (1021, 9, 1, 3),
    (1032, 10, 0, 3),
    (1049, 10, 1, 12),
    (1059, 5, 0, 3),
    (1066, 11, 0, 3),
    (1068, 8, 0, 3),
    (1070, 7, 0, 3),
    (1073, 6, 0, 3),
    (1084, 9, 0, 3),
    (1095, 10, 1, 3),
    (1123, 11, 1, 3),
    (1148, 7, 1, 3),
)


MESH = pl.DeviceIdType.MESH
WEIGHTS = ("qkv", "box", "out", "up", "down")
ROT = 4
ALL = slice(None)


def window(piece):
    return (pl.ds(piece[0], piece[1]), pl.ds(piece[2], piece[3]))


class Place:
    def __init__(self):
        dp = lax.axis_index("dp")
        self.y = lax.axis_index("blk")
        self.z = lax.div(dp, 4)
        self.x = lax.rem(lax.div(dp, 2), 2)
        self.c = lax.rem(dp, 2)
        x, y, z, c = self.x, self.y, self.z, self.c
        self.near = z + 1 - 2 * lax.rem(z, 2)
        self.far = lax.rem(z + 2, 4)
        self.mirror = 3 - z
        self.inner = jnp.logical_or(z == 1, z == 2)
        self.end = jnp.logical_or(z == 0, z == 3)
        at = lambda other: (other * 4 + x * 2 + c, y)
        self.near_peer, self.far_peer, self.mirror_peer = at(self.near), at(self.far), at(self.mirror)
        self.x_peer = (dp + 2 - 4 * x, y)
        self.y_peer = (dp, 1 - y)
        self.c_peer = (dp + 1 - 2 * c, y)

    def own(self):
        return dict(y=self.y, z=self.z, x=self.x)

    def vector_offset(self):
        device = ((self.z * 2 + self.x) * 2 + self.c) * 2 + self.y
        return lax.rem(device * (VECTORS // 32), 128)

    def greet(self):
        barrier = pltpu.get_barrier_semaphore()
        peers = [self.near_peer, self.far_peer, self.mirror_peer]
        peers += [self.x_peer, self.y_peer, self.c_peer]
        for peer in peers:
            pl.semaphore_signal(barrier, inc=1, device_id=peer, device_id_type=MESH)
        pl.semaphore_wait(barrier, len(peers))


def semaphore_table(groups, slots):
    table = {}
    for g, group in enumerate(groups):
        for part, (path, _) in enumerate(group[-1]):
            for hop, axis in enumerate(path):
                for slot in range(slots if axis == "z" else 1):
                    table[g, part, hop, slot] = len(table)
    return table


SEND_RINGS = dict(all=(0, 24), inner=(24, 12), end=(36, 12))
SENDS = 48


class Sends:
    def __init__(self, place, events, started):
        self.place = place
        self.index, self.before, self.kind, self.after = {}, {}, {}, {}
        turns = {kind: [] for kind in SEND_RINGS}
        for at, (_, *event) in enumerate(events):
            for key, kind in started(*event):
                base, size = SEND_RINGS[kind]
                turn = turns[kind]
                self.index[key], self.kind[key] = base + len(turn) % size, kind
                if len(turn) >= size:
                    self.before[key] = turn[-size]
                    self.after[turn[-size]] = at
                turn.append(key)
        self.done = set()

    def when(self, key, act):
        kind = self.kind[key]
        if kind == "all":
            act()
        else:
            pl.when(self.place.inner if kind == "inner" else self.place.end)(act)

    def start(self, copy, *key):
        before = self.before.get(key)
        if before is not None and before not in self.done:
            copy(*before).wait_send()
        copy(*key).start()

    def left(self, copy, now=None, chosen=lambda key: True):
        for key in self.index:
            at = self.after.get(key)
            if key in self.done or not chosen(key) or (at is not None and (now is None or at < now)):
                continue
            self.done.add(key)
            self.when(key, copy(*key).wait_send)


def remote(src, dst, sems, at, peer, send=None):
    return pltpu.make_async_remote_copy(
        src,
        dst,
        sems[0].at[at if send is None else send],
        sems[1].at[at],
        device_id=peer,
        device_id_type=MESH,
    )


def core_table(groups):
    keys = [(g, part) for g, group in enumerate(groups) for part in range(len(group[-1]))]
    return {key: n for n, key in enumerate(keys)}


class Gather:
    def __init__(self, place, groups, shards, full, sems, own_sem):
        self.place, self.groups, self.shards, self.full = place, groups, shards, full
        self.sems, self.own_sem = sems, own_sem
        self.count = len(groups)
        self.table = semaphore_table(groups, 3)
        self.c_table = core_table(groups)
        self.sends = Sends(place, GATHER_EVENTS, self.started)
        self.owned = False

    def started(self, g, part, step):
        if g < 0 or step == 4:
            return []
        if step == 3:
            return [((g, part, 3, 0), "all")]
        if step >= 10:
            return [((g, part, step - 10, 3), "inner")]
        if self.groups[g][2][part][0][step] != "z":
            return [((g, part, step, 0), "all")]
        return [
            ((g, part, step, 1), "all"),
            ((g, part, step, 0), "all"),
            ((g, part, step, 2), "inner"),
        ]

    def copy(self, g, part, hop, slot, arriving=False):
        p = self.place
        name, _, parts = self.groups[g]
        path, piece = parts[part]
        cut = window(piece)
        send = self.sends.index[g, part, hop, slot]
        if hop == 3:
            c = 1 - p.c if arriving else p.c
            ref = self.full[name].at[(ALL, ALL, ALL, c) + cut]
            at = len(self.table) + self.c_table[g, part]
            return remote(ref, ref, self.sems, (at,), p.c_peer, (send,))
        axis = path[hop]
        at = p.own()
        at.update({earlier: ALL for earlier in path[:hop]})
        if axis == "z":
            peer = (p.near_peer, p.far_peer, p.mirror_peer, p.near_peer)[slot]
            if slot == 3:
                at["z"] = p.mirror if arriving else p.far
            elif arriving:
                at["z"] = (p.near, p.far, p.mirror)[slot]
        else:
            peer = p.x_peer if axis == "x" else p.y_peer
            if arriving:
                at[axis] = 1 - at[axis]
        ref = self.full[name].at[(at["y"], at["z"], at["x"], p.c) + cut]
        source = self.shards[name].at[cut] if hop == 0 and slot < 3 else ref
        at = self.table[g, part, hop, min(slot, 2)]
        return remote(source, ref, self.sems, (at,), peer, (send,))

    def own_copy(self, g):
        p = self.place
        name, both, _ = self.groups[g]
        cut = window(both)
        return pltpu.make_async_copy(
            self.shards[name].at[cut],
            self.full[name].at[(p.y, p.z, p.x, p.c) + cut],
            self.own_sem.at[g],
        )

    def relay(self, g, part, hop):
        @pl.when(self.place.inner)
        def _():
            self.copy(g, part, hop, 1, True).wait_recv()
            self.sends.start(self.copy, g, part, hop, 3)

    def start(self, g, part, hop):
        if self.groups[g][2][part][0][hop] != "z":
            self.sends.start(self.copy, g, part, hop, 0)
            return
        self.sends.start(self.copy, g, part, hop, 1)
        self.sends.start(self.copy, g, part, hop, 0)

        @pl.when(self.place.inner)
        def _():
            self.sends.start(self.copy, g, part, hop, 2)

    def finish(self, g, part, hop):
        self.copy(g, part, hop, 0, True).wait_recv()
        if self.groups[g][2][part][0][hop] != "z":
            return

        @pl.when(self.place.inner)
        def _():
            self.copy(g, part, hop, 2, True).wait_recv()

        @pl.when(self.place.end)
        def _():
            self.copy(g, part, hop, 1, True).wait_recv()
            self.copy(g, part, hop, 3, True).wait_recv()

    def own(self):
        for g in range(self.count):
            self.own_copy(g).start()

    def step(self, g, part, step):
        if step >= 10:
            self.relay(g, part, step - 10)
            return
        if step >= 1 and not self.owned:
            self.owned = True
            for other in range(self.count):
                self.own_copy(other).wait()
        if 1 <= step <= 3:
            self.finish(g, part, step - 1)
        if step <= 2:
            self.start(g, part, step)
        if step == 3:
            self.sends.start(self.copy, g, part, 3, 0)
        if step == 4:
            self.copy(g, part, 3, 0, True).wait_recv()


class Clock:
    def __init__(self, events, run, begun=None):
        self.events, self.run, self.now, self.at, self.begun = events, run, 0, 0, begun

    def may(self, event):
        return self.begun is None or event[1] < 0 or event[1] in self.begun

    def take(self):
        self.now += 1
        first = self.at
        while self.at < len(self.events):
            event = self.events[self.at]
            if event[0] > self.now or not self.may(event):
                break
            self.at += 1
        return self.events[first : self.at]

    def point(self):
        for _, *event in self.take():
            self.run(*event)

    def upto(self, *wanted):
        self.now += 1
        last = max(i for i, (_, *event) in enumerate(self.events) if tuple(event) in wanted)
        while self.at <= last:
            assert self.may(self.events[self.at])
            _, *event = self.events[self.at]
            self.at += 1
            self.run(*event)

    def loop(self, count, body, points=1):
        due = [[self.take() for _ in range(points)] for _ in range(count)]

        def wrapped(i, carry):
            point = iter(range(points))

            def serve():
                k = next(point)
                for n in range(count):
                    if due[n][k]:

                        @pl.when(i == n)
                        def _():
                            for _, *event in due[n][k]:
                                self.run(*event)

            serve()
            return body(i, carry, serve)

        lax.fori_loop(0, count, wrapped, 0)
        self.point()


def sine_cosine(angle):
    turns = jnp.floor(angle * (2.0 / math.pi) + 0.5)
    rest = angle - turns * 1.5703125
    rest = rest - turns * 4.837512969970703125e-4
    rest = rest - turns * 7.54978995489188216e-8
    square = rest * rest
    sine = rest + rest * square * (
        -1.6666654611e-1 + square * (8.3321608736e-3 + square * -1.9515295891e-4)
    )
    cosine = (
        1.0
        - 0.5 * square
        + square
        * square
        * (
            4.166664568298827e-2
            + square * (-1.388731625493765e-3 + square * 2.443315711809948e-5)
        )
    )
    quarter = turns.astype(jnp.int32)
    odd = (quarter & 1) == 1
    sine_sign = jnp.where((quarter & 2) == 2, -1.0, 1.0)
    cosine_sign = jnp.where(((quarter + 1) & 2) == 2, -1.0, 1.0)
    return (
        sine_sign * jnp.where(odd, cosine, sine),
        cosine_sign * jnp.where(odd, sine, cosine),
    )


def dot_t(a, b):
    return lax.dot_general(a, b, (((1,), (1,)), ((), ())), preferred_element_type=jnp.float32)


def dot_n(a, b):
    return lax.dot_general(a, b, (((0,), (0,)), ((), ())), preferred_element_type=jnp.float32)


def lanes(start, size):
    return pl.ds(pl.multiple_of(start, 128), size)


BQ, BV, BO, G1, E1, B1, B2, G2, E2 = 0, 768, 1536, 2304, 3072, 3840, 6912, 7680, 8448
VECTORS = 9216


def forward_kernel(plan, *refs):
    groups, page_len, width = plan
    block = page_len // 2
    refs = iter(refs)
    take = lambda n: [next(refs) for _ in range(n)]
    tokens, cotangent, boxes, lengths, vectors = take(5)
    shards = dict(zip(WEIGHTS, take(5)))
    full_out = dict(zip(WEIGHTS, take(5)))
    (x_out, ct_out, qkv_out, table_out, p_out, o_out, unit1_out, inv1_out) = take(8)
    (g_out, d_out, unit2_out, inv2_out, vec_out) = take(5)
    full = dict(zip(WEIGHTS, take(5)))
    (x_own, boxes_peer, pieces, vec, qkv, table, keys, box_w, p_slots, o_own, o_low) = take(11)
    (unit1, inv1, y1_low, hidden, slope, unit2, inv2) = take(7)
    w_sems = take(2)
    (own_sem,) = take(1)
    vz_sems, vxy_sems, vc_sems = take(2), take(2), take(2)
    ex_sems = take(2)
    (local_sem, p_sem, out_sem) = take(3)
    bias_qkv, piece = take(2)

    place = Place()
    y, z, x, c = place.y, place.z, place.x, place.c
    gather = Gather(place, groups, shards, full, w_sems, own_sem)

    def swap(i, source, target, arriving=False):
        at = (1 - y) if arriving else y
        return remote(
            source.at[1 - y], target.at[pl.ds(pl.multiple_of(at * block, block), block)],
            ex_sems, (i,), place.y_peer,
        )

    def keep(i, source, target):
        return pltpu.make_async_copy(
            source.at[y], target.at[pl.ds(pl.multiple_of(y * block, block), block)],
            local_sem.at[i],
        )

    box_swap = remote(boxes, boxes_peer, ex_sems, (2,), place.y_peer)

    def vector_y(arriving=False):
        at = 1 - y if arriving else y
        return remote(piece, pieces.at[at, z, x, c], vxy_sems, (0,), place.y_peer)

    def vector_x(arriving=False):
        ref = pieces.at[:, z, 1 - x if arriving else x, c]
        return remote(ref, ref, vxy_sems, (1,), place.x_peer)

    def vector_z(k, arriving=False):
        ref = pieces.at[:, lax.rem(z + 4 - k, 4) if arriving else z, :, c]
        peer = (lax.rem(z + k, 4) * 4 + x * 2 + c, y)
        return remote(ref, ref, vz_sems, (k - 1,), peer)

    def vector_c(arriving=False):
        ref = pieces.at[:, :, :, 1 - c if arriving else c]
        return remote(ref, ref, vc_sems, (0,), place.c_peer)

    vector_own = pltpu.make_async_copy(piece, pieces.at[y, z, x, c], local_sem.at[2])

    def event(g, part, step):
        if g < 0:
            swap(1, cotangent, ct_out).start()
        else:
            gather.step(g, part, step)

    clock = Clock(GATHER_EVENTS, event)

    def need(g):
        clock.upto(*((g, part, 4) for part in range(len(groups[g][2]))))

    outgoing = []

    def send_out(ref, out):
        copy = pltpu.make_async_copy(ref, out, out_sem.at[len(outgoing)])
        copy.start()
        outgoing.append(copy)

    own_vector = vectors[...].astype(jnp.float32).reshape(1, -1)
    own_vector = jnp.concatenate(
        [own_vector, jnp.zeros((1, 384 - own_vector.shape[1]), jnp.float32)], axis=1
    )
    own_vector = jnp.broadcast_to(own_vector, (8, 384))
    piece[...] = pltpu.roll(own_vector, place.vector_offset(), 1)[0:1, :]
    place.greet()
    gather.own()
    box_swap.start()
    vector_y().start()
    vector_own.start()
    swap(0, tokens, x_own).start()
    clock.point()
    keep(0, tokens, x_own).start()
    keep(1, cotangent, ct_out).start()

    box_swap.wait_recv()
    mine, other = boxes[...], boxes_peer[...]
    first_block = y == 0
    mine = jnp.where(first_block, mine[:, 0, :], mine[:, 1, :])
    other = jnp.where(first_block, other[:, 0, :], other[:, 1, :])
    both = jnp.concatenate(
        [jnp.where(first_block, mine, other), jnp.where(first_block, other, mine)], axis=1
    ).astype(jnp.float32)
    both = jnp.concatenate([both, jnp.zeros((6, page_len), jnp.float32)], axis=0)
    across_up = both.T
    lane = lax.broadcasted_iota(jnp.int32, (1, 2 * FREQ), 1)
    step = jnp.where(lane < FREQ, lane, lane - FREQ).astype(jnp.float32)
    frequency = jnp.exp(step * (-math.log(10000.0) / FREQ))
    angle = jnp.where(lane < FREQ, across_up[:, 0:1], across_up[:, 1:2]) * frequency
    sine, cosine = sine_cosine(angle)
    table[0], table[1] = cosine, sine
    keys[0 : 2 * FREQ, :] = cosine.astype(jnp.bfloat16).T
    keys[2 * FREQ :, :] = sine.astype(jnp.bfloat16).T
    send_out(table, table_out)
    clock.point()
    vector_own.wait()
    vector_y(True).wait_recv()
    vector_x().start()
    clock.point()
    vector_x(True).wait_recv()
    for k in range(1, 4):
        vector_z(k).start()
    clock.point()
    clock.upto(*((0, part, 3) for part in range(len(groups[0][2]))))
    for k in range(1, 4):
        vector_z(k, True).wait_recv()
    vector_c().start()
    need(0)
    vector_c(True).wait_recv()
    vec[...] = jnp.zeros_like(vec)
    for dz in range(4):
        for dx in range(2):
            for dc in range(2):
                for dy in range(2):
                    device = ((dz * 2 + dx) * 2 + dc) * 2 + dy
                    start = device * (VECTORS // 32) // 128 * 128
                    vec[:, start : start + 384] += pieces[dy, dz, dx, dc]
    send_out(vec, vec_out)

    def vector(start, size=width):
        return vec[:, start : start + size]

    def project(first, count):
        def project_tile(h, carry):
            w = full["qkv"].at[h][:, :, :, :, first : first + count].reshape(width, count)
            out = jnp.dot(x_own[...], w, preferred_element_type=jnp.float32)
            start = pl.multiple_of(h * 1152 + first, 128)
            column = start + lax.broadcasted_iota(jnp.int32, (1, count), 1)
            bias = bias_qkv[:, lanes(start, count)]
            qkv[:, lanes(start, count)] = (out + bias).astype(jnp.bfloat16)
            return carry

        lax.fori_loop(0, 2, project_tile, 0)

    bias_qkv[:, 0:width] = vector(BQ)
    bias_qkv[:, width : 2 * width] = jnp.zeros((1, width), jnp.float32)
    bias_qkv[:, 2 * width : 3 * width] = vector(BV)
    for g, (name, cut, _) in enumerate(groups):
        if name == "qkv":
            if g == 0:
                keep(0, tokens, x_own).wait()
                swap(0, tokens, x_own, True).wait_recv()
                send_out(x_own, x_out)
            else:
                need(g)
            project(cut[2], cut[3])
            clock.point()
    send_out(qkv, qkv_out)

    box_group = [g for g, group in enumerate(groups) if group[0] == "box"][-1]
    need(box_group)
    low = full["box"].at[0][...].reshape(width, 2 * FREQ)
    high = full["box"].at[1][...].reshape(width, 2 * FREQ)
    box_w[...] = jnp.concatenate(
        [low[:, :FREQ], high[:, :FREQ], low[:, FREQ:], high[:, FREQ:]], axis=1
    )
    page_length = jnp.where(first_block, lengths[0], lengths[1])
    valid = lax.broadcasted_iota(jnp.int32, (1, page_len), 1) < page_length
    head_lane = lax.broadcasted_iota(jnp.int32, (1, 128), 1)

    def p_copy(p, slot):
        return pltpu.make_async_copy(p_slots.at[slot], p_out.at[p], p_sem.at[slot])

    def pair(p, carry, serve):
        slot = lax.rem(p, 2)

        @pl.when(p >= 2)
        def _():
            p_copy(p - 2, slot).wait()

        q = qkv[:, lanes(p * 128, 128)]
        k = qkv[:, lanes(width + p * 128, 128)].T
        v = qkv[:, lanes(2 * width + p * 128, 128)]
        w = box_w[pl.ds(pl.multiple_of(p * 128, 128), 128), :]
        outs = []
        for i in range(2):
            if i:
                serve()
            of_head = (head_lane < HEAD) == (i == 0)
            q_head = jnp.where(of_head, q, jnp.zeros_like(q))
            u = jnp.dot(q_head, w, preferred_element_type=jnp.float32)
            on_sine, on_cosine = u[:, : 2 * FREQ], u[:, 2 * FREQ :]
            cosine, sine = table[0], table[1]
            b_cosine = (on_sine * sine + on_cosine * cosine).astype(jnp.bfloat16)
            b_sine = (on_cosine * sine - on_sine * cosine).astype(jnp.bfloat16)
            serve()
            b = jnp.concatenate([q_head, b_cosine, b_sine], axis=1)
            s = jnp.dot(b, jnp.concatenate([k, keys[...]], axis=0), preferred_element_type=jnp.float32)
            s = jnp.where(valid, s, MASKED)
            top = jnp.max(s, axis=1, keepdims=True)
            e = jnp.exp((s - top) * (HEAD**-0.5))
            probs = (e * (1.0 / jnp.sum(e, axis=1, keepdims=True))).astype(jnp.bfloat16)
            p_slots[slot, i] = probs
            outs.append(jnp.dot(probs, v, preferred_element_type=jnp.float32))
        mixed = jnp.where(head_lane < HEAD, outs[0], outs[1])
        o_own[:, lanes(p * 128, 128)] = mixed
        o_low[:, lanes(p * 128, 128)] = mixed.astype(jnp.bfloat16)
        p_copy(p, slot).start()
        return carry

    clock.loop(HEADS // 2, pair, 4)
    p_copy(4, 0).wait()
    p_copy(5, 1).wait()
    send_out(o_own, o_out)

    def last_of(name):
        return [g for g, group in enumerate(groups) if group[0] == name][-1]

    def weight_out(name):
        send_out(full[name], full_out[name])

    weight_out("qkv")
    weight_out("box")
    need(last_of("out"))
    weight_out("out")
    for h in range(2):
        w = full["out"].at[h][...].reshape(width, 384)
        cut = slice(h * 384, (h + 1) * 384)
        o_own_part = jnp.dot(o_low[...], w, preferred_element_type=jnp.float32)
        unit2[:, cut] = x_own[:, cut].astype(jnp.float32) + o_own_part + vec[:, BO + h * 384 : BO + (h + 1) * 384]

    def norm(hidden_sum):
        mean = jnp.mean(hidden_sum, axis=1, keepdims=True)
        centered = hidden_sum - mean
        inverse = lax.rsqrt(jnp.mean(centered * centered, axis=1, keepdims=True) + EPSILON)
        return centered * inverse, inverse

    unit, inverse = norm(unit2[...])
    unit1[...] = unit
    inv1[...] = jnp.broadcast_to(inverse, (page_len, 128))
    y1 = unit * vector(G1) + vector(E1)
    y1_low[...] = y1.astype(jnp.bfloat16)
    unit2[...] = y1 + vector(B2)
    send_out(unit1, unit1_out)
    send_out(inv1, inv1_out)

    def up_tile(first, h, t):
        start = pl.multiple_of(first + t * UP_TILE, 128)
        w = full["up"].at[h][:, :, :, :, pl.ds(start, UP_TILE)].reshape(width, UP_TILE)
        at = lanes(h * 1536 + start, UP_TILE)
        pre = jnp.dot(y1_low[...], w, preferred_element_type=jnp.float32)
        pre = pre + vec[:, lanes(B1 + h * 1536 + start, UP_TILE)]
        half = 0.5 + 0.5 * lax.erf(pre * (2.0**-0.5))
        hidden[:, at] = (pre * half).astype(jnp.bfloat16)
        bell = jnp.exp(pre * pre * -0.5) * ((2.0 * math.pi) ** -0.5)
        slope[:, at] = (half + pre * bell).astype(jnp.bfloat16)

    clock.point()
    for g, (name, cut, _) in enumerate(groups):
        if name == "up":
            need(g)
            tiles = cut[3] // UP_TILE

            def up_body(i, carry, first=cut[2], tiles=tiles):
                up_tile(first, lax.div(i, tiles), lax.rem(i, tiles))
                return carry

            lax.fori_loop(0, 2 * tiles, up_body, 0)
            clock.point()
    send_out(hidden, g_out)
    send_out(slope, d_out)
    weight_out("up")

    for g, (name, cut, _) in enumerate(groups):
        if name == "down":
            need(g)
            first, count = cut[2], cut[3]
            columns = (ALL,) * 4 + window(cut)
            send_out(full["down"].at[columns], full_out["down"].at[columns])

            def down_body(h, carry, first=first, count=count):
                w = full["down"].at[h][:, :, :, :, first : first + count].reshape(4 * width, count)
                at = lanes(h * 384 + first, count)
                unit2[:, at] += jnp.dot(hidden[...], w, preferred_element_type=jnp.float32)
                return carry

            lax.fori_loop(0, 2, down_body, 0)
            clock.point()
    clock.upto(*(tuple(event) for _, *event in GATHER_EVENTS))
    unit, inverse = norm(unit2[...])
    unit2[...] = unit
    inv2[...] = jnp.broadcast_to(inverse, (page_len, 128))
    send_out(unit2, unit2_out)
    send_out(inv2, inv2_out)

    gather.sends.left(gather.copy)
    for k in range(1, 4):
        vector_z(k).wait_send()
    vector_y().wait_send()
    vector_x().wait_send()
    vector_c().wait_send()
    box_swap.wait_send()
    swap(0, tokens, x_own).wait_send()
    swap(1, cotangent, ct_out).wait_send()
    swap(1, cotangent, ct_out, True).wait_recv()
    keep(1, cotangent, ct_out).wait()
    for copy in outgoing:
        copy.wait()


UP_TILE = 384


def forward_call(tokens, cotangent, boxes, lengths, vectors, shards):
    page_len = tokens.shape[1] * 2
    width = tokens.shape[2]
    groups = GATHER_GROUPS
    count = len(groups)
    full = [jax.ShapeDtypeStruct((2, 4, 2, 2) + s.shape, jnp.bfloat16) for s in shards]
    low, single = jnp.bfloat16, jnp.float32
    kinds = dict(
        x=((page_len, width), low),
        ct=((page_len, width), low),
        qkv=((page_len, 3 * width), low),
        table=((2, page_len, 2 * FREQ), single),
        p=((HEADS // 2, 2, page_len, page_len), low),
        o=((page_len, width), single),
        unit1=((page_len, width), single),
        inv1=((page_len, 128), single),
        g=((page_len, 4 * width), low),
        d=((page_len, 4 * width), low),
        unit2=((page_len, width), single),
        inv2=((page_len, 128), single),
        vec=((1, VECTORS + 128), single),
    )
    outs = full + [jax.ShapeDtypeStruct(*kinds[k]) for k in kinds]
    anywhere = pl.BlockSpec(memory_space=pl.ANY)
    vmem = pl.BlockSpec(memory_space=pltpu.VMEM)
    smem = pl.BlockSpec(memory_space=pltpu.SMEM)
    dma = pltpu.SemaphoreType.DMA
    scratch = [pltpu.VMEM(f.shape, f.dtype) for f in full]
    scratch += [
        pltpu.VMEM((page_len, width), low),
        pltpu.VMEM(boxes.shape, jnp.int32),
        pltpu.VMEM((2, 4, 2, 2, 1, 384), single),
        pltpu.VMEM((1, VECTORS + 128), single),
        pltpu.VMEM((page_len, 3 * width), low),
        pltpu.VMEM((2, page_len, 2 * FREQ), single),
        pltpu.VMEM((BOX_DIM, page_len), low),
        pltpu.VMEM((width, BOX_DIM), low),
        pltpu.VMEM((2, 2, page_len, page_len), low),
        pltpu.VMEM((page_len, width), single),
        pltpu.VMEM((page_len, width), low),
        pltpu.VMEM((page_len, width), single),
        pltpu.VMEM((page_len, 128), single),
        pltpu.VMEM((page_len, width), low),
        pltpu.VMEM((page_len, 4 * width), low),
        pltpu.VMEM((page_len, 4 * width), low),
        pltpu.VMEM((page_len, width), single),
        pltpu.VMEM((page_len, 128), single),
    ]
    arrivals = len(semaphore_table(groups, 3)) + len(core_table(groups))
    scratch += [dma((SENDS,)), dma((arrivals,))]
    scratch += [dma((count,))]
    scratch += [dma((3,))] * 2 + [dma((2,))] * 2 + [dma((1,))] * 2
    scratch += [dma((3,))] * 2 + [dma((3,)), dma((2,)), dma((20,))]
    scratch += [pltpu.VMEM((1, 3 * width), single), pltpu.VMEM((1, 384), single)]
    plan = (groups, page_len, width)
    results = pl.pallas_call(
        partial(forward_kernel, plan),
        out_shape=outs,
        in_specs=[anywhere, anywhere, vmem, smem, vmem] + [anywhere] * 5,
        out_specs=[anywhere] * len(outs),
        scratch_shapes=scratch,
        compiler_params=pltpu.CompilerParams(
            collective_id=0, has_side_effects=True, vmem_limit_bytes=VMEM_LIMIT
        ),
    )(tokens, cotangent, boxes, lengths, vectors, *shards)
    return dict(zip(WEIGHTS, results[:5])), dict(zip(kinds, results[5:]))


VMEM_LIMIT = 60 * 2**20


def landing_shape(path, hop, piece):
    sizes = dict(y=2, z=4, x=2)
    to_come = [sizes[axis] for axis in "yzx" if axis in path[hop + 1 :]]
    return (4 if path[hop] == "z" else 1, *to_come, piece[1], piece[3])


THIRDS = ((0, 1, 2), (1, 0, 2))


class Scatter:
    def __init__(self, place, groups, stored, c_land, landing, summed, sems, c_sems):
        self.place, self.groups, self.stored, self.summed = place, groups, stored, summed
        self.c_land, self.landing = c_land, landing
        self.sems, self.c_sems = sems, c_sems
        self.table = semaphore_table(groups, 4)
        self.sends = Sends(place, SCATTER_EVENTS, self.started)
        self.sent = set()

    def started(self, g, part, step):
        if g < 0 or step == 3:
            return []
        if step >= 10:
            return [((g, part, step - 10, 1), "inner")]
        out = []
        for other in range(len(self.groups[g][-1])) if step == 0 else (part,):
            if self.groups[g][-1][other][0][step] != "z":
                out.append(((g, other, step, 0), "all"))
                continue
            out.append(((g, other, step, 3), "end"))
            out.append(((g, other, step, "end"), "end"))
            out.append(((g, other, step, 0), "all"))
            out.append(((g, other, step, 2), "inner"))
        return out

    def c_copy(self, g):
        p = self.place
        store, both = self.groups[g][1], self.groups[g][2]
        ref = self.stored[store].at[(ALL, ALL, ALL, 1 - p.c) + window(both)]
        return remote(ref, self.c_land[g], self.c_sems, (g,), p.c_peer)

    def copy(self, g, part, hop, slot):
        p = self.place
        send = self.sends.index[g, part, hop, slot]
        slot = 1 if slot == "end" else slot
        path, piece = self.groups[g][-1][part]
        axis = path[hop]
        at = p.own()
        at.update({later: ALL for later in path[hop + 1 :]})
        if axis == "z":
            at["z"] = (p.near, p.far, p.mirror, p.mirror)[slot]
            peer = (p.near_peer, p.far_peer, p.mirror_peer, p.near_peer)[slot]
        else:
            at[axis] = 1 - at[axis]
            peer = p.x_peer if axis == "x" else p.y_peer
        ref = self.stored[self.groups[g][1]].at[(at["y"], at["z"], at["x"], p.c) + window(piece)]
        land = self.landing[g][part][hop].at[slot]
        at = self.table[g, part, hop, slot]
        return remote(ref, land, self.sems, (at,), peer, (send,))

    def add(self, g, part, hop, slots, place_z=None):
        p = self.place
        name, store, both, result, parts = self.groups[g]
        store = self.stored[store]
        path, piece = ("yzx", both) if hop < 0 else parts[part]
        cut = window(piece)
        sizes = dict(y=2, z=4, x=2)
        to_come = [axis for axis in "yzx" if axis in path[hop + 1 :]]
        count = math.prod(sizes[axis] for axis in to_come)
        land = self.c_land[g] if hop < 0 else self.landing[g][part][hop]

        def block(i):
            at = p.own()
            if place_z is not None:
                at["z"] = place_z
            inner = []
            for axis in to_come[::-1]:
                at[axis] = lax.rem(i, sizes[axis])
                i = lax.div(i, sizes[axis])
                inner.insert(0, at[axis])
            here = (at["y"], at["z"], at["x"], p.c) + cut
            arrived = [land[tuple(inner)] if hop < 0 else land[(slot, *inner)] for slot in slots]
            if len(arrived) == 1 and not (hop == 2 and place_z is None):
                return here, store[here] + arrived[0]
            value = store[here].astype(jnp.float32)
            for other in arrived:
                value = value + other.astype(jnp.float32)
            return here, value

        if hop == 2 and place_z is None:
            _, value = block(0)
            top, height, first, size = piece
            if name == "qkv":
                third = jnp.where(p.y == 0, THIRDS[0][result], THIRDS[1][result])
                self.summed[name][:, lanes(first + 384 * third, size)] = value
                return
            top, first = top - both[0] + result[0], first - both[2] + result[2]
            self.summed[name][top : top + height, first : first + size] = value
            return

        together = min(count, 4)

        def body(i, carry):
            for k in range(together):
                here, value = block(i * together + k)
                store[here] = value.astype(jnp.bfloat16)
            return carry

        lax.fori_loop(0, count // together, body, 0)

    def begin(self, g):
        self.c_copy(g).start()

    def start(self, g, part, hop):
        p = self.place
        if self.groups[g][-1][part][0][hop] != "z":
            self.sends.start(self.copy, g, part, hop, 0)
            return

        @pl.when(p.end)
        def _():
            self.sends.start(self.copy, g, part, hop, 3)
            self.sends.start(self.copy, g, part, hop, "end")

        self.sends.start(self.copy, g, part, hop, 0)

        @pl.when(p.inner)
        def _():
            self.sends.start(self.copy, g, part, hop, 2)

    def relay(self, g, part, hop):
        p = self.place

        @pl.when(p.inner)
        def _():
            self.copy(g, part, hop, 3).wait_recv()
            self.add(g, part, hop, (3,), p.far)
            self.sends.start(self.copy, g, part, hop, 1)

    def finish(self, g, part, hop):
        p = self.place
        self.copy(g, part, hop, 0).wait_recv()
        if self.groups[g][-1][part][0][hop] != "z":
            self.add(g, part, hop, (0,))
            return
        self.copy(g, part, hop, 1).wait_recv()

        @pl.when(p.inner)
        def _():
            self.copy(g, part, hop, 2).wait_recv()
            self.add(g, part, hop, (0, 1, 2))

        @pl.when(p.end)
        def _():
            self.add(g, part, hop, (0, 1))

    def step(self, g, part, step):
        if step >= 10:
            self.relay(g, part, step - 10)
            return
        if step == 0:
            self.c_copy(g).wait_recv()
            self.add(g, 0, -1, (0,))
            for part in range(len(self.groups[g][-1])):
                self.start(g, part, 0)
            return
        self.finish(g, part, step - 1)
        if step < 3:
            self.start(g, part, step)

    def left(self, chosen, now=None):
        for g in chosen:
            if g not in self.sent:
                self.sent.add(g)
                self.c_copy(g).wait_send()
        self.sends.left(self.copy, now, lambda key: key[0] in chosen)


def backward_kernel(plan, *refs):
    groups, page_len, width = plan
    block = page_len // 2
    refs = iter(refs)
    take = lambda n: [next(refs) for _ in range(n)]
    w_in = dict(zip(WEIGHTS, take(5)))
    (x_in, ct_in, qkv_in, table_in, p_in, o_in, unit1_in, inv1_in) = take(8)
    (g_in, d_in, unit2_in, inv2_in, vec_in) = take(5)
    out_out, dx_out = take(2)
    grad_out = dict(zip(WEIGHTS, take(5)))
    (piece_out,) = take(1)
    stored = dict(zip(("box", "out", "up", "down"), take(4)))
    count = len(groups)
    c_land = take(count)
    landing = [[take(3) for _ in group[-1]] for group in groups]
    summed = dict(zip(WEIGHTS, take(5)))
    w_box, w_out, box_w, box_g = take(4)
    (ct, qkv, table, keys, o_own, unit1, inv1, hidden, slope, unit2, inv2, vec) = take(12)
    (y1_low, d_a, d_mixed, out_low, dx_low, vec_g) = take(6)
    pieces, pc_land, py_land, px_land, pz_land, piece_sum = take(6)
    w_sems, c_sems = take(2), take(2)
    v_sems, vz_sems, ex_sems = take(2), take(2), take(2)
    in_sem, p_sem, out_sem = take(3)

    place = Place()
    y, z, x, c = place.y, place.z, place.x, place.c
    scatter = Scatter(place, groups, stored, c_land, landing, summed, w_sems, c_sems)

    sources = dict(
        unit2=(unit2_in, unit2),
        ct=(ct_in, ct),
        inv2=(inv2_in, inv2),
        vec=(vec_in, vec),
        g=(g_in, hidden),
        d=(d_in, slope),
        unit1=(unit1_in, unit1),
        inv1=(inv1_in, inv1),
        w_out=(w_in["out"], w_out),
        w_box=(w_in["box"], w_box),
        o=(o_in, o_own),
        qkv=(qkv_in, qkv),
        table=(table_in, table),
        x=(x_in, y1_low),
    )
    order = list(sources)

    def fetch(name):
        source, target = sources[name]
        return pltpu.make_async_copy(source, target, in_sem.at[order.index(name)])

    def fetch_weight(name, target):
        at = len(order) + ("down", "up", "qkv").index(name)
        return pltpu.make_async_copy(w_in[name], target, in_sem.at[at])

    def vector(start, size=width):
        return vec[:, start : start + size]

    def total(value):
        return jnp.sum(value.astype(jnp.float32), axis=0, keepdims=True)

    def norm_back(grad, unit, inverse, gain):
        scaled = grad * gain
        mean_grad = jnp.mean(scaled, axis=1, keepdims=True)
        mean_unit = jnp.mean(scaled * unit, axis=1, keepdims=True)
        return inverse * (scaled - mean_grad - unit * mean_unit)

    names = [group[0] for group in groups]

    def event(g, part, step):
        if g == -2:
            vector_step(step)
        elif g < 0:
            out_swap.start()
        else:
            scatter.step(g, part, step)

    clock = Clock(SCATTER_EVENTS, event, set())

    def begin(g):
        clock.begun.add(g)
        scatter.begin(g)

    for name in ("unit2", "ct", "inv2", "vec", "g"):
        fetch(name).start()
    place.greet()

    fetch("unit2").wait()
    fetch("ct").wait()
    fetch("inv2").wait()
    fetch("vec").wait()
    unit = unit2[...]
    out_low[...] = (unit * vector(G2) + vector(E2)).astype(jnp.bfloat16)
    seed = ct[...].astype(jnp.float32)
    vec_g[:, G2 : G2 + width] = total(seed * unit)
    vec_g[:, E2 : E2 + width] = total(seed)
    d_h2 = norm_back(seed, unit, inv2[:, 0:1], vector(G2))
    unit2[...] = d_h2
    ct[...] = d_h2.astype(jnp.bfloat16)
    d_f = ct
    vec_g[:, B2 : B2 + width] = total(d_f[...])

    def rows(at):
        return pl.ds(pl.multiple_of(at * block, block), block)

    out_swap = remote(out_low.at[rows(1 - y)], out_out.at[y], ex_sems, (0,), place.y_peer)
    out_keep = pltpu.make_async_copy(out_low.at[rows(y)], out_out.at[y], out_sem.at[0])
    dx_swap = remote(dx_low.at[0], dx_low.at[1], ex_sems, (1,), place.y_peer)

    def with_down(w_down):
        fetch_weight("down", w_down).start()
        fetch("g").wait()

        for name in ("d", "unit1", "inv1", "w_out", "o", "w_box", "qkv", "table"):
            fetch(name).start()

        def down_grads(first, size):
            left = d_f[:, first : first + size]
            right = d_f[:, 384 + first : 384 + first + size]
            both = jnp.concatenate([left, right], axis=1)

            def grad_tile(t, carry):
                part = dot_n(hidden[:, lanes(t * width, width)], both).astype(jnp.bfloat16)
                for h in range(2):
                    stored["down"][h, t, :, :, :, first : first + size] = part[
                        :, h * size : (h + 1) * size
                    ].reshape(2, 2, -1, size)
                return carry

            lax.fori_loop(0, 4, grad_tile, 0)
            for g, group in enumerate(groups):
                if group[0] == "down" and first <= group[2][2] < first + size:
                    begin(g)
            clock.point()

        down_grads(0, 128)
        down_grads(128, 256)
        out_keep.start()
        fetch_weight("down", w_down).wait()
        fetch("d").wait()

        def slope_tile(t, carry, serve):
            w0 = w_down.at[0, t][...].reshape(width, 384)
            w1 = w_down.at[1, t][...].reshape(width, 384)
            d_hidden = dot_t(d_f[...], jnp.concatenate([w0, w1], axis=1))
            at = lanes(t * width, width)
            d_pre = (d_hidden * slope[:, at].astype(jnp.float32)).astype(jnp.bfloat16)
            slope[:, at] = d_pre
            vec_g[:, lanes(B1 + t * width, width)] = total(d_pre)
            return carry

        clock.loop(4, slope_tile)

    pl.run_scoped(with_down, pltpu.VMEM(w_in["down"].shape, jnp.bfloat16))

    fetch("unit1").wait()
    fetch("inv1").wait()
    y1_low[...] = (unit1[...] * vector(G1) + vector(E1)).astype(jnp.bfloat16)

    def with_up(w_up):
        fetch_weight("up", w_up).start()

        def up_tile(i, carry, serve, part):
            tile = dot_n(y1_low[...], slope[:, lanes(i * 1536 + part * width, width)])
            stored["up"][i, :, :, :, :, part * width : (part + 1) * width] = tile.astype(
                jnp.bfloat16
            ).reshape(4, 2, 2, -1, width)
            return carry

        for part in range(2):
            clock.loop(2, partial(up_tile, part=part))
            for g, group in enumerate(groups):
                if group[0] == "up" and group[2][2] // width == part:
                    begin(g)
        fetch_weight("up", w_up).wait()

        def back_tile(h, carry, serve):
            w = w_up.at[h][...].reshape(width, 1536)
            unit2[...] += dot_t(slope[:, lanes(h * 1536, 1536)], w)
            return carry

        clock.loop(2, back_tile)

    pl.run_scoped(with_up, pltpu.VMEM(w_in["up"].shape, jnp.bfloat16))

    x_own = y1_low
    fetch("x").start()
    unit = unit1[...]
    d_y1 = unit2[...]
    vec_g[:, G1 : G1 + width] = total(d_y1 * unit)
    vec_g[:, E1 : E1 + width] = total(d_y1)
    d_h1 = norm_back(d_y1, unit, inv1[:, 0:1], vector(G1))
    unit1[...] = d_h1
    d_a[...] = d_h1.astype(jnp.bfloat16)
    vec_g[:, BO : BO + width] = total(d_a[...])
    fetch("w_out").wait()
    fetch("o").wait()
    both = jnp.concatenate([w_out.at[h][...].reshape(width, 384) for h in range(2)], axis=1)
    d_mixed[...] = dot_t(d_a[...], both).astype(jnp.bfloat16)
    part = dot_n(o_own[...].astype(jnp.bfloat16), d_a[...]).astype(jnp.bfloat16)
    for h in range(2):
        stored["out"][h] = part[:, h * 384 : (h + 1) * 384].reshape(4, 2, 2, -1, 384)
    begin(names.index("out"))
    clock.point()

    for name in ("w_box", "qkv", "table", "x"):
        fetch(name).wait()
    low = w_box.at[0][...].reshape(width, 2 * FREQ)
    high = w_box.at[1][...].reshape(width, 2 * FREQ)
    box_w[...] = jnp.concatenate(
        [low[:, :FREQ], high[:, :FREQ], low[:, FREQ:], high[:, FREQ:]], axis=1
    ).T
    keys[:, : 2 * FREQ] = table[0].astype(jnp.bfloat16)
    keys[:, 2 * FREQ :] = table[1].astype(jnp.bfloat16)
    table[...] = table[...] * (HEAD**-0.5)
    head_lane = lax.broadcasted_iota(jnp.int32, (1, 128), 1)

    def p_copy(p, slot, i):
        at = lanes((slot * 2 + i) * page_len, page_len)
        return pltpu.make_async_copy(p_in.at[p, i], hidden.at[:, at], p_sem.at[slot, i])

    p_copy(0, 0, 0).start()
    p_copy(0, 0, 1).start()

    vector_c = remote(pieces.at[:, :, :, 1 - c], pc_land, v_sems, (0,), place.c_peer)
    vector_y = remote(pieces.at[1 - y, :, :, c], py_land, v_sems, (1,), place.y_peer)
    vector_x = remote(pieces.at[y, :, 1 - x, c], px_land, v_sems, (2,), place.x_peer)

    def vector_z(k):
        there = lax.rem(z + k + 1, 4)
        peer = (there * 4 + x * 2 + c, y)
        return remote(pieces.at[y, there, x, c], pz_land.at[k], vz_sems, (k,), peer)

    def vector_step(step):
        if step == 0:
            vector_c.wait_recv()
            pieces[:, :, :, c] += pc_land[...]
            vector_y.start()
        if step == 1:
            vector_y.wait_recv()
            pieces[y, :, :, c] += py_land[...]
            vector_x.start()
        if step == 2:
            vector_x.wait_recv()
            pieces[y, :, x, c] += px_land[...]
            for k in range(3):
                vector_z(k).start()

    def with_qkv(w_qkv, early):
        stored["early"] = early
        fetch_weight("qkv", w_qkv).start()

        def pair(p, carry, serve):
            slot = lax.rem(p, 2)

            @pl.when(p < HEADS // 2 - 1)
            def _():
                p_copy(p + 1, 1 - slot, 0).start()
                p_copy(p + 1, 1 - slot, 1).start()

            p_copy(p, slot, 0).wait()
            p_copy(p, slot, 1).wait()
            q_t = qkv[:, lanes(p * 128, 128)].T
            k = qkv[:, lanes(width + p * 128, 128)]
            v_t = qkv[:, lanes(2 * width + p * 128, 128)].T
            w_t = box_w[:, lanes(p * 128, 128)]
            d_o = d_mixed[:, lanes(p * 128, 128)]
            d_o_t = d_o.T
            weighted = d_o.astype(jnp.float32) * o_own[:, lanes(p * 128, 128)]
            keys_k = jnp.concatenate([keys[...], k], axis=1)
            grads = []
            for i in range(2):
                if i:
                    serve()
                of_head = (head_lane < HEAD) == (i == 0)
                rows_head = slice(i * HEAD, (i + 1) * HEAD)
                probs = hidden[:, lanes((slot * 2 + i) * page_len, page_len)]
                delta = jnp.sum(jnp.where(of_head, weighted, 0.0), axis=1, keepdims=True)
                d_probs = jnp.dot(
                    jnp.where(of_head, d_o, jnp.zeros_like(d_o)),
                    v_t,
                    preferred_element_type=jnp.float32,
                )
                d_s = (probs.astype(jnp.float32) * (d_probs - delta)).astype(jnp.bfloat16)
                serve()
                d_b = jnp.dot(d_s, keys_k, preferred_element_type=jnp.float32)
                d_1, d_2 = d_b[:, : 2 * FREQ], d_b[:, 2 * FREQ : 4 * FREQ]
                cosine, sine = table[0], table[1]
                d_sine = (d_1 * sine - d_2 * cosine).astype(jnp.bfloat16)
                d_cosine = (d_1 * cosine + d_2 * sine).astype(jnp.bfloat16)
                d_u = jnp.concatenate([d_sine, d_cosine], axis=1)
                d_q = d_b[:, 4 * FREQ :] * (HEAD**-0.5) + jnp.dot(
                    d_u, w_t, preferred_element_type=jnp.float32
                )
                d_w = jnp.dot(q_t[rows_head], d_u, preferred_element_type=jnp.float32)
                box_g[pl.ds(pl.multiple_of(p * 128 + i * HEAD, HEAD), HEAD), :] = d_w.astype(
                    jnp.bfloat16
                )
                d_k = jnp.dot(q_t[rows_head], d_s, preferred_element_type=jnp.float32)
                d_v = jnp.dot(d_o_t[rows_head], probs, preferred_element_type=jnp.float32)
                grads.append((d_q, d_k * (HEAD**-0.5), d_v))
            (q_one, k_one, v_one), (q_two, k_two, v_two) = grads
            d_q = jnp.where(head_lane < HEAD, q_one, q_two).astype(jnp.bfloat16)
            d_k = jnp.concatenate([k_one, k_two], axis=0).astype(jnp.bfloat16).T
            d_v = jnp.concatenate([v_one, v_two], axis=0).astype(jnp.bfloat16).T
            for n, value in enumerate((d_q, d_k, d_v)):
                slope[:, lanes(n * width + p * 128, 128)] = value
            vec_g[:, lanes(BQ + p * 128, 128)] = total(d_q)
            vec_g[:, lanes(BV + p * 128, 128)] = total(d_v)
            return carry

        def qkv_grads(slot):
            store, top = ("early", 0) if slot == 0 else ("down", (slot - 1) * 48)
            for h in range(2):
                first = h * 1152 + THIRDS[h][slot] * 384
                tile = dot_n(x_own[...], slope[:, first : first + 384])
                stored[store][h, :, :, :, top : top + 48, :] = tile.astype(
                    jnp.bfloat16
                ).reshape(4, 2, 2, -1, 384)
            begin([g for g in range(count) if names[g] == "qkv"][slot])

        half = HEADS // 4
        clock.loop(half, pair, 4)
        qkv_grads(0)
        clock.point()
        clock.loop(half, lambda p, carry, serve: pair(p + half, carry, serve), 4)

        for dz in range(4):
            for dx in range(2):
                for dc in range(2):
                    for dy in range(2):
                        device = ((dz * 2 + dx) * 2 + dc) * 2 + dy
                        start = device * (VECTORS // 32) // 128 * 128
                        pieces[dy, dz, dx, dc] = vec_g[:, start : start + 384]
        vector_c.start()
        part = box_g[...]
        stored["box"][0] = jnp.concatenate(
            [part[:, :FREQ], part[:, 2 * FREQ : 3 * FREQ]], axis=1
        ).reshape(4, 2, 2, -1, 384)
        stored["box"][1] = jnp.concatenate(
            [part[:, FREQ : 2 * FREQ], part[:, 3 * FREQ :]], axis=1
        ).reshape(4, 2, 2, -1, 384)
        begin(names.index("box"))
        clock.point()
        clock.upto(*[
            (g, part, 3)
            for g, group in enumerate(groups)
            if names[g] == "down"
            for part in range(len(group[-1]))
        ])
        scatter.left([g for g in range(count) if names[g] == "down"], clock.at)

        for slot in (1, 2):
            qkv_grads(slot)
            clock.point()

        fetch_weight("qkv", w_qkv).wait()

        def back_tile(h, carry, serve):
            w = w_qkv.at[h][...].reshape(width, 1152)
            unit1[...] += dot_t(slope[:, lanes(h * 1152, 1152)], w)
            return carry

        clock.loop(2, back_tile)
        dx_low[0] = unit1[rows(1 - y), :].astype(jnp.bfloat16)
        dx_swap.start()
        pltpu.make_async_copy(unit1.at[rows(y)], dx_out.at[y], out_sem.at[1]).start()

        clock.point()
        clock.point()
        clock.upto(*(tuple(event) for _, *event in SCATTER_EVENTS))
        dx_swap.wait_recv()
        unit2[0:block, :] = dx_low[1].astype(jnp.float32)
        pltpu.make_async_copy(unit2.at[0:block], dx_out.at[1 - y], out_sem.at[2]).start()
        for k in range(3):
            vector_z(k).wait_recv()
        piece_total = pieces[y, z, x, c]
        for k in range(3):
            piece_total = piece_total + pz_land[k]
        piece_sum[...] = piece_total
        finals = [pltpu.make_async_copy(piece_sum, piece_out, out_sem.at[3])]
        for i, name in enumerate(WEIGHTS):
            finals.append(pltpu.make_async_copy(summed[name], grad_out[name], out_sem.at[4 + i]))
        for copy in finals:
            copy.start()
        scatter.left(range(count))
        for copy in (vector_c, vector_y, vector_x, out_swap, dx_swap):
            copy.wait_send()
        for k in range(3):
            vector_z(k).wait_send()
        out_swap.wait_recv()
        out_keep.wait()
        pltpu.make_async_copy(unit1.at[rows(y)], dx_out.at[y], out_sem.at[1]).wait()
        pltpu.make_async_copy(unit2.at[0:block], dx_out.at[1 - y], out_sem.at[2]).wait()
        for copy in finals:
            copy.wait()

    pl.run_scoped(
        with_qkv,
        pltpu.VMEM(w_in["qkv"].shape, jnp.bfloat16),
        pltpu.VMEM(stored["box"].shape, jnp.bfloat16),
    )


def backward_call(full, kept, shards):
    low, single = jnp.bfloat16, jnp.float32
    page_len, width = kept["x"].shape
    groups = SCATTER_GROUPS
    count = len(groups)
    outs = [
        jax.ShapeDtypeStruct((2, page_len // 2, width), low),
        jax.ShapeDtypeStruct((2, page_len // 2, width), single),
    ]
    outs += [jax.ShapeDtypeStruct(s.shape, single) for s in shards]
    outs += [jax.ShapeDtypeStruct((1, 384), single)]
    by_name = dict(zip(WEIGHTS, shards))

    def vmem(*shape, kind=low):
        return pltpu.VMEM(shape, kind)

    size = lambda cut: (cut[1], cut[3])
    dma = pltpu.SemaphoreType.DMA
    scratch = [vmem(2, 4, 2, 2, *by_name[n].shape) for n in ("box", "out", "up", "down")]
    scratch += [vmem(2, 4, 2, *size(g[2])) for g in groups]
    for group in groups:
        for path, piece in group[-1]:
            scratch += [vmem(*landing_shape(path, hop, piece)) for hop in range(3)]
    scratch += [vmem(*s.shape, kind=single) for s in shards]
    scratch += [vmem(*full[n].shape) for n in ("box", "out")]
    scratch += [vmem(width, BOX_DIM), vmem(width, BOX_DIM)]
    scratch += [vmem(*kept[n].shape, kind=kept[n].dtype) for n in ("ct", "qkv", "table")]
    scratch += [vmem(page_len, BOX_DIM)]
    scratch += [
        vmem(*kept[n].shape, kind=kept[n].dtype)
        for n in ("o", "unit1", "inv1", "g", "d", "unit2", "inv2", "vec")
    ]
    scratch += [vmem(page_len, width)] * 4
    scratch += [vmem(2, page_len // 2, width), vmem(1, VECTORS + 128, kind=single)]
    scratch += [
        vmem(2, 4, 2, 2, 1, 384, kind=single),
        vmem(2, 4, 2, 1, 384, kind=single),
        vmem(4, 2, 1, 384, kind=single),
        vmem(4, 1, 384, kind=single),
        vmem(3, 1, 384, kind=single),
        vmem(1, 384, kind=single),
    ]
    scratch += [dma((SENDS,)), dma((len(semaphore_table(groups, 4)),))] + [dma((count,))] * 2
    scratch += [dma((3,))] * 2 + [dma((3,))] * 2 + [dma((2,))] * 2
    scratch += [dma((17,)), dma((2, 2)), dma((9,))]
    anywhere = pl.BlockSpec(memory_space=pl.ANY)
    operands = [full[n] for n in WEIGHTS] + list(kept.values())
    plan = (groups, page_len, width)
    results = pl.pallas_call(
        partial(backward_kernel, plan),
        out_shape=outs,
        in_specs=[anywhere] * len(operands),
        out_specs=[anywhere] * len(outs),
        scratch_shapes=scratch,
        compiler_params=pltpu.CompilerParams(
            collective_id=1, has_side_effects=True, vmem_limit_bytes=VMEM_BACK
        ),
    )(*operands)
    return results


VMEM_BACK = 63 * 2**20


def finish_kernel(*refs):
    count = len(refs) // 2
    ins, outs = refs[:count], refs[count:]
    for i in range(count - 1):
        outs[i][...] = ins[i][...]
    rows = jnp.broadcast_to(ins[-1][...], (8, 384))
    rows = pltpu.roll(rows, 384 - Place().vector_offset(), 1)
    outs[-1][...] = rows[0:1, : VECTORS // 32].reshape(VECTORS // 32)


def finish_call(results):
    outs = [jax.ShapeDtypeStruct(r.shape, r.dtype) for r in results[:-1]]
    outs += [jax.ShapeDtypeStruct((VECTORS // 32,), jnp.float32)]

    def half(shape):
        block = (shape[0] // 2,) + shape[1:]
        return pl.BlockSpec(block, lambda i: (i,) + (0,) * (len(shape) - 1))

    halves = [half(r.shape) for r in results[:-1]]
    return pl.pallas_call(
        finish_kernel,
        out_shape=outs,
        grid=(2,),
        in_specs=halves + [pl.BlockSpec((1, 384), lambda i: (0, 0))],
        out_specs=halves + [pl.BlockSpec((VECTORS // 32,), lambda i: (0,))],
        compiler_params=pltpu.CompilerParams(vmem_limit_bytes=VMEM_BACK),
    )(*results)


def fast_layer(tokens, boxes, lengths, wqkv, wbox, wout, wup, wdown, vectors, cotangent):
    shards = (wqkv, wbox, wout, wup, wdown)
    full, kept = forward_call(tokens, cotangent, boxes, lengths, vectors, shards)
    return tuple(finish_call(backward_call(full, kept, shards)))


def on_device(*args):
    tokens, wqkv, wbox, wdown = args[0], args[3], args[4], args[7]
    blocks, groups = lax.axis_size("blk"), lax.axis_size("dp")
    fits = (
        blocks == 2
        and groups == 16
        and tokens.shape[0] == 2
        and wqkv.shape == (48, 1152)
        and wdown.shape == (192, 384)
        and wbox.shape == (48, 2 * FREQ)
    )
    return fast_layer(*args) if fits else general_layer(*args)


def solution(mesh):
    in_specs = (
        P("dp", "blk", None),
        P(None, "dp", "blk"),
        P("dp"),
        P("dp", "blk"),
        P("dp", "blk"),
        P("dp", "blk"),
        P("dp", "blk"),
        P("dp", "blk"),
        P(("dp", "blk")),
        P("dp", "blk", None),
    )
    out_specs = (
        P("dp", "blk", None),
        P("dp", "blk", None),
        P("dp", "blk"),
        P("dp", "blk"),
        P("dp", "blk"),
        P("dp", "blk"),
        P("dp", "blk"),
        P(("dp", "blk")),
    )
    return jax.shard_map(
        on_device, mesh=mesh, in_specs=in_specs, out_specs=out_specs, check_vma=False
    )
```

```python
from functools import partial
import math

import jax
import jax.numpy as jnp
import numpy as np
from jax import lax
from jax.experimental import pallas as pl
from jax.experimental.pallas import tpu as pltpu
from jax.sharding import PartitionSpec as P

HEADS = 12
HEAD = 64
FREQ = 192
BOX_DIM = 768

EPSILON = 1e-12
MASKED = -1e30


def box_table(boxes):
    frequency = jnp.exp(jnp.arange(FREQ, dtype=jnp.float32) * (-math.log(10000.0) / FREQ))
    across = boxes[0].astype(jnp.float32)[..., None] * frequency
    upward = boxes[1].astype(jnp.float32)[..., None] * frequency
    return jnp.concatenate(
        [jnp.cos(across), jnp.sin(across), jnp.cos(upward), jnp.sin(upward)], axis=-1
    )


def rotate(coeffs, own_table):
    cos_across, sin_across, cos_upward, sin_upward = jnp.split(own_table[..., None, :], 4, axis=-1)
    sa, ca, sb, cb = jnp.split(coeffs, 4, axis=-1)
    return jnp.concatenate(
        [
            sa * sin_across + ca * cos_across,
            ca * sin_across - sa * cos_across,
            sb * sin_upward + cb * cos_upward,
            cb * sin_upward - sb * cos_upward,
        ],
        axis=-1,
    )


def unrotate(grad_rows, own_table):
    cos_across, sin_across, cos_upward, sin_upward = jnp.split(own_table[..., None, :], 4, axis=-1)
    d1a, d2a, d1b, d2b = jnp.split(grad_rows, 4, axis=-1)
    return jnp.concatenate(
        [
            d1a * sin_across - d2a * cos_across,
            d1a * cos_across + d2a * sin_across,
            d1b * sin_upward - d2b * cos_upward,
            d1b * cos_upward + d2b * sin_upward,
        ],
        axis=-1,
    )


def normalize(hidden):
    row_mean = jnp.mean(hidden, axis=-1, keepdims=True)
    centered = hidden - row_mean
    inverse = lax.rsqrt(jnp.mean(centered * centered, axis=-1, keepdims=True) + EPSILON)
    return centered * inverse, inverse


def normalize_back(grad, unit, inverse, gain):
    scaled = grad * gain
    mean_grad = jnp.mean(scaled, axis=-1, keepdims=True)
    mean_unit = jnp.mean(scaled * unit, axis=-1, keepdims=True)
    d_hidden = inverse * (scaled - mean_grad - unit * mean_unit)
    return d_hidden, jnp.sum(grad * unit, axis=0), jnp.sum(grad, axis=0)


def unpack(vector_all, model_width, hidden_units):
    cuts = [model_width] * 5 + [hidden_units] + [model_width] * 3
    pieces = []
    offset = 0
    for length_here in cuts:
        pieces.append(vector_all[offset : offset + length_here])
        offset = offset + length_here
    return pieces


def dot32(a, b):
    return jnp.dot(a, b, preferred_element_type=jnp.float32)


def gather_weight(shard):
    part = lax.all_gather(shard, "blk", axis=1, tiled=True)
    return lax.all_gather(part, "dp", axis=0, tiled=True)


def scatter_weight(grad):
    part = lax.psum_scatter(grad.astype(jnp.bfloat16), "dp", scatter_dimension=0, tiled=True)
    return lax.psum_scatter(part, "blk", scatter_dimension=1, tiled=True).astype(jnp.float32)


def general_layer(tokens, boxes, lengths, wqkv, wbox, wout, wup, wdown, vectors, cotangent):
    blocks = lax.axis_size("blk")
    pages_here = tokens.shape[0] // blocks
    model_width = tokens.shape[2]
    to_pages = partial(
        lax.all_to_all, axis_name="blk", split_axis=0, concat_axis=1, tiled=True
    )
    from_pages = partial(
        lax.all_to_all, axis_name="blk", split_axis=1, concat_axis=0, tiled=True
    )
    page_tokens = to_pages(tokens)
    page_boxes = lax.all_to_all(boxes, "blk", split_axis=1, concat_axis=2, tiled=True)
    page_lengths = lax.dynamic_slice(lengths, (lax.axis_index("blk") * pages_here,), (pages_here,))
    full_qkv = gather_weight(wqkv)
    full_box = gather_weight(wbox)
    full_out = gather_weight(wout)
    full_up = gather_weight(wup)
    full_down = gather_weight(wdown)
    full_vec = lax.all_gather(vectors, ("dp", "blk"), axis=0, tiled=True).astype(jnp.float32)
    page_cotangent = to_pages(cotangent)
    hidden_units = full_up.shape[1]
    bq, bv, bo, g1, e1, b1, b2, g2, e2 = unpack(full_vec, model_width, hidden_units)
    page_len = page_tokens.shape[1]
    score_scale = HEAD ** (-0.5)

    x = page_tokens.reshape(-1, model_width)
    projected = dot32(x, full_qkv)
    head_shape = (pages_here, page_len, HEADS, HEAD)
    q = (projected[:, :model_width] + bq).astype(jnp.bfloat16).reshape(head_shape)
    k = projected[:, model_width : 2 * model_width].astype(jnp.bfloat16).reshape(head_shape)
    v = (projected[:, 2 * model_width :] + bv).astype(jnp.bfloat16).reshape(head_shape)
    table = box_table(page_boxes)
    box_heads = full_box.reshape(HEADS, HEAD, BOX_DIM)
    coeffs = jnp.einsum("pqhd,hdc->pqhc", q, box_heads, preferred_element_type=jnp.float32)
    box_query = rotate(coeffs, table).astype(jnp.bfloat16)
    box_keys = table.astype(jnp.bfloat16)
    scores = (
        jnp.einsum("pqhd,pkhd->phqk", q, k, preferred_element_type=jnp.float32)
        + jnp.einsum("pqhc,pkc->phqk", box_query, box_keys, preferred_element_type=jnp.float32)
    ) * score_scale
    is_valid = (jnp.arange(page_len)[None, :] < page_lengths[:, None])[:, None, None, :]
    masked = jnp.where(is_valid, scores, MASKED)
    probs = jax.nn.softmax(masked, axis=-1)
    probs_low = probs.astype(jnp.bfloat16)
    mixed = jnp.einsum("phqk,pkhd->pqhd", probs_low, v, preferred_element_type=jnp.float32)
    mixed_low = mixed.astype(jnp.bfloat16).reshape(-1, model_width)
    unit1, inv1 = normalize(x.astype(jnp.float32) + dot32(mixed_low, full_out) + bo)
    y1 = unit1 * g1 + e1
    y1_low = y1.astype(jnp.bfloat16)
    pre = dot32(y1_low, full_up) + b1
    hidden = jax.nn.gelu(pre, approximate=False).astype(jnp.bfloat16)
    unit2, inv2 = normalize(y1 + dot32(hidden, full_down) + b2)
    output = (unit2 * g2 + e2).astype(jnp.bfloat16)

    seed = page_cotangent.reshape(-1, model_width).astype(jnp.float32)
    d_h2, d_g2, d_e2 = normalize_back(seed, unit2, inv2, g2)
    d_f = d_h2.astype(jnp.bfloat16)
    d_hidden = dot32(d_f, full_down.T)
    d_pre = jax.vjp(partial(jax.nn.gelu, approximate=False), pre)[1](d_hidden)[0]
    d_pre = d_pre.astype(jnp.bfloat16)
    d_wdown = dot32(hidden.T, d_f)
    d_wup = dot32(y1_low.T, d_pre)
    d_y1 = dot32(d_pre, full_up.T) + d_h2
    d_h1, d_g1, d_e1 = normalize_back(d_y1, unit1, inv1, g1)
    d_a = d_h1.astype(jnp.bfloat16)
    d_wout = dot32(mixed_low.T, d_a)
    d_mixed = dot32(d_a, full_out.T).astype(jnp.bfloat16).reshape(head_shape)
    row_delta = jnp.einsum("pqhd,pqhd->phq", d_mixed.astype(jnp.float32), mixed)
    d_probs = jnp.einsum("pqhd,pkhd->phqk", d_mixed, v, preferred_element_type=jnp.float32)
    d_raw = (probs * (d_probs - row_delta[..., None])).astype(jnp.bfloat16)
    d_q = jnp.einsum("phqk,pkhd->pqhd", d_raw, k, preferred_element_type=jnp.float32)
    d_box_q = jnp.einsum("phqk,pkc->pqhc", d_raw, box_keys, preferred_element_type=jnp.float32)
    d_k = jnp.einsum("phqk,pqhd->pkhd", d_raw, q, preferred_element_type=jnp.float32)
    d_v = jnp.einsum("phqk,pqhd->pkhd", probs_low, d_mixed, preferred_element_type=jnp.float32)
    d_coeffs = unrotate(d_box_q * score_scale, table).astype(jnp.bfloat16)
    d_q = d_q * score_scale + jnp.einsum(
        "pqhc,hdc->pqhd", d_coeffs, box_heads, preferred_element_type=jnp.float32
    )
    d_wbox = jnp.einsum("pqhd,pqhc->hdc", q, d_coeffs, preferred_element_type=jnp.float32)
    flat = (-1, model_width)
    d_q = d_q.astype(jnp.bfloat16).reshape(flat)
    d_k = (d_k * score_scale).astype(jnp.bfloat16).reshape(flat)
    d_v = d_v.astype(jnp.bfloat16).reshape(flat)
    d_c = jnp.concatenate([d_q, d_k, d_v], axis=1)
    d_wqkv = dot32(x.T, d_c)
    d_x = dot32(d_c, full_qkv.T) + d_h1
    total = partial(jnp.sum, axis=0, dtype=jnp.float32)
    vector_grad = jnp.concatenate(
        [total(d_q), total(d_v), total(d_a), d_g1, d_e1, total(d_pre), total(d_f), d_g2, d_e2]
    )
    return (
        from_pages(output.reshape(page_tokens.shape)),
        from_pages(d_x.reshape(page_tokens.shape)),
        scatter_weight(d_wqkv),
        scatter_weight(d_wbox.reshape(model_width, BOX_DIM)),
        scatter_weight(d_wout),
        scatter_weight(d_wup),
        scatter_weight(d_wdown),
        lax.psum_scatter(vector_grad, ("dp", "blk"), scatter_dimension=0, tiled=True),
    )


GATHER_GROUPS = (
    ("qkv", (0, 48, 0, 384), (("zxy", (0, 48, 0, 384)),)),
    ("qkv", (0, 48, 384, 384), (("zyx", (0, 48, 384, 256)), ("yzx", (0, 48, 640, 128)),)),
    ("qkv", (0, 48, 768, 384), (("zxy", (0, 48, 768, 384)),)),
    ("box", (0, 48, 0, 384), (("zyx", (0, 48, 0, 256)), ("yzx", (0, 48, 256, 128)),)),
    ("out", (0, 48, 0, 384), (("zxy", (0, 48, 0, 256)), ("yxz", (0, 48, 256, 128)),)),
    ("up", (0, 48, 0, 384), (("zxy", (0, 48, 0, 256)), ("yzx", (0, 48, 256, 128)),)),
    ("up", (0, 48, 384, 384), (("yxz", (0, 48, 384, 384)),)),
    ("up", (0, 48, 768, 384), (("yxz", (0, 48, 768, 384)),)),
    ("up", (0, 48, 1152, 384), (("zxy", (0, 48, 1152, 256)), ("zyx", (0, 48, 1408, 128)),)),
    ("down", (0, 192, 0, 128), (("zxy", (0, 64, 0, 128)), ("yxz", (64, 128, 0, 128)),)),
    ("down", (0, 192, 128, 128), (("zxy", (0, 128, 128, 128)), ("yzx", (128, 64, 128, 128)),)),
    ("down", (0, 192, 256, 128), (("zyx", (0, 192, 256, 128)),)),
)
GATHER_EVENTS = (
    (1, 0, 0, 0),
    (1, 1, 0, 0),
    (1, 2, 0, 0),
    (1, 3, 0, 0),
    (1, 4, 1, 0),
    (1, 0, 0, 10),
    (1, 1, 0, 10),
    (1, 0, 0, 1),
    (1, 8, 0, 0),
    (1, 6, 0, 0),
    (1, 10, 1, 0),
    (1, 3, 1, 0),
    (1, 5, 1, 0),
    (1, 1, 1, 0),
    (1, 2, 0, 10),
    (1, 1, 0, 1),
    (1, 10, 0, 0),
    (2, 3, 0, 10),
    (2, 7, 0, 0),
    (2, 2, 0, 1),
    (3, 4, 0, 0),
    (3, 1, 1, 1),
    (3, 0, 0, 2),
    (3, 4, 1, 1),
    (3, 3, 1, 1),
    (4, 6, 0, 1),
    (4, 4, 0, 10),
    (4, 1, 0, 2),
    (5, 3, 0, 1),
    (5, 5, 0, 0),
    (5, 5, 1, 1),
    (5, 10, 1, 1),
    (6, 1, 1, 11),
    (6, 5, 0, 10),
    (6, 2, 0, 2),
    (7, 4, 0, 1),
    (7, 8, 0, 10),
    (7, 9, 0, 0),
    (7, 9, 1, 0),
    (7, 5, 1, 11),
    (7, 3, 1, 11),
    (8, 1, 1, 2),
    (8, 8, 1, 0),
    (8, 0, 0, 3),
    (9, 9, 0, 10),
    (9, 7, 0, 1),
    (9, 3, 0, 2),
    (9, 3, 1, 2),
    (10, 11, 0, 0),
    (10, 0, 0, 4),
    (10, 4, 1, 2),
    (10, 1, 0, 3),
    (10, 8, 1, 10),
    (10, 9, 0, 1),
    (10, 4, 0, 2),
    (10, 1, 1, 3),
    (10, 10, 1, 11),
    (11, 10, 0, 10),
    (11, 1, 0, 4),
    (11, 11, 0, 10),
    (12, 2, 0, 3),
    (12, 6, 0, 2),
    (12, 1, 1, 4),
    (12, 2, 0, 4),
    (12, 10, 0, 1),
    (13, 5, 0, 1),
    (13, 8, 1, 1),
    (13, 3, 0, 3),
    (14, 5, 1, 2),
    (14, 8, 0, 1),
    (14, 7, 0, 2),
    (14, 10, 1, 2),
    (15, 3, 1, 3),
    (16, 9, 1, 1),
    (16, 11, 0, 1),
    (16, 4, 0, 3),
    (16, 3, 0, 4),
    (17, 9, 0, 2),
    (19, 3, 1, 4),
    (20, 5, 0, 2),
    (20, 4, 1, 12),
    (22, 6, 0, 12),
    (26, 8, 0, 2),
    (26, 8, 1, 2),
    (26, 4, 1, 3),
    (27, 4, 0, 4),
    (27, 5, 1, 3),
    (28, 11, 0, 2),
    (28, 10, 0, 2),
    (29, 10, 1, 3),
    (29, 7, 0, 12),
    (29, 9, 1, 2),
    (32, 5, 0, 3),
    (32, 6, 0, 3),
    (34, 9, 0, 3),
    (34, -1, 0, 0),
    (35, 4, 1, 4),
    (37, 8, 1, 3),
    (39, 9, 1, 12),
    (46, 7, 0, 3),
    (47, 10, 0, 3),
    (51, 8, 0, 3),
    (54, 5, 0, 4),
    (54, 9, 0, 4),
    (55, 6, 0, 4),
    (56, 11, 0, 3),
    (67, 5, 1, 4),
    (71, 7, 0, 4),
    (71, 9, 1, 3),
    (75, 10, 1, 4),
    (78, 11, 0, 4),
    (82, 8, 0, 4),
    (87, 8, 1, 4),
    (88, 9, 1, 4),
    (111, 10, 0, 4),
)
SCATTER_GROUPS = (
    ("down", "down", (0, 192, 0, 128), (0, 192, 0, 128), (("zyx", (0, 64, 0, 128)), ("xzy", (64, 128, 0, 128)),)),
    ("down", "down", (0, 192, 128, 128), (0, 192, 128, 128), (("zxy", (0, 64, 128, 128)), ("yxz", (64, 128, 128, 128)),)),
    ("down", "down", (0, 192, 256, 128), (0, 192, 256, 128), (("yzx", (0, 192, 256, 128)),)),
    ("up", "up", (0, 48, 0, 384), (0, 48, 0, 384), (("xyz", (0, 48, 0, 128)), ("yxz", (0, 48, 128, 256)),)),
    ("up", "up", (0, 48, 384, 384), (0, 48, 384, 384), (("xyz", (0, 48, 384, 384)),)),
    ("up", "up", (0, 48, 768, 384), (0, 48, 768, 384), (("xyz", (0, 48, 768, 384)),)),
    ("up", "up", (0, 48, 1152, 384), (0, 48, 1152, 384), (("xyz", (0, 48, 1152, 384)),)),
    ("out", "out", (0, 48, 0, 384), (0, 48, 0, 384), (("zxy", (0, 48, 0, 256)), ("xyz", (0, 48, 256, 128)),)),
    ("qkv", "early", (0, 48, 0, 384), 0, (("zxy", (0, 48, 0, 384)),)),
    ("box", "box", (0, 48, 0, 384), (0, 48, 0, 384), (("yxz", (0, 48, 0, 128)), ("xyz", (0, 48, 128, 256)),)),
    ("qkv", "down", (0, 48, 0, 384), 1, (("yxz", (0, 48, 0, 128)), ("yxz", (0, 48, 128, 256)),)),
    ("qkv", "down", (48, 48, 0, 384), 2, (("yxz", (48, 48, 0, 128)), ("xzy", (48, 48, 128, 256)),)),
)
SCATTER_EVENTS = (
    (5, 0, 0, 0),
    (6, 1, 0, 0),
    (11, 2, 0, 0),
    (12, 0, 0, 10),
    (13, 3, 0, 0),
    (13, 4, 0, 0),
    (16, 0, 1, 1),
    (16, 1, 0, 10),
    (17, 0, 0, 1),
    (17, 5, 0, 0),
    (18, 7, 0, 0),
    (21, 0, 1, 11),
    (25, 2, 0, 1),
    (25, 1, 1, 1),
    (25, -1, 0, 0),
    (26, 7, 0, 10),
    (28, 1, 0, 1),
    (29, 6, 0, 0),
    (30, 3, 1, 1),
    (31, 4, 0, 1),
    (31, 2, 0, 11),
    (32, 0, 0, 2),
    (32, 5, 0, 1),
    (34, 1, 1, 2),
    (34, 8, 0, 0),
    (35, 0, 1, 2),
    (35, 1, 0, 2),
    (36, 1, 1, 12),
    (42, 2, 0, 2),
    (42, 6, 0, 1),
    (43, 8, 0, 10),
    (44, 1, 1, 3),
    (45, 3, 0, 1),
    (46, 2, 0, 3),
    (46, 4, 0, 2),
    (47, 1, 0, 3),
    (47, 7, 1, 1),
    (48, 0, 0, 3),
    (48, 9, 0, 0),
    (48, 0, 1, 3),
    (48, -2, 0, 0),
    (48, 6, 0, 2),
    (49, 10, 0, 0),
    (49, 7, 1, 2),
    (49, 11, 0, 0),
    (49, 3, 1, 2),
    (51, 9, 1, 1),
    (51, 7, 0, 1),
    (57, 3, 0, 2),
    (64, 9, 0, 1),
    (65, 4, 0, 12),
    (65, 3, 0, 12),
    (68, -2, 0, 1),
    (75, 5, 0, 2),
    (75, 11, 1, 1),
    (81, 10, 1, 1),
    (88, 7, 0, 2),
    (95, -2, 0, 2),
    (117, 4, 0, 3),
    (146, 3, 0, 3),
    (198, 8, 0, 1),
    (530, 3, 1, 12),
    (543, 6, 0, 12),
    (567, 5, 0, 12),
    (567, 11, 1, 11),
    (568, 7, 1, 12),
    (898, 10, 0, 1),
    (912, 9, 1, 2),
    (915, 9, 0, 2),
    (936, 11, 0, 1),
    (956, 8, 0, 2),
    (959, 10, 0, 2),
    (975, 9, 1, 12),
    (988, 11, 0, 2),
    (991, 10, 0, 12),
    (1004, 10, 1, 2),
    (1005, 9, 0, 12),
    (1009, 11, 1, 2),
    (1017, 9, 1, 3),
    (1019, 11, 0, 12),
    (1022, 3, 1, 3),
    (1030, 10, 0, 3),
    (1046, 6, 0, 3),
    (1054, 10, 1, 12),
    (1058, 5, 0, 3),
    (1068, 7, 0, 3),
    (1069, 11, 0, 3),
    (1069, -2, 0, 3),
    (1070, 8, 0, 3),
    (1084, 9, 0, 3),
    (1086, 10, 1, 3),
    (1111, 11, 1, 3),
    (1136, 7, 1, 3),
)


MESH = pl.DeviceIdType.MESH
WEIGHTS = ("qkv", "box", "out", "up", "down")
ROT = 4
ALL = slice(None)


def window(piece):
    return (pl.ds(piece[0], piece[1]), pl.ds(piece[2], piece[3]))


class Place:
    def __init__(self):
        dp = lax.axis_index("dp")
        self.y = lax.axis_index("blk")
        self.z = lax.div(dp, 4)
        self.x = lax.rem(lax.div(dp, 2), 2)
        self.c = lax.rem(dp, 2)
        x, y, z, c = self.x, self.y, self.z, self.c
        self.near = z + 1 - 2 * lax.rem(z, 2)
        self.far = lax.rem(z + 2, 4)
        self.mirror = 3 - z
        self.inner = jnp.logical_or(z == 1, z == 2)
        self.end = jnp.logical_or(z == 0, z == 3)
        at = lambda other: (other * 4 + x * 2 + c, y)
        self.near_peer, self.far_peer, self.mirror_peer = at(self.near), at(self.far), at(self.mirror)
        self.x_peer = (dp + 2 - 4 * x, y)
        self.y_peer = (dp, 1 - y)
        self.c_peer = (dp + 1 - 2 * c, y)

    def own(self):
        return dict(y=self.y, z=self.z, x=self.x)

    def vector_offset(self):
        device = ((self.z * 2 + self.x) * 2 + self.c) * 2 + self.y
        return lax.rem(device * (VECTORS // 32), 128)

    def hail(self):
        peers = [self.near_peer, self.far_peer, self.mirror_peer]
        peers += [self.x_peer, self.y_peer, self.c_peer]
        for peer in peers:
            pl.semaphore_signal(
                pltpu.get_barrier_semaphore(), inc=1, device_id=peer, device_id_type=MESH
            )

    def meet(self):
        pl.semaphore_wait(pltpu.get_barrier_semaphore(), 6)


def semaphore_table(groups, slots):
    table = {}
    for g, group in enumerate(groups):
        for part, (path, _) in enumerate(group[-1]):
            for hop, axis in enumerate(path):
                for slot in range(slots if axis == "z" else 1):
                    table[g, part, hop, slot] = len(table)
    return table


SEND_RINGS = dict(all=(0, 24), inner=(24, 12), end=(36, 12))
SENDS = 48


class Sends:
    def __init__(self, place, events, started):
        self.place = place
        self.index, self.before, self.kind, self.after = {}, {}, {}, {}
        turns = {kind: [] for kind in SEND_RINGS}
        for at, (_, *event) in enumerate(events):
            for key, kind in started(*event):
                base, size = SEND_RINGS[kind]
                turn = turns[kind]
                self.index[key], self.kind[key] = base + len(turn) % size, kind
                if len(turn) >= size:
                    self.before[key] = turn[-size]
                    self.after[turn[-size]] = at
                turn.append(key)
        self.done = set()

    def when(self, key, act):
        kind = self.kind[key]
        if kind == "all":
            act()
        else:
            pl.when(self.place.inner if kind == "inner" else self.place.end)(act)

    def start(self, copy, *key):
        before = self.before.get(key)
        if before is not None and before not in self.done:
            copy(*before).wait_send()
        copy(*key).start()

    def left(self, copy, now=None, chosen=lambda key: True):
        for key in self.index:
            at = self.after.get(key)
            if key in self.done or not chosen(key) or (at is not None and (now is None or at < now)):
                continue
            self.done.add(key)
            self.when(key, copy(*key).wait_send)


def remote(src, dst, sems, at, peer, send=None):
    return pltpu.make_async_remote_copy(
        src,
        dst,
        sems[0].at[at if send is None else send],
        sems[1].at[at],
        device_id=peer,
        device_id_type=MESH,
    )


def core_table(groups):
    keys = [(g, part) for g, group in enumerate(groups) for part in range(len(group[-1]))]
    return {key: n for n, key in enumerate(keys)}


class Gather:
    def __init__(self, place, groups, shards, full, sems, own_sem):
        self.place, self.groups, self.shards, self.full = place, groups, shards, full
        self.sems, self.own_sem = sems, own_sem
        self.count = len(groups)
        self.table = semaphore_table(groups, 3)
        self.c_table = core_table(groups)
        self.sends = Sends(place, GATHER_EVENTS, self.started)
        self.owned = False

    def started(self, g, part, step):
        if g < 0 or step == 4:
            return []
        if step == 3:
            return [((g, part, 3, 0), "all")]
        if step >= 10:
            return [((g, part, step - 10, 3), "inner")]
        if self.groups[g][2][part][0][step] != "z":
            return [((g, part, step, 0), "all")]
        return [
            ((g, part, step, 1), "all"),
            ((g, part, step, 0), "all"),
            ((g, part, step, 2), "inner"),
        ]

    def copy(self, g, part, hop, slot, arriving=False):
        p = self.place
        name, _, parts = self.groups[g]
        path, piece = parts[part]
        cut = window(piece)
        send = self.sends.index[g, part, hop, slot]
        if hop == 3:
            c = 1 - p.c if arriving else p.c
            ref = self.full[name].at[(ALL, ALL, ALL, c) + cut]
            at = len(self.table) + self.c_table[g, part]
            return remote(ref, ref, self.sems, (at,), p.c_peer, (send,))
        axis = path[hop]
        at = p.own()
        at.update({earlier: ALL for earlier in path[:hop]})
        if axis == "z":
            peer = (p.near_peer, p.far_peer, p.mirror_peer, p.near_peer)[slot]
            if slot == 3:
                at["z"] = p.mirror if arriving else p.far
            elif arriving:
                at["z"] = (p.near, p.far, p.mirror)[slot]
        else:
            peer = p.x_peer if axis == "x" else p.y_peer
            if arriving:
                at[axis] = 1 - at[axis]
        ref = self.full[name].at[(at["y"], at["z"], at["x"], p.c) + cut]
        source = self.shards[name].at[cut] if hop == 0 and slot < 3 else ref
        at = self.table[g, part, hop, min(slot, 2)]
        return remote(source, ref, self.sems, (at,), peer, (send,))

    def own_copy(self, g):
        p = self.place
        name, both, _ = self.groups[g]
        cut = window(both)
        return pltpu.make_async_copy(
            self.shards[name].at[cut],
            self.full[name].at[(p.y, p.z, p.x, p.c) + cut],
            self.own_sem.at[g],
        )

    def relay(self, g, part, hop):
        @pl.when(self.place.inner)
        def _():
            self.copy(g, part, hop, 1, True).wait_recv()
            self.sends.start(self.copy, g, part, hop, 3)

    def start(self, g, part, hop):
        if self.groups[g][2][part][0][hop] != "z":
            self.sends.start(self.copy, g, part, hop, 0)
            return
        self.sends.start(self.copy, g, part, hop, 1)
        self.sends.start(self.copy, g, part, hop, 0)

        @pl.when(self.place.inner)
        def _():
            self.sends.start(self.copy, g, part, hop, 2)

    def finish(self, g, part, hop):
        self.copy(g, part, hop, 0, True).wait_recv()
        if self.groups[g][2][part][0][hop] != "z":
            return

        @pl.when(self.place.inner)
        def _():
            self.copy(g, part, hop, 2, True).wait_recv()

        @pl.when(self.place.end)
        def _():
            self.copy(g, part, hop, 1, True).wait_recv()
            self.copy(g, part, hop, 3, True).wait_recv()

    def own(self):
        for g in range(self.count):
            self.own_copy(g).start()

    def step(self, g, part, step):
        if step >= 10:
            self.relay(g, part, step - 10)
            return
        if step >= 1 and not self.owned:
            self.owned = True
            for other in range(self.count):
                self.own_copy(other).wait()
        if 1 <= step <= 3:
            self.finish(g, part, step - 1)
        if step <= 2:
            self.start(g, part, step)
        if step == 3:
            self.sends.start(self.copy, g, part, 3, 0)
        if step == 4:
            self.copy(g, part, 3, 0, True).wait_recv()


class Clock:
    def __init__(self, events, run, begun=None):
        self.events, self.run, self.now, self.at, self.begun = events, run, 0, 0, begun

    def may(self, event):
        return self.begun is None or event[1] < 0 or event[1] in self.begun

    def take(self):
        self.now += 1
        first = self.at
        while self.at < len(self.events):
            event = self.events[self.at]
            if event[0] > self.now or not self.may(event):
                break
            self.at += 1
        return self.events[first : self.at]

    def point(self):
        for _, *event in self.take():
            self.run(*event)

    def upto(self, *wanted):
        self.now += 1
        last = max(i for i, (_, *event) in enumerate(self.events) if tuple(event) in wanted)
        while self.at <= last:
            assert self.may(self.events[self.at])
            _, *event = self.events[self.at]
            self.at += 1
            self.run(*event)

    def loop(self, count, body, points=1):
        due = [[self.take() for _ in range(points)] for _ in range(count)]

        def wrapped(i, carry):
            point = iter(range(points))

            def serve():
                k = next(point)
                for n in range(count):
                    if due[n][k]:

                        @pl.when(i == n)
                        def _():
                            for _, *event in due[n][k]:
                                self.run(*event)

            serve()
            return body(i, carry, serve)

        lax.fori_loop(0, count, wrapped, 0)
        self.point()


def sine_cosine(angle):
    turns = jnp.floor(angle * (2.0 / math.pi) + 0.5)
    rest = angle - turns * 1.5703125
    rest = rest - turns * 4.837512969970703125e-4
    rest = rest - turns * 7.54978995489188216e-8
    square = rest * rest
    sine = rest + rest * square * (
        -1.6666654611e-1 + square * (8.3321608736e-3 + square * -1.9515295891e-4)
    )
    cosine = (
        1.0
        - 0.5 * square
        + square
        * square
        * (
            4.166664568298827e-2
            + square * (-1.388731625493765e-3 + square * 2.443315711809948e-5)
        )
    )
    quarter = turns.astype(jnp.int32)
    odd = (quarter & 1) == 1
    sine_sign = jnp.where((quarter & 2) == 2, -1.0, 1.0)
    cosine_sign = jnp.where(((quarter + 1) & 2) == 2, -1.0, 1.0)
    return (
        sine_sign * jnp.where(odd, cosine, sine),
        cosine_sign * jnp.where(odd, sine, cosine),
    )


def dot_t(a, b):
    return lax.dot_general(a, b, (((1,), (1,)), ((), ())), preferred_element_type=jnp.float32)


def dot_n(a, b):
    return lax.dot_general(a, b, (((0,), (0,)), ((), ())), preferred_element_type=jnp.float32)


def lanes(start, size):
    return pl.ds(pl.multiple_of(start, 128), size)


BQ, BV, BO, G1, E1, B1, B2, G2, E2 = 0, 768, 1536, 2304, 3072, 3840, 6912, 7680, 8448
VECTORS = 9216
SUMS = VECTORS + 128


def total(value):
    return jnp.sum(value.astype(jnp.float32), axis=0, keepdims=True)


def norm_back(grad, unit, inverse, gain):
    scaled = grad * gain
    mean_grad = jnp.mean(scaled, axis=1, keepdims=True)
    mean_unit = jnp.mean(scaled * unit, axis=1, keepdims=True)
    return inverse * (scaled - mean_grad - unit * mean_unit)


def forward_kernel(plan, *refs):
    groups, page_len, width = plan
    block = page_len // 2
    refs = iter(refs)
    take = lambda n: [next(refs) for _ in range(n)]
    tokens, cotangent, boxes, lengths, vectors = take(5)
    shards = dict(zip(WEIGHTS, take(5)))
    full_out = dict(zip(WEIGHTS, take(5)))
    (x_out, ct_out, qkv_out, table_out, p_out, o_out, unit1_out, inv1_out) = take(8)
    (g_out, d_out, unit2_out, low_out, vec_out) = take(5)
    full = dict(zip(WEIGHTS, take(5)))
    (ct_own, x_own, boxes_peer, pieces, vec, qkv, table, keys, box_w, p_slots, o_own, o_low) = take(12)
    (unit1, inv1, y1_low, hidden, slope, unit2) = take(6)
    w_sems = take(2)
    (own_sem,) = take(1)
    vz_sems, vxy_sems, vc_sems = take(2), take(2), take(2)
    ex_sems = take(2)
    (local_sem, p_sem, out_sem) = take(3)
    bias_qkv, piece = take(2)

    place = Place()
    y, z, x, c = place.y, place.z, place.x, place.c
    gather = Gather(place, groups, shards, full, w_sems, own_sem)

    def swap(i, source, target, arriving=False):
        at = (1 - y) if arriving else y
        return remote(
            source.at[1 - y], target.at[pl.ds(pl.multiple_of(at * block, block), block)],
            ex_sems, (i,), place.y_peer,
        )

    def keep(i, source, target):
        return pltpu.make_async_copy(
            source.at[y], target.at[pl.ds(pl.multiple_of(y * block, block), block)],
            local_sem.at[i],
        )

    box_swap = remote(boxes, boxes_peer, ex_sems, (2,), place.y_peer)

    def vector_y(arriving=False):
        at = 1 - y if arriving else y
        return remote(piece, pieces.at[at, z, x, c], vxy_sems, (0,), place.y_peer)

    def vector_x(arriving=False):
        ref = pieces.at[:, z, 1 - x if arriving else x, c]
        return remote(ref, ref, vxy_sems, (1,), place.x_peer)

    def vector_z(k, arriving=False):
        ref = pieces.at[:, lax.rem(z + 4 - k, 4) if arriving else z, :, c]
        peer = (lax.rem(z + k, 4) * 4 + x * 2 + c, y)
        return remote(ref, ref, vz_sems, (k - 1,), peer)

    def vector_c(arriving=False):
        ref = pieces.at[:, :, :, 1 - c if arriving else c]
        return remote(ref, ref, vc_sems, (0,), place.c_peer)

    vector_own = pltpu.make_async_copy(piece, pieces.at[y, z, x, c], local_sem.at[2])

    def event(g, part, step):
        if g < 0:
            swap(1, cotangent, ct_own).start()
        else:
            gather.step(g, part, step)

    clock = Clock(GATHER_EVENTS, event)

    def need(g):
        clock.upto(*((g, part, 4) for part in range(len(groups[g][2]))))

    outgoing = []

    def send_out(ref, out):
        copy = pltpu.make_async_copy(ref, out, out_sem.at[len(outgoing)])
        copy.start()
        outgoing.append(copy)

    place.hail()
    gather.own()
    own_vector = vectors[...].astype(jnp.float32).reshape(1, -1)
    own_vector = jnp.concatenate(
        [own_vector, jnp.zeros((1, 384 - own_vector.shape[1]), jnp.float32)], axis=1
    )
    own_vector = jnp.broadcast_to(own_vector, (8, 384))
    piece[...] = pltpu.roll(own_vector, place.vector_offset(), 1)[0:1, :]
    place.meet()
    box_swap.start()
    vector_y().start()
    vector_own.start()
    swap(0, tokens, x_own).start()
    clock.point()
    keep(0, tokens, x_own).start()
    keep(1, cotangent, ct_own).start()

    box_swap.wait_recv()
    mine, other = boxes[...], boxes_peer[...]
    first_block = y == 0
    mine = jnp.where(first_block, mine[:, 0, :], mine[:, 1, :])
    other = jnp.where(first_block, other[:, 0, :], other[:, 1, :])
    both = jnp.concatenate(
        [jnp.where(first_block, mine, other), jnp.where(first_block, other, mine)], axis=1
    ).astype(jnp.float32)
    both = jnp.concatenate([both, jnp.zeros((6, page_len), jnp.float32)], axis=0)
    across_up = both.T
    lane = lax.broadcasted_iota(jnp.int32, (1, 2 * FREQ), 1)
    step = jnp.where(lane < FREQ, lane, lane - FREQ).astype(jnp.float32)
    frequency = jnp.exp(step * (-math.log(10000.0) / FREQ))
    angle = jnp.where(lane < FREQ, across_up[:, 0:1], across_up[:, 1:2]) * frequency
    sine, cosine = sine_cosine(angle)
    table[0], table[1] = cosine, sine
    keys[0 : 2 * FREQ, :] = cosine.astype(jnp.bfloat16).T
    keys[2 * FREQ :, :] = sine.astype(jnp.bfloat16).T
    send_out(table, table_out)
    clock.point()
    vector_own.wait()
    vector_y(True).wait_recv()
    vector_x().start()
    clock.point()
    vector_x(True).wait_recv()
    for k in range(1, 4):
        vector_z(k).start()
    clock.point()
    clock.upto(*((0, part, 3) for part in range(len(groups[0][2]))))
    for k in range(1, 4):
        vector_z(k, True).wait_recv()
    vector_c().start()
    need(0)
    vector_c(True).wait_recv()
    vec[...] = jnp.zeros_like(vec)
    for dz in range(4):
        for dx in range(2):
            for dc in range(2):
                for dy in range(2):
                    device = ((dz * 2 + dx) * 2 + dc) * 2 + dy
                    start = device * (VECTORS // 32) // 128 * 128
                    vec[:, start : start + 384] += pieces[dy, dz, dx, dc]

    def vector(start, size=width):
        return vec[:, start : start + size]

    def columns_of(name, first, count):
        halves = [
            full[name].at[h][:, :, :, :, first : first + count].reshape(-1, count)
            for h in range(2)
        ]
        return jnp.concatenate(halves, axis=1)

    def project(first, count):
        both = jnp.dot(
            x_own[...], columns_of("qkv", first, count), preferred_element_type=jnp.float32
        )
        for h in range(2):
            at = slice(h * 1152 + first, h * 1152 + first + count)
            part = both[:, h * count : (h + 1) * count]
            qkv[:, at] = (part + bias_qkv[:, at]).astype(jnp.bfloat16)

    bias_qkv[:, 0:width] = vector(BQ)
    bias_qkv[:, width : 2 * width] = jnp.zeros((1, width), jnp.float32)
    bias_qkv[:, 2 * width : 3 * width] = vector(BV)
    for g, (name, cut, _) in enumerate(groups):
        if name == "qkv":
            if g == 0:
                keep(0, tokens, x_own).wait()
                swap(0, tokens, x_own, True).wait_recv()
                send_out(x_own, x_out)
            else:
                need(g)
            project(cut[2], cut[3])
            clock.point()
    send_out(qkv, qkv_out)

    box_group = [g for g, group in enumerate(groups) if group[0] == "box"][-1]
    need(box_group)
    low = full["box"].at[0][...].reshape(width, 2 * FREQ)
    high = full["box"].at[1][...].reshape(width, 2 * FREQ)
    box_w[...] = jnp.concatenate(
        [low[:, :FREQ], high[:, :FREQ], low[:, FREQ:], high[:, FREQ:]], axis=1
    )
    page_length = jnp.where(first_block, lengths[0], lengths[1])
    valid = lax.broadcasted_iota(jnp.int32, (1, page_len), 1) < page_length
    head_lane = lax.broadcasted_iota(jnp.int32, (1, 128), 1)

    def p_copy(p, slot):
        return pltpu.make_async_copy(p_slots.at[slot], p_out.at[p], p_sem.at[slot])

    def pair(p, carry, serve):
        slot = lax.rem(p, 2)

        @pl.when(p >= 2)
        def _():
            p_copy(p - 2, slot).wait()

        q = qkv[:, lanes(p * 128, 128)]
        k = qkv[:, lanes(width + p * 128, 128)].T
        v = qkv[:, lanes(2 * width + p * 128, 128)]
        w = box_w[pl.ds(pl.multiple_of(p * 128, 128), 128), :]
        outs = []
        for i in range(2):
            if i:
                serve()
            of_head = (head_lane < HEAD) == (i == 0)
            q_head = jnp.where(of_head, q, jnp.zeros_like(q))
            u = jnp.dot(q_head, w, preferred_element_type=jnp.float32)
            on_sine, on_cosine = u[:, : 2 * FREQ], u[:, 2 * FREQ :]
            cosine, sine = table[0], table[1]
            b_cosine = (on_sine * sine + on_cosine * cosine).astype(jnp.bfloat16)
            b_sine = (on_cosine * sine - on_sine * cosine).astype(jnp.bfloat16)
            serve()
            b = jnp.concatenate([q_head, b_cosine, b_sine], axis=1)
            s = jnp.dot(b, jnp.concatenate([k, keys[...]], axis=0), preferred_element_type=jnp.float32)
            s = jnp.where(valid, s, MASKED)
            top = jnp.max(s, axis=1, keepdims=True)
            e = jnp.exp((s - top) * (HEAD**-0.5))
            probs = (e * (1.0 / jnp.sum(e, axis=1, keepdims=True))).astype(jnp.bfloat16)
            p_slots[slot, i] = probs
            outs.append(jnp.dot(probs, v, preferred_element_type=jnp.float32))
        mixed = jnp.where(head_lane < HEAD, outs[0], outs[1])
        o_own[:, lanes(p * 128, 128)] = mixed
        o_low[:, lanes(p * 128, 128)] = mixed.astype(jnp.bfloat16)
        p_copy(p, slot).start()
        return carry

    clock.loop(HEADS // 2, pair, 4)
    p_copy(4, 0).wait()
    p_copy(5, 1).wait()
    send_out(o_own, o_out)

    def last_of(name):
        return [g for g, group in enumerate(groups) if group[0] == name][-1]

    def weight_out(name):
        send_out(full[name], full_out[name])

    weight_out("qkv")
    weight_out("box")
    need(last_of("out"))
    weight_out("out")
    for h in range(2):
        w = full["out"].at[h][...].reshape(width, 384)
        cut = slice(h * 384, (h + 1) * 384)
        o_own_part = jnp.dot(o_low[...], w, preferred_element_type=jnp.float32)
        unit2[:, cut] = x_own[:, cut].astype(jnp.float32) + o_own_part + vec[:, BO + h * 384 : BO + (h + 1) * 384]

    def norm(hidden_sum):
        mean = jnp.mean(hidden_sum, axis=1, keepdims=True)
        centered = hidden_sum - mean
        inverse = lax.rsqrt(jnp.mean(centered * centered, axis=1, keepdims=True) + EPSILON)
        return centered * inverse, inverse

    unit, inverse = norm(unit2[...])
    unit1[...] = unit
    inv1[...] = jnp.broadcast_to(inverse, (page_len, 128))
    y1 = unit * vector(G1) + vector(E1)
    y1_low[...] = y1.astype(jnp.bfloat16)
    unit2[...] = y1 + vector(B2)
    send_out(unit1, unit1_out)
    send_out(inv1, inv1_out)

    def up_tile(first, h, t):
        start = pl.multiple_of(first + t * UP_TILE, 128)
        w = full["up"].at[h][:, :, :, :, pl.ds(start, UP_TILE)].reshape(width, UP_TILE)
        at = lanes(h * 1536 + start, UP_TILE)
        pre = jnp.dot(y1_low[...], w, preferred_element_type=jnp.float32)
        pre = pre + vec[:, lanes(B1 + h * 1536 + start, UP_TILE)]
        half = 0.5 + 0.5 * lax.erf(pre * (2.0**-0.5))
        hidden[:, at] = (pre * half).astype(jnp.bfloat16)
        bell = jnp.exp(pre * pre * -0.5) * ((2.0 * math.pi) ** -0.5)
        slope[:, at] = (half + pre * bell).astype(jnp.bfloat16)

    clock.point()
    for g, (name, cut, _) in enumerate(groups):
        if name == "up":
            need(g)
            tiles = cut[3] // UP_TILE

            def up_body(i, carry, first=cut[2], tiles=tiles):
                up_tile(first, lax.div(i, tiles), lax.rem(i, tiles))
                return carry

            lax.fori_loop(0, 2 * tiles, up_body, 0)
            clock.point()
    send_out(hidden, g_out)
    send_out(slope, d_out)
    weight_out("up")

    for g, (name, cut, _) in enumerate(groups):
        if name == "down":
            need(g)
            first, count = cut[2], cut[3]
            columns = (ALL,) * 4 + window(cut)
            send_out(full["down"].at[columns], full_out["down"].at[columns])

            both = jnp.dot(
                hidden[...], columns_of("down", first, count), preferred_element_type=jnp.float32
            )
            for h in range(2):
                at = slice(h * 384 + first, h * 384 + first + count)
                unit2[:, at] += both[:, h * count : (h + 1) * count]
            clock.point()
    clock.upto(*(tuple(event) for _, *event in GATHER_EVENTS))
    swap(1, cotangent, ct_own, True).wait_recv()
    keep(1, cotangent, ct_own).wait()
    unit, inverse = norm(unit2[...])
    y1_low[...] = (unit * vector(G2) + vector(E2)).astype(jnp.bfloat16)
    send_out(y1_low, low_out)
    seed = ct_own[...].astype(jnp.float32)
    d_h2 = norm_back(seed, unit, inverse, vector(G2))
    unit2[...] = d_h2
    send_out(unit2, unit2_out)
    d_f = d_h2.astype(jnp.bfloat16)
    ct_own[...] = d_f
    send_out(ct_own, ct_out)
    for n, value in enumerate((d_f, seed * unit, seed)):
        vec[:, SUMS + n * width : SUMS + (n + 1) * width] = total(value)
    send_out(vec, vec_out)

    gather.sends.left(gather.copy)
    for k in range(1, 4):
        vector_z(k).wait_send()
    vector_y().wait_send()
    vector_x().wait_send()
    vector_c().wait_send()
    box_swap.wait_send()
    swap(0, tokens, x_own).wait_send()
    swap(1, cotangent, ct_own).wait_send()
    for copy in outgoing:
        copy.wait()


UP_TILE = 384


def forward_call(tokens, cotangent, boxes, lengths, vectors, shards):
    page_len = tokens.shape[1] * 2
    width = tokens.shape[2]
    groups = GATHER_GROUPS
    count = len(groups)
    full = [jax.ShapeDtypeStruct((2, 4, 2, 2) + s.shape, jnp.bfloat16) for s in shards]
    low, single = jnp.bfloat16, jnp.float32
    kinds = dict(
        x=((page_len, width), low),
        ct=((page_len, width), low),
        qkv=((page_len, 3 * width), low),
        table=((2, page_len, 2 * FREQ), single),
        p=((HEADS // 2, 2, page_len, page_len), low),
        o=((page_len, width), single),
        unit1=((page_len, width), single),
        inv1=((page_len, 128), single),
        g=((page_len, 4 * width), low),
        d=((page_len, 4 * width), low),
        unit2=((page_len, width), single),
        low=((page_len, width), low),
        vec=((1, SUMS + 3 * width), single),
    )
    outs = full + [jax.ShapeDtypeStruct(*kinds[k]) for k in kinds]
    anywhere = pl.BlockSpec(memory_space=pl.ANY)
    vmem = pl.BlockSpec(memory_space=pltpu.VMEM)
    smem = pl.BlockSpec(memory_space=pltpu.SMEM)
    dma = pltpu.SemaphoreType.DMA
    scratch = [pltpu.VMEM(f.shape, f.dtype) for f in full]
    scratch += [
        pltpu.VMEM((page_len, width), low),
        pltpu.VMEM((page_len, width), low),
        pltpu.VMEM(boxes.shape, jnp.int32),
        pltpu.VMEM((2, 4, 2, 2, 1, 384), single),
        pltpu.VMEM((1, SUMS + 3 * width), single),
        pltpu.VMEM((page_len, 3 * width), low),
        pltpu.VMEM((2, page_len, 2 * FREQ), single),
        pltpu.VMEM((BOX_DIM, page_len), low),
        pltpu.VMEM((width, BOX_DIM), low),
        pltpu.VMEM((2, 2, page_len, page_len), low),
        pltpu.VMEM((page_len, width), single),
        pltpu.VMEM((page_len, width), low),
        pltpu.VMEM((page_len, width), single),
        pltpu.VMEM((page_len, 128), single),
        pltpu.VMEM((page_len, width), low),
        pltpu.VMEM((page_len, 4 * width), low),
        pltpu.VMEM((page_len, 4 * width), low),
        pltpu.VMEM((page_len, width), single),
    ]
    arrivals = len(semaphore_table(groups, 3)) + len(core_table(groups))
    scratch += [dma((SENDS,)), dma((arrivals,))]
    scratch += [dma((count,))]
    scratch += [dma((3,))] * 2 + [dma((2,))] * 2 + [dma((1,))] * 2
    scratch += [dma((3,))] * 2 + [dma((3,)), dma((2,)), dma((20,))]
    scratch += [pltpu.VMEM((1, 3 * width), single), pltpu.VMEM((1, 384), single)]
    plan = (groups, page_len, width)
    results = pl.pallas_call(
        partial(forward_kernel, plan),
        out_shape=outs,
        in_specs=[anywhere, anywhere, vmem, smem, vmem] + [anywhere] * 5,
        out_specs=[anywhere] * len(outs),
        scratch_shapes=scratch,
        compiler_params=pltpu.CompilerParams(
            collective_id=0, has_side_effects=True, vmem_limit_bytes=VMEM_LIMIT
        ),
    )(tokens, cotangent, boxes, lengths, vectors, *shards)
    return dict(zip(WEIGHTS, results[:5])), dict(zip(kinds, results[5:]))


VMEM_LIMIT = 60 * 2**20


def landing_shape(path, hop, piece):
    sizes = dict(y=2, z=4, x=2)
    to_come = [sizes[axis] for axis in "yzx" if axis in path[hop + 1 :]]
    return (4 if path[hop] == "z" else 1, *to_come, piece[1], piece[3])


THIRDS = ((0, 1, 2), (1, 0, 2))


class Scatter:
    def __init__(self, place, groups, stored, c_land, landing, summed, sems, c_sems):
        self.place, self.groups, self.stored, self.summed = place, groups, stored, summed
        self.c_land, self.landing = c_land, landing
        self.sems, self.c_sems = sems, c_sems
        self.table = semaphore_table(groups, 4)
        self.sends = Sends(place, SCATTER_EVENTS, self.started)
        self.sent = set()

    def started(self, g, part, step):
        if g < 0 or step == 3:
            return []
        if step >= 10:
            return [((g, part, step - 10, 1), "inner")]
        out = []
        for other in range(len(self.groups[g][-1])) if step == 0 else (part,):
            if self.groups[g][-1][other][0][step] != "z":
                out.append(((g, other, step, 0), "all"))
                continue
            out.append(((g, other, step, 3), "end"))
            out.append(((g, other, step, "end"), "end"))
            out.append(((g, other, step, 0), "all"))
            out.append(((g, other, step, 2), "inner"))
        return out

    def c_copy(self, g):
        p = self.place
        store, both = self.groups[g][1], self.groups[g][2]
        ref = self.stored[store].at[(ALL, ALL, ALL, 1 - p.c) + window(both)]
        return remote(ref, self.c_land[g], self.c_sems, (g,), p.c_peer)

    def copy(self, g, part, hop, slot):
        p = self.place
        send = self.sends.index[g, part, hop, slot]
        slot = 1 if slot == "end" else slot
        path, piece = self.groups[g][-1][part]
        axis = path[hop]
        at = p.own()
        at.update({later: ALL for later in path[hop + 1 :]})
        if axis == "z":
            at["z"] = (p.near, p.far, p.mirror, p.mirror)[slot]
            peer = (p.near_peer, p.far_peer, p.mirror_peer, p.near_peer)[slot]
        else:
            at[axis] = 1 - at[axis]
            peer = p.x_peer if axis == "x" else p.y_peer
        ref = self.stored[self.groups[g][1]].at[(at["y"], at["z"], at["x"], p.c) + window(piece)]
        land = self.landing[g][part][hop].at[slot]
        at = self.table[g, part, hop, slot]
        return remote(ref, land, self.sems, (at,), peer, (send,))

    def add(self, g, part, hop, slots, place_z=None):
        p = self.place
        name, store, both, result, parts = self.groups[g]
        store = self.stored[store]
        path, piece = ("yzx", both) if hop < 0 else parts[part]
        cut = window(piece)
        sizes = dict(y=2, z=4, x=2)
        to_come = [axis for axis in "yzx" if axis in path[hop + 1 :]]
        count = math.prod(sizes[axis] for axis in to_come)
        land = self.c_land[g] if hop < 0 else self.landing[g][part][hop]

        def block(i):
            at = p.own()
            if place_z is not None:
                at["z"] = place_z
            inner = []
            for axis in to_come[::-1]:
                at[axis] = lax.rem(i, sizes[axis])
                i = lax.div(i, sizes[axis])
                inner.insert(0, at[axis])
            here = (at["y"], at["z"], at["x"], p.c) + cut
            arrived = [land[tuple(inner)] if hop < 0 else land[(slot, *inner)] for slot in slots]
            if len(arrived) == 1 and not (hop == 2 and place_z is None):
                return here, store[here] + arrived[0]
            value = store[here].astype(jnp.float32)
            for other in arrived:
                value = value + other.astype(jnp.float32)
            return here, value

        if hop == 2 and place_z is None:
            _, value = block(0)
            top, height, first, size = piece
            if name == "qkv":
                third = jnp.where(p.y == 0, THIRDS[0][result], THIRDS[1][result])
                self.summed[name][:, lanes(first + 384 * third, size)] = value
                return
            top, first = top - both[0] + result[0], first - both[2] + result[2]
            self.summed[name][top : top + height, first : first + size] = value
            return

        together = min(count, 4)

        def body(i, carry):
            for k in range(together):
                here, value = block(i * together + k)
                store[here] = value.astype(jnp.bfloat16)
            return carry

        lax.fori_loop(0, count // together, body, 0)

    def begin(self, g):
        self.c_copy(g).start()

    def start(self, g, part, hop):
        p = self.place
        if self.groups[g][-1][part][0][hop] != "z":
            self.sends.start(self.copy, g, part, hop, 0)
            return

        @pl.when(p.end)
        def _():
            self.sends.start(self.copy, g, part, hop, 3)
            self.sends.start(self.copy, g, part, hop, "end")

        self.sends.start(self.copy, g, part, hop, 0)

        @pl.when(p.inner)
        def _():
            self.sends.start(self.copy, g, part, hop, 2)

    def relay(self, g, part, hop):
        p = self.place

        @pl.when(p.inner)
        def _():
            self.copy(g, part, hop, 3).wait_recv()
            self.add(g, part, hop, (3,), p.far)
            self.sends.start(self.copy, g, part, hop, 1)

    def finish(self, g, part, hop):
        p = self.place
        self.copy(g, part, hop, 0).wait_recv()
        if self.groups[g][-1][part][0][hop] != "z":
            self.add(g, part, hop, (0,))
            return
        self.copy(g, part, hop, 1).wait_recv()

        @pl.when(p.inner)
        def _():
            self.copy(g, part, hop, 2).wait_recv()
            self.add(g, part, hop, (0, 1, 2))

        @pl.when(p.end)
        def _():
            self.add(g, part, hop, (0, 1))

    def step(self, g, part, step):
        if step >= 10:
            self.relay(g, part, step - 10)
            return
        if step == 0:
            self.c_copy(g).wait_recv()
            self.add(g, 0, -1, (0,))
            for part in range(len(self.groups[g][-1])):
                self.start(g, part, 0)
            return
        self.finish(g, part, step - 1)
        if step < 3:
            self.start(g, part, step)

    def left(self, chosen, now=None):
        for g in chosen:
            if g not in self.sent:
                self.sent.add(g)
                self.c_copy(g).wait_send()
        self.sends.left(self.copy, now, lambda key: key[0] in chosen)


def backward_kernel(plan, *refs):
    groups, page_len, width = plan
    block = page_len // 2
    refs = iter(refs)
    take = lambda n: [next(refs) for _ in range(n)]
    w_in = dict(zip(WEIGHTS, take(5)))
    (x_in, ct_in, qkv_in, table_in, p_in, o_in, unit1_in, inv1_in) = take(8)
    (g_in, d_in, unit2_in, low_in, vec_in) = take(5)
    out_out, dx_out = take(2)
    grad_out = dict(zip(WEIGHTS, take(5)))
    (piece_out,) = take(1)
    stored = dict(zip(("box", "out", "up", "down"), take(4)))
    count = len(groups)
    c_land = take(count)
    landing = [[take(3) for _ in group[-1]] for group in groups]
    summed = dict(zip(WEIGHTS, take(5)))
    w_box, w_out, box_w, box_g = take(4)
    (ct, qkv, table, keys, o_own, unit1, inv1, hidden, slope, unit2, out_low, vec) = take(12)
    (y1_low, d_a, d_mixed, dx_low, vec_g) = take(5)
    pieces, pc_land, py_land, px_land, pz_land, piece_sum = take(6)
    w_sems, c_sems = take(2), take(2)
    v_sems, vz_sems, ex_sems = take(2), take(2), take(2)
    in_sem, p_sem, out_sem = take(3)

    place = Place()
    y, z, x, c = place.y, place.z, place.x, place.c
    scatter = Scatter(place, groups, stored, c_land, landing, summed, w_sems, c_sems)

    sources = dict(
        unit2=(unit2_in, unit2),
        ct=(ct_in, ct),
        low=(low_in, out_low),
        vec=(vec_in, vec),
        g=(g_in, hidden),
        d=(d_in, slope),
        unit1=(unit1_in, unit1),
        inv1=(inv1_in, inv1),
        w_out=(w_in["out"], w_out),
        w_box=(w_in["box"], w_box),
        o=(o_in, o_own),
        qkv=(qkv_in, qkv),
        table=(table_in, table),
        x=(x_in, y1_low),
    )
    order = list(sources)

    def fetch(name):
        source, target = sources[name]
        return pltpu.make_async_copy(source, target, in_sem.at[order.index(name)])

    def fetch_weight(name, target):
        at = len(order) + ("down", "up", "qkv").index(name)
        return pltpu.make_async_copy(w_in[name], target, in_sem.at[at])

    def vector(start, size=width):
        return vec[:, start : start + size]

    names = [group[0] for group in groups]

    def event(g, part, step):
        if g == -2 and step == 3:
            dx_swap.wait_recv()
            unit2[0:block, :] = dx_low[1].astype(jnp.float32)
            dx_other.start()
        elif g == -2:
            vector_step(step)
        elif g < 0:
            fetch("low").wait()
            out_swap.start()
            out_keep.start()
        else:
            scatter.step(g, part, step)
            if (g, part, step) in last:
                result_copy(names[g]).start()

    ends = {}
    for _, g, part, step in SCATTER_EVENTS:
        if g >= 0 and step == 3:
            ends[names[g]] = (g, part, step)
    last = set(ends.values())

    def result_copy(name):
        at = 4 + WEIGHTS.index(name)
        return pltpu.make_async_copy(summed[name], grad_out[name], out_sem.at[at])

    clock = Clock(SCATTER_EVENTS, event, set())

    def begin(g):
        clock.begun.add(g)
        scatter.begin(g)

    for name in ("ct", "g", "vec"):
        fetch(name).start()
    place.hail()

    fetch("ct").wait()
    d_f = ct
    fetch("vec").wait()
    for n, start in enumerate((B2, G2, E2)):
        vec_g[:, start : start + width] = vec[:, SUMS + n * width : SUMS + (n + 1) * width]

    def rows(at):
        return pl.ds(pl.multiple_of(at * block, block), block)

    out_swap = remote(out_low.at[rows(1 - y)], out_out.at[y], ex_sems, (0,), place.y_peer)
    out_keep = pltpu.make_async_copy(out_low.at[rows(y)], out_out.at[y], out_sem.at[0])
    dx_other = pltpu.make_async_copy(unit2.at[0:block], dx_out.at[1 - y], out_sem.at[2])
    dx_swap = remote(dx_low.at[0], dx_low.at[1], ex_sems, (1,), place.y_peer)

    def with_down(w_down):
        fetch_weight("down", w_down).start()
        fetch("g").wait()

        for name in ("d", "unit2", "low", "unit1", "inv1", "w_out", "o", "w_box", "qkv", "table"):
            fetch(name).start()

        def down_grads(first, size):
            left = d_f[:, first : first + size]
            right = d_f[:, 384 + first : 384 + first + size]
            both = jnp.concatenate([left, right], axis=1)

            def grad_tile(t, carry):
                part = dot_n(hidden[:, lanes(t * width, width)], both).astype(jnp.bfloat16)
                for h in range(2):
                    stored["down"][h, t, :, :, :, first : first + size] = part[
                        :, h * size : (h + 1) * size
                    ].reshape(2, 2, -1, size)
                return carry

            lax.fori_loop(0, 4, grad_tile, 0)
            if first == 0:
                place.meet()
            for g, group in enumerate(groups):
                if group[0] == "down" and first <= group[2][2] < first + size:
                    begin(g)
            clock.point()

        down_grads(0, 128)
        down_grads(128, 256)
        fetch_weight("down", w_down).wait()
        fetch("d").wait()

        def slope_tile(t, carry, serve):
            w0 = w_down.at[0, t][...].reshape(width, 384)
            w1 = w_down.at[1, t][...].reshape(width, 384)
            d_hidden = dot_t(d_f[...], jnp.concatenate([w0, w1], axis=1))
            at = lanes(t * width, width)
            d_pre = (d_hidden * slope[:, at].astype(jnp.float32)).astype(jnp.bfloat16)
            slope[:, at] = d_pre
            vec_g[:, lanes(B1 + t * width, width)] = total(d_pre)
            return carry

        clock.loop(4, slope_tile)

    pl.run_scoped(with_down, pltpu.VMEM(w_in["down"].shape, jnp.bfloat16))

    fetch("unit1").wait()
    fetch("inv1").wait()
    fetch("unit2").wait()
    y1_low[...] = (unit1[...] * vector(G1) + vector(E1)).astype(jnp.bfloat16)

    def with_up(w_up):
        fetch_weight("up", w_up).start()

        def up_tile(i, carry, serve, part):
            tile = dot_n(y1_low[...], slope[:, lanes(i * 1536 + part * width, width)])
            stored["up"][i, :, :, :, :, part * width : (part + 1) * width] = tile.astype(
                jnp.bfloat16
            ).reshape(4, 2, 2, -1, width)
            return carry

        for part in range(2):
            clock.loop(2, partial(up_tile, part=part))
            for g, group in enumerate(groups):
                if group[0] == "up" and group[2][2] // width == part:
                    begin(g)
        fetch_weight("up", w_up).wait()

        def back_tile(h, carry, serve):
            w = w_up.at[h][...].reshape(width, 1536)
            unit2[...] += dot_t(slope[:, lanes(h * 1536, 1536)], w)
            return carry

        clock.loop(2, back_tile)

    pl.run_scoped(with_up, pltpu.VMEM(w_in["up"].shape, jnp.bfloat16))

    x_own = y1_low
    fetch("x").start()
    unit = unit1[...]
    d_y1 = unit2[...]
    vec_g[:, G1 : G1 + width] = total(d_y1 * unit)
    vec_g[:, E1 : E1 + width] = total(d_y1)
    d_h1 = norm_back(d_y1, unit, inv1[:, 0:1], vector(G1))
    unit1[...] = d_h1
    d_a[...] = d_h1.astype(jnp.bfloat16)
    vec_g[:, BO : BO + width] = total(d_a[...])
    fetch("w_out").wait()
    fetch("o").wait()
    both = jnp.concatenate([w_out.at[h][...].reshape(width, 384) for h in range(2)], axis=1)
    d_mixed[...] = dot_t(d_a[...], both).astype(jnp.bfloat16)
    part = dot_n(o_own[...].astype(jnp.bfloat16), d_a[...]).astype(jnp.bfloat16)
    for h in range(2):
        stored["out"][h] = part[:, h * 384 : (h + 1) * 384].reshape(4, 2, 2, -1, 384)
    begin(names.index("out"))
    clock.point()

    for name in ("w_box", "qkv", "table", "x"):
        fetch(name).wait()
    low = w_box.at[0][...].reshape(width, 2 * FREQ)
    high = w_box.at[1][...].reshape(width, 2 * FREQ)
    box_w[...] = jnp.concatenate(
        [low[:, :FREQ], high[:, :FREQ], low[:, FREQ:], high[:, FREQ:]], axis=1
    ).T
    keys[:, : 2 * FREQ] = table[0].astype(jnp.bfloat16)
    keys[:, 2 * FREQ :] = table[1].astype(jnp.bfloat16)
    table[...] = table[...] * (HEAD**-0.5)
    head_lane = lax.broadcasted_iota(jnp.int32, (1, 128), 1)

    def p_copy(p, slot, i):
        at = lanes((slot * 2 + i) * page_len, page_len)
        return pltpu.make_async_copy(p_in.at[p, i], hidden.at[:, at], p_sem.at[slot, i])

    p_copy(0, 0, 0).start()
    p_copy(0, 0, 1).start()

    vector_c = remote(pieces.at[:, :, :, 1 - c], pc_land, v_sems, (0,), place.c_peer)
    vector_y = remote(pieces.at[1 - y, :, :, c], py_land, v_sems, (1,), place.y_peer)
    vector_x = remote(pieces.at[y, :, 1 - x, c], px_land, v_sems, (2,), place.x_peer)

    def vector_z(k):
        there = lax.rem(z + k + 1, 4)
        peer = (there * 4 + x * 2 + c, y)
        return remote(pieces.at[y, there, x, c], pz_land.at[k], vz_sems, (k,), peer)

    def vector_step(step):
        if step == 0:
            vector_c.wait_recv()
            pieces[:, :, :, c] += pc_land[...]
            vector_y.start()
        if step == 1:
            vector_y.wait_recv()
            pieces[y, :, :, c] += py_land[...]
            vector_x.start()
        if step == 2:
            vector_x.wait_recv()
            pieces[y, :, x, c] += px_land[...]
            for k in range(3):
                vector_z(k).start()

    def with_qkv(w_qkv, early):
        stored["early"] = early
        fetch_weight("qkv", w_qkv).start()

        def pair(p, carry, serve):
            slot = lax.rem(p, 2)

            @pl.when(p < HEADS // 2 - 1)
            def _():
                p_copy(p + 1, 1 - slot, 0).start()
                p_copy(p + 1, 1 - slot, 1).start()

            p_copy(p, slot, 0).wait()
            p_copy(p, slot, 1).wait()
            q_t = qkv[:, lanes(p * 128, 128)].T
            k = qkv[:, lanes(width + p * 128, 128)]
            v_t = qkv[:, lanes(2 * width + p * 128, 128)].T
            w_t = box_w[:, lanes(p * 128, 128)]
            d_o = d_mixed[:, lanes(p * 128, 128)]
            d_o_t = d_o.T
            weighted = d_o.astype(jnp.float32) * o_own[:, lanes(p * 128, 128)]
            keys_k = jnp.concatenate([keys[...], k], axis=1)
            grads = []
            for i in range(2):
                if i:
                    serve()
                of_head = (head_lane < HEAD) == (i == 0)
                rows_head = slice(i * HEAD, (i + 1) * HEAD)
                probs = hidden[:, lanes((slot * 2 + i) * page_len, page_len)]
                delta = jnp.sum(jnp.where(of_head, weighted, 0.0), axis=1, keepdims=True)
                d_probs = jnp.dot(
                    jnp.where(of_head, d_o, jnp.zeros_like(d_o)),
                    v_t,
                    preferred_element_type=jnp.float32,
                )
                d_s = (probs.astype(jnp.float32) * (d_probs - delta)).astype(jnp.bfloat16)
                serve()
                d_b = jnp.dot(d_s, keys_k, preferred_element_type=jnp.float32)
                d_1, d_2 = d_b[:, : 2 * FREQ], d_b[:, 2 * FREQ : 4 * FREQ]
                cosine, sine = table[0], table[1]
                d_sine = (d_1 * sine - d_2 * cosine).astype(jnp.bfloat16)
                d_cosine = (d_1 * cosine + d_2 * sine).astype(jnp.bfloat16)
                d_u = jnp.concatenate([d_sine, d_cosine], axis=1)
                d_q = d_b[:, 4 * FREQ :] * (HEAD**-0.5) + jnp.dot(
                    d_u, w_t, preferred_element_type=jnp.float32
                )
                d_w = jnp.dot(q_t[rows_head], d_u, preferred_element_type=jnp.float32)
                box_g[pl.ds(pl.multiple_of(p * 128 + i * HEAD, HEAD), HEAD), :] = d_w.astype(
                    jnp.bfloat16
                )
                d_k = jnp.dot(q_t[rows_head], d_s, preferred_element_type=jnp.float32)
                d_v = jnp.dot(d_o_t[rows_head], probs, preferred_element_type=jnp.float32)
                grads.append((d_q, d_k * (HEAD**-0.5), d_v))
            (q_one, k_one, v_one), (q_two, k_two, v_two) = grads
            d_q = jnp.where(head_lane < HEAD, q_one, q_two).astype(jnp.bfloat16)
            d_k = jnp.concatenate([k_one, k_two], axis=0).astype(jnp.bfloat16).T
            d_v = jnp.concatenate([v_one, v_two], axis=0).astype(jnp.bfloat16).T
            for n, value in enumerate((d_q, d_k, d_v)):
                slope[:, lanes(n * width + p * 128, 128)] = value
            vec_g[:, lanes(BQ + p * 128, 128)] = total(d_q)
            vec_g[:, lanes(BV + p * 128, 128)] = total(d_v)
            return carry

        def qkv_grads(slot):
            store, top = ("early", 0) if slot == 0 else ("down", (slot - 1) * 48)
            for h in range(2):
                first = h * 1152 + THIRDS[h][slot] * 384
                tile = dot_n(x_own[...], slope[:, first : first + 384])
                stored[store][h, :, :, :, top : top + 48, :] = tile.astype(
                    jnp.bfloat16
                ).reshape(4, 2, 2, -1, 384)
            begin([g for g in range(count) if names[g] == "qkv"][slot])

        half = HEADS // 4
        clock.loop(half, pair, 4)
        qkv_grads(0)
        clock.point()
        clock.loop(half, lambda p, carry, serve: pair(p + half, carry, serve), 4)

        for dz in range(4):
            for dx in range(2):
                for dc in range(2):
                    for dy in range(2):
                        device = ((dz * 2 + dx) * 2 + dc) * 2 + dy
                        start = device * (VECTORS // 32) // 128 * 128
                        pieces[dy, dz, dx, dc] = vec_g[:, start : start + 384]
        vector_c.start()
        part = box_g[...]
        stored["box"][0] = jnp.concatenate(
            [part[:, :FREQ], part[:, 2 * FREQ : 3 * FREQ]], axis=1
        ).reshape(4, 2, 2, -1, 384)
        stored["box"][1] = jnp.concatenate(
            [part[:, FREQ : 2 * FREQ], part[:, 3 * FREQ :]], axis=1
        ).reshape(4, 2, 2, -1, 384)
        begin(names.index("box"))
        clock.point()
        clock.upto(*[
            (g, part, 3)
            for g, group in enumerate(groups)
            if names[g] == "down"
            for part in range(len(group[-1]))
        ])
        scatter.left([g for g in range(count) if names[g] == "down"], clock.at)

        for slot in (1, 2):
            qkv_grads(slot)
            clock.point()

        fetch_weight("qkv", w_qkv).wait()

        def back_tile(h, carry, serve):
            w = w_qkv.at[h][...].reshape(width, 1152)
            unit1[...] += dot_t(slope[:, lanes(h * 1152, 1152)], w)
            return carry

        clock.loop(2, back_tile)
        dx_low[0] = unit1[rows(1 - y), :].astype(jnp.bfloat16)
        dx_swap.start()
        pltpu.make_async_copy(unit1.at[rows(y)], dx_out.at[y], out_sem.at[1]).start()

        clock.point()
        clock.point()
        clock.upto(*(tuple(event) for _, *event in SCATTER_EVENTS))
        for k in range(3):
            vector_z(k).wait_recv()
        piece_total = pieces[y, z, x, c]
        for k in range(3):
            piece_total = piece_total + pz_land[k]
        piece_sum[...] = piece_total
        piece_copy = pltpu.make_async_copy(piece_sum, piece_out, out_sem.at[3])
        piece_copy.start()
        scatter.left(range(count))
        for copy in (vector_c, vector_y, vector_x, out_swap, dx_swap):
            copy.wait_send()
        for k in range(3):
            vector_z(k).wait_send()
        out_swap.wait_recv()
        out_keep.wait()
        pltpu.make_async_copy(unit1.at[rows(y)], dx_out.at[y], out_sem.at[1]).wait()
        dx_other.wait()
        piece_copy.wait()
        for name in WEIGHTS:
            result_copy(name).wait()

    pl.run_scoped(
        with_qkv,
        pltpu.VMEM(w_in["qkv"].shape, jnp.bfloat16),
        pltpu.VMEM(stored["box"].shape, jnp.bfloat16),
    )


def backward_call(full, kept, shards):
    low, single = jnp.bfloat16, jnp.float32
    page_len, width = kept["x"].shape
    groups = SCATTER_GROUPS
    count = len(groups)
    outs = [
        jax.ShapeDtypeStruct((2, page_len // 2, width), low),
        jax.ShapeDtypeStruct((2, page_len // 2, width), single),
    ]
    outs += [jax.ShapeDtypeStruct(s.shape, single) for s in shards]
    outs += [jax.ShapeDtypeStruct((1, 384), single)]
    by_name = dict(zip(WEIGHTS, shards))

    def vmem(*shape, kind=low):
        return pltpu.VMEM(shape, kind)

    size = lambda cut: (cut[1], cut[3])
    dma = pltpu.SemaphoreType.DMA
    scratch = [vmem(2, 4, 2, 2, *by_name[n].shape) for n in ("box", "out", "up", "down")]
    scratch += [vmem(2, 4, 2, *size(g[2])) for g in groups]
    for group in groups:
        for path, piece in group[-1]:
            scratch += [vmem(*landing_shape(path, hop, piece)) for hop in range(3)]
    scratch += [vmem(*s.shape, kind=single) for s in shards]
    scratch += [vmem(*full[n].shape) for n in ("box", "out")]
    scratch += [vmem(width, BOX_DIM), vmem(width, BOX_DIM)]
    scratch += [vmem(*kept[n].shape, kind=kept[n].dtype) for n in ("ct", "qkv", "table")]
    scratch += [vmem(page_len, BOX_DIM)]
    scratch += [
        vmem(*kept[n].shape, kind=kept[n].dtype)
        for n in ("o", "unit1", "inv1", "g", "d", "unit2", "low", "vec")
    ]
    scratch += [vmem(page_len, width)] * 3
    scratch += [vmem(2, page_len // 2, width), vmem(1, VECTORS + 128, kind=single)]
    scratch += [
        vmem(2, 4, 2, 2, 1, 384, kind=single),
        vmem(2, 4, 2, 1, 384, kind=single),
        vmem(4, 2, 1, 384, kind=single),
        vmem(4, 1, 384, kind=single),
        vmem(3, 1, 384, kind=single),
        vmem(1, 384, kind=single),
    ]
    scratch += [dma((SENDS,)), dma((len(semaphore_table(groups, 4)),))] + [dma((count,))] * 2
    scratch += [dma((3,))] * 2 + [dma((3,))] * 2 + [dma((2,))] * 2
    scratch += [dma((17,)), dma((2, 2)), dma((9,))]
    anywhere = pl.BlockSpec(memory_space=pl.ANY)
    operands = [full[n] for n in WEIGHTS] + list(kept.values())
    plan = (groups, page_len, width)
    results = pl.pallas_call(
        partial(backward_kernel, plan),
        out_shape=outs,
        in_specs=[anywhere] * len(operands),
        out_specs=[anywhere] * len(outs),
        scratch_shapes=scratch,
        compiler_params=pltpu.CompilerParams(
            collective_id=1, has_side_effects=True, vmem_limit_bytes=VMEM_BACK
        ),
    )(*operands)
    return results


VMEM_BACK = 63 * 2**20


def finish_kernel(*refs):
    count = len(refs) // 2
    ins, outs = refs[:count], refs[count:]
    for i in range(count - 1):
        outs[i][...] = ins[i][...]
    rows = jnp.broadcast_to(ins[-1][...], (8, 384))
    rows = pltpu.roll(rows, 384 - Place().vector_offset(), 1)
    outs[-1][...] = rows[0:1, : VECTORS // 32].reshape(VECTORS // 32)


def finish_call(results):
    outs = [jax.ShapeDtypeStruct(r.shape, r.dtype) for r in results[:-1]]
    outs += [jax.ShapeDtypeStruct((VECTORS // 32,), jnp.float32)]

    def half(shape):
        block = (shape[0] // 2,) + shape[1:]
        return pl.BlockSpec(block, lambda i: (i,) + (0,) * (len(shape) - 1))

    halves = [half(r.shape) for r in results[:-1]]
    return pl.pallas_call(
        finish_kernel,
        out_shape=outs,
        grid=(2,),
        in_specs=halves + [pl.BlockSpec((1, 384), lambda i: (0, 0))],
        out_specs=halves + [pl.BlockSpec((VECTORS // 32,), lambda i: (0,))],
        compiler_params=pltpu.CompilerParams(vmem_limit_bytes=VMEM_BACK),
    )(*results)


def fast_layer(tokens, boxes, lengths, wqkv, wbox, wout, wup, wdown, vectors, cotangent):
    shards = (wqkv, wbox, wout, wup, wdown)
    full, kept = forward_call(tokens, cotangent, boxes, lengths, vectors, shards)
    return tuple(finish_call(backward_call(full, kept, shards)))


def on_device(*args):
    tokens, wqkv, wbox, wdown = args[0], args[3], args[4], args[7]
    blocks, groups = lax.axis_size("blk"), lax.axis_size("dp")
    fits = (
        blocks == 2
        and groups == 16
        and tokens.shape[0] == 2
        and wqkv.shape == (48, 1152)
        and wdown.shape == (192, 384)
        and wbox.shape == (48, 2 * FREQ)
    )
    return fast_layer(*args) if fits else general_layer(*args)


def solution(mesh):
    in_specs = (
        P("dp", "blk", None),
        P(None, "dp", "blk"),
        P("dp"),
        P("dp", "blk"),
        P("dp", "blk"),
        P("dp", "blk"),
        P("dp", "blk"),
        P("dp", "blk"),
        P(("dp", "blk")),
        P("dp", "blk", None),
    )
    out_specs = (
        P("dp", "blk", None),
        P("dp", "blk", None),
        P("dp", "blk"),
        P("dp", "blk"),
        P("dp", "blk"),
        P("dp", "blk"),
        P("dp", "blk"),
        P(("dp", "blk")),
    )
    return jax.shard_map(
        on_device, mesh=mesh, in_specs=in_specs, out_specs=out_specs, check_vma=False
    )
```

```python
from functools import partial
import math

import jax
import jax.numpy as jnp
import numpy as np
from jax import lax
from jax.experimental import pallas as pl
from jax.experimental.pallas import tpu as pltpu
from jax.sharding import PartitionSpec as P

HEADS = 12
HEAD = 64
FREQ = 192
BOX_DIM = 768

EPSILON = 1e-12
MASKED = -1e30


def box_table(boxes):
    frequency = jnp.exp(jnp.arange(FREQ, dtype=jnp.float32) * (-math.log(10000.0) / FREQ))
    across = boxes[0].astype(jnp.float32)[..., None] * frequency
    upward = boxes[1].astype(jnp.float32)[..., None] * frequency
    return jnp.concatenate(
        [jnp.cos(across), jnp.sin(across), jnp.cos(upward), jnp.sin(upward)], axis=-1
    )


def rotate(coeffs, own_table):
    cos_across, sin_across, cos_upward, sin_upward = jnp.split(own_table[..., None, :], 4, axis=-1)
    sa, ca, sb, cb = jnp.split(coeffs, 4, axis=-1)
    return jnp.concatenate(
        [
            sa * sin_across + ca * cos_across,
            ca * sin_across - sa * cos_across,
            sb * sin_upward + cb * cos_upward,
            cb * sin_upward - sb * cos_upward,
        ],
        axis=-1,
    )


def unrotate(grad_rows, own_table):
    cos_across, sin_across, cos_upward, sin_upward = jnp.split(own_table[..., None, :], 4, axis=-1)
    d1a, d2a, d1b, d2b = jnp.split(grad_rows, 4, axis=-1)
    return jnp.concatenate(
        [
            d1a * sin_across - d2a * cos_across,
            d1a * cos_across + d2a * sin_across,
            d1b * sin_upward - d2b * cos_upward,
            d1b * cos_upward + d2b * sin_upward,
        ],
        axis=-1,
    )


def normalize(hidden):
    row_mean = jnp.mean(hidden, axis=-1, keepdims=True)
    centered = hidden - row_mean
    inverse = lax.rsqrt(jnp.mean(centered * centered, axis=-1, keepdims=True) + EPSILON)
    return centered * inverse, inverse


def normalize_back(grad, unit, inverse, gain):
    scaled = grad * gain
    mean_grad = jnp.mean(scaled, axis=-1, keepdims=True)
    mean_unit = jnp.mean(scaled * unit, axis=-1, keepdims=True)
    d_hidden = inverse * (scaled - mean_grad - unit * mean_unit)
    return d_hidden, jnp.sum(grad * unit, axis=0), jnp.sum(grad, axis=0)


def unpack(vector_all, model_width, hidden_units):
    cuts = [model_width] * 5 + [hidden_units] + [model_width] * 3
    pieces = []
    offset = 0
    for length_here in cuts:
        pieces.append(vector_all[offset : offset + length_here])
        offset = offset + length_here
    return pieces


def dot32(a, b):
    return jnp.dot(a, b, preferred_element_type=jnp.float32)


def gather_weight(shard):
    part = lax.all_gather(shard, "blk", axis=1, tiled=True)
    return lax.all_gather(part, "dp", axis=0, tiled=True)


def scatter_weight(grad):
    part = lax.psum_scatter(grad.astype(jnp.bfloat16), "dp", scatter_dimension=0, tiled=True)
    return lax.psum_scatter(part, "blk", scatter_dimension=1, tiled=True).astype(jnp.float32)


def general_layer(tokens, boxes, lengths, wqkv, wbox, wout, wup, wdown, vectors, cotangent):
    blocks = lax.axis_size("blk")
    pages_here = tokens.shape[0] // blocks
    model_width = tokens.shape[2]
    to_pages = partial(
        lax.all_to_all, axis_name="blk", split_axis=0, concat_axis=1, tiled=True
    )
    from_pages = partial(
        lax.all_to_all, axis_name="blk", split_axis=1, concat_axis=0, tiled=True
    )
    page_tokens = to_pages(tokens)
    page_boxes = lax.all_to_all(boxes, "blk", split_axis=1, concat_axis=2, tiled=True)
    page_lengths = lax.dynamic_slice(lengths, (lax.axis_index("blk") * pages_here,), (pages_here,))
    full_qkv = gather_weight(wqkv)
    full_box = gather_weight(wbox)
    full_out = gather_weight(wout)
    full_up = gather_weight(wup)
    full_down = gather_weight(wdown)
    full_vec = lax.all_gather(vectors, ("dp", "blk"), axis=0, tiled=True).astype(jnp.float32)
    page_cotangent = to_pages(cotangent)
    hidden_units = full_up.shape[1]
    bq, bv, bo, g1, e1, b1, b2, g2, e2 = unpack(full_vec, model_width, hidden_units)
    page_len = page_tokens.shape[1]
    score_scale = HEAD ** (-0.5)

    x = page_tokens.reshape(-1, model_width)
    projected = dot32(x, full_qkv)
    head_shape = (pages_here, page_len, HEADS, HEAD)
    q = (projected[:, :model_width] + bq).astype(jnp.bfloat16).reshape(head_shape)
    k = projected[:, model_width : 2 * model_width].astype(jnp.bfloat16).reshape(head_shape)
    v = (projected[:, 2 * model_width :] + bv).astype(jnp.bfloat16).reshape(head_shape)
    table = box_table(page_boxes)
    box_heads = full_box.reshape(HEADS, HEAD, BOX_DIM)
    coeffs = jnp.einsum("pqhd,hdc->pqhc", q, box_heads, preferred_element_type=jnp.float32)
    box_query = rotate(coeffs, table).astype(jnp.bfloat16)
    box_keys = table.astype(jnp.bfloat16)
    scores = (
        jnp.einsum("pqhd,pkhd->phqk", q, k, preferred_element_type=jnp.float32)
        + jnp.einsum("pqhc,pkc->phqk", box_query, box_keys, preferred_element_type=jnp.float32)
    ) * score_scale
    is_valid = (jnp.arange(page_len)[None, :] < page_lengths[:, None])[:, None, None, :]
    masked = jnp.where(is_valid, scores, MASKED)
    probs = jax.nn.softmax(masked, axis=-1)
    probs_low = probs.astype(jnp.bfloat16)
    mixed = jnp.einsum("phqk,pkhd->pqhd", probs_low, v, preferred_element_type=jnp.float32)
    mixed_low = mixed.astype(jnp.bfloat16).reshape(-1, model_width)
    unit1, inv1 = normalize(x.astype(jnp.float32) + dot32(mixed_low, full_out) + bo)
    y1 = unit1 * g1 + e1
    y1_low = y1.astype(jnp.bfloat16)
    pre = dot32(y1_low, full_up) + b1
    hidden = jax.nn.gelu(pre, approximate=False).astype(jnp.bfloat16)
    unit2, inv2 = normalize(y1 + dot32(hidden, full_down) + b2)
    output = (unit2 * g2 + e2).astype(jnp.bfloat16)

    seed = page_cotangent.reshape(-1, model_width).astype(jnp.float32)
    d_h2, d_g2, d_e2 = normalize_back(seed, unit2, inv2, g2)
    d_f = d_h2.astype(jnp.bfloat16)
    d_hidden = dot32(d_f, full_down.T)
    d_pre = jax.vjp(partial(jax.nn.gelu, approximate=False), pre)[1](d_hidden)[0]
    d_pre = d_pre.astype(jnp.bfloat16)
    d_wdown = dot32(hidden.T, d_f)
    d_wup = dot32(y1_low.T, d_pre)
    d_y1 = dot32(d_pre, full_up.T) + d_h2
    d_h1, d_g1, d_e1 = normalize_back(d_y1, unit1, inv1, g1)
    d_a = d_h1.astype(jnp.bfloat16)
    d_wout = dot32(mixed_low.T, d_a)
    d_mixed = dot32(d_a, full_out.T).astype(jnp.bfloat16).reshape(head_shape)
    row_delta = jnp.einsum("pqhd,pqhd->phq", d_mixed.astype(jnp.float32), mixed)
    d_probs = jnp.einsum("pqhd,pkhd->phqk", d_mixed, v, preferred_element_type=jnp.float32)
    d_raw = (probs * (d_probs - row_delta[..., None])).astype(jnp.bfloat16)
    d_q = jnp.einsum("phqk,pkhd->pqhd", d_raw, k, preferred_element_type=jnp.float32)
    d_box_q = jnp.einsum("phqk,pkc->pqhc", d_raw, box_keys, preferred_element_type=jnp.float32)
    d_k = jnp.einsum("phqk,pqhd->pkhd", d_raw, q, preferred_element_type=jnp.float32)
    d_v = jnp.einsum("phqk,pqhd->pkhd", probs_low, d_mixed, preferred_element_type=jnp.float32)
    d_coeffs = unrotate(d_box_q * score_scale, table).astype(jnp.bfloat16)
    d_q = d_q * score_scale + jnp.einsum(
        "pqhc,hdc->pqhd", d_coeffs, box_heads, preferred_element_type=jnp.float32
    )
    d_wbox = jnp.einsum("pqhd,pqhc->hdc", q, d_coeffs, preferred_element_type=jnp.float32)
    flat = (-1, model_width)
    d_q = d_q.astype(jnp.bfloat16).reshape(flat)
    d_k = (d_k * score_scale).astype(jnp.bfloat16).reshape(flat)
    d_v = d_v.astype(jnp.bfloat16).reshape(flat)
    d_c = jnp.concatenate([d_q, d_k, d_v], axis=1)
    d_wqkv = dot32(x.T, d_c)
    d_x = dot32(d_c, full_qkv.T) + d_h1
    total = partial(jnp.sum, axis=0, dtype=jnp.float32)
    vector_grad = jnp.concatenate(
        [total(d_q), total(d_v), total(d_a), d_g1, d_e1, total(d_pre), total(d_f), d_g2, d_e2]
    )
    return (
        from_pages(output.reshape(page_tokens.shape)),
        from_pages(d_x.reshape(page_tokens.shape)),
        scatter_weight(d_wqkv),
        scatter_weight(d_wbox.reshape(model_width, BOX_DIM)),
        scatter_weight(d_wout),
        scatter_weight(d_wup),
        scatter_weight(d_wdown),
        lax.psum_scatter(vector_grad, ("dp", "blk"), scatter_dimension=0, tiled=True),
    )


GATHER_GROUPS = (
    ("qkv", (0, 48, 0, 384), (("zxy", (0, 48, 0, 384)),)),
    ("qkv", (0, 48, 384, 384), (("zyx", (0, 48, 384, 256)), ("yzx", (0, 48, 640, 128)),)),
    ("qkv", (0, 48, 768, 384), (("zxy", (0, 48, 768, 384)),)),
    ("box", (0, 48, 0, 384), (("zyx", (0, 48, 0, 256)), ("yzx", (0, 48, 256, 128)),)),
    ("out", (0, 48, 0, 384), (("zxy", (0, 48, 0, 256)), ("yxz", (0, 48, 256, 128)),)),
    ("up", (0, 48, 0, 384), (("zxy", (0, 48, 0, 256)), ("yzx", (0, 48, 256, 128)),)),
    ("up", (0, 48, 384, 384), (("yxz", (0, 48, 384, 384)),)),
    ("up", (0, 48, 768, 384), (("yxz", (0, 48, 768, 384)),)),
    ("up", (0, 48, 1152, 384), (("zxy", (0, 48, 1152, 256)), ("zyx", (0, 48, 1408, 128)),)),
    ("down", (0, 192, 0, 128), (("zxy", (0, 64, 0, 128)), ("yxz", (64, 128, 0, 128)),)),
    ("down", (0, 192, 128, 128), (("zxy", (0, 128, 128, 128)), ("yzx", (128, 64, 128, 128)),)),
    ("down", (0, 192, 256, 128), (("zyx", (0, 192, 256, 128)),)),
)
GATHER_EVENTS = (
    (1, 0, 0, 0),
    (1, 1, 0, 0),
    (1, 2, 0, 0),
    (1, 3, 0, 0),
    (1, 4, 1, 0),
    (1, 0, 0, 10),
    (1, 1, 0, 10),
    (1, 0, 0, 1),
    (1, 8, 0, 0),
    (1, 6, 0, 0),
    (1, 10, 1, 0),
    (1, 3, 1, 0),
    (1, 5, 1, 0),
    (1, 1, 1, 0),
    (1, 2, 0, 10),
    (1, 1, 0, 1),
    (1, 10, 0, 0),
    (2, 3, 0, 10),
    (2, 7, 0, 0),
    (2, 2, 0, 1),
    (3, 4, 0, 0),
    (3, 1, 1, 1),
    (3, 0, 0, 2),
    (3, 4, 1, 1),
    (3, 3, 1, 1),
    (4, 6, 0, 1),
    (4, 4, 0, 10),
    (4, 1, 0, 2),
    (5, 3, 0, 1),
    (5, 5, 0, 0),
    (5, 5, 1, 1),
    (5, 10, 1, 1),
    (6, 1, 1, 11),
    (6, 5, 0, 10),
    (6, 2, 0, 2),
    (7, 4, 0, 1),
    (7, 8, 0, 10),
    (7, 9, 0, 0),
    (7, 9, 1, 0),
    (7, 5, 1, 11),
    (7, 3, 1, 11),
    (8, 1, 1, 2),
    (8, 8, 1, 0),
    (8, 0, 0, 3),
    (9, 9, 0, 10),
    (9, 7, 0, 1),
    (9, 3, 0, 2),
    (9, 3, 1, 2),
    (10, 11, 0, 0),
    (10, 0, 0, 4),
    (10, 4, 1, 2),
    (10, 1, 0, 3),
    (10, 8, 1, 10),
    (10, 9, 0, 1),
    (10, 4, 0, 2),
    (10, 1, 1, 3),
    (10, 10, 1, 11),
    (11, 10, 0, 10),
    (11, 1, 0, 4),
    (11, 11, 0, 10),
    (12, 2, 0, 3),
    (12, 6, 0, 2),
    (12, 1, 1, 4),
    (12, 2, 0, 4),
    (12, 10, 0, 1),
    (13, 5, 0, 1),
    (13, 8, 1, 1),
    (13, 3, 0, 3),
    (14, 5, 1, 2),
    (14, 8, 0, 1),
    (14, 7, 0, 2),
    (14, 10, 1, 2),
    (15, 3, 1, 3),
    (16, 9, 1, 1),
    (16, 11, 0, 1),
    (16, 4, 0, 3),
    (16, 3, 0, 4),
    (17, 9, 0, 2),
    (19, 3, 1, 4),
    (20, 5, 0, 2),
    (20, 4, 1, 12),
    (22, 6, 0, 12),
    (26, 8, 0, 2),
    (26, 8, 1, 2),
    (26, 4, 1, 3),
    (27, 4, 0, 4),
    (27, 5, 1, 3),
    (28, 11, 0, 2),
    (28, 10, 0, 2),
    (29, 10, 1, 3),
    (29, 7, 0, 12),
    (29, 9, 1, 2),
    (32, 5, 0, 3),
    (32, 6, 0, 3),
    (34, 9, 0, 3),
    (34, -1, 0, 0),
    (35, 4, 1, 4),
    (37, 8, 1, 3),
    (39, 9, 1, 12),
    (46, 7, 0, 3),
    (47, 10, 0, 3),
    (51, 8, 0, 3),
    (54, 5, 0, 4),
    (54, 9, 0, 4),
    (55, 6, 0, 4),
    (56, 11, 0, 3),
    (67, 5, 1, 4),
    (71, 7, 0, 4),
    (71, 9, 1, 3),
    (75, 10, 1, 4),
    (78, 11, 0, 4),
    (82, 8, 0, 4),
    (87, 8, 1, 4),
    (88, 9, 1, 4),
    (111, 10, 0, 4),
)
SCATTER_GROUPS = (
    ("down", "down", (0, 192, 0, 128), (0, 192, 0, 128), (("zyx", (0, 64, 0, 128)), ("xzy", (64, 128, 0, 128)),)),
    ("down", "down", (0, 192, 128, 128), (0, 192, 128, 128), (("zxy", (0, 64, 128, 128)), ("yxz", (64, 128, 128, 128)),)),
    ("down", "down", (0, 192, 256, 128), (0, 192, 256, 128), (("yzx", (0, 192, 256, 128)),)),
    ("up", "up", (0, 48, 0, 384), (0, 48, 0, 384), (("xyz", (0, 48, 0, 128)), ("yxz", (0, 48, 128, 256)),)),
    ("up", "up", (0, 48, 384, 384), (0, 48, 384, 384), (("xyz", (0, 48, 384, 384)),)),
    ("up", "up", (0, 48, 768, 384), (0, 48, 768, 384), (("xyz", (0, 48, 768, 384)),)),
    ("up", "up", (0, 48, 1152, 384), (0, 48, 1152, 384), (("xyz", (0, 48, 1152, 384)),)),
    ("out", "out", (0, 48, 0, 384), (0, 48, 0, 384), (("zxy", (0, 48, 0, 256)), ("xyz", (0, 48, 256, 128)),)),
    ("qkv", "early", (0, 48, 0, 384), 0, (("zxy", (0, 48, 0, 384)),)),
    ("box", "box", (0, 48, 0, 384), (0, 48, 0, 384), (("yxz", (0, 48, 0, 128)), ("xyz", (0, 48, 128, 256)),)),
    ("qkv", "down", (0, 48, 0, 384), 1, (("yxz", (0, 48, 0, 128)), ("yxz", (0, 48, 128, 256)),)),
    ("qkv", "down", (48, 48, 0, 384), 2, (("yxz", (48, 48, 0, 128)), ("xzy", (48, 48, 128, 256)),)),
)
SCATTER_EVENTS = (
    (5, 0, 0, 0),
    (6, 1, 0, 0),
    (11, 2, 0, 0),
    (12, 0, 0, 10),
    (13, 3, 0, 0),
    (13, 4, 0, 0),
    (16, 0, 1, 1),
    (16, 1, 0, 10),
    (17, 0, 0, 1),
    (17, 5, 0, 0),
    (18, 7, 0, 0),
    (21, 0, 1, 11),
    (25, 2, 0, 1),
    (25, 1, 1, 1),
    (25, -1, 0, 0),
    (26, 7, 0, 10),
    (28, 1, 0, 1),
    (29, 6, 0, 0),
    (30, 3, 1, 1),
    (31, 4, 0, 1),
    (31, 2, 0, 11),
    (32, 0, 0, 2),
    (32, 5, 0, 1),
    (34, 1, 1, 2),
    (34, 8, 0, 0),
    (35, 0, 1, 2),
    (35, 1, 0, 2),
    (36, 1, 1, 12),
    (42, 2, 0, 2),
    (42, 6, 0, 1),
    (43, 8, 0, 10),
    (44, 1, 1, 3),
    (45, 3, 0, 1),
    (46, 2, 0, 3),
    (46, 4, 0, 2),
    (47, 1, 0, 3),
    (47, 7, 1, 1),
    (48, 0, 0, 3),
    (48, 9, 0, 0),
    (48, 0, 1, 3),
    (48, -2, 0, 0),
    (48, 6, 0, 2),
    (49, 10, 0, 0),
    (49, 7, 1, 2),
    (49, 11, 0, 0),
    (49, 3, 1, 2),
    (51, 9, 1, 1),
    (51, 7, 0, 1),
    (57, 3, 0, 2),
    (64, 9, 0, 1),
    (65, 4, 0, 12),
    (65, 3, 0, 12),
    (68, -2, 0, 1),
    (75, 5, 0, 2),
    (75, 11, 1, 1),
    (81, 10, 1, 1),
    (88, 7, 0, 2),
    (95, -2, 0, 2),
    (117, 4, 0, 3),
    (146, 3, 0, 3),
    (198, 8, 0, 1),
    (530, 3, 1, 12),
    (543, 6, 0, 12),
    (567, 5, 0, 12),
    (567, 11, 1, 11),
    (568, 7, 1, 12),
    (898, 10, 0, 1),
    (912, 9, 1, 2),
    (915, 9, 0, 2),
    (936, 11, 0, 1),
    (956, 8, 0, 2),
    (959, 10, 0, 2),
    (975, 9, 1, 12),
    (988, 11, 0, 2),
    (991, 10, 0, 12),
    (1004, 10, 1, 2),
    (1005, 9, 0, 12),
    (1009, 11, 1, 2),
    (1017, 9, 1, 3),
    (1019, 11, 0, 12),
    (1022, 3, 1, 3),
    (1030, 10, 0, 3),
    (1046, 6, 0, 3),
    (1054, 10, 1, 12),
    (1058, 5, 0, 3),
    (1068, 7, 0, 3),
    (1069, 11, 0, 3),
    (1069, -2, 0, 3),
    (1070, 8, 0, 3),
    (1084, 9, 0, 3),
    (1086, 10, 1, 3),
    (1111, 11, 1, 3),
    (1136, 7, 1, 3),
)


MESH = pl.DeviceIdType.MESH
WEIGHTS = ("qkv", "box", "out", "up", "down")
ROT = 4
ALL = slice(None)


def window(piece):
    return (pl.ds(piece[0], piece[1]), pl.ds(piece[2], piece[3]))


class Place:
    def __init__(self):
        dp = lax.axis_index("dp")
        self.y = lax.axis_index("blk")
        self.z = lax.div(dp, 4)
        self.x = lax.rem(lax.div(dp, 2), 2)
        self.c = lax.rem(dp, 2)
        x, y, z, c = self.x, self.y, self.z, self.c
        self.near = z + 1 - 2 * lax.rem(z, 2)
        self.far = lax.rem(z + 2, 4)
        self.mirror = 3 - z
        self.inner = jnp.logical_or(z == 1, z == 2)
        self.end = jnp.logical_or(z == 0, z == 3)
        at = lambda other: (other * 4 + x * 2 + c, y)
        self.near_peer, self.far_peer, self.mirror_peer = at(self.near), at(self.far), at(self.mirror)
        self.x_peer = (dp + 2 - 4 * x, y)
        self.y_peer = (dp, 1 - y)
        self.c_peer = (dp + 1 - 2 * c, y)

    def own(self):
        return dict(y=self.y, z=self.z, x=self.x)

    def vector_offset(self):
        device = ((self.z * 2 + self.x) * 2 + self.c) * 2 + self.y
        return lax.rem(device * (VECTORS // 32), 128)

    def hail(self):
        peers = [self.near_peer, self.far_peer, self.mirror_peer]
        peers += [self.x_peer, self.y_peer, self.c_peer]
        for peer in peers:
            pl.semaphore_signal(
                pltpu.get_barrier_semaphore(), inc=1, device_id=peer, device_id_type=MESH
            )

    def meet(self):
        pl.semaphore_wait(pltpu.get_barrier_semaphore(), 6)


def semaphore_table(groups, slots):
    table = {}
    for g, group in enumerate(groups):
        for part, (path, _) in enumerate(group[-1]):
            for hop, axis in enumerate(path):
                for slot in range(slots if axis == "z" else 1):
                    table[g, part, hop, slot] = len(table)
    return table


SEND_RINGS = dict(all=(0, 24), inner=(24, 12), end=(36, 12))
SENDS = 48


class Sends:
    def __init__(self, place, events, started):
        self.place = place
        self.index, self.before, self.kind, self.after = {}, {}, {}, {}
        turns = {kind: [] for kind in SEND_RINGS}
        for at, (_, *event) in enumerate(events):
            for key, kind in started(*event):
                base, size = SEND_RINGS[kind]
                turn = turns[kind]
                self.index[key], self.kind[key] = base + len(turn) % size, kind
                if len(turn) >= size:
                    self.before[key] = turn[-size]
                    self.after[turn[-size]] = at
                turn.append(key)
        self.done = set()

    def when(self, key, act):
        kind = self.kind[key]
        if kind == "all":
            act()
        else:
            pl.when(self.place.inner if kind == "inner" else self.place.end)(act)

    def start(self, copy, *key):
        before = self.before.get(key)
        if before is not None and before not in self.done:
            copy(*before).wait_send()
        copy(*key).start()

    def left(self, copy, now=None, chosen=lambda key: True):
        for key in self.index:
            at = self.after.get(key)
            if key in self.done or not chosen(key) or (at is not None and (now is None or at < now)):
                continue
            self.done.add(key)
            self.when(key, copy(*key).wait_send)


def remote(src, dst, sems, at, peer, send=None):
    return pltpu.make_async_remote_copy(
        src,
        dst,
        sems[0].at[at if send is None else send],
        sems[1].at[at],
        device_id=peer,
        device_id_type=MESH,
    )


def core_table(groups):
    keys = [(g, part) for g, group in enumerate(groups) for part in range(len(group[-1]))]
    return {key: n for n, key in enumerate(keys)}


class Gather:
    def __init__(self, place, groups, shards, full, sems, own_sem):
        self.place, self.groups, self.shards, self.full = place, groups, shards, full
        self.sems, self.own_sem = sems, own_sem
        self.count = len(groups)
        self.table = semaphore_table(groups, 3)
        self.c_table = core_table(groups)
        self.sends = Sends(place, GATHER_EVENTS, self.started)
        self.owned = False

    def started(self, g, part, step):
        if g < 0 or step == 4:
            return []
        if step == 3:
            return [((g, part, 3, 0), "all")]
        if step >= 10:
            return [((g, part, step - 10, 3), "inner")]
        if self.groups[g][2][part][0][step] != "z":
            return [((g, part, step, 0), "all")]
        return [
            ((g, part, step, 1), "all"),
            ((g, part, step, 0), "all"),
            ((g, part, step, 2), "inner"),
        ]

    def copy(self, g, part, hop, slot, arriving=False):
        p = self.place
        name, _, parts = self.groups[g]
        path, piece = parts[part]
        cut = window(piece)
        send = self.sends.index[g, part, hop, slot]
        if hop == 3:
            c = 1 - p.c if arriving else p.c
            ref = self.full[name].at[(ALL, ALL, ALL, c) + cut]
            at = len(self.table) + self.c_table[g, part]
            return remote(ref, ref, self.sems, (at,), p.c_peer, (send,))
        axis = path[hop]
        at = p.own()
        at.update({earlier: ALL for earlier in path[:hop]})
        if axis == "z":
            peer = (p.near_peer, p.far_peer, p.mirror_peer, p.near_peer)[slot]
            if slot == 3:
                at["z"] = p.mirror if arriving else p.far
            elif arriving:
                at["z"] = (p.near, p.far, p.mirror)[slot]
        else:
            peer = p.x_peer if axis == "x" else p.y_peer
            if arriving:
                at[axis] = 1 - at[axis]
        ref = self.full[name].at[(at["y"], at["z"], at["x"], p.c) + cut]
        source = self.shards[name].at[cut] if hop == 0 and slot < 3 else ref
        at = self.table[g, part, hop, min(slot, 2)]
        return remote(source, ref, self.sems, (at,), peer, (send,))

    def own_copy(self, g):
        p = self.place
        name, both, _ = self.groups[g]
        cut = window(both)
        return pltpu.make_async_copy(
            self.shards[name].at[cut],
            self.full[name].at[(p.y, p.z, p.x, p.c) + cut],
            self.own_sem.at[g],
        )

    def relay(self, g, part, hop):
        @pl.when(self.place.inner)
        def _():
            self.copy(g, part, hop, 1, True).wait_recv()
            self.sends.start(self.copy, g, part, hop, 3)

    def start(self, g, part, hop):
        if self.groups[g][2][part][0][hop] != "z":
            self.sends.start(self.copy, g, part, hop, 0)
            return
        self.sends.start(self.copy, g, part, hop, 1)
        self.sends.start(self.copy, g, part, hop, 0)

        @pl.when(self.place.inner)
        def _():
            self.sends.start(self.copy, g, part, hop, 2)

    def finish(self, g, part, hop):
        self.copy(g, part, hop, 0, True).wait_recv()
        if self.groups[g][2][part][0][hop] != "z":
            return

        @pl.when(self.place.inner)
        def _():
            self.copy(g, part, hop, 2, True).wait_recv()

        @pl.when(self.place.end)
        def _():
            self.copy(g, part, hop, 1, True).wait_recv()
            self.copy(g, part, hop, 3, True).wait_recv()

    def own(self):
        for g in range(self.count):
            self.own_copy(g).start()

    def step(self, g, part, step):
        if step >= 10:
            self.relay(g, part, step - 10)
            return
        if step >= 1 and not self.owned:
            self.owned = True
            for other in range(self.count):
                self.own_copy(other).wait()
        if 1 <= step <= 3:
            self.finish(g, part, step - 1)
        if step <= 2:
            self.start(g, part, step)
        if step == 3:
            self.sends.start(self.copy, g, part, 3, 0)
        if step == 4:
            self.copy(g, part, 3, 0, True).wait_recv()


class Clock:
    def __init__(self, events, run, begun=None):
        self.events, self.run, self.now, self.at, self.begun = events, run, 0, 0, begun

    def may(self, event):
        return self.begun is None or event[1] < 0 or event[1] in self.begun

    def take(self):
        self.now += 1
        first = self.at
        while self.at < len(self.events):
            event = self.events[self.at]
            if event[0] > self.now or not self.may(event):
                break
            self.at += 1
        return self.events[first : self.at]

    def point(self):
        for _, *event in self.take():
            self.run(*event)

    def upto(self, *wanted):
        self.now += 1
        last = max(i for i, (_, *event) in enumerate(self.events) if tuple(event) in wanted)
        while self.at <= last:
            assert self.may(self.events[self.at])
            _, *event = self.events[self.at]
            self.at += 1
            self.run(*event)

    def loop(self, count, body, points=1):
        due = [[self.take() for _ in range(points)] for _ in range(count)]

        def wrapped(i, carry):
            point = iter(range(points))

            def serve():
                k = next(point)
                for n in range(count):
                    if due[n][k]:

                        @pl.when(i == n)
                        def _():
                            for _, *event in due[n][k]:
                                self.run(*event)

            serve()
            return body(i, carry, serve)

        lax.fori_loop(0, count, wrapped, 0)
        self.point()


def sine_cosine(angle):
    turns = jnp.floor(angle * (2.0 / math.pi) + 0.5)
    rest = angle - turns * 1.5703125
    rest = rest - turns * 4.837512969970703125e-4
    rest = rest - turns * 7.54978995489188216e-8
    square = rest * rest
    sine = rest + rest * square * (
        -1.6666654611e-1 + square * (8.3321608736e-3 + square * -1.9515295891e-4)
    )
    cosine = (
        1.0
        - 0.5 * square
        + square
        * square
        * (
            4.166664568298827e-2
            + square * (-1.388731625493765e-3 + square * 2.443315711809948e-5)
        )
    )
    quarter = turns.astype(jnp.int32)
    odd = (quarter & 1) == 1
    sine_sign = jnp.where((quarter & 2) == 2, -1.0, 1.0)
    cosine_sign = jnp.where(((quarter + 1) & 2) == 2, -1.0, 1.0)
    return (
        sine_sign * jnp.where(odd, cosine, sine),
        cosine_sign * jnp.where(odd, sine, cosine),
    )


def dot_t(a, b):
    return lax.dot_general(a, b, (((1,), (1,)), ((), ())), preferred_element_type=jnp.float32)


def dot_n(a, b):
    return lax.dot_general(a, b, (((0,), (0,)), ((), ())), preferred_element_type=jnp.float32)


def lanes(start, size):
    return pl.ds(pl.multiple_of(start, 128), size)


BQ, BV, BO, G1, E1, B1, B2, G2, E2 = 0, 768, 1536, 2304, 3072, 3840, 6912, 7680, 8448
VECTORS = 9216
SUMS = VECTORS + 128


def total(value):
    return jnp.sum(value.astype(jnp.float32), axis=0, keepdims=True)


def norm_back(grad, unit, inverse, gain):
    scaled = grad * gain
    mean_grad = jnp.mean(scaled, axis=1, keepdims=True)
    mean_unit = jnp.mean(scaled * unit, axis=1, keepdims=True)
    return inverse * (scaled - mean_grad - unit * mean_unit)


def forward_kernel(plan, *refs):
    groups, page_len, width = plan
    block = page_len // 2
    refs = iter(refs)
    take = lambda n: [next(refs) for _ in range(n)]
    tokens, cotangent, boxes, lengths, vectors = take(5)
    shards = dict(zip(WEIGHTS, take(5)))
    full_out = dict(zip(WEIGHTS, take(5)))
    (x_out, ct_out, qkv_out, table_out, p_out, o_out, unit1_out, inv1_out) = take(8)
    (g_out, d_out, unit2_out, low_out, vec_out) = take(5)
    full = dict(zip(WEIGHTS, take(5)))
    (ct_own, x_own, boxes_peer, pieces, vec, qkv, table, keys, box_w, p_slots, o_own, o_low) = take(12)
    (unit1, inv1, y1_low, hidden, slope, unit2) = take(6)
    w_sems = take(2)
    (own_sem,) = take(1)
    vz_sems, vxy_sems, vc_sems = take(2), take(2), take(2)
    ex_sems = take(2)
    (local_sem, p_sem, out_sem) = take(3)
    bias_qkv, piece = take(2)

    place = Place()
    y, z, x, c = place.y, place.z, place.x, place.c
    gather = Gather(place, groups, shards, full, w_sems, own_sem)

    def swap(i, source, target, arriving=False):
        at = (1 - y) if arriving else y
        return remote(
            source.at[1 - y], target.at[pl.ds(pl.multiple_of(at * block, block), block)],
            ex_sems, (i,), place.y_peer,
        )

    def keep(i, source, target):
        return pltpu.make_async_copy(
            source.at[y], target.at[pl.ds(pl.multiple_of(y * block, block), block)],
            local_sem.at[i],
        )

    box_swap = remote(boxes, boxes_peer, ex_sems, (2,), place.y_peer)

    def vector_y(arriving=False):
        at = 1 - y if arriving else y
        return remote(piece, pieces.at[at, z, x, c], vxy_sems, (0,), place.y_peer)

    def vector_x(arriving=False):
        ref = pieces.at[:, z, 1 - x if arriving else x, c]
        return remote(ref, ref, vxy_sems, (1,), place.x_peer)

    def vector_z(k, arriving=False):
        ref = pieces.at[:, lax.rem(z + 4 - k, 4) if arriving else z, :, c]
        peer = (lax.rem(z + k, 4) * 4 + x * 2 + c, y)
        return remote(ref, ref, vz_sems, (k - 1,), peer)

    def vector_c(arriving=False):
        ref = pieces.at[:, :, :, 1 - c if arriving else c]
        return remote(ref, ref, vc_sems, (0,), place.c_peer)

    vector_own = pltpu.make_async_copy(piece, pieces.at[y, z, x, c], local_sem.at[2])

    def event(g, part, step):
        if g < 0:
            swap(1, cotangent, ct_own).start()
        else:
            gather.step(g, part, step)

    clock = Clock(GATHER_EVENTS, event)

    def need(g):
        clock.upto(*((g, part, 4) for part in range(len(groups[g][2]))))

    outgoing = []

    def send_out(ref, out):
        copy = pltpu.make_async_copy(ref, out, out_sem.at[len(outgoing)])
        copy.start()
        outgoing.append(copy)

    place.hail()
    gather.own()
    own_vector = vectors[...].astype(jnp.float32).reshape(1, -1)
    own_vector = jnp.concatenate(
        [own_vector, jnp.zeros((1, 384 - own_vector.shape[1]), jnp.float32)], axis=1
    )
    own_vector = jnp.broadcast_to(own_vector, (8, 384))
    piece[...] = pltpu.roll(own_vector, place.vector_offset(), 1)[0:1, :]
    place.meet()
    box_swap.start()
    vector_y().start()
    vector_own.start()
    swap(0, tokens, x_own).start()
    clock.point()
    keep(0, tokens, x_own).start()
    keep(1, cotangent, ct_own).start()

    box_swap.wait_recv()
    mine, other = boxes[...], boxes_peer[...]
    first_block = y == 0
    mine = jnp.where(first_block, mine[:, 0, :], mine[:, 1, :])
    other = jnp.where(first_block, other[:, 0, :], other[:, 1, :])
    both = jnp.concatenate(
        [jnp.where(first_block, mine, other), jnp.where(first_block, other, mine)], axis=1
    ).astype(jnp.float32)
    both = jnp.concatenate([both, jnp.zeros((6, page_len), jnp.float32)], axis=0)
    across_up = both.T
    lane = lax.broadcasted_iota(jnp.int32, (1, 2 * FREQ), 1)
    step = jnp.where(lane < FREQ, lane, lane - FREQ).astype(jnp.float32)
    frequency = jnp.exp(step * (-math.log(10000.0) / FREQ))
    angle = jnp.where(lane < FREQ, across_up[:, 0:1], across_up[:, 1:2]) * frequency
    sine, cosine = sine_cosine(angle)
    table[0], table[1] = cosine, sine
    keys[0 : 2 * FREQ, :] = cosine.astype(jnp.bfloat16).T
    keys[2 * FREQ :, :] = sine.astype(jnp.bfloat16).T
    send_out(table, table_out)
    clock.point()
    vector_own.wait()
    vector_y(True).wait_recv()
    vector_x().start()
    clock.point()
    vector_x(True).wait_recv()
    for k in range(1, 4):
        vector_z(k).start()
    clock.point()
    clock.upto(*((0, part, 3) for part in range(len(groups[0][2]))))
    for k in range(1, 4):
        vector_z(k, True).wait_recv()
    vector_c().start()
    need(0)
    vector_c(True).wait_recv()
    vec[...] = jnp.zeros_like(vec)
    for dz in range(4):
        for dx in range(2):
            for dc in range(2):
                for dy in range(2):
                    device = ((dz * 2 + dx) * 2 + dc) * 2 + dy
                    start = device * (VECTORS // 32) // 128 * 128
                    vec[:, start : start + 384] += pieces[dy, dz, dx, dc]

    def vector(start, size=width):
        return vec[:, start : start + size]

    def columns_of(name, first, count):
        halves = [
            full[name].at[h][:, :, :, :, first : first + count].reshape(-1, count)
            for h in range(2)
        ]
        return jnp.concatenate(halves, axis=1)

    def project(first, count):
        both = jnp.dot(
            x_own[...], columns_of("qkv", first, count), preferred_element_type=jnp.float32
        )
        for h in range(2):
            at = slice(h * 1152 + first, h * 1152 + first + count)
            part = both[:, h * count : (h + 1) * count]
            qkv[:, at] = (part + bias_qkv[:, at]).astype(jnp.bfloat16)

    bias_qkv[:, 0:width] = vector(BQ)
    bias_qkv[:, width : 2 * width] = jnp.zeros((1, width), jnp.float32)
    bias_qkv[:, 2 * width : 3 * width] = vector(BV)
    for g, (name, cut, _) in enumerate(groups):
        if name == "qkv":
            if g == 0:
                keep(0, tokens, x_own).wait()
                swap(0, tokens, x_own, True).wait_recv()
                send_out(x_own, x_out)
            else:
                need(g)
            project(cut[2], cut[3])
            clock.point()
    send_out(qkv, qkv_out)

    box_group = [g for g, group in enumerate(groups) if group[0] == "box"][-1]
    need(box_group)
    low = full["box"].at[0][...].reshape(width, 2 * FREQ)
    high = full["box"].at[1][...].reshape(width, 2 * FREQ)
    box_w[...] = jnp.concatenate(
        [low[:, :FREQ], high[:, :FREQ], low[:, FREQ:], high[:, FREQ:]], axis=1
    )
    page_length = jnp.where(first_block, lengths[0], lengths[1])
    valid = lax.broadcasted_iota(jnp.int32, (1, page_len), 1) < page_length
    head_lane = lax.broadcasted_iota(jnp.int32, (1, 128), 1)

    def p_copy(p, slot):
        return pltpu.make_async_copy(p_slots.at[slot], p_out.at[p], p_sem.at[slot])

    def pair(p, carry, serve):
        slot = lax.rem(p, 2)

        @pl.when(p >= 2)
        def _():
            p_copy(p - 2, slot).wait()

        q = qkv[:, lanes(p * 128, 128)]
        k = qkv[:, lanes(width + p * 128, 128)].T
        v = qkv[:, lanes(2 * width + p * 128, 128)]
        w = box_w[pl.ds(pl.multiple_of(p * 128, 128), 128), :]
        outs = []
        for i in range(2):
            if i:
                serve()
            of_head = (head_lane < HEAD) == (i == 0)
            q_head = jnp.where(of_head, q, jnp.zeros_like(q))
            u = jnp.dot(q_head, w, preferred_element_type=jnp.float32)
            on_sine, on_cosine = u[:, : 2 * FREQ], u[:, 2 * FREQ :]
            cosine, sine = table[0], table[1]
            b_cosine = (on_sine * sine + on_cosine * cosine).astype(jnp.bfloat16)
            b_sine = (on_cosine * sine - on_sine * cosine).astype(jnp.bfloat16)
            serve()
            b = jnp.concatenate([q_head, b_cosine, b_sine], axis=1)
            s = jnp.dot(b, jnp.concatenate([k, keys[...]], axis=0), preferred_element_type=jnp.float32)
            s = jnp.where(valid, s, MASKED)
            top = jnp.max(s, axis=1, keepdims=True)
            e = jnp.exp((s - top) * (HEAD**-0.5))
            probs = (e * (1.0 / jnp.sum(e, axis=1, keepdims=True))).astype(jnp.bfloat16)
            p_slots[slot, i] = probs
            outs.append(jnp.dot(probs, v, preferred_element_type=jnp.float32))
        mixed = jnp.where(head_lane < HEAD, outs[0], outs[1])
        o_own[:, lanes(p * 128, 128)] = mixed
        o_low[:, lanes(p * 128, 128)] = mixed.astype(jnp.bfloat16)
        p_copy(p, slot).start()
        return carry

    clock.loop(HEADS // 2, pair, 4)
    p_copy(4, 0).wait()
    p_copy(5, 1).wait()
    send_out(o_own, o_out)

    def last_of(name):
        return [g for g, group in enumerate(groups) if group[0] == name][-1]

    def weight_out(name):
        send_out(full[name], full_out[name])

    weight_out("qkv")
    weight_out("box")
    need(last_of("out"))
    weight_out("out")
    unit2[...] = (
        x_own[...].astype(jnp.float32)
        + jnp.dot(o_low[...], columns_of("out", 0, 384), preferred_element_type=jnp.float32)
        + vector(BO)
    )

    def norm(hidden_sum):
        mean = jnp.mean(hidden_sum, axis=1, keepdims=True)
        centered = hidden_sum - mean
        inverse = lax.rsqrt(jnp.mean(centered * centered, axis=1, keepdims=True) + EPSILON)
        return centered * inverse, inverse

    unit, inverse = norm(unit2[...])
    unit1[...] = unit
    inv1[...] = jnp.broadcast_to(inverse, (page_len, 128))
    y1 = unit * vector(G1) + vector(E1)
    y1_low[...] = y1.astype(jnp.bfloat16)
    unit2[...] = y1 + vector(B2)
    send_out(unit1, unit1_out)
    send_out(inv1, inv1_out)

    clock.point()
    for g, (name, cut, _) in enumerate(groups):
        if name == "up":
            need(g)
            first, count = cut[2], cut[3]
            places = [slice(h * 1536 + first, h * 1536 + first + count) for h in range(2)]
            bias = [vec[:, B1 + at.start : B1 + at.stop] for at in places]
            pre = jnp.dot(
                y1_low[...], columns_of("up", first, count), preferred_element_type=jnp.float32
            )
            pre = pre + jnp.concatenate(bias, axis=1)
            half = 0.5 + 0.5 * lax.erf(pre * (2.0**-0.5))
            bell = jnp.exp(pre * pre * -0.5) * ((2.0 * math.pi) ** -0.5)
            acted = (pre * half).astype(jnp.bfloat16)
            turned = (half + pre * bell).astype(jnp.bfloat16)
            for h, at in enumerate(places):
                hidden[:, at] = acted[:, h * count : (h + 1) * count]
                slope[:, at] = turned[:, h * count : (h + 1) * count]
            clock.point()
    send_out(hidden, g_out)
    send_out(slope, d_out)
    weight_out("up")

    for g, (name, cut, _) in enumerate(groups):
        if name == "down":
            need(g)
            first, count = cut[2], cut[3]
            columns = (ALL,) * 4 + window(cut)
            send_out(full["down"].at[columns], full_out["down"].at[columns])

            both = jnp.dot(
                hidden[...], columns_of("down", first, count), preferred_element_type=jnp.float32
            )
            for h in range(2):
                at = slice(h * 384 + first, h * 384 + first + count)
                unit2[:, at] += both[:, h * count : (h + 1) * count]
            clock.point()
    clock.upto(*(tuple(event) for _, *event in GATHER_EVENTS))
    swap(1, cotangent, ct_own, True).wait_recv()
    keep(1, cotangent, ct_own).wait()
    unit, inverse = norm(unit2[...])
    y1_low[...] = (unit * vector(G2) + vector(E2)).astype(jnp.bfloat16)
    send_out(y1_low, low_out)
    seed = ct_own[...].astype(jnp.float32)
    d_h2 = norm_back(seed, unit, inverse, vector(G2))
    unit2[...] = d_h2
    send_out(unit2, unit2_out)
    d_f = d_h2.astype(jnp.bfloat16)
    ct_own[...] = d_f
    send_out(ct_own, ct_out)
    for n, value in enumerate((d_f, seed * unit, seed)):
        vec[:, SUMS + n * width : SUMS + (n + 1) * width] = total(value)
    send_out(vec, vec_out)

    gather.sends.left(gather.copy)
    for k in range(1, 4):
        vector_z(k).wait_send()
    vector_y().wait_send()
    vector_x().wait_send()
    vector_c().wait_send()
    box_swap.wait_send()
    swap(0, tokens, x_own).wait_send()
    swap(1, cotangent, ct_own).wait_send()
    for copy in outgoing:
        copy.wait()


def forward_call(tokens, cotangent, boxes, lengths, vectors, shards):
    page_len = tokens.shape[1] * 2
    width = tokens.shape[2]
    groups = GATHER_GROUPS
    count = len(groups)
    full = [jax.ShapeDtypeStruct((2, 4, 2, 2) + s.shape, jnp.bfloat16) for s in shards]
    low, single = jnp.bfloat16, jnp.float32
    kinds = dict(
        x=((page_len, width), low),
        ct=((page_len, width), low),
        qkv=((page_len, 3 * width), low),
        table=((2, page_len, 2 * FREQ), single),
        p=((HEADS // 2, 2, page_len, page_len), low),
        o=((page_len, width), single),
        unit1=((page_len, width), single),
        inv1=((page_len, 128), single),
        g=((page_len, 4 * width), low),
        d=((page_len, 4 * width), low),
        unit2=((page_len, width), single),
        low=((page_len, width), low),
        vec=((1, SUMS + 3 * width), single),
    )
    outs = full + [jax.ShapeDtypeStruct(*kinds[k]) for k in kinds]
    anywhere = pl.BlockSpec(memory_space=pl.ANY)
    vmem = pl.BlockSpec(memory_space=pltpu.VMEM)
    smem = pl.BlockSpec(memory_space=pltpu.SMEM)
    dma = pltpu.SemaphoreType.DMA
    scratch = [pltpu.VMEM(f.shape, f.dtype) for f in full]
    scratch += [
        pltpu.VMEM((page_len, width), low),
        pltpu.VMEM((page_len, width), low),
        pltpu.VMEM(boxes.shape, jnp.int32),
        pltpu.VMEM((2, 4, 2, 2, 1, 384), single),
        pltpu.VMEM((1, SUMS + 3 * width), single),
        pltpu.VMEM((page_len, 3 * width), low),
        pltpu.VMEM((2, page_len, 2 * FREQ), single),
        pltpu.VMEM((BOX_DIM, page_len), low),
        pltpu.VMEM((width, BOX_DIM), low),
        pltpu.VMEM((2, 2, page_len, page_len), low),
        pltpu.VMEM((page_len, width), single),
        pltpu.VMEM((page_len, width), low),
        pltpu.VMEM((page_len, width), single),
        pltpu.VMEM((page_len, 128), single),
        pltpu.VMEM((page_len, width), low),
        pltpu.VMEM((page_len, 4 * width), low),
        pltpu.VMEM((page_len, 4 * width), low),
        pltpu.VMEM((page_len, width), single),
    ]
    arrivals = len(semaphore_table(groups, 3)) + len(core_table(groups))
    scratch += [dma((SENDS,)), dma((arrivals,))]
    scratch += [dma((count,))]
    scratch += [dma((3,))] * 2 + [dma((2,))] * 2 + [dma((1,))] * 2
    scratch += [dma((3,))] * 2 + [dma((3,)), dma((2,)), dma((20,))]
    scratch += [pltpu.VMEM((1, 3 * width), single), pltpu.VMEM((1, 384), single)]
    plan = (groups, page_len, width)
    results = pl.pallas_call(
        partial(forward_kernel, plan),
        out_shape=outs,
        in_specs=[anywhere, anywhere, vmem, smem, vmem] + [anywhere] * 5,
        out_specs=[anywhere] * len(outs),
        scratch_shapes=scratch,
        compiler_params=pltpu.CompilerParams(
            collective_id=0, has_side_effects=True, vmem_limit_bytes=VMEM_LIMIT
        ),
    )(tokens, cotangent, boxes, lengths, vectors, *shards)
    return dict(zip(WEIGHTS, results[:5])), dict(zip(kinds, results[5:]))


VMEM_LIMIT = 60 * 2**20


def landing_shape(path, hop, piece):
    sizes = dict(y=2, z=4, x=2)
    to_come = [sizes[axis] for axis in "yzx" if axis in path[hop + 1 :]]
    return (4 if path[hop] == "z" else 1, *to_come, piece[1], piece[3])


THIRDS = ((0, 1, 2), (1, 0, 2))


class Scatter:
    def __init__(self, place, groups, stored, c_land, landing, summed, sems, c_sems):
        self.place, self.groups, self.stored, self.summed = place, groups, stored, summed
        self.c_land, self.landing = c_land, landing
        self.sems, self.c_sems = sems, c_sems
        self.table = semaphore_table(groups, 4)
        self.sends = Sends(place, SCATTER_EVENTS, self.started)
        self.sent = set()

    def started(self, g, part, step):
        if g < 0 or step == 3:
            return []
        if step >= 10:
            return [((g, part, step - 10, 1), "inner")]
        out = []
        for other in range(len(self.groups[g][-1])) if step == 0 else (part,):
            if self.groups[g][-1][other][0][step] != "z":
                out.append(((g, other, step, 0), "all"))
                continue
            out.append(((g, other, step, 3), "end"))
            out.append(((g, other, step, "end"), "end"))
            out.append(((g, other, step, 0), "all"))
            out.append(((g, other, step, 2), "inner"))
        return out

    def c_copy(self, g):
        p = self.place
        store, both = self.groups[g][1], self.groups[g][2]
        ref = self.stored[store].at[(ALL, ALL, ALL, 1 - p.c) + window(both)]
        return remote(ref, self.c_land[g], self.c_sems, (g,), p.c_peer)

    def copy(self, g, part, hop, slot):
        p = self.place
        send = self.sends.index[g, part, hop, slot]
        slot = 1 if slot == "end" else slot
        path, piece = self.groups[g][-1][part]
        axis = path[hop]
        at = p.own()
        at.update({later: ALL for later in path[hop + 1 :]})
        if axis == "z":
            at["z"] = (p.near, p.far, p.mirror, p.mirror)[slot]
            peer = (p.near_peer, p.far_peer, p.mirror_peer, p.near_peer)[slot]
        else:
            at[axis] = 1 - at[axis]
            peer = p.x_peer if axis == "x" else p.y_peer
        ref = self.stored[self.groups[g][1]].at[(at["y"], at["z"], at["x"], p.c) + window(piece)]
        land = self.landing[g][part][hop].at[slot]
        at = self.table[g, part, hop, slot]
        return remote(ref, land, self.sems, (at,), peer, (send,))

    def add(self, g, part, hop, slots, place_z=None):
        p = self.place
        name, store, both, result, parts = self.groups[g]
        store = self.stored[store]
        path, piece = ("yzx", both) if hop < 0 else parts[part]
        cut = window(piece)
        sizes = dict(y=2, z=4, x=2)
        to_come = [axis for axis in "yzx" if axis in path[hop + 1 :]]
        count = math.prod(sizes[axis] for axis in to_come)
        land = self.c_land[g] if hop < 0 else self.landing[g][part][hop]

        def block(i):
            at = p.own()
            if place_z is not None:
                at["z"] = place_z
            inner = []
            for axis in to_come[::-1]:
                at[axis] = lax.rem(i, sizes[axis])
                i = lax.div(i, sizes[axis])
                inner.insert(0, at[axis])
            here = (at["y"], at["z"], at["x"], p.c) + cut
            arrived = [land[tuple(inner)] if hop < 0 else land[(slot, *inner)] for slot in slots]
            if len(arrived) == 1 and not (hop == 2 and place_z is None):
                return here, store[here] + arrived[0]
            value = store[here].astype(jnp.float32)
            for other in arrived:
                value = value + other.astype(jnp.float32)
            return here, value

        if hop == 2 and place_z is None:
            _, value = block(0)
            top, height, first, size = piece
            if name == "qkv":
                third = jnp.where(p.y == 0, THIRDS[0][result], THIRDS[1][result])
                self.summed[name][:, lanes(first + 384 * third, size)] = value
                return
            top, first = top - both[0] + result[0], first - both[2] + result[2]
            self.summed[name][top : top + height, first : first + size] = value
            return

        together = min(count, 4)

        def body(i, carry):
            for k in range(together):
                here, value = block(i * together + k)
                store[here] = value.astype(jnp.bfloat16)
            return carry

        lax.fori_loop(0, count // together, body, 0)

    def begin(self, g):
        self.c_copy(g).start()

    def start(self, g, part, hop):
        p = self.place
        if self.groups[g][-1][part][0][hop] != "z":
            self.sends.start(self.copy, g, part, hop, 0)
            return

        @pl.when(p.end)
        def _():
            self.sends.start(self.copy, g, part, hop, 3)
            self.sends.start(self.copy, g, part, hop, "end")

        self.sends.start(self.copy, g, part, hop, 0)

        @pl.when(p.inner)
        def _():
            self.sends.start(self.copy, g, part, hop, 2)

    def relay(self, g, part, hop):
        p = self.place

        @pl.when(p.inner)
        def _():
            self.copy(g, part, hop, 3).wait_recv()
            self.add(g, part, hop, (3,), p.far)
            self.sends.start(self.copy, g, part, hop, 1)

    def finish(self, g, part, hop):
        p = self.place
        self.copy(g, part, hop, 0).wait_recv()
        if self.groups[g][-1][part][0][hop] != "z":
            self.add(g, part, hop, (0,))
            return
        self.copy(g, part, hop, 1).wait_recv()

        @pl.when(p.inner)
        def _():
            self.copy(g, part, hop, 2).wait_recv()
            self.add(g, part, hop, (0, 1, 2))

        @pl.when(p.end)
        def _():
            self.add(g, part, hop, (0, 1))

    def step(self, g, part, step):
        if step >= 10:
            self.relay(g, part, step - 10)
            return
        if step == 0:
            self.c_copy(g).wait_recv()
            self.add(g, 0, -1, (0,))
            for part in range(len(self.groups[g][-1])):
                self.start(g, part, 0)
            return
        self.finish(g, part, step - 1)
        if step < 3:
            self.start(g, part, step)

    def left(self, chosen, now=None):
        for g in chosen:
            if g not in self.sent:
                self.sent.add(g)
                self.c_copy(g).wait_send()
        self.sends.left(self.copy, now, lambda key: key[0] in chosen)


def backward_kernel(plan, *refs):
    groups, page_len, width = plan
    block = page_len // 2
    refs = iter(refs)
    take = lambda n: [next(refs) for _ in range(n)]
    w_in = dict(zip(WEIGHTS, take(5)))
    (x_in, ct_in, qkv_in, table_in, p_in, o_in, unit1_in, inv1_in) = take(8)
    (g_in, d_in, unit2_in, low_in, vec_in) = take(5)
    out_out, dx_out = take(2)
    grad_out = dict(zip(WEIGHTS, take(5)))
    (piece_out,) = take(1)
    stored = dict(zip(("box", "out", "up", "down"), take(4)))
    count = len(groups)
    c_land = take(count)
    landing = [[take(3) for _ in group[-1]] for group in groups]
    summed = dict(zip(WEIGHTS, take(5)))
    w_box, w_out, box_w, box_g = take(4)
    (ct, qkv, table, keys, o_own, unit1, inv1, hidden, slope, unit2, out_low, vec) = take(12)
    (y1_low, d_a, d_mixed, dx_low, vec_g) = take(5)
    pieces, pc_land, py_land, px_land, pz_land, piece_sum = take(6)
    w_sems, c_sems = take(2), take(2)
    v_sems, vz_sems, ex_sems = take(2), take(2), take(2)
    in_sem, p_sem, out_sem = take(3)

    place = Place()
    y, z, x, c = place.y, place.z, place.x, place.c
    scatter = Scatter(place, groups, stored, c_land, landing, summed, w_sems, c_sems)

    sources = dict(
        unit2=(unit2_in, unit2),
        ct=(ct_in, ct),
        low=(low_in, out_low),
        vec=(vec_in, vec),
        g=(g_in, hidden),
        d=(d_in, slope),
        unit1=(unit1_in, unit1),
        inv1=(inv1_in, inv1),
        w_out=(w_in["out"], w_out),
        w_box=(w_in["box"], w_box),
        o=(o_in, o_own),
        qkv=(qkv_in, qkv),
        table=(table_in, table),
        x=(x_in, y1_low),
    )
    order = list(sources)

    def fetch(name):
        source, target = sources[name]
        return pltpu.make_async_copy(source, target, in_sem.at[order.index(name)])

    def fetch_weight(name, target):
        at = len(order) + ("down", "up", "qkv").index(name)
        return pltpu.make_async_copy(w_in[name], target, in_sem.at[at])

    def vector(start, size=width):
        return vec[:, start : start + size]

    names = [group[0] for group in groups]

    def event(g, part, step):
        if g == -2 and step == 3:
            dx_swap.wait_recv()
            unit2[0:block, :] = dx_low[1].astype(jnp.float32)
            dx_other.start()
        elif g == -2:
            vector_step(step)
        elif g < 0:
            fetch("low").wait()
            out_swap.start()
            out_keep.start()
        else:
            scatter.step(g, part, step)
            if (g, part, step) in last:
                result_copy(names[g]).start()

    ends = {}
    for _, g, part, step in SCATTER_EVENTS:
        if g >= 0 and step == 3:
            ends[names[g]] = (g, part, step)
    last = set(ends.values())

    def result_copy(name):
        at = 4 + WEIGHTS.index(name)
        return pltpu.make_async_copy(summed[name], grad_out[name], out_sem.at[at])

    clock = Clock(SCATTER_EVENTS, event, set())

    def begin(g):
        clock.begun.add(g)
        scatter.begin(g)

    for name in ("ct", "g", "vec"):
        fetch(name).start()
    place.hail()

    fetch("ct").wait()
    d_f = ct
    fetch("vec").wait()
    for n, start in enumerate((B2, G2, E2)):
        vec_g[:, start : start + width] = vec[:, SUMS + n * width : SUMS + (n + 1) * width]

    def rows(at):
        return pl.ds(pl.multiple_of(at * block, block), block)

    out_swap = remote(out_low.at[rows(1 - y)], out_out.at[y], ex_sems, (0,), place.y_peer)
    out_keep = pltpu.make_async_copy(out_low.at[rows(y)], out_out.at[y], out_sem.at[0])
    dx_other = pltpu.make_async_copy(unit2.at[0:block], dx_out.at[1 - y], out_sem.at[2])
    dx_swap = remote(dx_low.at[0], dx_low.at[1], ex_sems, (1,), place.y_peer)

    def with_down(w_down):
        fetch_weight("down", w_down).start()
        fetch("g").wait()

        for name in ("d", "unit2", "low", "unit1", "inv1", "w_out", "o", "w_box", "qkv", "table"):
            fetch(name).start()

        def down_grads(first, size):
            left = d_f[:, first : first + size]
            right = d_f[:, 384 + first : 384 + first + size]
            both = jnp.concatenate([left, right], axis=1)

            def grad_tile(t, carry):
                part = dot_n(hidden[:, lanes(t * width, width)], both).astype(jnp.bfloat16)
                for h in range(2):
                    stored["down"][h, t, :, :, :, first : first + size] = part[
                        :, h * size : (h + 1) * size
                    ].reshape(2, 2, -1, size)
                return carry

            lax.fori_loop(0, 4, grad_tile, 0)
            if first == 0:
                place.meet()
            for g, group in enumerate(groups):
                if group[0] == "down" and first <= group[2][2] < first + size:
                    begin(g)
            clock.point()

        down_grads(0, 128)
        down_grads(128, 256)
        fetch_weight("down", w_down).wait()
        fetch("d").wait()

        def slope_tile(t, carry, serve):
            w0 = w_down.at[0, t][...].reshape(width, 384)
            w1 = w_down.at[1, t][...].reshape(width, 384)
            d_hidden = dot_t(d_f[...], jnp.concatenate([w0, w1], axis=1))
            at = lanes(t * width, width)
            d_pre = (d_hidden * slope[:, at].astype(jnp.float32)).astype(jnp.bfloat16)
            slope[:, at] = d_pre
            vec_g[:, lanes(B1 + t * width, width)] = total(d_pre)
            return carry

        clock.loop(4, slope_tile)

    pl.run_scoped(with_down, pltpu.VMEM(w_in["down"].shape, jnp.bfloat16))

    fetch("unit1").wait()
    fetch("inv1").wait()
    fetch("unit2").wait()
    y1_low[...] = (unit1[...] * vector(G1) + vector(E1)).astype(jnp.bfloat16)

    def with_up(w_up):
        fetch_weight("up", w_up).start()

        def up_tile(i, carry, serve, part):
            tile = dot_n(y1_low[...], slope[:, lanes(i * 1536 + part * width, width)])
            stored["up"][i, :, :, :, :, part * width : (part + 1) * width] = tile.astype(
                jnp.bfloat16
            ).reshape(4, 2, 2, -1, width)
            return carry

        for part in range(2):
            clock.loop(2, partial(up_tile, part=part))
            for g, group in enumerate(groups):
                if group[0] == "up" and group[2][2] // width == part:
                    begin(g)
        fetch_weight("up", w_up).wait()

        def back_tile(h, carry, serve):
            w = w_up.at[h][...].reshape(width, 1536)
            unit2[...] += dot_t(slope[:, lanes(h * 1536, 1536)], w)
            return carry

        clock.loop(2, back_tile)

    pl.run_scoped(with_up, pltpu.VMEM(w_in["up"].shape, jnp.bfloat16))

    x_own = y1_low
    fetch("x").start()
    unit = unit1[...]
    d_y1 = unit2[...]
    vec_g[:, G1 : G1 + width] = total(d_y1 * unit)
    vec_g[:, E1 : E1 + width] = total(d_y1)
    d_h1 = norm_back(d_y1, unit, inv1[:, 0:1], vector(G1))
    unit1[...] = d_h1
    d_a[...] = d_h1.astype(jnp.bfloat16)
    vec_g[:, BO : BO + width] = total(d_a[...])
    fetch("w_out").wait()
    fetch("o").wait()
    both = jnp.concatenate([w_out.at[h][...].reshape(width, 384) for h in range(2)], axis=1)
    d_mixed[...] = dot_t(d_a[...], both).astype(jnp.bfloat16)
    part = dot_n(o_own[...].astype(jnp.bfloat16), d_a[...]).astype(jnp.bfloat16)
    for h in range(2):
        stored["out"][h] = part[:, h * 384 : (h + 1) * 384].reshape(4, 2, 2, -1, 384)
    begin(names.index("out"))
    clock.point()

    for name in ("w_box", "qkv", "table", "x"):
        fetch(name).wait()
    low = w_box.at[0][...].reshape(width, 2 * FREQ)
    high = w_box.at[1][...].reshape(width, 2 * FREQ)
    box_w[...] = jnp.concatenate(
        [low[:, :FREQ], high[:, :FREQ], low[:, FREQ:], high[:, FREQ:]], axis=1
    ).T
    keys[:, : 2 * FREQ] = table[0].astype(jnp.bfloat16)
    keys[:, 2 * FREQ :] = table[1].astype(jnp.bfloat16)
    table[...] = table[...] * (HEAD**-0.5)
    head_lane = lax.broadcasted_iota(jnp.int32, (1, 128), 1)

    def p_copy(p, slot, i):
        at = lanes((slot * 2 + i) * page_len, page_len)
        return pltpu.make_async_copy(p_in.at[p, i], hidden.at[:, at], p_sem.at[slot, i])

    p_copy(0, 0, 0).start()
    p_copy(0, 0, 1).start()

    vector_c = remote(pieces.at[:, :, :, 1 - c], pc_land, v_sems, (0,), place.c_peer)
    vector_y = remote(pieces.at[1 - y, :, :, c], py_land, v_sems, (1,), place.y_peer)
    vector_x = remote(pieces.at[y, :, 1 - x, c], px_land, v_sems, (2,), place.x_peer)

    def vector_z(k):
        there = lax.rem(z + k + 1, 4)
        peer = (there * 4 + x * 2 + c, y)
        return remote(pieces.at[y, there, x, c], pz_land.at[k], vz_sems, (k,), peer)

    def vector_step(step):
        if step == 0:
            vector_c.wait_recv()
            pieces[:, :, :, c] += pc_land[...]
            vector_y.start()
        if step == 1:
            vector_y.wait_recv()
            pieces[y, :, :, c] += py_land[...]
            vector_x.start()
        if step == 2:
            vector_x.wait_recv()
            pieces[y, :, x, c] += px_land[...]
            for k in range(3):
                vector_z(k).start()

    def with_qkv(w_qkv, early):
        stored["early"] = early
        fetch_weight("qkv", w_qkv).start()

        def pair(p, carry, serve):
            slot = lax.rem(p, 2)

            @pl.when(p < HEADS // 2 - 1)
            def _():
                p_copy(p + 1, 1 - slot, 0).start()
                p_copy(p + 1, 1 - slot, 1).start()

            p_copy(p, slot, 0).wait()
            p_copy(p, slot, 1).wait()
            q_t = qkv[:, lanes(p * 128, 128)].T
            k = qkv[:, lanes(width + p * 128, 128)]
            v_t = qkv[:, lanes(2 * width + p * 128, 128)].T
            w_t = box_w[:, lanes(p * 128, 128)]
            d_o = d_mixed[:, lanes(p * 128, 128)]
            d_o_t = d_o.T
            weighted = d_o.astype(jnp.float32) * o_own[:, lanes(p * 128, 128)]
            keys_k = jnp.concatenate([keys[...], k], axis=1)
            grads = []
            for i in range(2):
                if i:
                    serve()
                of_head = (head_lane < HEAD) == (i == 0)
                rows_head = slice(i * HEAD, (i + 1) * HEAD)
                probs = hidden[:, lanes((slot * 2 + i) * page_len, page_len)]
                delta = jnp.sum(jnp.where(of_head, weighted, 0.0), axis=1, keepdims=True)
                d_probs = jnp.dot(
                    jnp.where(of_head, d_o, jnp.zeros_like(d_o)),
                    v_t,
                    preferred_element_type=jnp.float32,
                )
                d_s = (probs.astype(jnp.float32) * (d_probs - delta)).astype(jnp.bfloat16)
                serve()
                d_b = jnp.dot(d_s, keys_k, preferred_element_type=jnp.float32)
                d_1, d_2 = d_b[:, : 2 * FREQ], d_b[:, 2 * FREQ : 4 * FREQ]
                cosine, sine = table[0], table[1]
                d_sine = (d_1 * sine - d_2 * cosine).astype(jnp.bfloat16)
                d_cosine = (d_1 * cosine + d_2 * sine).astype(jnp.bfloat16)
                d_u = jnp.concatenate([d_sine, d_cosine], axis=1)
                d_q = d_b[:, 4 * FREQ :] * (HEAD**-0.5) + jnp.dot(
                    d_u, w_t, preferred_element_type=jnp.float32
                )
                d_w = jnp.dot(q_t[rows_head], d_u, preferred_element_type=jnp.float32)
                box_g[pl.ds(pl.multiple_of(p * 128 + i * HEAD, HEAD), HEAD), :] = d_w.astype(
                    jnp.bfloat16
                )
                d_k = jnp.dot(q_t[rows_head], d_s, preferred_element_type=jnp.float32)
                d_v = jnp.dot(d_o_t[rows_head], probs, preferred_element_type=jnp.float32)
                grads.append((d_q, d_k * (HEAD**-0.5), d_v))
            (q_one, k_one, v_one), (q_two, k_two, v_two) = grads
            d_q = jnp.where(head_lane < HEAD, q_one, q_two).astype(jnp.bfloat16)
            d_k = jnp.concatenate([k_one, k_two], axis=0).astype(jnp.bfloat16).T
            d_v = jnp.concatenate([v_one, v_two], axis=0).astype(jnp.bfloat16).T
            for n, value in enumerate((d_q, d_k, d_v)):
                slope[:, lanes(n * width + p * 128, 128)] = value
            vec_g[:, lanes(BQ + p * 128, 128)] = total(d_q)
            vec_g[:, lanes(BV + p * 128, 128)] = total(d_v)
            return carry

        def qkv_grads(slot):
            store, top = ("early", 0) if slot == 0 else ("down", (slot - 1) * 48)
            for h in range(2):
                first = h * 1152 + THIRDS[h][slot] * 384
                tile = dot_n(x_own[...], slope[:, first : first + 384])
                stored[store][h, :, :, :, top : top + 48, :] = tile.astype(
                    jnp.bfloat16
                ).reshape(4, 2, 2, -1, 384)
            begin([g for g in range(count) if names[g] == "qkv"][slot])

        half = HEADS // 4
        clock.loop(half, pair, 4)
        qkv_grads(0)
        clock.point()
        clock.loop(half, lambda p, carry, serve: pair(p + half, carry, serve), 4)

        for dz in range(4):
            for dx in range(2):
                for dc in range(2):
                    for dy in range(2):
                        device = ((dz * 2 + dx) * 2 + dc) * 2 + dy
                        start = device * (VECTORS // 32) // 128 * 128
                        pieces[dy, dz, dx, dc] = vec_g[:, start : start + 384]
        vector_c.start()
        part = box_g[...]
        stored["box"][0] = jnp.concatenate(
            [part[:, :FREQ], part[:, 2 * FREQ : 3 * FREQ]], axis=1
        ).reshape(4, 2, 2, -1, 384)
        stored["box"][1] = jnp.concatenate(
            [part[:, FREQ : 2 * FREQ], part[:, 3 * FREQ :]], axis=1
        ).reshape(4, 2, 2, -1, 384)
        begin(names.index("box"))
        clock.point()
        clock.upto(*[
            (g, part, 3)
            for g, group in enumerate(groups)
            if names[g] == "down"
            for part in range(len(group[-1]))
        ])
        scatter.left([g for g in range(count) if names[g] == "down"], clock.at)

        for slot in (1, 2):
            qkv_grads(slot)
            clock.point()

        fetch_weight("qkv", w_qkv).wait()

        def back_tile(h, carry, serve):
            w = w_qkv.at[h][...].reshape(width, 1152)
            unit1[...] += dot_t(slope[:, lanes(h * 1152, 1152)], w)
            return carry

        clock.loop(2, back_tile)
        dx_low[0] = unit1[rows(1 - y), :].astype(jnp.bfloat16)
        dx_swap.start()
        pltpu.make_async_copy(unit1.at[rows(y)], dx_out.at[y], out_sem.at[1]).start()

        clock.point()
        clock.point()
        clock.upto(*(tuple(event) for _, *event in SCATTER_EVENTS))
        for k in range(3):
            vector_z(k).wait_recv()
        piece_total = pieces[y, z, x, c]
        for k in range(3):
            piece_total = piece_total + pz_land[k]
        piece_sum[...] = piece_total
        piece_copy = pltpu.make_async_copy(piece_sum, piece_out, out_sem.at[3])
        piece_copy.start()
        scatter.left(range(count))
        for copy in (vector_c, vector_y, vector_x, out_swap, dx_swap):
            copy.wait_send()
        for k in range(3):
            vector_z(k).wait_send()
        out_swap.wait_recv()
        out_keep.wait()
        pltpu.make_async_copy(unit1.at[rows(y)], dx_out.at[y], out_sem.at[1]).wait()
        dx_other.wait()
        piece_copy.wait()
        for name in WEIGHTS:
            result_copy(name).wait()

    pl.run_scoped(
        with_qkv,
        pltpu.VMEM(w_in["qkv"].shape, jnp.bfloat16),
        pltpu.VMEM(stored["box"].shape, jnp.bfloat16),
    )


def backward_call(full, kept, shards):
    low, single = jnp.bfloat16, jnp.float32
    page_len, width = kept["x"].shape
    groups = SCATTER_GROUPS
    count = len(groups)
    outs = [
        jax.ShapeDtypeStruct((2, page_len // 2, width), low),
        jax.ShapeDtypeStruct((2, page_len // 2, width), single),
    ]
    outs += [jax.ShapeDtypeStruct(s.shape, single) for s in shards]
    outs += [jax.ShapeDtypeStruct((1, 384), single)]
    by_name = dict(zip(WEIGHTS, shards))

    def vmem(*shape, kind=low):
        return pltpu.VMEM(shape, kind)

    size = lambda cut: (cut[1], cut[3])
    dma = pltpu.SemaphoreType.DMA
    scratch = [vmem(2, 4, 2, 2, *by_name[n].shape) for n in ("box", "out", "up", "down")]
    scratch += [vmem(2, 4, 2, *size(g[2])) for g in groups]
    for group in groups:
        for path, piece in group[-1]:
            scratch += [vmem(*landing_shape(path, hop, piece)) for hop in range(3)]
    scratch += [vmem(*s.shape, kind=single) for s in shards]
    scratch += [vmem(*full[n].shape) for n in ("box", "out")]
    scratch += [vmem(width, BOX_DIM), vmem(width, BOX_DIM)]
    scratch += [vmem(*kept[n].shape, kind=kept[n].dtype) for n in ("ct", "qkv", "table")]
    scratch += [vmem(page_len, BOX_DIM)]
    scratch += [
        vmem(*kept[n].shape, kind=kept[n].dtype)
        for n in ("o", "unit1", "inv1", "g", "d", "unit2", "low", "vec")
    ]
    scratch += [vmem(page_len, width)] * 3
    scratch += [vmem(2, page_len // 2, width), vmem(1, VECTORS + 128, kind=single)]
    scratch += [
        vmem(2, 4, 2, 2, 1, 384, kind=single),
        vmem(2, 4, 2, 1, 384, kind=single),
        vmem(4, 2, 1, 384, kind=single),
        vmem(4, 1, 384, kind=single),
        vmem(3, 1, 384, kind=single),
        vmem(1, 384, kind=single),
    ]
    scratch += [dma((SENDS,)), dma((len(semaphore_table(groups, 4)),))] + [dma((count,))] * 2
    scratch += [dma((3,))] * 2 + [dma((3,))] * 2 + [dma((2,))] * 2
    scratch += [dma((17,)), dma((2, 2)), dma((9,))]
    anywhere = pl.BlockSpec(memory_space=pl.ANY)
    operands = [full[n] for n in WEIGHTS] + list(kept.values())
    plan = (groups, page_len, width)
    results = pl.pallas_call(
        partial(backward_kernel, plan),
        out_shape=outs,
        in_specs=[anywhere] * len(operands),
        out_specs=[anywhere] * len(outs),
        scratch_shapes=scratch,
        compiler_params=pltpu.CompilerParams(
            collective_id=1, has_side_effects=True, vmem_limit_bytes=VMEM_BACK
        ),
    )(*operands)
    return results


VMEM_BACK = 63 * 2**20


def finish_kernel(*refs):
    count = len(refs) // 2
    ins, outs = refs[:count], refs[count:]
    for i in range(count - 1):
        outs[i][...] = ins[i][...]
    rows = jnp.broadcast_to(ins[-1][...], (8, 384))
    rows = pltpu.roll(rows, 384 - Place().vector_offset(), 1)
    outs[-1][...] = rows[0:1, : VECTORS // 32].reshape(VECTORS // 32)


def finish_call(results):
    outs = [jax.ShapeDtypeStruct(r.shape, r.dtype) for r in results[:-1]]
    outs += [jax.ShapeDtypeStruct((VECTORS // 32,), jnp.float32)]

    def half(shape):
        block = (shape[0] // 2,) + shape[1:]
        return pl.BlockSpec(block, lambda i: (i,) + (0,) * (len(shape) - 1))

    halves = [half(r.shape) for r in results[:-1]]
    return pl.pallas_call(
        finish_kernel,
        out_shape=outs,
        grid=(2,),
        in_specs=halves + [pl.BlockSpec((1, 384), lambda i: (0, 0))],
        out_specs=halves + [pl.BlockSpec((VECTORS // 32,), lambda i: (0,))],
        compiler_params=pltpu.CompilerParams(vmem_limit_bytes=VMEM_BACK),
    )(*results)


def fast_layer(tokens, boxes, lengths, wqkv, wbox, wout, wup, wdown, vectors, cotangent):
    shards = (wqkv, wbox, wout, wup, wdown)
    full, kept = forward_call(tokens, cotangent, boxes, lengths, vectors, shards)
    return tuple(finish_call(backward_call(full, kept, shards)))


def on_device(*args):
    tokens, wqkv, wbox, wdown = args[0], args[3], args[4], args[7]
    blocks, groups = lax.axis_size("blk"), lax.axis_size("dp")
    fits = (
        blocks == 2
        and groups == 16
        and tokens.shape[0] == 2
        and wqkv.shape == (48, 1152)
        and wdown.shape == (192, 384)
        and wbox.shape == (48, 2 * FREQ)
    )
    return fast_layer(*args) if fits else general_layer(*args)


def solution(mesh):
    in_specs = (
        P("dp", "blk", None),
        P(None, "dp", "blk"),
        P("dp"),
        P("dp", "blk"),
        P("dp", "blk"),
        P("dp", "blk"),
        P("dp", "blk"),
        P("dp", "blk"),
        P(("dp", "blk")),
        P("dp", "blk", None),
    )
    out_specs = (
        P("dp", "blk", None),
        P("dp", "blk", None),
        P("dp", "blk"),
        P("dp", "blk"),
        P("dp", "blk"),
        P("dp", "blk"),
        P("dp", "blk"),
        P(("dp", "blk")),
    )
    return jax.shard_map(
        on_device, mesh=mesh, in_specs=in_specs, out_specs=out_specs, check_vma=False
    )
```
